32 devices in a mesh: wide: 8 (over y, x, core), narrow: 4 (over z).
Axes of the slice: x: 2, y: 2, z: 4, core: 2. Of those that a mesh axis runs over, the one named last changes fastest.
Arguments:
- tokens: bfloat16 [8192, 768], P(('wide', 'narrow')), may hold values from -6 to 6
- lengths: int32 [32], P(('wide', 'narrow')), may hold values from 1 to 256, 4096 in all
- cotangent: bfloat16 [8192, 768], P(('wide', 'narrow')), may hold values from -6 to 6
- w_query: bfloat16 [768, 768], P(('wide', 'narrow')), may hold values from -0.21875 to 0.21875
- w_key: bfloat16 [768, 768], P(('wide', 'narrow')), may hold values from -0.21875 to 0.21875
- w_value: bfloat16 [768, 768], P(('wide', 'narrow')), may hold values from -0.21875 to 0.21875
- w_out: bfloat16 [768, 768], P(('wide', 'narrow')), may hold values from -0.875 to 0.875
- w_fc1: bfloat16 [768, 3072], P(None, ('wide', 'narrow')), may hold values from -0.21875 to 0.21875
- w_fc2: bfloat16 [3072, 768], P(('wide', 'narrow')), may hold values from -0.109375 to 0.109375
- fc1_bias: bfloat16 [3072], P(('wide', 'narrow')), may hold values from -3 to 3
- vectors: bfloat16 [15, 768], P(None, ('wide', 'narrow')), may hold values from -4 to 4
Outputs:
- output: bfloat16 [8192, 768], P(('wide', 'narrow'))
- input_grad: bfloat16 [8192, 768], P(('wide', 'narrow'))
- grad_query: float32 [768, 768], P(('wide', 'narrow'))
- grad_key: float32 [768, 768], P(('wide', 'narrow'))
- grad_value: float32 [768, 768], P(('wide', 'narrow'))
- grad_out: float32 [768, 768], P(('wide', 'narrow'))
- grad_fc1: float32 [768, 3072], P(None, ('wide', 'narrow'))
- grad_fc2: float32 [3072, 768], P(('wide', 'narrow'))
- grad_fc1_bias: float32 [3072], P(('wide', 'narrow'))
- grad_vectors: float32 [15, 768], P(None, ('wide', 'narrow'))
The draws below stay inside these ranges and needn't reach their ends.
Inputs may be any that keep to these rules, and one draw needn't show every extreme that they name: `lengths`: one slot has exactly 256 used rows in every draw.
All inputs are finite; a program needn't handle non-finite values. No bound on the sum of `lengths` on one device may be relied on, other than what follows from the above.
Results may differ from the reference program's by a relative error of at most 0.019.
Values may be sent and summed in bfloat16 or wider, within the bound.
A program may use at most 192 MiB of HBM per device.

```python
import math
from functools import partial
import jax
import jax.numpy as jnp
import numpy as np
from jax import lax

HEAD_SIZE = 64
D = 768
FF = 3072
STATE = 64
SEQ = 256
TOKENS = 8192
DEVICES = 32


def draw_vectors(key, part):
    key = jax.random.fold_in(key, 11)
    subkeys = jax.random.split(key, 3)
    base_draw = jnp.clip(jax.random.normal(subkeys[0], (15, D), jnp.float32), -4.0, 4.0)
    slow_end = 0.5 / SEQ
    fast_end = 1.0 / 16.0
    near_one = 1.0 + 0.3 * jax.random.uniform(subkeys[1], (15, D), jnp.float32, -1.0, 1.0)
    rates = jnp.exp(jax.random.uniform(subkeys[2], (D,), jnp.float32, math.log(slow_end), math.log(fast_end)))
    row_index = jnp.arange(15)[:, None]
    gain_rows = (row_index == 0) | (row_index == 12) | (row_index == 5)
    tap_rows = (row_index >= 6) & (row_index <= 8)
    scaled = jnp.where(gain_rows, near_one, jnp.where(row_index == 9, base_draw, jnp.where(tap_rows, 0.5 * base_draw, 0.3 * base_draw)))
    return jnp.where(row_index == 10, rates[None, :], scaled).astype(jnp.bfloat16)


def with_spikes(values, own_key, source, target, parts, factor):
    owner, partner = [(jnp.arange(values.shape[position]) // (values.shape[position] // parts)).reshape([-1 if axis == position else 1 for axis in range(values.ndim)]) for position in (source, target)]
    chosen = jax.random.permutation(own_key, parts)[partner]
    strong = (owner == chosen) | (owner == (partner + parts // 2) % parts)
    return jnp.where(strong, factor * values, values)


def levels(rng, shape, pieces, least, largest):
    level, own = 1.0, jax.random.fold_in(rng, 6)
    for position, blocks in pieces:
        heights = jnp.exp(jax.random.uniform(jax.random.fold_in(own, position), (blocks,), jnp.float32, least / len(pieces), largest / len(pieces)))
        level = level * jnp.repeat(heights, shape[position] // blocks).reshape([-1 if axis == position else 1 for axis in range(len(shape))])
    return level


def split_up(amount, total, reach, skew):
    loads = [(1 << 20) // math.isqrt(standing ** skew) + 1 for standing in range(2, amount + 1)]
    surplus, holding = total - reach - (amount - 1), [1] * (amount - 1)
    while surplus > 0:
        free = [i for i in range(amount - 1) if holding[i] < reach]
        pool, remaining = sum([loads[i] for i in free]), surplus
        for i in free:
            addition = min(reach - holding[i], max(1, remaining * loads[i] // pool), surplus)
            holding[i] = holding[i] + addition
            surplus = surplus - addition
    return np.array([reach] + holding)


def uneven(key, count, total, most, skew):
    if count == 2:
        one = jax.random.randint(key, (), max(1, total - most), min(most, total - 1) + 1)
        return jnp.stack([one, total - one])
    sizes = jnp.asarray(split_up(count, total, most, skew), jnp.int32)
    pairs = (count - 1) // 2
    source_of, taker = sizes[1:1 + 2 * pairs:2], sizes[2:2 + 2 * pairs:2]
    slack = jnp.minimum(source_of - 1, most - taker)
    passed = jax.random.randint(jax.random.fold_in(key, 1), (pairs,), 0, 1 << 20) % (slack + 1)
    sizes = sizes.at[1:1 + 2 * pairs:2].set(source_of - passed).at[2:2 + 2 * pairs:2].set(taker + passed)
    return sizes[jax.random.permutation(jax.random.fold_in(key, 2), count)]


def scatter_about(own_key, extent, spread, limit, cuts=(), kind=jnp.bfloat16):
    level = levels(own_key, extent, cuts, -0.22, 0.18) if cuts else 1.0
    values = jax.random.normal(own_key, extent, jnp.float32) * spread * level
    return jnp.minimum(jnp.maximum(values, -limit), limit).astype(kind)


def noise_with(key, extent, deviation, most, shards, heavy, held_as=jnp.bfloat16):
    entries = deviation * jax.random.normal(key, extent, jnp.float32)
    if shards:
        entries = entries * levels(key, extent, shards, -0.22, 0.18)
    return jnp.clip(with_spikes(entries, jax.random.fold_in(key, 3), *heavy), -most, most).astype(held_as)


def setup_inputs(seed: int = 0) -> dict:
    splits = jax.random.split(jax.random.key(seed), 12)
    tokens = scatter_about(splits[0], (TOKENS, D), 1.0, 6.0, ((0, 32),))
    lengths = uneven(splits[1], DEVICES, DEVICES * SEQ // 2, SEQ, 2).astype(jnp.int32)
    cotangent = noise_with(splits[2], (TOKENS, D), 1.0, 6.0, ((0, 32),), (0, 1, 32, 2.75))
    w_query = scatter_about(splits[3], (D, D), D ** -0.5, 0.21875, ((0, 32),))
    w_key = scatter_about(splits[4], (D, D), D ** -0.5, 0.21875, ((0, 32),))
    w_value = scatter_about(splits[5], (D, D), D ** -0.5, 0.21875, ((0, 32),))
    w_out = scatter_about(splits[6], (D, D), (D // 16) ** -0.5, 0.875, ((0, 32),))
    w_fc1 = scatter_about(splits[7], (D, FF), D ** -0.5, 0.21875, ((1, 32),))
    w_fc2 = scatter_about(splits[8], (FF, D), FF ** -0.5, 0.109375, ((0, 32),))
    fc1_bias = scatter_about(splits[9], (FF,), 0.3, 3.0, ((0, 32),))
    vectors = draw_vectors(jax.random.fold_in(splits[11], 71), 0)
    return dict(tokens=tokens, lengths=lengths, cotangent=cotangent, w_query=w_query, w_key=w_key, w_value=w_value, w_out=w_out, w_fc1=w_fc1, w_fc2=w_fc2, fc1_bias=fc1_bias, vectors=vectors)


EPSILON = 1e-05

@jax.custom_vjp
def low(v):
    return lax.optimization_barrier(v.astype(jnp.bfloat16)).astype(jnp.float32)

@jax.custom_vjp
def low_back(v):
    return v

def low_keep(v):
    return (low(v), None)

def low_pass(kept, grad):
    return (grad,)

def back_keep(v):
    return (v, None)

def back_low(kept, grad):
    return (low(grad),)
low.defvjp(low_keep, low_pass)
low_back.defvjp(back_keep, back_low)

def matmul_high(left, right):
    return jnp.dot(left, right, precision=lax.Precision.HIGHEST, preferred_element_type=jnp.float32)

def normalize(values):
    average = lax.optimization_barrier(jnp.mean(values, axis=-1, keepdims=True))
    centred = values - average
    variance = lax.optimization_barrier(jnp.mean(centred * centred, axis=-1, keepdims=True))
    return centred * lax.rsqrt(variance + EPSILON)

def shift_mix(key_raw, shift_taps):
    summed = key_raw * shift_taps[0]
    for offset in range(1, 4):
        delayed = jnp.concatenate([jnp.zeros((offset, key_raw.shape[1]), key_raw.dtype), key_raw[:-offset]], axis=0)
        summed = summed + delayed * shift_taps[offset]
    return summed

def kernel_rows(coefficient, decay_rate, length_all):
    distance = jnp.arange(length_all).astype(jnp.float32)
    decays = jnp.exp(-decay_rate[:, :, None] * distance[None, None, :])
    return lax.optimization_barrier(jnp.sum(coefficient[:, :, None] * decays, axis=1)) / STATE

def toeplitz(kernel_row):
    length_all = kernel_row.shape[0]
    wrapped = jnp.concatenate([kernel_row[:1], jnp.zeros((length_all,), kernel_row.dtype), kernel_row[:0:-1]])
    tiled_row = jnp.tile(wrapped, length_all)[:length_all * (2 * length_all - 1)]
    return tiled_row.reshape(length_all, 2 * length_all - 1)[:, :length_all]

def forward(valid_mask, residual, w_query, w_key, w_value, w_out, w_fc1, w_fc2, fc1_bias, vectors):
    seq_len = residual.shape[0]
    head_count = w_query.shape[1] // HEAD_SIZE
    normed = low(normalize(residual) * vectors[0] + vectors[1])
    queries = low(low_back(matmul_high(normed, w_query) + vectors[2]))
    key_raw = low_back(matmul_high(normed, w_key) + vectors[3])
    keys = low(shift_mix(key_raw, vectors[5:9]) * valid_mask)
    values = low(low_back(matmul_high(normed, w_value) + vectors[4]) * valid_mask)
    kernel = kernel_rows(vectors[9].reshape(head_count, STATE), vectors[10].reshape(head_count, STATE), seq_len)
    toeplitz_all = jax.vmap(toeplitz)(kernel)
    query_heads = queries.reshape(seq_len, head_count, HEAD_SIZE)
    key_heads = keys.reshape(seq_len, head_count, HEAD_SIZE)
    value_heads = values.reshape(seq_len, head_count, HEAD_SIZE)
    scores = low_back(jnp.einsum('thd,shd->hts', query_heads, key_heads, precision=lax.Precision.HIGHEST) / HEAD_SIZE)
    weights_mix = low(scores * toeplitz_all)
    mixed = jnp.einsum('hts,shd->thd', weights_mix, value_heads, precision=lax.Precision.HIGHEST).reshape(seq_len, head_count * HEAD_SIZE)
    mixed_out = low(low_back(mixed) * valid_mask)
    hidden = residual + low_back(matmul_high(mixed_out, w_out) + vectors[11])
    normed2 = low(normalize(hidden) * vectors[12] + vectors[13])
    pre_act = low_back(matmul_high(normed2, w_fc1) + fc1_bias)
    activated = low(jax.nn.gelu(pre_act))
    return hidden + matmul_high(activated, w_fc2) + vectors[14]

def reference(tokens, lengths, cotangent, w_query, w_key, w_value, w_out, w_fc1, w_fc2, fc1_bias, vectors):
    weights = tuple((matrix.astype(jnp.float32) for matrix in (w_query, w_key, w_value, w_out, w_fc1, w_fc2, fc1_bias, vectors)))
    width = tokens.shape[1]
    seq_tokens = tokens.astype(jnp.float32).reshape(DEVICES, SEQ, width)
    seq_cot = cotangent.astype(jnp.float32).reshape(DEVICES, SEQ, width)

    def seq_step(totals, seq_item):
        residual, grad_top, seq_length = seq_item
        valid_mask = (jnp.arange(SEQ) < seq_length).astype(jnp.float32)[:, None]
        result, pullback = jax.vjp(partial(forward, valid_mask), residual, *weights)
        gradients = pullback(grad_top)
        totals = tuple((running + fresh for running, fresh in zip(totals, gradients[1:])))
        return (totals, (result.astype(jnp.bfloat16), gradients[0].astype(jnp.bfloat16)))
    start = tuple((jnp.zeros_like(matrix) for matrix in weights))
    totals, (results, input_grads) = lax.scan(seq_step, start, (seq_tokens, seq_cot, lengths))
    output = results.reshape(DEVICES * SEQ, width)
    input_grad = input_grads.reshape(DEVICES * SEQ, width)
    return (output, input_grad, totals[0], totals[1], totals[2], totals[3], totals[4], totals[5], totals[6], totals[7])
```

```python
import math
from functools import partial
from types import SimpleNamespace

import jax
import jax.numpy as jnp
from jax import lax
from jax.experimental import pallas as pl
from jax.experimental.pallas import tpu as pltpu
from jax.sharding import PartitionSpec as P

HEAD_SIZE = 64
STATE = 64


EPSILON = 1e-05


def normalize(values):
    average = jnp.mean(values, axis=-1, keepdims=True)
    centred = values - average
    variance = jnp.mean(centred * centred, axis=-1, keepdims=True)
    inverse = lax.rsqrt(variance + EPSILON)
    return (centred * inverse, inverse)


def norm_back(grad_in, scaled, inverse):
    first = jnp.mean(grad_in, axis=-1, keepdims=True)
    second = jnp.mean(grad_in * scaled, axis=-1, keepdims=True)
    return inverse * (grad_in - first - scaled * second)


def shift_mix(key_raw, shift_taps):
    summed = key_raw * shift_taps[0]
    for offset in range(1, 4):
        delayed = jnp.concatenate(
            [jnp.zeros((offset, key_raw.shape[1]), key_raw.dtype), key_raw[:-offset]], axis=0
        )
        summed = summed + delayed * shift_taps[offset]
    return summed


def kernel_rows(coefficient, decay_rate, length_all):
    distance = jnp.arange(length_all).astype(jnp.float32)
    decays = jnp.exp(-decay_rate[:, :, None] * distance[None, None, :])
    return jnp.sum(coefficient[:, :, None] * decays, axis=1) / STATE


def toeplitz(kernel_row):
    length_all = kernel_row.shape[0]
    wrapped = jnp.concatenate(
        [kernel_row[:1], jnp.zeros((length_all,), kernel_row.dtype), kernel_row[:0:-1]]
    )
    tiled_row = jnp.tile(wrapped, length_all)[: length_all * (2 * length_all - 1)]
    return tiled_row.reshape(length_all, 2 * length_all - 1)[:, :length_all]


def split_heads(values, row_count):
    return values.reshape(row_count, -1, HEAD_SIZE).transpose(1, 0, 2)


def merge_heads(per_head):
    head_count = per_head.shape[0]
    row_count = per_head.shape[1]
    merged = per_head.transpose(1, 0, 2).reshape(row_count, head_count * HEAD_SIZE)
    return merged


def pack_rows(matrices, shard_count):
    return jnp.concatenate(
        [matrix.reshape(shard_count, -1) for matrix in matrices], axis=1
    ).reshape(-1)


def unpack_rows(flat, matrices, shard_count):
    pieces = []
    offset = 0
    for matrix in matrices:
        rows_own = matrix.shape[0] // shard_count
        extent = matrix.size // shard_count
        pieces.append(flat[offset : offset + extent].reshape((rows_own,) + matrix.shape[1:]))
        offset = offset + extent
    return pieces


def mixer_forward(queries, keys, values, kernel, row_count):

    def head_forward(parts):
        query_head, key_head, value_head, kernel_row = parts
        scores = jnp.dot(query_head, key_head.T, preferred_element_type=jnp.float32) / HEAD_SIZE
        weights_mix = (scores * toeplitz(kernel_row)).astype(jnp.bfloat16)
        return jnp.dot(weights_mix, value_head, preferred_element_type=jnp.float32)

    per_head = lax.map(
        head_forward,
        (
            split_heads(queries, row_count),
            split_heads(keys, row_count),
            split_heads(values, row_count),
            kernel,
        ),
    )
    return merge_heads(per_head)


def mixer_backward(queries, keys, values, grad_mixed, kernel, row_count):

    def head_backward(parts):
        query_head, key_head, value_head, grad_head, kernel_row = parts
        scores = jnp.dot(query_head, key_head.T, preferred_element_type=jnp.float32) / HEAD_SIZE
        toeplitz_mat, pullback = jax.vjp(toeplitz, kernel_row)
        weights_mix = (scores * toeplitz_mat).astype(jnp.bfloat16)
        grad_weights = jnp.dot(grad_head, value_head.T, preferred_element_type=jnp.float32)
        grad_values = jnp.dot(weights_mix.T, grad_head, preferred_element_type=jnp.float32)
        grad_scores = (grad_weights * toeplitz_mat).astype(jnp.bfloat16)
        grad_queries = (
            jnp.dot(grad_scores, key_head, preferred_element_type=jnp.float32) / HEAD_SIZE
        )
        grad_keys = (
            jnp.dot(grad_scores.T, query_head, preferred_element_type=jnp.float32) / HEAD_SIZE
        )
        grad_kernel = pullback(grad_weights * scores)[0]
        return (grad_queries, grad_keys, grad_values, grad_kernel)

    head_grads = lax.map(
        head_backward,
        (
            split_heads(queries, row_count),
            split_heads(keys, row_count),
            split_heads(values, row_count),
            split_heads(grad_mixed, row_count),
            kernel,
        ),
    )
    grad_kernel = head_grads[3]
    return (
        merge_heads(head_grads[0]),
        merge_heads(head_grads[1]),
        merge_heads(head_grads[2]),
        grad_kernel,
    )


def on_device(
    tokens, lengths, cotangent, w_query, w_key, w_value, w_out, w_fc1, w_fc2, fc1_bias, vectors
):
    shard_count = lax.axis_size(("wide", "narrow"))
    gathered = (
        lax.all_gather(w_query, ("wide", "narrow"), axis=0, tiled=True),
        lax.all_gather(w_key, ("wide", "narrow"), axis=0, tiled=True),
        lax.all_gather(w_value, ("wide", "narrow"), axis=0, tiled=True),
        lax.all_gather(w_out, ("wide", "narrow"), axis=0, tiled=True),
        lax.all_gather(w_fc1, ("wide", "narrow"), axis=1, tiled=True),
        lax.all_gather(w_fc2, ("wide", "narrow"), axis=0, tiled=True),
        lax.all_gather(fc1_bias, ("wide", "narrow"), axis=0, tiled=True),
        lax.all_gather(vectors, ("wide", "narrow"), axis=1, tiled=True),
    )
    query_full, key_full, value_full, out_full, fc1_full, fc2_full, bias_full, vector_full = (
        gathered
    )
    params = vector_full.astype(jnp.float32)
    fc1_shift = bias_full.astype(jnp.float32)
    seq_len = tokens.shape[0]
    head_count = params.shape[1] // HEAD_SIZE
    seq_length = lengths[0]
    valid_mask = (jnp.arange(seq_len) < seq_length).astype(jnp.float32)[:, None]
    residual = tokens.astype(jnp.float32)
    scaled1, inverse1 = normalize(residual)
    normed = (scaled1 * params[0] + params[1]).astype(jnp.bfloat16)
    queries = (jnp.dot(normed, query_full, preferred_element_type=jnp.float32) + params[2]).astype(
        jnp.bfloat16
    )
    key_raw = jnp.dot(normed, key_full, preferred_element_type=jnp.float32) + params[3]
    keys = (shift_mix(key_raw, params[5:9]) * valid_mask).astype(jnp.bfloat16)
    values = (
        (jnp.dot(normed, value_full, preferred_element_type=jnp.float32) + params[4]) * valid_mask
    ).astype(jnp.bfloat16)
    coefficient = params[9].reshape(head_count, STATE)
    decay_rate = params[10].reshape(head_count, STATE)
    kernel_fn = partial(kernel_rows, length_all=seq_len)
    kernel, kernel_pull = jax.vjp(kernel_fn, coefficient, decay_rate)
    mixed = mixer_forward(queries, keys, values, kernel, seq_len)
    mixed_out = (mixed * valid_mask).astype(jnp.bfloat16)
    hidden = (
        residual + jnp.dot(mixed_out, out_full, preferred_element_type=jnp.float32) + params[11]
    )
    scaled2, inverse2 = normalize(hidden)
    normed2 = (scaled2 * params[12] + params[13]).astype(jnp.bfloat16)
    pre_act = jnp.dot(normed2, fc1_full, preferred_element_type=jnp.float32) + fc1_shift
    activated = jax.nn.gelu(pre_act).astype(jnp.bfloat16)
    output = (
        hidden + jnp.dot(activated, fc2_full, preferred_element_type=jnp.float32) + params[14]
    ).astype(jnp.bfloat16)
    again = (
        lax.all_gather(w_query, ("wide", "narrow"), axis=0, tiled=True),
        lax.all_gather(w_key, ("wide", "narrow"), axis=0, tiled=True),
        lax.all_gather(w_value, ("wide", "narrow"), axis=0, tiled=True),
        lax.all_gather(w_out, ("wide", "narrow"), axis=0, tiled=True),
        lax.all_gather(w_fc1, ("wide", "narrow"), axis=1, tiled=True),
        lax.all_gather(w_fc2, ("wide", "narrow"), axis=0, tiled=True),
        lax.all_gather(fc1_bias, ("wide", "narrow"), axis=0, tiled=True),
        lax.all_gather(vectors, ("wide", "narrow"), axis=1, tiled=True),
    )
    query_back, key_back, value_back, out_back, fc1_back, fc2_back = (
        again[0],
        again[1],
        again[2],
        again[3],
        again[4],
        again[5],
    )
    grad_top = cotangent.astype(jnp.float32)
    grad_fc2 = jnp.dot(activated.T, cotangent, preferred_element_type=jnp.float32)
    grad_activated = jnp.dot(cotangent, fc2_back.T, preferred_element_type=jnp.float32)
    gelu_value, gelu_pull = jax.vjp(jax.nn.gelu, pre_act)
    grad_pre = gelu_pull(grad_activated)[0].astype(jnp.bfloat16)
    grad_fc1_turned = jnp.dot(grad_pre.T, normed2, preferred_element_type=jnp.float32)
    grad_fc1_bias = jnp.sum(grad_pre.astype(jnp.float32), axis=0)[:, None]
    mlp_terms = [grad_fc1_turned, grad_fc2, grad_fc1_bias]
    mlp_flat = lax.psum_scatter(
        pack_rows(mlp_terms, shard_count), ("wide", "narrow"), scatter_dimension=0, tiled=True
    )
    mlp_sums = unpack_rows(mlp_flat, mlp_terms, shard_count)
    grad_normed2 = jnp.dot(grad_pre, fc1_back.T, preferred_element_type=jnp.float32)
    grad_hidden = grad_top + norm_back(grad_normed2 * params[12], scaled2, inverse2)
    grad_attn = grad_hidden.astype(jnp.bfloat16)
    grad_out = jnp.dot(mixed_out.T, grad_attn, preferred_element_type=jnp.float32)
    grad_mixed = (
        jnp.dot(grad_attn, out_back.T, preferred_element_type=jnp.float32) * valid_mask
    ).astype(jnp.bfloat16)
    grad_q, grad_k, grad_v, grad_kernel = mixer_backward(
        queries, keys, values, grad_mixed, kernel, seq_len
    )
    grad_queries = grad_q.astype(jnp.bfloat16)
    grad_values = (grad_v * valid_mask).astype(jnp.bfloat16)
    shift_value, shift_pull = jax.vjp(shift_mix, key_raw, params[5:9])
    grad_key_full, grad_taps = shift_pull(grad_k * valid_mask)
    grad_key_raw = grad_key_full.astype(jnp.bfloat16)
    grad_query = jnp.dot(normed.T, grad_queries, preferred_element_type=jnp.float32)
    grad_key = jnp.dot(normed.T, grad_key_raw, preferred_element_type=jnp.float32)
    grad_value = jnp.dot(normed.T, grad_values, preferred_element_type=jnp.float32)
    grad_normed = jnp.dot(grad_queries, query_back.T, preferred_element_type=jnp.float32)
    grad_normed = grad_normed + jnp.dot(
        grad_key_raw, key_back.T, preferred_element_type=jnp.float32
    )
    grad_normed = grad_normed + jnp.dot(
        grad_values, value_back.T, preferred_element_type=jnp.float32
    )
    input_grad = (grad_hidden + norm_back(grad_normed * params[0], scaled1, inverse1)).astype(
        jnp.bfloat16
    )
    grad_coef, grad_rate = kernel_pull(grad_kernel)
    grad_vectors = jnp.concatenate(
        [
            jnp.sum(grad_normed * scaled1, axis=0)[None],
            jnp.sum(grad_normed, axis=0)[None],
            jnp.sum(grad_queries.astype(jnp.float32), axis=0)[None],
            jnp.sum(grad_key_raw.astype(jnp.float32), axis=0)[None],
            jnp.sum(grad_values.astype(jnp.float32), axis=0)[None],
            grad_taps,
            grad_coef.reshape(1, -1),
            grad_rate.reshape(1, -1),
            jnp.sum(grad_attn.astype(jnp.float32), axis=0)[None],
            jnp.sum(grad_normed2 * scaled2, axis=0)[None],
            jnp.sum(grad_normed2, axis=0)[None],
            jnp.sum(grad_top, axis=0)[None],
        ],
        axis=0,
    )
    mixer_terms = [grad_query, grad_key, grad_value, grad_out, grad_vectors.T]
    mixer_flat = lax.psum_scatter(
        pack_rows(mixer_terms, shard_count), ("wide", "narrow"), scatter_dimension=0, tiled=True
    )
    mixer_sums = unpack_rows(mixer_flat, mixer_terms, shard_count)
    return (
        output,
        input_grad,
        mixer_sums[0],
        mixer_sums[1],
        mixer_sums[2],
        mixer_sums[3],
        mlp_sums[0].T,
        mlp_sums[1],
        mlp_sums[2].reshape(-1),
        mixer_sums[4].T,
    )


f32, bf16 = jnp.float32, jnp.bfloat16
MESH = pl.DeviceIdType.MESH


def dg(left, right, left_dim, right_dim):
    return lax.dot_general(
        left, right, (((left_dim,), (right_dim,)), ((), ())), preferred_element_type=f32
    )


def when(condition, body):
    if condition is None:
        body()
    else:
        pl.when(condition)(body)


def both(first, second):
    if first is None:
        return second
    if second is None:
        return first
    return jnp.logical_and(first, second)


class Links:
    def __init__(self, depth):
        wide, z = lax.axis_index("wide"), lax.axis_index("narrow")
        self.depth = depth
        self.z, self.core = z, lax.rem(wide, 2)
        self.x, self.y = lax.rem(lax.div(wide, 2), 2), lax.div(wide, 4)
        self.me = self.y * 2 + self.x
        self.xs = self.y * 2 + (1 - self.x)
        self.ys = (1 - self.y) * 2 + self.x
        self.ds = (1 - self.y) * 2 + (1 - self.x)
        self.sib_dev = (self.me * 2 + (1 - self.core), z)
        self.x_dev = (self.xs * 2 + self.core, z)
        self.y_dev = (self.ys * 2 + self.core, z)
        self.up_dev = (wide, z + 1)
        self.down_dev = (wide, z - 1)
        self.has_up = z < depth - 1
        self.has_down = z > 0
        self.pending = []

    def barrier(self):
        semaphore = pltpu.get_barrier_semaphore()

        def greet(device):
            pl.semaphore_signal(semaphore, inc=1, device_id=device, device_id_type=MESH)

        for device in (self.sib_dev, self.x_dev, self.y_dev):
            greet(device)
        pl.when(self.has_up)(lambda: greet(self.up_dev))
        pl.when(self.has_down)(lambda: greet(self.down_dev))
        peers = 3 + self.has_up.astype(jnp.int32) + self.has_down.astype(jnp.int32)
        pl.semaphore_wait(semaphore, peers)

    def start(self, condition, source, target, send, receive, device):
        def build():
            return pltpu.make_async_remote_copy(
                src_ref=source(),
                dst_ref=target(),
                send_sem=send(),
                recv_sem=receive(),
                device_id=device,
                device_id_type=MESH,
            )

        when(condition, lambda: build().start())
        self.pending.append((condition, build))

    def arrive(self, target, receive):
        pltpu.make_async_remote_copy(
            src_ref=target,
            dst_ref=target,
            send_sem=receive,
            recv_sem=receive,
            device_id=self.sib_dev,
            device_id_type=MESH,
        ).wait_recv()

    def drain(self):
        for condition, build in self.pending:
            when(condition, lambda build=build: build().wait_send())
        self.pending = []


def gather_z_first(k, buf, index, low, rows, half, ss, rs, sib_index=None):
    depth = k.depth

    def block(yx, zs, lo=0, n=rows):
        return buf.at[index(yx, zs), pl.ds(low + lo, n)]

    def send(condition, yx, zs, lo, n, device, s, r):
        ref = lambda: block(yx, zs, lo, n)
        k.start(condition, ref, ref, lambda: ss.at[s], lambda: rs.at[r], device)

    def to_sib(condition, yx, zs):
        if sib_index is not None:
            send(condition, yx, zs, 0, rows, k.sib_dev, 6 * depth + yx * depth + zs, 5 * depth + yx * depth + zs)

    def outward(condition, zs):
        send(condition, k.me, zs, 0, rows, k.x_dev, 2 * depth + zs, depth + zs)
        send(condition, k.me, zs, 0, rows, k.y_dev, 3 * depth + zs, 2 * depth + zs)
        to_sib(condition, k.me, zs)

    def along(condition, zs, up, down):
        if up:
            send(both(condition, k.has_up), k.me, zs, 0, rows, k.up_dev, zs, zs)
        if down:
            send(both(condition, k.has_down), k.me, zs, 0, rows, k.down_dev, depth + zs, zs)

    def z_step(d):
        for condition, zs, up in ((k.z >= d, k.z - d, True), (k.z + d < depth, k.z + d, False)):
            pl.when(condition)(lambda zs=zs: k.arrive(block(k.me, zs), rs.at[zs]))
            along(condition, zs, up, not up)
            outward(condition, zs)

    def places(d):
        if d == 0:
            return ((None, k.z),)
        return ((k.z >= d, k.z - d), (k.z + d < depth, k.z + d))

    def xy_step(d):
        for condition, zs in places(d):
            when(condition, lambda zs=zs: k.arrive(block(k.xs, zs), rs.at[depth + zs]))
            send(condition, k.xs, zs, 0, half, k.y_dev, 5 * depth + zs, 4 * depth + zs)
            to_sib(condition, k.xs, zs)
            when(condition, lambda zs=zs: k.arrive(block(k.ys, zs), rs.at[2 * depth + zs]))
            send(condition, k.ys, zs, half, rows - half, k.x_dev, 4 * depth + zs, 3 * depth + zs)
            to_sib(condition, k.ys, zs)

    def diagonal(d):
        for condition, zs in places(d):
            when(condition, lambda zs=zs: k.arrive(block(k.ds, zs, 0, half), rs.at[4 * depth + zs]))
            when(condition, lambda zs=zs: k.arrive(block(k.ds, zs, half, rows - half), rs.at[3 * depth + zs]))
            to_sib(condition, k.ds, zs)

    along(None, k.z, True, True)
    outward(None, k.z)
    yield
    for d in range(1, depth):
        z_step(d)
        yield
        xy_step(d - 1)
        yield
    xy_step(depth - 1)
    yield
    for d in range(depth):
        diagonal(d)
    yield
    if sib_index is not None:
        for yx in range(4):
            for zs in range(depth):
                k.arrive(buf.at[sib_index(yx, zs), pl.ds(low, rows)], rs.at[5 * depth + yx * depth + zs])
    yield


def gather_z_last(k, buf, index, low, rows, half, ss, rs):
    depth = k.depth
    yx_of = (k.me, k.xs, k.ys, k.ds)

    def block(yx, zs, lo=0, n=rows):
        return buf.at[index(yx, zs), pl.ds(low + lo, n)]

    def send(condition, yx, zs, lo, n, device, s, r):
        ref = lambda: block(yx, zs, lo, n)
        k.start(condition, ref, ref, lambda: ss.at[s], lambda: rs.at[r], device)

    def along(condition, which, zs, up, down):
        yx = yx_of[which]
        place = which * depth + zs
        if up:
            send(both(condition, k.has_up), yx, zs, 0, rows, k.up_dev, 4 + place, 4 + place)
        if down:
            send(both(condition, k.has_down), yx, zs, 0, rows, k.down_dev, 4 + 4 * depth + place, 4 + place)

    def z_step(which, d):
        for condition, zs, up in ((k.z >= d, k.z - d, True), (k.z + d < depth, k.z + d, False)):
            pl.when(condition)(
                lambda zs=zs: k.arrive(block(yx_of[which], zs), rs.at[4 + which * depth + zs])
            )
            along(condition, which, zs, up, not up)

    send(None, k.me, k.z, 0, rows, k.x_dev, 0, 0)
    send(None, k.me, k.z, 0, rows, k.y_dev, 1, 1)
    along(None, 0, k.z, True, True)
    yield
    k.arrive(block(k.xs, k.z), rs.at[0])
    send(None, k.xs, k.z, 0, half, k.y_dev, 2, 2)
    along(None, 1, k.z, True, True)
    k.arrive(block(k.ys, k.z), rs.at[1])
    send(None, k.ys, k.z, half, rows - half, k.x_dev, 3, 3)
    along(None, 2, k.z, True, True)
    yield
    k.arrive(block(k.ds, k.z, 0, half), rs.at[2])
    k.arrive(block(k.ds, k.z, half, rows - half), rs.at[3])
    along(None, 3, k.z, True, True)
    yield
    for d in range(1, depth):
        for which in range(4):
            z_step(which, d)
        yield


def add_into(ref, *others):
    total = ref[...].astype(f32)
    for other in others:
        total = total + other[...].astype(f32)
    ref[...] = total.astype(ref.dtype)


def scatter_z_last(k, buf, index, low, rows, half, slots, ss, rs, finish):
    depth = k.depth
    from_x_diag, from_y_diag, from_x, from_y, from_up, from_down = slots
    order = ([0, depth - 1] + list(range(1, depth - 1)))[:depth]

    def block(yx, zd, lo=0, n=rows):
        return buf.at[index(yx, zd), pl.ds(low + lo, n)]

    def send(condition, source, target, device, s, r):
        k.start(condition, source, target, lambda: ss.at[s], lambda: rs.at[r], device)

    rest = rows - half
    for zd in order:
        send(None, lambda zd=zd: block(k.ds, zd, 0, half), lambda zd=zd: from_y_diag.at[zd], k.y_dev, zd, zd)
        send(None, lambda zd=zd: block(k.ds, zd, half, rest), lambda zd=zd: from_x_diag.at[zd], k.x_dev, depth + zd, depth + zd)
    yield
    for zd in order:
        send(None, lambda zd=zd: block(k.xs, zd, half, rest), lambda zd=zd: from_x.at[zd, pl.ds(half, rest)], k.x_dev, 2 * depth + zd, 2 * depth + zd)
        send(None, lambda zd=zd: block(k.ys, zd, 0, half), lambda zd=zd: from_y.at[zd, pl.ds(0, half)], k.y_dev, 3 * depth + zd, 3 * depth + zd)
    yield
    for zd in order:
        k.arrive(from_y_diag.at[zd], rs.at[zd])
        add_into(block(k.xs, zd, 0, half), from_y_diag.at[zd])
        send(None, lambda zd=zd: block(k.xs, zd, 0, half), lambda zd=zd: from_x.at[zd, pl.ds(0, half)], k.x_dev, 4 * depth + zd, 4 * depth + zd)
        k.arrive(from_x_diag.at[zd], rs.at[depth + zd])
        add_into(block(k.ys, zd, half, rest), from_x_diag.at[zd])
        send(None, lambda zd=zd: block(k.ys, zd, half, rest), lambda zd=zd: from_y.at[zd, pl.ds(half, rest)], k.y_dev, 5 * depth + zd, 5 * depth + zd)
        yield

    def collect(zd):
        k.arrive(from_x.at[zd, pl.ds(half, rest)], rs.at[2 * depth + zd])
        k.arrive(from_y.at[zd, pl.ds(0, half)], rs.at[3 * depth + zd])
        k.arrive(from_x.at[zd, pl.ds(0, half)], rs.at[4 * depth + zd])
        k.arrive(from_y.at[zd, pl.ds(half, rest)], rs.at[5 * depth + zd])
        add_into(block(k.me, zd), from_x.at[zd], from_y.at[zd])

    for zd in order:
        collect(zd)

        def down(zd=zd):
            def take():
                k.arrive(from_up.at[zd], rs.at[6 * depth + zd])
                add_into(block(k.me, zd), from_up.at[zd])

            pl.when(k.has_up)(take)

        def up(zd=zd):
            def take():
                k.arrive(from_down.at[zd], rs.at[7 * depth + zd])
                add_into(block(k.me, zd), from_down.at[zd])

            pl.when(k.has_down)(take)

        pl.when(k.z > zd)(down)
        send(k.z > zd, lambda zd=zd: block(k.me, zd), lambda zd=zd: from_up.at[zd], k.down_dev, 6 * depth + zd, 6 * depth + zd)
        pl.when(k.z < zd)(up)
        send(k.z < zd, lambda zd=zd: block(k.me, zd), lambda zd=zd: from_down.at[zd], k.up_dev, 7 * depth + zd, 7 * depth + zd)
        yield

    finish(block(k.me, k.z), False)

    def last_up():
        k.arrive(from_up.at[k.z], rs.at[6 * depth + k.z])
        finish(from_up.at[k.z], True)

    def last_down():
        k.arrive(from_down.at[k.z], rs.at[7 * depth + k.z])
        finish(from_down.at[k.z], True)

    pl.when(k.has_up)(last_up)
    pl.when(k.has_down)(last_down)
    yield


def scatter_z_first(k, buf, index, low, rows, half, slots, ss, rs, finish):
    depth = k.depth
    from_x_diag, from_y_diag, from_x, from_y, from_up, from_down = slots
    yx_of = (k.me, k.xs, k.ys, k.ds)
    order = ([0, depth - 1] + list(range(1, depth - 1)))[:depth]
    rest = rows - half

    def block(yx, zd, lo=0, n=rows):
        return buf.at[index(yx, zd), pl.ds(low + lo, n)]

    def send(condition, source, target, device, s, r):
        k.start(condition, source, target, lambda: ss.at[s], lambda: rs.at[r], device)

    def z_step(zd, which):
        yx = yx_of[which]
        place = which * depth + zd

        def down():
            def take():
                k.arrive(from_up.at[place], rs.at[place])
                add_into(block(yx, zd), from_up.at[place])

            pl.when(k.has_up)(take)

        def up():
            def take():
                k.arrive(from_down.at[place], rs.at[4 * depth + place])
                add_into(block(yx, zd), from_down.at[place])

            pl.when(k.has_down)(take)

        pl.when(k.z > zd)(down)
        send(k.z > zd, lambda: block(yx, zd), lambda: from_up.at[place], k.down_dev, place, place)
        pl.when(k.z < zd)(up)
        send(k.z < zd, lambda: block(yx, zd), lambda: from_down.at[place], k.up_dev, 4 * depth + place, 4 * depth + place)

    for zd in order:
        for which in (3, 1, 2, 0):
            z_step(zd, which)
        yield

    def own(which):
        yx = yx_of[which]
        place = which * depth + k.z

        def take_up():
            k.arrive(from_up.at[place], rs.at[place])
            add_into(block(yx, k.z), from_up.at[place])

        def take_down():
            k.arrive(from_down.at[place], rs.at[4 * depth + place])
            add_into(block(yx, k.z), from_down.at[place])

        pl.when(k.has_up)(take_up)
        pl.when(k.has_down)(take_down)

    base = 8 * depth
    own(3)
    send(None, lambda: block(k.ds, k.z, 0, half), lambda: from_y_diag.at[0], k.y_dev, base, base)
    send(None, lambda: block(k.ds, k.z, half, rest), lambda: from_x_diag.at[0], k.x_dev, base + 1, base + 1)
    own(1)
    send(None, lambda: block(k.xs, k.z, half, rest), lambda: from_x.at[0, pl.ds(half, rest)], k.x_dev, base + 2, base + 2)
    own(2)
    send(None, lambda: block(k.ys, k.z, 0, half), lambda: from_y.at[0, pl.ds(0, half)], k.y_dev, base + 3, base + 3)
    own(0)
    yield
    k.arrive(from_y_diag.at[0], rs.at[base])
    add_into(block(k.xs, k.z, 0, half), from_y_diag.at[0])
    send(None, lambda: block(k.xs, k.z, 0, half), lambda: from_x.at[0, pl.ds(0, half)], k.x_dev, base + 4, base + 4)
    k.arrive(from_x_diag.at[0], rs.at[base + 1])
    add_into(block(k.ys, k.z, half, rest), from_x_diag.at[0])
    send(None, lambda: block(k.ys, k.z, half, rest), lambda: from_y.at[0, pl.ds(half, rest)], k.y_dev, base + 5, base + 5)
    yield
    finish(block(k.me, k.z), False)
    k.arrive(from_x.at[0, pl.ds(half, rest)], rs.at[base + 2])
    k.arrive(from_x.at[0, pl.ds(0, half)], rs.at[base + 4])
    finish(from_x.at[0], True)
    k.arrive(from_y.at[0, pl.ds(0, half)], rs.at[base + 3])
    k.arrive(from_y.at[0, pl.ds(half, rest)], rs.at[base + 5])
    finish(from_y.at[0], True)
    yield


def advance(steps, count=None):
    if count is None:
        for _ in steps:
            pass
    else:
        for _ in range(count):
            next(steps, None)


SEQ, WIDTH, UNITS = 256, 768, 96
HEADS = WIDTH // HEAD_SIZE


def row_loop(total, step, body):
    def once(i, carry):
        body(pl.multiple_of(i * step, step), step)
        return carry

    lax.fori_loop(0, total // step, once, 0)


def lane_shift(values, offset, left):
    extent = values.shape[1]
    lane = lax.broadcasted_iota(jnp.int32, values.shape, 1)
    if left:
        return jnp.where(lane < extent - offset, pltpu.roll(values, extent - offset, 1), 0.0)
    return jnp.where(lane >= offset, pltpu.roll(values, offset, 1), 0.0)


def head_rows(h):
    return pl.ds(pl.multiple_of(h * HEAD_SIZE, HEAD_SIZE), HEAD_SIZE)


def scratch_of(depth):
    devices, blocks = 8 * depth, 4 * depth
    table = {
        "qk": ((devices, UNITS, WIDTH), bf16),
        "ff": ((blocks, 2 * UNITS, WIDTH), bf16),
        "sm": ((devices, 16, 128), f32),
        "gff": ((blocks, 2 * UNITS, WIDTH), bf16),
        "gs": ((devices, 16, 128), f32),
        "sr": ((blocks, UNITS, WIDTH), bf16),
        "srs": ((blocks, 16, 128), f32),
        "wq": ((WIDTH, WIDTH), bf16),
        "wk": ((WIDTH, WIDTH), bf16),
        "wv": ((WIDTH, WIDTH), bf16),
        "wo": ((WIDTH, WIDTH), bf16),
        "s1": ((SEQ, WIDTH), f32),
        "i1": ((SEQ, 128), f32),
        "nm": ((SEQ, WIDTH), bf16),
        "hid": ((SEQ, WIDTH), f32),
        "s2": ((SEQ, WIDTH), f32),
        "i2": ((SEQ, 128), f32),
        "n2": ((2 * SEQ, WIDTH), bf16),
        "ct": ((2 * SEQ, WIDTH), bf16),
        "outp": ((2 * SEQ, WIDTH), f32),
        "dn2": ((2 * SEQ, WIDTH), f32),
        "outr": ((SEQ, WIDTH), f32),
        "dn2r": ((SEQ, WIDTH), f32),
        "act": ((2 * SEQ, UNITS * depth), bf16),
        "dp": ((2 * SEQ, UNITS * depth), bf16),
        "da": ((SEQ, WIDTH), bf16),
        "dn": ((SEQ, WIDTH), f32),
        "nmt": ((WIDTH, SEQ), bf16),
        "qt": ((WIDTH, SEQ), bf16),
        "kt": ((WIDTH, SEQ), bf16),
        "vt": ((WIDTH, SEQ), bf16),
        "krt": ((WIDTH, SEQ), f32),
        "mt": ((WIDTH, SEQ), bf16),
        "dmt": ((WIDTH, SEQ), bf16),
        "dqt": ((WIDTH, SEQ), bf16),
        "dkt": ((WIDTH, SEQ), bf16),
        "dvt": ((WIDTH, SEQ), bf16),
        "kft": ((WIDTH, SEQ), bf16),
        "vft": ((WIDTH, SEQ), bf16),
        "ex": ((WIDTH, SEQ), f32),
        "tt": ((HEADS, SEQ, SEQ), f32),
        "vec": ((16, WIDTH), f32),
        "vecc": ((WIDTH, 128), f32),
        "colsum": ((WIDTH, 128), f32),
        "gvec": ((16, WIDTH), f32),
        "bias": ((4, 8, UNITS * depth), f32),
        "gbias": ((blocks, 8, 128), f32),
    }
    for name, rows, half, lanes, kind in (
        ("q", UNITS, UNITS // 2, WIDTH, bf16),
        ("b", 128, 64, WIDTH, bf16),
        ("t", 16, 8, 128, f32),
    ):
        table["r" + name + "dx"] = ((depth, rows - half, lanes), kind)
        table["r" + name + "dy"] = ((depth, half, lanes), kind)
        for place in ("x", "y", "u", "d"):
            table["r" + name + place] = ((depth, rows, lanes), kind)
    table["rcdx"] = table["rcdy"] = ((1, 32, WIDTH), bf16)
    table["rcx"] = table["rcy"] = ((1, 64, WIDTH), bf16)
    table["rcu"] = table["rcd"] = ((blocks, 64, WIDTH), bf16)
    for name, count in (
        ("gq", 10 * depth), ("gb", 10 * depth), ("gt", 10 * depth), ("gc", 4 + 8 * depth),
        ("sq", 8 * depth), ("sb", 8 * depth), ("st", 8 * depth), ("sc", 8 * depth + 6), ("e", 12),
    ):
        table[name + "_s"] = table[name + "_r"] = count
    return table


INPUTS = ("tok", "cot", "length", "mats", "feed", "small")
OUTPUTS = ("out", "dinp", "gwq", "gwk", "gwv", "gwo", "gfc1", "gfc2", "gsmall")


def layer_kernel(depth, *refs):
    names = INPUTS + OUTPUTS + tuple(scratch_of(depth))
    m = SimpleNamespace(**dict(zip(names, refs, strict=True)))
    k = Links(depth)
    core = k.core

    def in_all(yx, zs):
        return (yx * 2 + core) * depth + zs

    def in_all_sib(yx, zs):
        return (yx * 2 + (1 - core)) * depth + zs

    def in_core(yx, zs):
        return yx * depth + zs

    def chip_rows(start, step):
        return pl.ds(pl.multiple_of(core * SEQ + start, step), step)

    core_rows = pl.ds(pl.multiple_of(core * SEQ, SEQ), SEQ)
    sib_rows = pl.ds(pl.multiple_of((1 - core) * SEQ, SEQ), SEQ)

    def swap(place, source, target):
        k.start(None, lambda: source, lambda: target, lambda: m.e_s.at[place], lambda: m.e_r.at[place], k.sib_dev)

    own_all, own_core = in_all(k.me, k.z), in_core(k.me, k.z)
    m.qk[own_all] = m.mats[...]
    m.sm[own_all] = m.small[...]
    m.ff[own_core] = m.feed[...]
    m.ct[core_rows] = m.cot[...]

    k.barrier()
    g_small = gather_z_first(k, m.sm, in_all, 0, 16, 8, m.gt_s, m.gt_r, in_all_sib)
    g_mats = gather_z_first(k, m.qk, in_all, 0, UNITS, UNITS // 2, m.gq_s, m.gq_r, in_all_sib)
    g_feed = gather_z_first(k, m.ff, in_core, 0, 128, 64, m.gb_s, m.gb_r)
    g_last = gather_z_last(k, m.ff, in_core, 128, 64, 32, m.gc_s, m.gc_r)
    advance(g_small, 1)
    advance(g_mats, 1)
    swap(0, m.ct.at[core_rows], m.ct.at[core_rows])

    def norm1(start, step):
        rows = pl.ds(start, step)
        tokens = m.tok[rows].astype(f32)
        centred = tokens - jnp.mean(tokens, axis=1, keepdims=True)
        inverse = lax.rsqrt(jnp.mean(centred * centred, axis=1, keepdims=True) + EPSILON)
        m.s1[rows] = centred * inverse
        m.i1[rows] = jnp.broadcast_to(inverse, (step, 128))

    row_loop(SEQ, 32, norm1)
    advance(g_small)

    total = jnp.zeros((16, WIDTH), f32)
    for wide in range(8):
        part = jnp.zeros((16, 128), f32)
        for zs in range(depth):
            tile = m.sm[wide * depth + zs]
            part = part + (pltpu.roll(tile, 24 * zs, 1) if zs else tile)
        padded = jnp.concatenate([part, jnp.zeros((16, WIDTH - 128), f32)], axis=1)
        total = total + (pltpu.roll(padded, 96 * wide, 1) if wide else padded)
    m.vec[...] = total
    m.vecc[...] = jnp.transpose(jnp.concatenate([total, jnp.zeros((112, WIDTH), f32)], axis=0))
    for yx in range(4):
        line = jnp.zeros((16, UNITS * depth), f32)
        for zs in range(depth):
            tile = jnp.concatenate([m.sm[in_all(yx, zs)], jnp.zeros((16, UNITS * depth - 128), f32)], axis=1)
            line = line + (pltpu.roll(tile, UNITS * zs, 1) if zs else tile)
        m.bias[yx] = line[8:16]

    day = lax.broadcasted_iota(jnp.int32, (1, SEQ), 1).astype(f32)
    s_at = lax.broadcasted_iota(jnp.int32, (SEQ, SEQ), 0)
    t_at = lax.broadcasted_iota(jnp.int32, (SEQ, SEQ), 1)
    valid = (lax.broadcasted_iota(jnp.int32, (1, SEQ), 1) < m.length[0]).astype(f32)

    def head_kernel(h, carry):
        rows = head_rows(h)
        decays = jnp.exp(-m.vecc[rows, 10:11] * day)
        m.ex[rows] = decays
        line = jnp.sum(m.vecc[rows, 9:10] * decays, axis=0, keepdims=True) * (1.0 / STATE)
        matrix = pltpu.roll(jnp.broadcast_to(line, (SEQ, SEQ)), 0, 1, stride=1, stride_axis=0)
        m.tt[h] = jnp.where(t_at >= s_at, matrix, 0.0)
        return carry

    lax.fori_loop(0, HEADS, head_kernel, 0)

    def gain1(start, step):
        rows = pl.ds(start, step)
        m.nm[rows] = (m.s1[rows] * m.vec[0:1] + m.vec[1:2]).astype(bf16)

    row_loop(SEQ, 32, gain1)
    m.nmt[...] = jnp.transpose(m.nm[...])

    advance(g_mats)
    advance(g_feed, 1)
    advance(g_last, 1)

    def unpack(w, carry):
        rows = pl.ds(pl.multiple_of(w * 96, 96), 96)
        for place, (first, second) in enumerate(((m.wq, m.wk), (m.wv, m.wo))):
            pair = m.qk[pl.ds(w * depth, depth), 48 * place : 48 * place + 48, :].astype(f32)
            first[rows] = pair[:, :24].reshape(96, WIDTH).astype(bf16)
            second[rows] = pair[:, 24:].reshape(96, WIDTH).astype(bf16)
        return carry

    lax.fori_loop(0, 8, unpack, 0)

    m.qt[...] = jnp.transpose(dg(m.nm[...], m.wq[...], 1, 0) + m.vec[2:3]).astype(bf16)
    m.krt[...] = jnp.transpose(dg(m.nm[...], m.wk[...], 1, 0) + m.vec[3:4])
    m.vt[...] = (jnp.transpose(dg(m.nm[...], m.wv[...], 1, 0) + m.vec[4:5]) * valid).astype(bf16)

    def mix_head(h, carry):
        rows = head_rows(h)
        raw = m.krt[rows]
        summed = raw * m.vecc[rows, 5:6]
        for j in range(1, 4):
            summed = summed + lane_shift(raw, j, False) * m.vecc[rows, 5 + j : 6 + j]
        keys = (summed * valid).astype(bf16)
        m.kt[rows] = keys
        scores = dg(keys, m.qt[rows], 0, 0) * (1.0 / HEAD_SIZE)
        weights = (scores * m.tt[h]).astype(bf16)
        m.mt[rows] = (dg(m.vt[rows], weights, 1, 0) * valid).astype(bf16)
        return carry

    lax.fori_loop(0, HEADS, mix_head, 0)
    m.hid[...] = dg(m.mt[...], m.wo[...], 0, 0)

    def norm2(start, step):
        rows = pl.ds(start, step)
        hidden = m.tok[rows].astype(f32) + m.hid[rows] + m.vec[11:12]
        m.hid[rows] = hidden
        centred = hidden - jnp.mean(hidden, axis=1, keepdims=True)
        inverse = lax.rsqrt(jnp.mean(centred * centred, axis=1, keepdims=True) + EPSILON)
        scaled = centred * inverse
        m.s2[rows] = scaled
        m.i2[rows] = jnp.broadcast_to(inverse, (step, 128))
        m.n2[chip_rows(start, step)] = (scaled * m.vec[12:13] + m.vec[13:14]).astype(bf16)

    row_loop(SEQ, 32, norm2)
    swap(1, m.n2.at[core_rows], m.n2.at[core_rows])

    advance(g_feed)
    advance(g_last)
    k.arrive(m.ct.at[sib_rows], m.e_r.at[0])
    k.arrive(m.n2.at[sib_rows], m.e_r.at[1])

    root = math.sqrt(2.0 / math.pi)
    chunk = UNITS * depth
    lane = lax.broadcasted_iota(jnp.int32, (1, 128), 1)
    for which, yx in enumerate((k.me, k.xs, k.ys, k.ds)):
        blocks = pl.ds(yx * depth, depth)
        fc1 = m.ff[blocks, 0:UNITS, :].reshape(chunk, WIDTH)
        fc2 = m.ff[blocks, UNITS : 2 * UNITS, :].reshape(chunk, WIDTH)
        for r in range(2):
            rows = pl.ds(r * SEQ, SEQ)
            pre = dg(m.n2[rows], fc1, 1, 1) + m.bias[yx, 7:8]
            square = pre * pre
            tanh = jnp.tanh(root * pre * (1.0 + 0.044715 * square))
            half = 0.5 * (1.0 + tanh)
            slope = half + 0.5 * pre * (1.0 - tanh * tanh) * (root * (1.0 + 3 * 0.044715 * square))
            activated = (pre * half).astype(bf16)
            grad_pre = (dg(m.ct[rows], fc2, 1, 1) * slope).astype(bf16)
            m.act[rows] = activated
            m.dp[rows] = grad_pre
            if which == 0:
                m.outp[rows] = dg(activated, fc2, 1, 0)
                m.dn2[rows] = dg(grad_pre, fc1, 1, 0)
            else:
                m.outp[rows] += dg(activated, fc2, 1, 0)
                m.dn2[rows] += dg(grad_pre, fc1, 1, 0)
        if which == 3:
            k.drain()
            swap(2, m.dn2.at[sib_rows], m.dn2r)
            swap(3, m.outp.at[sib_rows], m.outr)
        m.gff[blocks, 0:UNITS] = dg(m.dp[...], m.n2[...], 0, 0).astype(bf16).reshape(depth, UNITS, WIDTH)
        m.gff[blocks, UNITS : 2 * UNITS] = (
            dg(m.act[...], m.ct[...], 0, 0).astype(bf16).reshape(depth, UNITS, WIDTH)
        )
        sums = jnp.sum(m.dp[...].astype(f32), axis=0, keepdims=True)
        for zs in range(depth):
            line = (pltpu.roll(sums, chunk - UNITS * zs, 1) if zs else sums)[:, :128]
            m.gbias[yx * depth + zs] = jnp.broadcast_to(jnp.where(lane < UNITS, line, 0.0), (8, 128))

    def finish_feed(ref, more):
        value = ref[...].astype(f32)
        for target, low, high in ((m.gfc1, 0, UNITS), (m.gfc2.at[0:32], UNITS, 128)):
            target[...] = target[...] + value[low:high] if more else value[low:high]

    def finish_last(ref, more):
        value = ref[...].astype(f32)
        m.gfc2[32:96] = m.gfc2[32:96] + value if more else value

    def finish_mats(ref, more):
        value = ref[...].astype(f32)
        for place, target in enumerate((m.gwq, m.gwk, m.gwv, m.gwo)):
            part = value[24 * place : 24 * place + 24]
            target[...] = target[...] + part if more else part

    def finish_small(ref, more):
        m.gsmall[...] = m.gsmall[...] + ref[...] if more else ref[...]

    s_feed = scatter_z_last(
        k, m.gff, in_core, 0, 128, 64, (m.rbdx, m.rbdy, m.rbx, m.rby, m.rbu, m.rbd), m.sb_s, m.sb_r, finish_feed
    )
    s_last = scatter_z_first(
        k, m.gff, in_core, 128, 64, 32, (m.rcdx, m.rcdy, m.rcx, m.rcy, m.rcu, m.rcd), m.sc_s, m.sc_r, finish_last
    )
    s_mats = scatter_z_last(
        k, m.qk, in_all, 0, UNITS, UNITS // 2, (m.rqdx, m.rqdy, m.rqx, m.rqy, m.rqu, m.rqd), m.sq_s, m.sq_r, finish_mats
    )
    s_small = scatter_z_last(
        k, m.gs, in_all, 0, 16, 8, (m.rtdx, m.rtdy, m.rtx, m.rty, m.rtu, m.rtd), m.st_s, m.st_r, finish_small
    )
    advance(s_feed, 2)
    advance(s_last, 1)

    m.gvec[...] = jnp.zeros((16, WIDTH), f32)
    k.arrive(m.dn2r, m.e_r.at[2])

    def back2(start, step):
        rows = pl.ds(start, step)
        grad_normed = m.dn2[chip_rows(start, step)] + m.dn2r[rows]
        scaled = m.s2[rows]
        grad_in = grad_normed * m.vec[12:13]
        first = jnp.mean(grad_in, axis=1, keepdims=True)
        second = jnp.mean(grad_in * scaled, axis=1, keepdims=True)
        top = m.cot[rows].astype(f32)
        grad_hidden = top + m.i2[rows, 0:1] * (grad_in - first - scaled * second)
        m.s2[rows] = grad_hidden
        rounded = grad_hidden.astype(bf16)
        m.da[rows] = rounded
        m.gvec[11:12] += jnp.sum(rounded.astype(f32), axis=0, keepdims=True)
        m.gvec[12:13] += jnp.sum(grad_normed * scaled, axis=0, keepdims=True)
        m.gvec[13:14] += jnp.sum(grad_normed, axis=0, keepdims=True)
        m.gvec[14:15] += jnp.sum(top, axis=0, keepdims=True)

    row_loop(SEQ, 32, back2)
    m.dmt[...] = (jnp.transpose(dg(m.da[...], m.wo[...], 1, 1)) * valid).astype(bf16)

    def back_head(h, carry):
        rows = head_rows(h)
        queries, keys, grad_mixed, kernel = m.qt[rows], m.kt[rows], m.dmt[rows], m.tt[h]
        scores = dg(keys, queries, 0, 0) * (1.0 / HEAD_SIZE)
        weights = (scores * kernel).astype(bf16)
        grad_weights = dg(m.vt[rows], grad_mixed, 0, 0)
        grad_values = (dg(grad_mixed, weights, 1, 1) * valid).astype(bf16)
        m.dvt[rows] = grad_values
        grad_scores = (grad_weights * kernel).astype(bf16)
        grad_queries = (dg(keys, grad_scores, 1, 0) * (1.0 / HEAD_SIZE)).astype(bf16)
        m.dqt[rows] = grad_queries
        grad_keys = dg(queries, grad_scores, 1, 1) * (1.0 / HEAD_SIZE) * valid
        raw = m.krt[rows]
        at = lax.broadcasted_iota(jnp.int32, (HEAD_SIZE, 128), 1)
        grad_raw = grad_keys * m.vecc[rows, 5:6]
        sums = jnp.where(at == 5, jnp.sum(grad_keys * raw, axis=1, keepdims=True), 0.0)
        for j in range(1, 4):
            grad_raw = grad_raw + lane_shift(grad_keys, j, True) * m.vecc[rows, 5 + j : 6 + j]
            tap = jnp.sum(grad_keys * lane_shift(raw, j, False), axis=1, keepdims=True)
            sums = jnp.where(at == 5 + j, tap, sums)
        rounded = grad_raw.astype(bf16)
        m.dkt[rows] = rounded
        for place, value in ((2, grad_queries), (3, rounded), (4, grad_values)):
            sums = jnp.where(at == place, jnp.sum(value.astype(f32), axis=1, keepdims=True), sums)
        m.colsum[rows] = sums
        return carry

    lax.fori_loop(0, HEADS, back_head, 0)

    def pack(w, carry):
        rows = pl.ds(pl.multiple_of(w * 96, 96), 96)
        normed = m.nmt[rows]
        grads = (
            dg(normed, m.dqt[...], 1, 1),
            dg(normed, m.dkt[...], 1, 1),
            dg(normed, m.dvt[...], 1, 1),
            dg(m.mt[rows], m.da[...], 1, 0),
        )
        for place in range(2):
            pair = [grad.reshape(depth, 24, WIDTH) for grad in grads[2 * place : 2 * place + 2]]
            m.qk[pl.ds(w * depth, depth), 48 * place : 48 * place + 48, :] = jnp.concatenate(pair, axis=1).astype(bf16)
        return carry

    lax.fori_loop(0, 8, pack, 0)
    for yx in range(4):
        swap(4 + yx, m.qk.at[pl.ds(in_all_sib(yx, 0), depth)], m.sr.at[pl.ds(yx * depth, depth)])

    advance(s_feed, 2)

    m.dn[...] = jnp.transpose(
        dg(m.wq[...], m.dqt[...], 1, 0) + dg(m.wk[...], m.dkt[...], 1, 0) + dg(m.wv[...], m.dvt[...], 1, 0)
    )

    def back1(start, step):
        rows = pl.ds(start, step)
        grad_normed, scaled = m.dn[rows], m.s1[rows]
        grad_in = grad_normed * m.vec[0:1]
        first = jnp.mean(grad_in, axis=1, keepdims=True)
        second = jnp.mean(grad_in * scaled, axis=1, keepdims=True)
        m.dinp[rows] = (m.s2[rows] + m.i1[rows, 0:1] * (grad_in - first - scaled * second)).astype(bf16)
        m.gvec[0:1] += jnp.sum(grad_normed * scaled, axis=0, keepdims=True)
        m.gvec[1:2] += jnp.sum(grad_normed, axis=0, keepdims=True)

    row_loop(SEQ, 32, back1)

    for yx in range(4):
        k.arrive(m.sr.at[pl.ds(yx * depth, depth)], m.e_r.at[4 + yx])

        def presum(zs, carry, yx=yx):
            add_into(m.qk.at[in_all(yx, zs)], m.sr.at[yx * depth + zs])
            return carry

        lax.fori_loop(0, depth, presum, 0)
    advance(s_mats, 2)

    flip = (s_at + t_at == SEQ - 1).astype(bf16)
    m.kft[...] = dg(m.kt[...], flip, 1, 0).astype(bf16)
    m.vft[...] = dg(m.vt[...], flip, 1, 0).astype(bf16)

    def kernel_head(h, carry):
        rows = head_rows(h)
        scores = dg(m.kft[rows], m.qt[rows], 0, 0) * (1.0 / HEAD_SIZE)
        grad_weights = dg(m.vft[rows], m.dmt[rows], 0, 0)
        product = jnp.where(s_at + t_at >= SEQ - 1, scores * grad_weights, 0.0)
        lined = pltpu.roll(product, 1, 1, stride=1, stride_axis=0)
        grad_kernel = jnp.sum(lined, axis=0, keepdims=True) * (1.0 / STATE)
        part = m.ex[rows] * grad_kernel
        at = lax.broadcasted_iota(jnp.int32, (HEAD_SIZE, 128), 1)
        grad_rate = -m.vecc[rows, 9:10] * jnp.sum(part * day, axis=1, keepdims=True)
        sums = jnp.where(at == 9, jnp.sum(part, axis=1, keepdims=True), m.colsum[rows])
        m.colsum[rows] = jnp.where(at == 10, grad_rate, sums)
        return carry

    lax.fori_loop(0, HEADS, kernel_head, 0)
    grads = m.gvec[...] + jnp.transpose(m.colsum[...])[0:16]
    row_at = lax.broadcasted_iota(jnp.int32, (16, 128), 0)
    lane_at = lax.broadcasted_iota(jnp.int32, (16, 128), 1)
    for wide in range(8):
        turned = (pltpu.roll(grads, WIDTH - 96 * wide, 1) if wide else grads)[:, :128]
        for zs in range(depth):
            tile = pltpu.roll(turned, 128 - 24 * zs, 1) if zs else turned
            tile = jnp.where((lane_at < 24) & (row_at < 15), tile, 0.0)
            own = jnp.concatenate([jnp.zeros((8, 128), f32), m.gbias[(wide // 2) * depth + zs]], axis=0)
            mine = (row_at == 15) & (core == wide % 2)
            m.gs[wide * depth + zs] = jnp.where(mine, own, tile)
    for yx in range(4):
        swap(8 + yx, m.gs.at[pl.ds(in_all_sib(yx, 0), depth)], m.srs.at[pl.ds(yx * depth, depth)])

    def finish_out(start, step):
        rows = pl.ds(start, step)
        m.out[rows] = (m.hid[rows] + (m.outp[chip_rows(start, step)] + m.outr[rows]) + m.vec[14:15]).astype(bf16)

    k.arrive(m.outr, m.e_r.at[3])
    row_loop(SEQ, 32, finish_out)
    for yx in range(4):
        k.arrive(m.srs.at[pl.ds(yx * depth, depth)], m.e_r.at[8 + yx])
        for zs in range(depth):
            add_into(m.gs.at[in_all(yx, zs)], m.srs.at[yx * depth + zs])
    advance(s_small, 2)
    advance(s_feed)
    advance(s_last)
    advance(s_mats)
    advance(s_small)
    k.drain()


def on_device_fast(
    tokens, lengths, cotangent, w_query, w_key, w_value, w_out, w_fc1, w_fc2, fc1_bias, vectors
):
    depth = lax.axis_size("narrow")
    mats = jnp.concatenate([w_query, w_key, w_value, w_out], axis=0)
    feed = jnp.concatenate([w_fc1.T, w_fc2], axis=0)
    small = jnp.concatenate(
        [jnp.pad(vectors, ((0, 0), (0, 104))), jnp.pad(fc1_bias, (0, 32))[None]], axis=0
    ).astype(f32)
    scratch = []
    for entry in scratch_of(depth).values():
        scratch.append(pltpu.SemaphoreType.DMA((entry,)) if isinstance(entry, int) else pltpu.VMEM(*entry))
    in_vmem = pl.BlockSpec(memory_space=pltpu.VMEM)
    in_smem = pl.BlockSpec(memory_space=pltpu.SMEM)
    shape = jax.ShapeDtypeStruct
    got = pl.pallas_call(
        partial(layer_kernel, depth),
        out_shape=[shape((SEQ, WIDTH), bf16)] * 2
        + [shape((24, WIDTH), f32)] * 4
        + [shape((UNITS, WIDTH), f32)] * 2
        + [shape((16, 128), f32)],
        in_specs=[in_vmem, in_vmem, in_smem, in_vmem, in_vmem, in_vmem],
        out_specs=[in_vmem] * 9,
        scratch_shapes=scratch,
        compiler_params=pltpu.CompilerParams(
            collective_id=0, has_side_effects=True, vmem_limit_bytes=63 * 2**20
        ),
        name="h3_layer",
    )(tokens, cotangent, lengths, mats, feed, small)
    out, grad_in, g_query, g_key, g_value, g_out, g_fc1, g_fc2, g_small = got
    return (
        out, grad_in, g_query, g_key, g_value, g_out, g_fc1.T, g_fc2, g_small[15, :UNITS], g_small[:15, :24],
    )


def fits(mesh):
    return mesh.shape["wide"] == 8 and mesh.shape["narrow"] == 4


def solution(mesh):
    placed = (
        P(("wide", "narrow"), None),
        P(("wide", "narrow")),
        P(("wide", "narrow"), None),
        P(("wide", "narrow"), None),
        P(("wide", "narrow"), None),
        P(("wide", "narrow"), None),
        P(("wide", "narrow"), None),
        P(None, ("wide", "narrow")),
        P(("wide", "narrow"), None),
        P(("wide", "narrow")),
        P(None, ("wide", "narrow")),
    )
    return jax.shard_map(
        on_device_fast if fits(mesh) else on_device,
        mesh=mesh,
        in_specs=placed,
        out_specs=(
            P(("wide", "narrow"), None),
            P(("wide", "narrow"), None),
            P(("wide", "narrow"), None),
            P(("wide", "narrow"), None),
            P(("wide", "narrow"), None),
            P(("wide", "narrow"), None),
            P(None, ("wide", "narrow")),
            P(("wide", "narrow"), None),
            P(("wide", "narrow")),
            P(None, ("wide", "narrow")),
        ),
        check_vma=False,
    )
```

```python
import math
from functools import partial
from types import SimpleNamespace

import jax
import jax.numpy as jnp
from jax import lax
from jax.experimental import pallas as pl
from jax.experimental.pallas import tpu as pltpu
from jax.sharding import PartitionSpec as P

HEAD_SIZE = 64
STATE = 64


EPSILON = 1e-05


def normalize(values):
    average = jnp.mean(values, axis=-1, keepdims=True)
    centred = values - average
    variance = jnp.mean(centred * centred, axis=-1, keepdims=True)
    inverse = lax.rsqrt(variance + EPSILON)
    return (centred * inverse, inverse)


def norm_back(grad_in, scaled, inverse):
    first = jnp.mean(grad_in, axis=-1, keepdims=True)
    second = jnp.mean(grad_in * scaled, axis=-1, keepdims=True)
    return inverse * (grad_in - first - scaled * second)


def shift_mix(key_raw, shift_taps):
    summed = key_raw * shift_taps[0]
    for offset in range(1, 4):
        delayed = jnp.concatenate(
            [jnp.zeros((offset, key_raw.shape[1]), key_raw.dtype), key_raw[:-offset]], axis=0
        )
        summed = summed + delayed * shift_taps[offset]
    return summed


def kernel_rows(coefficient, decay_rate, length_all):
    distance = jnp.arange(length_all).astype(jnp.float32)
    decays = jnp.exp(-decay_rate[:, :, None] * distance[None, None, :])
    return jnp.sum(coefficient[:, :, None] * decays, axis=1) / STATE


def toeplitz(kernel_row):
    length_all = kernel_row.shape[0]
    wrapped = jnp.concatenate(
        [kernel_row[:1], jnp.zeros((length_all,), kernel_row.dtype), kernel_row[:0:-1]]
    )
    tiled_row = jnp.tile(wrapped, length_all)[: length_all * (2 * length_all - 1)]
    return tiled_row.reshape(length_all, 2 * length_all - 1)[:, :length_all]


def split_heads(values, row_count):
    return values.reshape(row_count, -1, HEAD_SIZE).transpose(1, 0, 2)


def merge_heads(per_head):
    head_count = per_head.shape[0]
    row_count = per_head.shape[1]
    merged = per_head.transpose(1, 0, 2).reshape(row_count, head_count * HEAD_SIZE)
    return merged


def pack_rows(matrices, shard_count):
    return jnp.concatenate(
        [matrix.reshape(shard_count, -1) for matrix in matrices], axis=1
    ).reshape(-1)


def unpack_rows(flat, matrices, shard_count):
    pieces = []
    offset = 0
    for matrix in matrices:
        rows_own = matrix.shape[0] // shard_count
        extent = matrix.size // shard_count
        pieces.append(flat[offset : offset + extent].reshape((rows_own,) + matrix.shape[1:]))
        offset = offset + extent
    return pieces


def mixer_forward(queries, keys, values, kernel, row_count):

    def head_forward(parts):
        query_head, key_head, value_head, kernel_row = parts
        scores = jnp.dot(query_head, key_head.T, preferred_element_type=jnp.float32) / HEAD_SIZE
        weights_mix = (scores * toeplitz(kernel_row)).astype(jnp.bfloat16)
        return jnp.dot(weights_mix, value_head, preferred_element_type=jnp.float32)

    per_head = lax.map(
        head_forward,
        (
            split_heads(queries, row_count),
            split_heads(keys, row_count),
            split_heads(values, row_count),
            kernel,
        ),
    )
    return merge_heads(per_head)


def mixer_backward(queries, keys, values, grad_mixed, kernel, row_count):

    def head_backward(parts):
        query_head, key_head, value_head, grad_head, kernel_row = parts
        scores = jnp.dot(query_head, key_head.T, preferred_element_type=jnp.float32) / HEAD_SIZE
        toeplitz_mat, pullback = jax.vjp(toeplitz, kernel_row)
        weights_mix = (scores * toeplitz_mat).astype(jnp.bfloat16)
        grad_weights = jnp.dot(grad_head, value_head.T, preferred_element_type=jnp.float32)
        grad_values = jnp.dot(weights_mix.T, grad_head, preferred_element_type=jnp.float32)
        grad_scores = (grad_weights * toeplitz_mat).astype(jnp.bfloat16)
        grad_queries = (
            jnp.dot(grad_scores, key_head, preferred_element_type=jnp.float32) / HEAD_SIZE
        )
        grad_keys = (
            jnp.dot(grad_scores.T, query_head, preferred_element_type=jnp.float32) / HEAD_SIZE
        )
        grad_kernel = pullback(grad_weights * scores)[0]
        return (grad_queries, grad_keys, grad_values, grad_kernel)

    head_grads = lax.map(
        head_backward,
        (
            split_heads(queries, row_count),
            split_heads(keys, row_count),
            split_heads(values, row_count),
            split_heads(grad_mixed, row_count),
            kernel,
        ),
    )
    grad_kernel = head_grads[3]
    return (
        merge_heads(head_grads[0]),
        merge_heads(head_grads[1]),
        merge_heads(head_grads[2]),
        grad_kernel,
    )


def on_device(
    tokens, lengths, cotangent, w_query, w_key, w_value, w_out, w_fc1, w_fc2, fc1_bias, vectors
):
    shard_count = lax.axis_size(("wide", "narrow"))
    gathered = (
        lax.all_gather(w_query, ("wide", "narrow"), axis=0, tiled=True),
        lax.all_gather(w_key, ("wide", "narrow"), axis=0, tiled=True),
        lax.all_gather(w_value, ("wide", "narrow"), axis=0, tiled=True),
        lax.all_gather(w_out, ("wide", "narrow"), axis=0, tiled=True),
        lax.all_gather(w_fc1, ("wide", "narrow"), axis=1, tiled=True),
        lax.all_gather(w_fc2, ("wide", "narrow"), axis=0, tiled=True),
        lax.all_gather(fc1_bias, ("wide", "narrow"), axis=0, tiled=True),
        lax.all_gather(vectors, ("wide", "narrow"), axis=1, tiled=True),
    )
    query_full, key_full, value_full, out_full, fc1_full, fc2_full, bias_full, vector_full = (
        gathered
    )
    params = vector_full.astype(jnp.float32)
    fc1_shift = bias_full.astype(jnp.float32)
    seq_len = tokens.shape[0]
    head_count = params.shape[1] // HEAD_SIZE
    seq_length = lengths[0]
    valid_mask = (jnp.arange(seq_len) < seq_length).astype(jnp.float32)[:, None]
    residual = tokens.astype(jnp.float32)
    scaled1, inverse1 = normalize(residual)
    normed = (scaled1 * params[0] + params[1]).astype(jnp.bfloat16)
    queries = (jnp.dot(normed, query_full, preferred_element_type=jnp.float32) + params[2]).astype(
        jnp.bfloat16
    )
    key_raw = jnp.dot(normed, key_full, preferred_element_type=jnp.float32) + params[3]
    keys = (shift_mix(key_raw, params[5:9]) * valid_mask).astype(jnp.bfloat16)
    values = (
        (jnp.dot(normed, value_full, preferred_element_type=jnp.float32) + params[4]) * valid_mask
    ).astype(jnp.bfloat16)
    coefficient = params[9].reshape(head_count, STATE)
    decay_rate = params[10].reshape(head_count, STATE)
    kernel_fn = partial(kernel_rows, length_all=seq_len)
    kernel, kernel_pull = jax.vjp(kernel_fn, coefficient, decay_rate)
    mixed = mixer_forward(queries, keys, values, kernel, seq_len)
    mixed_out = (mixed * valid_mask).astype(jnp.bfloat16)
    hidden = (
        residual + jnp.dot(mixed_out, out_full, preferred_element_type=jnp.float32) + params[11]
    )
    scaled2, inverse2 = normalize(hidden)
    normed2 = (scaled2 * params[12] + params[13]).astype(jnp.bfloat16)
    pre_act = jnp.dot(normed2, fc1_full, preferred_element_type=jnp.float32) + fc1_shift
    activated = jax.nn.gelu(pre_act).astype(jnp.bfloat16)
    output = (
        hidden + jnp.dot(activated, fc2_full, preferred_element_type=jnp.float32) + params[14]
    ).astype(jnp.bfloat16)
    again = (
        lax.all_gather(w_query, ("wide", "narrow"), axis=0, tiled=True),
        lax.all_gather(w_key, ("wide", "narrow"), axis=0, tiled=True),
        lax.all_gather(w_value, ("wide", "narrow"), axis=0, tiled=True),
        lax.all_gather(w_out, ("wide", "narrow"), axis=0, tiled=True),
        lax.all_gather(w_fc1, ("wide", "narrow"), axis=1, tiled=True),
        lax.all_gather(w_fc2, ("wide", "narrow"), axis=0, tiled=True),
        lax.all_gather(fc1_bias, ("wide", "narrow"), axis=0, tiled=True),
        lax.all_gather(vectors, ("wide", "narrow"), axis=1, tiled=True),
    )
    query_back, key_back, value_back, out_back, fc1_back, fc2_back = (
        again[0],
        again[1],
        again[2],
        again[3],
        again[4],
        again[5],
    )
    grad_top = cotangent.astype(jnp.float32)
    grad_fc2 = jnp.dot(activated.T, cotangent, preferred_element_type=jnp.float32)
    grad_activated = jnp.dot(cotangent, fc2_back.T, preferred_element_type=jnp.float32)
    gelu_value, gelu_pull = jax.vjp(jax.nn.gelu, pre_act)
    grad_pre = gelu_pull(grad_activated)[0].astype(jnp.bfloat16)
    grad_fc1_turned = jnp.dot(grad_pre.T, normed2, preferred_element_type=jnp.float32)
    grad_fc1_bias = jnp.sum(grad_pre.astype(jnp.float32), axis=0)[:, None]
    mlp_terms = [grad_fc1_turned, grad_fc2, grad_fc1_bias]
    mlp_flat = lax.psum_scatter(
        pack_rows(mlp_terms, shard_count), ("wide", "narrow"), scatter_dimension=0, tiled=True
    )
    mlp_sums = unpack_rows(mlp_flat, mlp_terms, shard_count)
    grad_normed2 = jnp.dot(grad_pre, fc1_back.T, preferred_element_type=jnp.float32)
    grad_hidden = grad_top + norm_back(grad_normed2 * params[12], scaled2, inverse2)
    grad_attn = grad_hidden.astype(jnp.bfloat16)
    grad_out = jnp.dot(mixed_out.T, grad_attn, preferred_element_type=jnp.float32)
    grad_mixed = (
        jnp.dot(grad_attn, out_back.T, preferred_element_type=jnp.float32) * valid_mask
    ).astype(jnp.bfloat16)
    grad_q, grad_k, grad_v, grad_kernel = mixer_backward(
        queries, keys, values, grad_mixed, kernel, seq_len
    )
    grad_queries = grad_q.astype(jnp.bfloat16)
    grad_values = (grad_v * valid_mask).astype(jnp.bfloat16)
    shift_value, shift_pull = jax.vjp(shift_mix, key_raw, params[5:9])
    grad_key_full, grad_taps = shift_pull(grad_k * valid_mask)
    grad_key_raw = grad_key_full.astype(jnp.bfloat16)
    grad_query = jnp.dot(normed.T, grad_queries, preferred_element_type=jnp.float32)
    grad_key = jnp.dot(normed.T, grad_key_raw, preferred_element_type=jnp.float32)
    grad_value = jnp.dot(normed.T, grad_values, preferred_element_type=jnp.float32)
    grad_normed = jnp.dot(grad_queries, query_back.T, preferred_element_type=jnp.float32)
    grad_normed = grad_normed + jnp.dot(
        grad_key_raw, key_back.T, preferred_element_type=jnp.float32
    )
    grad_normed = grad_normed + jnp.dot(
        grad_values, value_back.T, preferred_element_type=jnp.float32
    )
    input_grad = (grad_hidden + norm_back(grad_normed * params[0], scaled1, inverse1)).astype(
        jnp.bfloat16
    )
    grad_coef, grad_rate = kernel_pull(grad_kernel)
    grad_vectors = jnp.concatenate(
        [
            jnp.sum(grad_normed * scaled1, axis=0)[None],
            jnp.sum(grad_normed, axis=0)[None],
            jnp.sum(grad_queries.astype(jnp.float32), axis=0)[None],
            jnp.sum(grad_key_raw.astype(jnp.float32), axis=0)[None],
            jnp.sum(grad_values.astype(jnp.float32), axis=0)[None],
            grad_taps,
            grad_coef.reshape(1, -1),
            grad_rate.reshape(1, -1),
            jnp.sum(grad_attn.astype(jnp.float32), axis=0)[None],
            jnp.sum(grad_normed2 * scaled2, axis=0)[None],
            jnp.sum(grad_normed2, axis=0)[None],
            jnp.sum(grad_top, axis=0)[None],
        ],
        axis=0,
    )
    mixer_terms = [grad_query, grad_key, grad_value, grad_out, grad_vectors.T]
    mixer_flat = lax.psum_scatter(
        pack_rows(mixer_terms, shard_count), ("wide", "narrow"), scatter_dimension=0, tiled=True
    )
    mixer_sums = unpack_rows(mixer_flat, mixer_terms, shard_count)
    return (
        output,
        input_grad,
        mixer_sums[0],
        mixer_sums[1],
        mixer_sums[2],
        mixer_sums[3],
        mlp_sums[0].T,
        mlp_sums[1],
        mlp_sums[2].reshape(-1),
        mixer_sums[4].T,
    )


f32, bf16 = jnp.float32, jnp.bfloat16
MESH = pl.DeviceIdType.MESH


def dg(left, right, left_dim, right_dim):
    return lax.dot_general(
        left, right, (((left_dim,), (right_dim,)), ((), ())), preferred_element_type=f32
    )


def when(condition, body):
    if condition is None:
        body()
    else:
        pl.when(condition)(body)


def both(first, second):
    if first is None:
        return second
    if second is None:
        return first
    return jnp.logical_and(first, second)


class Links:
    def __init__(self, depth):
        wide, z = lax.axis_index("wide"), lax.axis_index("narrow")
        self.depth = depth
        self.z, self.core = z, lax.rem(wide, 2)
        self.x, self.y = lax.rem(lax.div(wide, 2), 2), lax.div(wide, 4)
        self.me = self.y * 2 + self.x
        self.xs = self.y * 2 + (1 - self.x)
        self.ys = (1 - self.y) * 2 + self.x
        self.ds = (1 - self.y) * 2 + (1 - self.x)
        self.sib_dev = (self.me * 2 + (1 - self.core), z)
        self.x_dev = (self.xs * 2 + self.core, z)
        self.y_dev = (self.ys * 2 + self.core, z)
        self.up_dev = (wide, z + 1)
        self.down_dev = (wide, z - 1)
        self.has_up = z < depth - 1
        self.has_down = z > 0
        self.pending = {}

    def barrier(self):
        semaphore = pltpu.get_barrier_semaphore()

        def greet(device):
            pl.semaphore_signal(semaphore, inc=1, device_id=device, device_id_type=MESH)

        for device in (self.sib_dev, self.x_dev, self.y_dev):
            greet(device)
        pl.when(self.has_up)(lambda: greet(self.up_dev))
        pl.when(self.has_down)(lambda: greet(self.down_dev))
        peers = 3 + self.has_up.astype(jnp.int32) + self.has_down.astype(jnp.int32)
        pl.semaphore_wait(semaphore, peers)

    def start(self, condition, source, target, send, receive, device, group=""):
        def build():
            return pltpu.make_async_remote_copy(
                src_ref=source(),
                dst_ref=target(),
                send_sem=send(),
                recv_sem=receive(),
                device_id=device,
                device_id_type=MESH,
            )

        when(condition, lambda: build().start())
        self.pending.setdefault(group, []).append((condition, build))

    def arrive(self, target, receive):
        pltpu.make_async_remote_copy(
            src_ref=target,
            dst_ref=target,
            send_sem=receive,
            recv_sem=receive,
            device_id=self.sib_dev,
            device_id_type=MESH,
        ).wait_recv()

    def drain(self, *groups):
        for group in groups or tuple(self.pending):
            for condition, build in self.pending.pop(group, ()):
                when(condition, lambda build=build: build().wait_send())


def near(k, distance):
    if distance == 0:
        return ((None, k.z, False),)
    return ((k.z >= distance, k.z - distance, True), (k.z + distance < k.depth, k.z + distance, False))


def gather_z_first(k, name, buf, index, low, rows, half, ss, rs, sib_index=None):
    depth = k.depth

    def block(yx, zs, lo=0, n=rows):
        return buf.at[index(yx, zs), pl.ds(low + lo, n)]

    def send(condition, yx, zs, lo, n, device, s, r):
        ref = lambda: block(yx, zs, lo, n)
        k.start(condition, ref, ref, lambda: ss.at[s], lambda: rs.at[r], device, name)

    def to_sib(condition, yx, zs):
        if sib_index is not None:
            send(condition, yx, zs, 0, rows, k.sib_dev, 6 * depth + yx * depth + zs, 5 * depth + yx * depth + zs)

    def outward(condition, zs):
        send(condition, k.me, zs, 0, rows, k.x_dev, 2 * depth + zs, depth + zs)
        send(condition, k.me, zs, 0, rows, k.y_dev, 3 * depth + zs, 2 * depth + zs)
        to_sib(condition, k.me, zs)

    def along(condition, zs, up, down):
        if up:
            send(both(condition, k.has_up), k.me, zs, 0, rows, k.up_dev, zs, zs)
        if down:
            send(both(condition, k.has_down), k.me, zs, 0, rows, k.down_dev, depth + zs, zs)

    def take(condition, yx, zs, lo, n, r):
        when(condition, lambda: k.arrive(block(yx, zs, lo, n), rs.at[r]))

    def own():
        along(None, k.z, True, True)
        outward(None, k.z)
        yield

    def z_steps():
        for d in range(1, depth):
            for condition, zs, below in near(k, d):
                take(condition, k.me, zs, 0, rows, zs)
                along(condition, zs, below, not below)
                outward(condition, zs)
            yield

    def x_steps():
        for d in range(depth):
            for condition, zs, _ in near(k, d):
                take(condition, k.xs, zs, 0, rows, depth + zs)
                send(condition, k.xs, zs, 0, half, k.y_dev, 5 * depth + zs, 4 * depth + zs)
                to_sib(condition, k.xs, zs)
            yield

    def y_steps():
        for d in range(depth):
            for condition, zs, _ in near(k, d):
                take(condition, k.ys, zs, 0, rows, 2 * depth + zs)
                send(condition, k.ys, zs, half, rows - half, k.x_dev, 4 * depth + zs, 3 * depth + zs)
                to_sib(condition, k.ys, zs)
            yield

    def d_steps():
        for d in range(depth):
            for condition, zs, _ in near(k, d):
                take(condition, k.ds, zs, 0, half, 4 * depth + zs)
                take(condition, k.ds, zs, half, rows - half, 3 * depth + zs)
                to_sib(condition, k.ds, zs)
            yield

    def sib_steps():
        for yx in range(4):
            for zs in range(depth):
                k.arrive(buf.at[sib_index(yx, zs), pl.ds(low, rows)], rs.at[5 * depth + yx * depth + zs])
        yield

    steps = {"0": own(), "z": z_steps(), "x": x_steps(), "y": y_steps(), "d": d_steps(), "s": sib_steps()}
    return {name + key: step for key, step in steps.items()}


def gather_z_last(k, name, buf, index, low, rows, half, ss, rs):
    depth = k.depth
    yx_of = (k.me, k.xs, k.ys, k.ds)

    def block(yx, zs, lo=0, n=rows):
        return buf.at[index(yx, zs), pl.ds(low + lo, n)]

    def send(condition, yx, zs, lo, n, device, s, r):
        ref = lambda: block(yx, zs, lo, n)
        k.start(condition, ref, ref, lambda: ss.at[s], lambda: rs.at[r], device, name)

    def along(condition, which, zs, up, down):
        yx = yx_of[which]
        place = which * depth + zs
        if up:
            send(both(condition, k.has_up), yx, zs, 0, rows, k.up_dev, 4 + place, 4 + place)
        if down:
            send(both(condition, k.has_down), yx, zs, 0, rows, k.down_dev, 4 + 4 * depth + place, 4 + place)

    def own():
        send(None, k.me, k.z, 0, rows, k.x_dev, 0, 0)
        send(None, k.me, k.z, 0, rows, k.y_dev, 1, 1)
        along(None, 0, k.z, True, True)
        yield

    def x_step():
        k.arrive(block(k.xs, k.z), rs.at[0])
        send(None, k.xs, k.z, 0, half, k.y_dev, 2, 2)
        along(None, 1, k.z, True, True)
        yield

    def y_step():
        k.arrive(block(k.ys, k.z), rs.at[1])
        send(None, k.ys, k.z, half, rows - half, k.x_dev, 3, 3)
        along(None, 2, k.z, True, True)
        yield

    def d_step():
        k.arrive(block(k.ds, k.z, 0, half), rs.at[2])
        k.arrive(block(k.ds, k.z, half, rows - half), rs.at[3])
        along(None, 3, k.z, True, True)
        yield

    def z_steps(which):
        for d in range(1, depth):
            for condition, zs, below in near(k, d):
                when(condition, lambda zs=zs: k.arrive(block(yx_of[which], zs), rs.at[4 + which * depth + zs]))
                along(condition, which, zs, below, not below)
            yield

    steps = {"0": own(), "x": x_step(), "y": y_step(), "d": d_step()}
    for which in range(4):
        steps[str(4 + which)] = z_steps(which)
    return {name + key: step for key, step in steps.items()}


def add_into(ref, *others):
    total = ref[...].astype(f32)
    for other in others:
        total = total + other[...].astype(f32)
    ref[...] = total.astype(ref.dtype)


def scatter_order(depth):
    return ([0, depth - 1] + list(range(1, depth - 1)))[:depth]


def along_z(k, zd, wave, block, from_up, from_down, rs_up, rs_down, send):
    top, low = k.depth - 1 - wave, wave

    def take(slot, semaphore):
        k.arrive(slot, semaphore)
        add_into(block, slot)

    if zd < top:
        if wave:
            pl.when(k.z == top)(lambda: take(from_up, rs_up))
        send(k.z == top, False)
    if zd > low:
        if wave:
            pl.when(k.z == low)(lambda: take(from_down, rs_down))
        send(k.z == low, True)


def scatter_z_last(k, name, buf, index, low, rows, half, slots, ss, rs, finish):
    depth = k.depth
    from_x_diag, from_y_diag, from_x, from_y, from_up, from_down = slots
    order = scatter_order(depth)
    rest = rows - half

    def block(yx, zd, lo=0, n=rows):
        return buf.at[index(yx, zd), pl.ds(low + lo, n)]

    def send(condition, source, target, device, s, r):
        k.start(condition, source, target, lambda: ss.at[s], lambda: rs.at[r], device)

    def pure_x():
        for zd in order:
            send(None, lambda zd=zd: block(k.xs, zd, half, rest), lambda zd=zd: from_x.at[zd, pl.ds(half, rest)], k.x_dev, 2 * depth + zd, 2 * depth + zd)
        yield

    def pure_y():
        for zd in order:
            send(None, lambda zd=zd: block(k.ys, zd, 0, half), lambda zd=zd: from_y.at[zd, pl.ds(0, half)], k.y_dev, 3 * depth + zd, 3 * depth + zd)
        yield

    def diagonal():
        for zd in order:
            send(None, lambda zd=zd: block(k.ds, zd, 0, half), lambda zd=zd: from_y_diag.at[zd], k.y_dev, zd, zd)
            send(None, lambda zd=zd: block(k.ds, zd, half, rest), lambda zd=zd: from_x_diag.at[zd], k.x_dev, depth + zd, depth + zd)
        yield

    def y_added():
        for zd in order:
            k.arrive(from_y_diag.at[zd], rs.at[zd])
            add_into(block(k.xs, zd, 0, half), from_y_diag.at[zd])
            send(None, lambda zd=zd: block(k.xs, zd, 0, half), lambda zd=zd: from_x.at[zd, pl.ds(0, half)], k.x_dev, 4 * depth + zd, 4 * depth + zd)
            yield

    def x_added():
        for zd in order:
            k.arrive(from_x_diag.at[zd], rs.at[depth + zd])
            add_into(block(k.ys, zd, half, rest), from_x_diag.at[zd])
            send(None, lambda zd=zd: block(k.ys, zd, half, rest), lambda zd=zd: from_y.at[zd, pl.ds(half, rest)], k.y_dev, 5 * depth + zd, 5 * depth + zd)
            yield

    def wave(zd, number):
        def send_z(condition, up):
            place = (7 if up else 6) * depth + zd
            slot = from_down if up else from_up
            send(condition, lambda: block(k.me, zd), lambda: slot.at[zd], k.up_dev if up else k.down_dev, place, place)

        along_z(
            k, zd, number, block(k.me, zd), from_up.at[zd], from_down.at[zd],
            rs.at[6 * depth + zd], rs.at[7 * depth + zd], send_z,
        )

    def collect():
        for zd in order:
            k.arrive(from_x.at[zd, pl.ds(half, rest)], rs.at[2 * depth + zd])
            k.arrive(from_y.at[zd, pl.ds(0, half)], rs.at[3 * depth + zd])
            k.arrive(from_x.at[zd, pl.ds(0, half)], rs.at[4 * depth + zd])
            k.arrive(from_y.at[zd, pl.ds(half, rest)], rs.at[5 * depth + zd])
            add_into(block(k.me, zd), from_x.at[zd], from_y.at[zd])
            wave(zd, 0)
            yield

    def waves(number):
        for zd in order:
            if zd < depth - 1 - number or zd > number:
                wave(zd, number)
                yield

    def end():
        finish(block(k.me, k.z), False)

        def last_up():
            k.arrive(from_up.at[k.z], rs.at[6 * depth + k.z])
            finish(from_up.at[k.z], True)

        def last_down():
            k.arrive(from_down.at[k.z], rs.at[7 * depth + k.z])
            finish(from_down.at[k.z], True)

        pl.when(k.has_up)(last_up)
        pl.when(k.has_down)(last_down)
        yield

    steps = {"X": pure_x(), "Y": pure_y(), "D": diagonal(), "a": y_added(), "b": x_added(), "c": collect(), "e": end()}
    steps |= {"v": waves(1), "w": waves(2)}
    return {name + key: step for key, step in steps.items()}


def scatter_z_first(k, name, buf, index, low, rows, half, slots, ss, rs, finish):
    depth = k.depth
    from_x_diag, from_y_diag, from_x, from_y, from_up, from_down = slots
    yx_of = (k.me, k.xs, k.ys, k.ds)
    rest = rows - half
    base = 8 * depth

    def block(yx, zd, lo=0, n=rows):
        return buf.at[index(yx, zd), pl.ds(low + lo, n)]

    def send(condition, source, target, device, s, r):
        k.start(condition, source, target, lambda: ss.at[s], lambda: rs.at[r], device)

    def waves(which):
        yx = yx_of[which]
        for number in range(depth - 1):
            for zd in scatter_order(depth):
                place = which * depth + zd

                def send_z(condition, up, zd=zd, place=place):
                    slot, number = (from_down, 4 * depth + place) if up else (from_up, place)
                    send(condition, lambda: block(yx, zd), lambda: slot.at[place], k.up_dev if up else k.down_dev, number, number)

                along_z(
                    k, zd, number, block(yx, zd), from_up.at[place], from_down.at[place],
                    rs.at[place], rs.at[4 * depth + place], send_z,
                )
            yield

    def own(which):
        yx = yx_of[which]
        place = which * depth + k.z

        def take(slot, semaphore):
            k.arrive(slot, semaphore)
            add_into(block(yx, k.z), slot)

        pl.when(k.has_up)(lambda: take(from_up.at[place], rs.at[place]))
        pl.when(k.has_down)(lambda: take(from_down.at[place], rs.at[4 * depth + place]))

    def own_me():
        own(0)
        yield

    def own_x():
        own(1)
        send(None, lambda: block(k.xs, k.z, half, rest), lambda: from_x.at[0, pl.ds(half, rest)], k.x_dev, base + 2, base + 2)
        yield

    def own_y():
        own(2)
        send(None, lambda: block(k.ys, k.z, 0, half), lambda: from_y.at[0, pl.ds(0, half)], k.y_dev, base + 3, base + 3)
        yield

    def own_d():
        own(3)
        send(None, lambda: block(k.ds, k.z, 0, half), lambda: from_y_diag.at[0], k.y_dev, base, base)
        send(None, lambda: block(k.ds, k.z, half, rest), lambda: from_x_diag.at[0], k.x_dev, base + 1, base + 1)
        yield

    def y_added():
        k.arrive(from_y_diag.at[0], rs.at[base])
        add_into(block(k.xs, k.z, 0, half), from_y_diag.at[0])
        send(None, lambda: block(k.xs, k.z, 0, half), lambda: from_x.at[0, pl.ds(0, half)], k.x_dev, base + 4, base + 4)
        yield

    def x_added():
        k.arrive(from_x_diag.at[0], rs.at[base + 1])
        add_into(block(k.ys, k.z, half, rest), from_x_diag.at[0])
        send(None, lambda: block(k.ys, k.z, half, rest), lambda: from_y.at[0, pl.ds(half, rest)], k.y_dev, base + 5, base + 5)
        yield

    def end():
        finish(block(k.me, k.z), False)
        k.arrive(from_x.at[0, pl.ds(half, rest)], rs.at[base + 2])
        k.arrive(from_x.at[0, pl.ds(0, half)], rs.at[base + 4])
        finish(from_x.at[0], True)
        k.arrive(from_y.at[0, pl.ds(0, half)], rs.at[base + 3])
        k.arrive(from_y.at[0, pl.ds(half, rest)], rs.at[base + 5])
        finish(from_y.at[0], True)
        yield

    steps = {"O": own_me(), "X": own_x(), "Y": own_y(), "D": own_d(), "a": y_added(), "b": x_added(), "e": end()}
    steps |= {str(which): waves(which) for which in range(4)}
    return {name + key: step for key, step in steps.items()}


SEQ, WIDTH, UNITS = 256, 768, 96
HEADS = WIDTH // HEAD_SIZE


def row_loop(total, step, body):
    def once(i, carry):
        body(pl.multiple_of(i * step, step), step)
        return carry

    lax.fori_loop(0, total // step, once, 0)


def lane_shift(values, offset, left):
    extent = values.shape[1]
    lane = lax.broadcasted_iota(jnp.int32, values.shape, 1)
    if left:
        return jnp.where(lane < extent - offset, pltpu.roll(values, extent - offset, 1), 0.0)
    return jnp.where(lane >= offset, pltpu.roll(values, offset, 1), 0.0)


def three_heads(first, body):
    for h in range(first, first + 3):
        body(h)


def head_rows(h):
    return pl.ds(pl.multiple_of(h * HEAD_SIZE, HEAD_SIZE), HEAD_SIZE)


def scratch_of(depth):
    devices, blocks = 8 * depth, 4 * depth
    table = {
        "qk": ((devices, UNITS, WIDTH), bf16),
        "ff": ((blocks, 2 * UNITS, WIDTH), bf16),
        "sm": ((devices, 16, 128), f32),
        "gff": ((blocks, 2 * UNITS, WIDTH), bf16),
        "gs": ((devices, 16, 128), f32),
        "sr": ((blocks, UNITS, WIDTH), bf16),
        "srs": ((blocks, 16, 128), f32),
        "wq": ((WIDTH, WIDTH), bf16),
        "wk": ((WIDTH, WIDTH), bf16),
        "wv": ((WIDTH, WIDTH), bf16),
        "wo": ((WIDTH, WIDTH), bf16),
        "s1": ((SEQ, WIDTH), f32),
        "i1": ((SEQ, 128), f32),
        "nm": ((SEQ, WIDTH), bf16),
        "hid": ((SEQ, WIDTH), f32),
        "s2": ((SEQ, WIDTH), f32),
        "i2": ((SEQ, 128), f32),
        "n2": ((2 * SEQ, WIDTH), bf16),
        "ct": ((2 * SEQ, WIDTH), bf16),
        "outp": ((2 * SEQ, WIDTH), f32),
        "dn2": ((2 * SEQ, WIDTH), f32),
        "outr": ((SEQ, WIDTH), f32),
        "dn2r": ((SEQ, WIDTH), f32),
        "act": ((2 * SEQ, UNITS * depth), bf16),
        "dp": ((2 * SEQ, UNITS * depth), bf16),
        "da": ((SEQ, WIDTH), bf16),
        "dn": ((SEQ, WIDTH), f32),
        "nmt": ((WIDTH, SEQ), bf16),
        "qt": ((WIDTH, SEQ), bf16),
        "kt": ((WIDTH, SEQ), bf16),
        "vt": ((WIDTH, SEQ), bf16),
        "krt": ((WIDTH, SEQ), f32),
        "mt": ((WIDTH, SEQ), bf16),
        "dmt": ((WIDTH, SEQ), bf16),
        "dqt": ((WIDTH, SEQ), bf16),
        "dkt": ((WIDTH, SEQ), bf16),
        "dvt": ((WIDTH, SEQ), bf16),
        "kft": ((WIDTH, SEQ), bf16),
        "vft": ((WIDTH, SEQ), bf16),
        "ex": ((WIDTH, SEQ), f32),
        "tt": ((HEADS, SEQ, SEQ), f32),
        "vec": ((16, WIDTH), f32),
        "vecc": ((WIDTH, 128), f32),
        "colsum": ((WIDTH, 128), f32),
        "gvec": ((16, WIDTH), f32),
        "bias": ((4, 8, UNITS * depth), f32),
        "gbias": ((blocks, 8, 128), f32),
    }
    for name, rows, half, lanes, kind in (
        ("q", UNITS, UNITS // 2, WIDTH, bf16),
        ("b", 128, 64, WIDTH, bf16),
        ("t", 16, 8, 128, f32),
    ):
        table["r" + name + "dx"] = ((depth, rows - half, lanes), kind)
        table["r" + name + "dy"] = ((depth, half, lanes), kind)
        for place in ("x", "y", "u", "d"):
            table["r" + name + place] = ((depth, rows, lanes), kind)
    table["rcdx"] = table["rcdy"] = ((1, 32, WIDTH), bf16)
    table["rcx"] = table["rcy"] = ((1, 64, WIDTH), bf16)
    table["rcu"] = table["rcd"] = ((blocks, 64, WIDTH), bf16)
    table["out"] = table["dinp"] = ((SEQ, WIDTH), bf16)
    for name in ("gwq", "gwk", "gwv", "gwo"):
        table[name] = ((24, WIDTH), f32)
    table["gfc1"] = table["gfc2"] = ((UNITS, WIDTH), f32)
    table["gsmall"] = ((16, 128), f32)
    table["store"] = len(RESULTS)
    for name, count in (
        ("gq", 10 * depth), ("gb", 10 * depth), ("gt", 10 * depth), ("gc", 4 + 8 * depth),
        ("sq", 8 * depth), ("sb", 8 * depth), ("st", 8 * depth), ("sc", 8 * depth + 6), ("e", 12),
    ):
        table[name + "_s"] = table[name + "_r"] = count
    return table


PLAN = (
    "own_blocks", "barrier", "S0", "M0", "L0", "own_cotangent", "norm1", "Sz", "Mz", "Sx", "Sy", "Mx", "My",
    "Lx", "Ly", "Sz", "Mz", "Sx", "Sy", "Mx", "My", "F0", "Ld", "Sz", "Mz", "Sx", "Sy", "Mx", "My", "Fz",
    "Sx", "Sy", "Mx", "My", "Sd", "Sd", "Sd", "Sd", "Ss", "vectors", "mixer_kernels", "gain1", "Md", "Md",
    "Md", "Md", "Fz", "L4", "L5", "Ms", "Fx", "Fy", "Fz", "L6", "L7", "unpack", "project", "Fx", "Fy",
    "mix0", "L4", "L5", "mix1", "L6", "L7", "Fx", "Fy", "mix2", "L4", "mix3", "hidden", "Fx", "Fy", "norm2",
    "L5", "L6", "L7", "sibling_rows", "feed0", "feed_grads0", "l0", "feed1", "feed_grads1", "fX", "l1", "l0",
    "feed2", "feed_grads2", "fY", "l2", "l1", "l0", "Fd", "Fd", "Fd", "Fd", "feed3", "feed_swap",
    "feed_grads3", "fD", "l3", "l2", "l1", "back2", "grad_mixed", "back4", "fa", "fb", "l2", "l3", "back5",
    "fa", "fb", "l3", "back6", "fa", "fb", "lX", "lY", "lO", "back7", "fa", "fb", "lD", "sent", "pack",
    "grad_normed", "fc", "fc", "la", "lb", "back1", "fc", "fc", "core_sums", "mD", "mX", "mY", "fv", "fv",
    "fv", "fv", "flip", "kernel0", "kernel1", "fw", "fw", "kernel2", "ma", "mb", "kernel3", "vector_tiles",
    "finish_out", "small_sums", "sD", "sX", "sY", "ma", "mb", "ma", "mb", "ma", "mb", "sa", "sb", "sa", "sb",
    "sa", "sb", "sa", "sb", "fe", "le", "mc", "sc", "mc", "sc", "mc", "sc", "mc", "sc", "mv", "sv", "mv",
    "sv", "mv", "sv", "mv", "sv", "mw", "sw", "mw", "sw", "me", "se", "store",
)
INPUTS = ("tok", "length", "cot", "iq", "ik", "iv", "io", "ifc1", "ifc2", "ibias", "ivec")
RESULTS = ("out", "dinp", "gwq", "gwk", "gwv", "gwo", "gfc1", "gfc2", "gsmall")
OUTPUTS = tuple("to_" + name for name in RESULTS)


def layer_kernel(depth, *refs):
    names = INPUTS + OUTPUTS + tuple(scratch_of(depth))
    m = SimpleNamespace(**dict(zip(names, refs, strict=True)))
    k = Links(depth)
    core = k.core

    def in_all(yx, zs):
        return (yx * 2 + core) * depth + zs

    def in_all_sib(yx, zs):
        return (yx * 2 + (1 - core)) * depth + zs

    def in_core(yx, zs):
        return yx * depth + zs

    def chip_rows(start, step):
        return pl.ds(pl.multiple_of(core * SEQ + start, step), step)

    def stored(name):
        place = RESULTS.index(name)
        return pltpu.make_async_copy(getattr(m, name), getattr(m, "to_" + name), m.store.at[place])

    core_rows = pl.ds(pl.multiple_of(core * SEQ, SEQ), SEQ)
    sib_rows = pl.ds(pl.multiple_of((1 - core) * SEQ, SEQ), SEQ)

    def swap(place, source, target):
        k.start(None, lambda: source, lambda: target, lambda: m.e_s.at[place], lambda: m.e_r.at[place], k.sib_dev)

    day = lax.broadcasted_iota(jnp.int32, (1, SEQ), 1).astype(f32)
    s_at = lax.broadcasted_iota(jnp.int32, (SEQ, SEQ), 0)
    t_at = lax.broadcasted_iota(jnp.int32, (SEQ, SEQ), 1)
    valid = (lax.broadcasted_iota(jnp.int32, (1, SEQ), 1) < m.length[0]).astype(f32)

    def own_blocks():
        here = in_all(k.me, k.z)
        for place, (first, second) in enumerate(((m.iq, m.ik), (m.iv, m.io))):
            pair = jnp.concatenate([first[...].astype(f32), second[...].astype(f32)], axis=0)
            m.qk[here, 48 * place : 48 * place + 48] = pair.astype(bf16)
        m.sm[here] = jnp.zeros((16, 128), f32)
        m.sm[here, 0:15, 0:24] = m.ivec[...].astype(f32)
        m.sm[here, 15:16, 0:UNITS] = m.ibias[...].astype(f32)
        m.ff[in_core(k.me, k.z), 0:UNITS] = m.ifc1[...]
        m.ff[in_core(k.me, k.z), UNITS : 2 * UNITS] = m.ifc2[...]

    def own_cotangent():
        m.ct[core_rows] = m.cot[...]
        swap(0, m.ct.at[core_rows], m.ct.at[core_rows])

    def norm1():
        def rows_of(start, step):
            rows = pl.ds(start, step)
            tokens = m.tok[rows].astype(f32)
            centred = tokens - jnp.mean(tokens, axis=1, keepdims=True)
            inverse = lax.rsqrt(jnp.mean(centred * centred, axis=1, keepdims=True) + EPSILON)
            m.s1[rows] = centred * inverse
            m.i1[rows] = jnp.broadcast_to(inverse, (step, 128))

        row_loop(SEQ, 32, rows_of)

    def vectors():
        total = jnp.zeros((16, WIDTH), f32)
        for wide in range(8):
            part = jnp.zeros((16, 128), f32)
            for zs in range(depth):
                tile = m.sm[wide * depth + zs]
                part = part + (pltpu.roll(tile, 24 * zs, 1) if zs else tile)
            padded = jnp.concatenate([part, jnp.zeros((16, WIDTH - 128), f32)], axis=1)
            total = total + (pltpu.roll(padded, 96 * wide, 1) if wide else padded)
        m.vec[...] = total
        m.vecc[...] = jnp.transpose(jnp.concatenate([total, jnp.zeros((112, WIDTH), f32)], axis=0))
        for yx in range(4):
            line = jnp.zeros((16, UNITS * depth), f32)
            for zs in range(depth):
                tile = jnp.concatenate([m.sm[in_all(yx, zs)], jnp.zeros((16, UNITS * depth - 128), f32)], axis=1)
                line = line + (pltpu.roll(tile, UNITS * zs, 1) if zs else tile)
            m.bias[yx] = line[8:16]

    def head_kernel(h, carry):
        rows = head_rows(h)
        decays = jnp.exp(-m.vecc[rows, 10:11] * day)
        m.ex[rows] = decays
        line = jnp.sum(m.vecc[rows, 9:10] * decays, axis=0, keepdims=True) * (1.0 / STATE)
        matrix = pltpu.roll(jnp.broadcast_to(line, (SEQ, SEQ)), 0, 1, stride=1, stride_axis=0)
        m.tt[h] = jnp.where(t_at >= s_at, matrix, 0.0)
        return carry

    def mixer_kernels():
        lax.fori_loop(0, HEADS, head_kernel, 0)

    def gain1():
        def rows_of(start, step):
            rows = pl.ds(start, step)
            m.nm[rows] = (m.s1[rows] * m.vec[0:1] + m.vec[1:2]).astype(bf16)

        row_loop(SEQ, 32, rows_of)
        m.nmt[...] = jnp.transpose(m.nm[...])

    def unpack_rows(w, carry):
        rows = pl.ds(pl.multiple_of(w * 96, 96), 96)
        for place, (first, second) in enumerate(((m.wq, m.wk), (m.wv, m.wo))):
            pair = m.qk[pl.ds(w * depth, depth), 48 * place : 48 * place + 48, :].astype(f32)
            first[rows] = pair[:, :24].reshape(96, WIDTH).astype(bf16)
            second[rows] = pair[:, 24:].reshape(96, WIDTH).astype(bf16)
        return carry

    def unpack():
        lax.fori_loop(0, 8, unpack_rows, 0)

    def project():
        m.qt[...] = jnp.transpose(dg(m.nm[...], m.wq[...], 1, 0) + m.vec[2:3]).astype(bf16)
        m.krt[...] = jnp.transpose(dg(m.nm[...], m.wk[...], 1, 0) + m.vec[3:4])
        m.vt[...] = (jnp.transpose(dg(m.nm[...], m.wv[...], 1, 0) + m.vec[4:5]) * valid).astype(bf16)

    def mix_head(h):
        rows = head_rows(h)
        raw = m.krt[rows]
        summed = raw * m.vecc[rows, 5:6]
        for j in range(1, 4):
            summed = summed + lane_shift(raw, j, False) * m.vecc[rows, 5 + j : 6 + j]
        keys = (summed * valid).astype(bf16)
        m.kt[rows] = keys
        scores = dg(keys, m.qt[rows], 0, 0) * (1.0 / HEAD_SIZE)
        weights = (scores * m.tt[h]).astype(bf16)
        m.mt[rows] = (dg(m.vt[rows], weights, 1, 0) * valid).astype(bf16)

    def hidden():
        m.hid[...] = dg(m.mt[...], m.wo[...], 0, 0)

    def norm2():
        def rows_of(start, step):
            rows = pl.ds(start, step)
            hidden = m.tok[rows].astype(f32) + m.hid[rows] + m.vec[11:12]
            m.hid[rows] = hidden
            centred = hidden - jnp.mean(hidden, axis=1, keepdims=True)
            inverse = lax.rsqrt(jnp.mean(centred * centred, axis=1, keepdims=True) + EPSILON)
            scaled = centred * inverse
            m.s2[rows] = scaled
            m.i2[rows] = jnp.broadcast_to(inverse, (step, 128))
            m.n2[chip_rows(start, step)] = (scaled * m.vec[12:13] + m.vec[13:14]).astype(bf16)

        row_loop(SEQ, 32, rows_of)
        swap(1, m.n2.at[core_rows], m.n2.at[core_rows])

    def sibling_rows():
        k.arrive(m.ct.at[sib_rows], m.e_r.at[0])
        k.arrive(m.n2.at[sib_rows], m.e_r.at[1])

    def finish_feed(ref, more):
        value = ref[...].astype(f32)
        for target, low, high in ((m.gfc1, 0, UNITS), (m.gfc2.at[0:32], UNITS, 128)):
            target[...] = target[...] + value[low:high] if more else value[low:high]

    def finish_last(ref, more):
        value = ref[...].astype(f32)
        m.gfc2[32:96] = m.gfc2[32:96] + value if more else value

    def finish_mats(ref, more):
        value = ref[...].astype(f32)
        for place, target in enumerate((m.gwq, m.gwk, m.gwv, m.gwo)):
            part = value[24 * place : 24 * place + 24]
            target[...] = target[...] + part if more else part

    def finish_small(ref, more):
        m.gsmall[...] = m.gsmall[...] + ref[...] if more else ref[...]

    steps = {}
    steps |= gather_z_first(k, "S", m.sm, in_all, 0, 16, 8, m.gt_s, m.gt_r, in_all_sib)
    steps |= gather_z_first(k, "M", m.qk, in_all, 0, UNITS, UNITS // 2, m.gq_s, m.gq_r, in_all_sib)
    steps |= gather_z_first(k, "F", m.ff, in_core, 0, 128, 64, m.gb_s, m.gb_r)
    steps |= gather_z_last(k, "L", m.ff, in_core, 128, 64, 32, m.gc_s, m.gc_r)
    slots = (m.rbdx, m.rbdy, m.rbx, m.rby, m.rbu, m.rbd)
    steps |= scatter_z_last(k, "f", m.gff, in_core, 0, 128, 64, slots, m.sb_s, m.sb_r, finish_feed)
    slots = (m.rcdx, m.rcdy, m.rcx, m.rcy, m.rcu, m.rcd)
    steps |= scatter_z_first(k, "l", m.gff, in_core, 128, 64, 32, slots, m.sc_s, m.sc_r, finish_last)
    slots = (m.rqdx, m.rqdy, m.rqx, m.rqy, m.rqu, m.rqd)
    steps |= scatter_z_last(k, "m", m.qk, in_all, 0, UNITS, UNITS // 2, slots, m.sq_s, m.sq_r, finish_mats)
    slots = (m.rtdx, m.rtdy, m.rtx, m.rty, m.rtu, m.rtd)
    steps |= scatter_z_last(k, "s", m.gs, in_all, 0, 16, 8, slots, m.st_s, m.st_r, finish_small)

    root = math.sqrt(2.0 / math.pi)
    chunk = UNITS * depth
    yx_of = (k.me, k.xs, k.ys, k.ds)

    def feed(which):
        yx = yx_of[which]
        blocks = pl.ds(yx * depth, depth)
        fc1 = m.ff[blocks, 0:UNITS, :].reshape(chunk, WIDTH)
        fc2 = m.ff[blocks, UNITS : 2 * UNITS, :].reshape(chunk, WIDTH)
        for r in range(2):
            rows = pl.ds(r * SEQ, SEQ)
            pre = dg(m.n2[rows], fc1, 1, 1) + m.bias[yx, 7:8]
            square = pre * pre
            tanh = jnp.tanh(root * pre * (1.0 + 0.044715 * square))
            half = 0.5 * (1.0 + tanh)
            slope = half + 0.5 * pre * (1.0 - tanh * tanh) * (root * (1.0 + 3 * 0.044715 * square))
            activated = (pre * half).astype(bf16)
            grad_pre = (dg(m.ct[rows], fc2, 1, 1) * slope).astype(bf16)
            m.act[rows] = activated
            m.dp[rows] = grad_pre
            if which == 0:
                m.outp[rows] = dg(activated, fc2, 1, 0)
                m.dn2[rows] = dg(grad_pre, fc1, 1, 0)
            else:
                m.outp[rows] += dg(activated, fc2, 1, 0)
                m.dn2[rows] += dg(grad_pre, fc1, 1, 0)

    def feed_swap():
        swap(2, m.dn2.at[sib_rows], m.dn2r)
        swap(3, m.outp.at[sib_rows], m.outr)

    def feed_grads(which):
        yx = yx_of[which]
        blocks = pl.ds(yx * depth, depth)
        m.gff[blocks, 0:UNITS] = dg(m.dp[...], m.n2[...], 0, 0).astype(bf16).reshape(depth, UNITS, WIDTH)
        m.gff[blocks, UNITS : 2 * UNITS] = (
            dg(m.act[...], m.ct[...], 0, 0).astype(bf16).reshape(depth, UNITS, WIDTH)
        )
        sums = jnp.sum(m.dp[...].astype(f32), axis=0, keepdims=True)
        lane = lax.broadcasted_iota(jnp.int32, (1, 128), 1)
        for zs in range(depth):
            line = (pltpu.roll(sums, chunk - UNITS * zs, 1) if zs else sums)[:, :128]
            m.gbias[yx * depth + zs] = jnp.broadcast_to(jnp.where(lane < UNITS, line, 0.0), (8, 128))

    def back2():
        m.gvec[...] = jnp.zeros((16, WIDTH), f32)
        k.arrive(m.dn2r, m.e_r.at[2])

        def rows_of(start, step):
            rows = pl.ds(start, step)
            grad_normed = m.dn2[chip_rows(start, step)] + m.dn2r[rows]
            scaled = m.s2[rows]
            grad_in = grad_normed * m.vec[12:13]
            first = jnp.mean(grad_in, axis=1, keepdims=True)
            second = jnp.mean(grad_in * scaled, axis=1, keepdims=True)
            top = m.cot[rows].astype(f32)
            grad_hidden = top + m.i2[rows, 0:1] * (grad_in - first - scaled * second)
            m.s2[rows] = grad_hidden
            rounded = grad_hidden.astype(bf16)
            m.da[rows] = rounded
            m.gvec[11:12] += jnp.sum(rounded.astype(f32), axis=0, keepdims=True)
            m.gvec[12:13] += jnp.sum(grad_normed * scaled, axis=0, keepdims=True)
            m.gvec[13:14] += jnp.sum(grad_normed, axis=0, keepdims=True)
            m.gvec[14:15] += jnp.sum(top, axis=0, keepdims=True)

        row_loop(SEQ, 32, rows_of)

    def grad_mixed():
        m.dmt[...] = (jnp.transpose(dg(m.da[...], m.wo[...], 1, 1)) * valid).astype(bf16)

    def back_head(h):
        rows = head_rows(h)
        queries, keys, grad_mixed, kernel = m.qt[rows], m.kt[rows], m.dmt[rows], m.tt[h]
        scores = dg(keys, queries, 0, 0) * (1.0 / HEAD_SIZE)
        weights = (scores * kernel).astype(bf16)
        grad_weights = dg(m.vt[rows], grad_mixed, 0, 0)
        grad_values = (dg(grad_mixed, weights, 1, 1) * valid).astype(bf16)
        m.dvt[rows] = grad_values
        grad_scores = (grad_weights * kernel).astype(bf16)
        grad_queries = (dg(keys, grad_scores, 1, 0) * (1.0 / HEAD_SIZE)).astype(bf16)
        m.dqt[rows] = grad_queries
        grad_keys = dg(queries, grad_scores, 1, 1) * (1.0 / HEAD_SIZE) * valid
        raw = m.krt[rows]
        at = lax.broadcasted_iota(jnp.int32, (HEAD_SIZE, 128), 1)
        grad_raw = grad_keys * m.vecc[rows, 5:6]
        sums = jnp.where(at == 5, jnp.sum(grad_keys * raw, axis=1, keepdims=True), 0.0)
        for j in range(1, 4):
            grad_raw = grad_raw + lane_shift(grad_keys, j, True) * m.vecc[rows, 5 + j : 6 + j]
            tap = jnp.sum(grad_keys * lane_shift(raw, j, False), axis=1, keepdims=True)
            sums = jnp.where(at == 5 + j, tap, sums)
        rounded = grad_raw.astype(bf16)
        m.dkt[rows] = rounded
        for place, value in ((2, grad_queries), (3, rounded), (4, grad_values)):
            sums = jnp.where(at == place, jnp.sum(value.astype(f32), axis=1, keepdims=True), sums)
        m.colsum[rows] = sums

    def pack_rows(part, carry):
        rows = pl.ds(pl.multiple_of(part * 384, 384), 384)
        normed = m.nmt[rows]
        grads = (
            dg(normed, m.dqt[...], 1, 1),
            dg(normed, m.dkt[...], 1, 1),
            dg(normed, m.dvt[...], 1, 1),
            dg(m.mt[rows], m.da[...], 1, 0),
        )
        for place in range(2):
            pair = [grad.reshape(4 * depth, 24, WIDTH) for grad in grads[2 * place : 2 * place + 2]]
            m.qk[pl.ds(part * 4 * depth, 4 * depth), 48 * place : 48 * place + 48, :] = jnp.concatenate(pair, axis=1).astype(bf16)
        return carry

    def pack():
        lax.fori_loop(0, 2, pack_rows, 0)
        for yx in range(4):
            swap(4 + yx, m.qk.at[pl.ds(in_all_sib(yx, 0), depth)], m.sr.at[pl.ds(yx * depth, depth)])

    def grad_normed():
        m.dn[...] = jnp.transpose(
            dg(m.wq[...], m.dqt[...], 1, 0) + dg(m.wk[...], m.dkt[...], 1, 0) + dg(m.wv[...], m.dvt[...], 1, 0)
        )

    def back1():
        def rows_of(start, step):
            rows = pl.ds(start, step)
            grad_out, scaled = m.dn[rows], m.s1[rows]
            grad_in = grad_out * m.vec[0:1]
            first = jnp.mean(grad_in, axis=1, keepdims=True)
            second = jnp.mean(grad_in * scaled, axis=1, keepdims=True)
            m.dinp[rows] = (m.s2[rows] + m.i1[rows, 0:1] * (grad_in - first - scaled * second)).astype(bf16)
            m.gvec[0:1] += jnp.sum(grad_out * scaled, axis=0, keepdims=True)
            m.gvec[1:2] += jnp.sum(grad_out, axis=0, keepdims=True)

        row_loop(SEQ, 32, rows_of)
        stored("dinp").start()

    def core_sum(yx):
        k.arrive(m.sr.at[pl.ds(yx * depth, depth)], m.e_r.at[4 + yx])

        def block_sum(zs, carry):
            add_into(m.qk.at[in_all(yx, zs)], m.sr.at[yx * depth + zs])
            return carry

        lax.fori_loop(0, depth, block_sum, 0)

    def core_sums():
        for yx in range(4):
            core_sum(yx)

    def flip():
        turn = (s_at + t_at == SEQ - 1).astype(bf16)
        m.kft[...] = dg(m.kt[...], turn, 1, 0).astype(bf16)
        m.vft[...] = dg(m.vt[...], turn, 1, 0).astype(bf16)

    def kernel_head(h):
        rows = head_rows(h)
        scores = dg(m.kft[rows], m.qt[rows], 0, 0) * (1.0 / HEAD_SIZE)
        grad_weights = dg(m.vft[rows], m.dmt[rows], 0, 0)
        product = jnp.where(s_at + t_at >= SEQ - 1, scores * grad_weights, 0.0)
        lined = pltpu.roll(product, 1, 1, stride=1, stride_axis=0)
        grad_kernel = jnp.sum(lined, axis=0, keepdims=True) * (1.0 / STATE)
        part = m.ex[rows] * grad_kernel
        at = lax.broadcasted_iota(jnp.int32, (HEAD_SIZE, 128), 1)
        grad_rate = -m.vecc[rows, 9:10] * jnp.sum(part * day, axis=1, keepdims=True)
        sums = jnp.where(at == 9, jnp.sum(part, axis=1, keepdims=True), m.colsum[rows])
        m.colsum[rows] = jnp.where(at == 10, grad_rate, sums)

    def vector_tiles():
        grads = m.gvec[...] + jnp.transpose(m.colsum[...])[0:16]
        row_at = lax.broadcasted_iota(jnp.int32, (16, 128), 0)
        lane_at = lax.broadcasted_iota(jnp.int32, (16, 128), 1)
        for wide in range(8):
            turned = (pltpu.roll(grads, WIDTH - 96 * wide, 1) if wide else grads)[:, :128]
            for zs in range(depth):
                tile = pltpu.roll(turned, 128 - 24 * zs, 1) if zs else turned
                tile = jnp.where((lane_at < 24) & (row_at < 15), tile, 0.0)
                own = jnp.concatenate([jnp.zeros((8, 128), f32), m.gbias[(wide // 2) * depth + zs]], axis=0)
                mine = (row_at == 15) & (core == wide % 2)
                m.gs[wide * depth + zs] = jnp.where(mine, own, tile)
        for yx in range(4):
            swap(8 + yx, m.gs.at[pl.ds(in_all_sib(yx, 0), depth)], m.srs.at[pl.ds(yx * depth, depth)])

    def small_sums():
        for yx in range(4):
            k.arrive(m.srs.at[pl.ds(yx * depth, depth)], m.e_r.at[8 + yx])
            for zs in range(depth):
                add_into(m.gs.at[in_all(yx, zs)], m.srs.at[yx * depth + zs])

    def finish_out():
        def rows_of(start, step):
            rows = pl.ds(start, step)
            m.out[rows] = (m.hid[rows] + (m.outp[chip_rows(start, step)] + m.outr[rows]) + m.vec[14:15]).astype(bf16)

        k.arrive(m.outr, m.e_r.at[3])
        row_loop(SEQ, 32, rows_of)
        stored("out").start()

    def store():
        for name in RESULTS[2:]:
            stored(name).start()
        k.drain()
        for name in RESULTS:
            stored(name).wait()

    compute = {
        "own_blocks": own_blocks, "barrier": k.barrier, "own_cotangent": own_cotangent, "norm1": norm1,
        "vectors": vectors, "mixer_kernels": mixer_kernels, "gain1": gain1, "unpack": unpack, "project": project,
        "hidden": hidden, "norm2": norm2, "sibling_rows": sibling_rows, "feed_swap": feed_swap, "sent": partial(k.drain, "M"), "store": store,
        "back2": back2, "grad_mixed": grad_mixed, "pack": pack, "grad_normed": grad_normed, "back1": back1,
        "core_sums": core_sums, "flip": flip, "vector_tiles": vector_tiles, "small_sums": small_sums, "finish_out": finish_out,
    }
    for which in range(4):
        compute["feed%d" % which] = partial(feed, which)
        compute["feed_grads%d" % which] = partial(feed_grads, which)
        compute["mix%d" % which] = partial(three_heads, 3 * which, mix_head)
        compute["back%d" % (4 + which)] = partial(three_heads, 3 * which, back_head)
        compute["kernel%d" % which] = partial(three_heads, 3 * which, kernel_head)
    for step in PLAN:
        if step in compute:
            compute[step]()
        else:
            next(steps[step])


def results_kernel(*refs):
    count = len(RESULTS) - 1
    sources, tile, targets, bias, vectors = refs[:count], refs[count], refs[9 : 9 + count], refs[17], refs[18]
    held, came, left = refs[19 : 19 + count], refs[-2], refs[-1]
    bring = [pltpu.make_async_copy(s, h, came.at[i]) for i, (s, h) in enumerate(zip(sources, held, strict=True))]
    take = [pltpu.make_async_copy(h, t, left.at[i]) for i, (h, t) in enumerate(zip(held, targets, strict=True))]
    for copy in bring:
        copy.start()
    bias[...] = tile[15:16, :UNITS]
    vectors[...] = tile[0:15, 0:24]
    for first, second in zip(bring, take, strict=True):
        first.wait()
        second.start()
    for copy in take:
        copy.wait()


def on_device_fast(
    tokens, lengths, cotangent, w_query, w_key, w_value, w_out, w_fc1, w_fc2, fc1_bias, vectors
):
    depth = lax.axis_size("narrow")
    scratch = []
    for entry in scratch_of(depth).values():
        scratch.append(pltpu.SemaphoreType.DMA((entry,)) if isinstance(entry, int) else pltpu.VMEM(*entry))
    in_vmem = pl.BlockSpec(memory_space=pltpu.VMEM)
    anywhere = pl.BlockSpec(memory_space=pl.ANY)
    in_smem = pl.BlockSpec(memory_space=pltpu.SMEM)
    shape = jax.ShapeDtypeStruct
    got = pl.pallas_call(
        partial(layer_kernel, depth),
        out_shape=[shape((SEQ, WIDTH), bf16)] * 2
        + [shape((24, WIDTH), f32)] * 4
        + [shape((UNITS, WIDTH), f32)] * 2
        + [shape((16, 128), f32)],
        in_specs=[in_vmem, in_smem] + [in_vmem] * 9,
        out_specs=[anywhere] * 9,
        scratch_shapes=scratch,
        compiler_params=pltpu.CompilerParams(
            collective_id=0, has_side_effects=True, vmem_limit_bytes=63 * 2**20
        ),
        name="h3_layer",
    )(
        tokens, lengths, cotangent, w_query, w_key, w_value, w_out, w_fc1.T, w_fc2, fc1_bias[None], vectors
    )
    results = pl.pallas_call(
        results_kernel,
        out_shape=[shape(x.shape, x.dtype) for x in got[:8]] + [shape((1, UNITS), f32), shape((15, 24), f32)],
        in_specs=[anywhere] * 8 + [in_vmem],
        out_specs=[anywhere] * 8 + [in_vmem] * 2,
        scratch_shapes=[pltpu.VMEM(x.shape, x.dtype) for x in got[:8]] + [pltpu.SemaphoreType.DMA((8,))] * 2,
        name="results",
    )(*got)
    out, grad_in, g_query, g_key, g_value, g_out, g_fc1, g_fc2, g_bias, g_vectors = results
    return out, grad_in, g_query, g_key, g_value, g_out, g_fc1.T, g_fc2, g_bias.reshape(-1), g_vectors


def fits(mesh):
    return mesh.shape["wide"] == 8 and mesh.shape["narrow"] == 4


def solution(mesh):
    placed = (
        P(("wide", "narrow"), None),
        P(("wide", "narrow")),
        P(("wide", "narrow"), None),
        P(("wide", "narrow"), None),
        P(("wide", "narrow"), None),
        P(("wide", "narrow"), None),
        P(("wide", "narrow"), None),
        P(None, ("wide", "narrow")),
        P(("wide", "narrow"), None),
        P(("wide", "narrow")),
        P(None, ("wide", "narrow")),
    )
    return jax.shard_map(
        on_device_fast if fits(mesh) else on_device,
        mesh=mesh,
        in_specs=placed,
        out_specs=(
            P(("wide", "narrow"), None),
            P(("wide", "narrow"), None),
            P(("wide", "narrow"), None),
            P(("wide", "narrow"), None),
            P(("wide", "narrow"), None),
            P(("wide", "narrow"), None),
            P(None, ("wide", "narrow")),
            P(("wide", "narrow"), None),
            P(("wide", "narrow")),
            P(None, ("wide", "narrow")),
        ),
        check_vma=False,
    )
```

```python
import math
from functools import partial
from types import SimpleNamespace

import jax
import jax.numpy as jnp
from jax import lax
from jax.experimental import pallas as pl
from jax.experimental.pallas import tpu as pltpu
from jax.sharding import PartitionSpec as P

HEAD_SIZE = 64
STATE = 64


EPSILON = 1e-05


def normalize(values):
    average = jnp.mean(values, axis=-1, keepdims=True)
    centred = values - average
    variance = jnp.mean(centred * centred, axis=-1, keepdims=True)
    inverse = lax.rsqrt(variance + EPSILON)
    return (centred * inverse, inverse)


def norm_back(grad_in, scaled, inverse):
    first = jnp.mean(grad_in, axis=-1, keepdims=True)
    second = jnp.mean(grad_in * scaled, axis=-1, keepdims=True)
    return inverse * (grad_in - first - scaled * second)


def shift_mix(key_raw, shift_taps):
    summed = key_raw * shift_taps[0]
    for offset in range(1, 4):
        delayed = jnp.concatenate(
            [jnp.zeros((offset, key_raw.shape[1]), key_raw.dtype), key_raw[:-offset]], axis=0
        )
        summed = summed + delayed * shift_taps[offset]
    return summed


def kernel_rows(coefficient, decay_rate, length_all):
    distance = jnp.arange(length_all).astype(jnp.float32)
    decays = jnp.exp(-decay_rate[:, :, None] * distance[None, None, :])
    return jnp.sum(coefficient[:, :, None] * decays, axis=1) / STATE


def toeplitz(kernel_row):
    length_all = kernel_row.shape[0]
    wrapped = jnp.concatenate(
        [kernel_row[:1], jnp.zeros((length_all,), kernel_row.dtype), kernel_row[:0:-1]]
    )
    tiled_row = jnp.tile(wrapped, length_all)[: length_all * (2 * length_all - 1)]
    return tiled_row.reshape(length_all, 2 * length_all - 1)[:, :length_all]


def split_heads(values, row_count):
    return values.reshape(row_count, -1, HEAD_SIZE).transpose(1, 0, 2)


def merge_heads(per_head):
    head_count = per_head.shape[0]
    row_count = per_head.shape[1]
    merged = per_head.transpose(1, 0, 2).reshape(row_count, head_count * HEAD_SIZE)
    return merged


def pack_rows(matrices, shard_count):
    return jnp.concatenate(
        [matrix.reshape(shard_count, -1) for matrix in matrices], axis=1
    ).reshape(-1)


def unpack_rows(flat, matrices, shard_count):
    pieces = []
    offset = 0
    for matrix in matrices:
        rows_own = matrix.shape[0] // shard_count
        extent = matrix.size // shard_count
        pieces.append(flat[offset : offset + extent].reshape((rows_own,) + matrix.shape[1:]))
        offset = offset + extent
    return pieces


def mixer_forward(queries, keys, values, kernel, row_count):

    def head_forward(parts):
        query_head, key_head, value_head, kernel_row = parts
        scores = jnp.dot(query_head, key_head.T, preferred_element_type=jnp.float32) / HEAD_SIZE
        weights_mix = (scores * toeplitz(kernel_row)).astype(jnp.bfloat16)
        return jnp.dot(weights_mix, value_head, preferred_element_type=jnp.float32)

    per_head = lax.map(
        head_forward,
        (
            split_heads(queries, row_count),
            split_heads(keys, row_count),
            split_heads(values, row_count),
            kernel,
        ),
    )
    return merge_heads(per_head)


def mixer_backward(queries, keys, values, grad_mixed, kernel, row_count):

    def head_backward(parts):
        query_head, key_head, value_head, grad_head, kernel_row = parts
        scores = jnp.dot(query_head, key_head.T, preferred_element_type=jnp.float32) / HEAD_SIZE
        toeplitz_mat, pullback = jax.vjp(toeplitz, kernel_row)
        weights_mix = (scores * toeplitz_mat).astype(jnp.bfloat16)
        grad_weights = jnp.dot(grad_head, value_head.T, preferred_element_type=jnp.float32)
        grad_values = jnp.dot(weights_mix.T, grad_head, preferred_element_type=jnp.float32)
        grad_scores = (grad_weights * toeplitz_mat).astype(jnp.bfloat16)
        grad_queries = (
            jnp.dot(grad_scores, key_head, preferred_element_type=jnp.float32) / HEAD_SIZE
        )
        grad_keys = (
            jnp.dot(grad_scores.T, query_head, preferred_element_type=jnp.float32) / HEAD_SIZE
        )
        grad_kernel = pullback(grad_weights * scores)[0]
        return (grad_queries, grad_keys, grad_values, grad_kernel)

    head_grads = lax.map(
        head_backward,
        (
            split_heads(queries, row_count),
            split_heads(keys, row_count),
            split_heads(values, row_count),
            split_heads(grad_mixed, row_count),
            kernel,
        ),
    )
    grad_kernel = head_grads[3]
    return (
        merge_heads(head_grads[0]),
        merge_heads(head_grads[1]),
        merge_heads(head_grads[2]),
        grad_kernel,
    )


def on_device(
    tokens, lengths, cotangent, w_query, w_key, w_value, w_out, w_fc1, w_fc2, fc1_bias, vectors
):
    shard_count = lax.axis_size(("wide", "narrow"))
    gathered = (
        lax.all_gather(w_query, ("wide", "narrow"), axis=0, tiled=True),
        lax.all_gather(w_key, ("wide", "narrow"), axis=0, tiled=True),
        lax.all_gather(w_value, ("wide", "narrow"), axis=0, tiled=True),
        lax.all_gather(w_out, ("wide", "narrow"), axis=0, tiled=True),
        lax.all_gather(w_fc1, ("wide", "narrow"), axis=1, tiled=True),
        lax.all_gather(w_fc2, ("wide", "narrow"), axis=0, tiled=True),
        lax.all_gather(fc1_bias, ("wide", "narrow"), axis=0, tiled=True),
        lax.all_gather(vectors, ("wide", "narrow"), axis=1, tiled=True),
    )
    query_full, key_full, value_full, out_full, fc1_full, fc2_full, bias_full, vector_full = (
        gathered
    )
    params = vector_full.astype(jnp.float32)
    fc1_shift = bias_full.astype(jnp.float32)
    seq_len = tokens.shape[0]
    head_count = params.shape[1] // HEAD_SIZE
    seq_length = lengths[0]
    valid_mask = (jnp.arange(seq_len) < seq_length).astype(jnp.float32)[:, None]
    residual = tokens.astype(jnp.float32)
    scaled1, inverse1 = normalize(residual)
    normed = (scaled1 * params[0] + params[1]).astype(jnp.bfloat16)
    queries = (jnp.dot(normed, query_full, preferred_element_type=jnp.float32) + params[2]).astype(
        jnp.bfloat16
    )
    key_raw = jnp.dot(normed, key_full, preferred_element_type=jnp.float32) + params[3]
    keys = (shift_mix(key_raw, params[5:9]) * valid_mask).astype(jnp.bfloat16)
    values = (
        (jnp.dot(normed, value_full, preferred_element_type=jnp.float32) + params[4]) * valid_mask
    ).astype(jnp.bfloat16)
    coefficient = params[9].reshape(head_count, STATE)
    decay_rate = params[10].reshape(head_count, STATE)
    kernel_fn = partial(kernel_rows, length_all=seq_len)
    kernel, kernel_pull = jax.vjp(kernel_fn, coefficient, decay_rate)
    mixed = mixer_forward(queries, keys, values, kernel, seq_len)
    mixed_out = (mixed * valid_mask).astype(jnp.bfloat16)
    hidden = (
        residual + jnp.dot(mixed_out, out_full, preferred_element_type=jnp.float32) + params[11]
    )
    scaled2, inverse2 = normalize(hidden)
    normed2 = (scaled2 * params[12] + params[13]).astype(jnp.bfloat16)
    pre_act = jnp.dot(normed2, fc1_full, preferred_element_type=jnp.float32) + fc1_shift
    activated = jax.nn.gelu(pre_act).astype(jnp.bfloat16)
    output = (
        hidden + jnp.dot(activated, fc2_full, preferred_element_type=jnp.float32) + params[14]
    ).astype(jnp.bfloat16)
    again = (
        lax.all_gather(w_query, ("wide", "narrow"), axis=0, tiled=True),
        lax.all_gather(w_key, ("wide", "narrow"), axis=0, tiled=True),
        lax.all_gather(w_value, ("wide", "narrow"), axis=0, tiled=True),
        lax.all_gather(w_out, ("wide", "narrow"), axis=0, tiled=True),
        lax.all_gather(w_fc1, ("wide", "narrow"), axis=1, tiled=True),
        lax.all_gather(w_fc2, ("wide", "narrow"), axis=0, tiled=True),
        lax.all_gather(fc1_bias, ("wide", "narrow"), axis=0, tiled=True),
        lax.all_gather(vectors, ("wide", "narrow"), axis=1, tiled=True),
    )
    query_back, key_back, value_back, out_back, fc1_back, fc2_back = (
        again[0],
        again[1],
        again[2],
        again[3],
        again[4],
        again[5],
    )
    grad_top = cotangent.astype(jnp.float32)
    grad_fc2 = jnp.dot(activated.T, cotangent, preferred_element_type=jnp.float32)
    grad_activated = jnp.dot(cotangent, fc2_back.T, preferred_element_type=jnp.float32)
    gelu_value, gelu_pull = jax.vjp(jax.nn.gelu, pre_act)
    grad_pre = gelu_pull(grad_activated)[0].astype(jnp.bfloat16)
    grad_fc1_turned = jnp.dot(grad_pre.T, normed2, preferred_element_type=jnp.float32)
    grad_fc1_bias = jnp.sum(grad_pre.astype(jnp.float32), axis=0)[:, None]
    mlp_terms = [grad_fc1_turned, grad_fc2, grad_fc1_bias]
    mlp_flat = lax.psum_scatter(
        pack_rows(mlp_terms, shard_count), ("wide", "narrow"), scatter_dimension=0, tiled=True
    )
    mlp_sums = unpack_rows(mlp_flat, mlp_terms, shard_count)
    grad_normed2 = jnp.dot(grad_pre, fc1_back.T, preferred_element_type=jnp.float32)
    grad_hidden = grad_top + norm_back(grad_normed2 * params[12], scaled2, inverse2)
    grad_attn = grad_hidden.astype(jnp.bfloat16)
    grad_out = jnp.dot(mixed_out.T, grad_attn, preferred_element_type=jnp.float32)
    grad_mixed = (
        jnp.dot(grad_attn, out_back.T, preferred_element_type=jnp.float32) * valid_mask
    ).astype(jnp.bfloat16)
    grad_q, grad_k, grad_v, grad_kernel = mixer_backward(
        queries, keys, values, grad_mixed, kernel, seq_len
    )
    grad_queries = grad_q.astype(jnp.bfloat16)
    grad_values = (grad_v * valid_mask).astype(jnp.bfloat16)
    shift_value, shift_pull = jax.vjp(shift_mix, key_raw, params[5:9])
    grad_key_full, grad_taps = shift_pull(grad_k * valid_mask)
    grad_key_raw = grad_key_full.astype(jnp.bfloat16)
    grad_query = jnp.dot(normed.T, grad_queries, preferred_element_type=jnp.float32)
    grad_key = jnp.dot(normed.T, grad_key_raw, preferred_element_type=jnp.float32)
    grad_value = jnp.dot(normed.T, grad_values, preferred_element_type=jnp.float32)
    grad_normed = jnp.dot(grad_queries, query_back.T, preferred_element_type=jnp.float32)
    grad_normed = grad_normed + jnp.dot(
        grad_key_raw, key_back.T, preferred_element_type=jnp.float32
    )
    grad_normed = grad_normed + jnp.dot(
        grad_values, value_back.T, preferred_element_type=jnp.float32
    )
    input_grad = (grad_hidden + norm_back(grad_normed * params[0], scaled1, inverse1)).astype(
        jnp.bfloat16
    )
    grad_coef, grad_rate = kernel_pull(grad_kernel)
    grad_vectors = jnp.concatenate(
        [
            jnp.sum(grad_normed * scaled1, axis=0)[None],
            jnp.sum(grad_normed, axis=0)[None],
            jnp.sum(grad_queries.astype(jnp.float32), axis=0)[None],
            jnp.sum(grad_key_raw.astype(jnp.float32), axis=0)[None],
            jnp.sum(grad_values.astype(jnp.float32), axis=0)[None],
            grad_taps,
            grad_coef.reshape(1, -1),
            grad_rate.reshape(1, -1),
            jnp.sum(grad_attn.astype(jnp.float32), axis=0)[None],
            jnp.sum(grad_normed2 * scaled2, axis=0)[None],
            jnp.sum(grad_normed2, axis=0)[None],
            jnp.sum(grad_top, axis=0)[None],
        ],
        axis=0,
    )
    mixer_terms = [grad_query, grad_key, grad_value, grad_out, grad_vectors.T]
    mixer_flat = lax.psum_scatter(
        pack_rows(mixer_terms, shard_count), ("wide", "narrow"), scatter_dimension=0, tiled=True
    )
    mixer_sums = unpack_rows(mixer_flat, mixer_terms, shard_count)
    return (
        output,
        input_grad,
        mixer_sums[0],
        mixer_sums[1],
        mixer_sums[2],
        mixer_sums[3],
        mlp_sums[0].T,
        mlp_sums[1],
        mlp_sums[2].reshape(-1),
        mixer_sums[4].T,
    )


f32, bf16 = jnp.float32, jnp.bfloat16
MESH = pl.DeviceIdType.MESH


def dg(left, right, left_dim, right_dim):
    return lax.dot_general(
        left, right, (((left_dim,), (right_dim,)), ((), ())), preferred_element_type=f32
    )


def when(condition, body):
    if condition is None:
        body()
    else:
        pl.when(condition)(body)


def both(first, second):
    if first is None:
        return second
    if second is None:
        return first
    return jnp.logical_and(first, second)


class Links:
    def __init__(self, depth):
        wide, z = lax.axis_index("wide"), lax.axis_index("narrow")
        self.depth = depth
        self.z, self.core = z, lax.rem(wide, 2)
        self.x, self.y = lax.rem(lax.div(wide, 2), 2), lax.div(wide, 4)
        self.me = self.y * 2 + self.x
        self.xs = self.y * 2 + (1 - self.x)
        self.ys = (1 - self.y) * 2 + self.x
        self.ds = (1 - self.y) * 2 + (1 - self.x)
        self.sib_dev = (self.me * 2 + (1 - self.core), z)
        self.x_dev = (self.xs * 2 + self.core, z)
        self.y_dev = (self.ys * 2 + self.core, z)
        self.up_dev = (wide, z + 1)
        self.down_dev = (wide, z - 1)
        self.has_up = z < depth - 1
        self.has_down = z > 0
        self.at_end = jnp.logical_or(z == 0, z == depth - 1)

    def barrier(self):
        semaphore = pltpu.get_barrier_semaphore()

        def greet(device):
            pl.semaphore_signal(semaphore, inc=1, device_id=device, device_id_type=MESH)

        for device in (self.sib_dev, self.x_dev, self.y_dev):
            greet(device)
        pl.when(self.has_up)(lambda: greet(self.up_dev))
        pl.when(self.has_down)(lambda: greet(self.down_dev))
        peers = 3 + self.has_up.astype(jnp.int32) + self.has_down.astype(jnp.int32)
        pl.semaphore_wait(semaphore, peers)

    def start(self, condition, source, target, send, receive, device):
        when(
            condition,
            lambda: pltpu.make_async_remote_copy(
                src_ref=source(),
                dst_ref=target(),
                send_sem=send,
                recv_sem=receive,
                device_id=device,
                device_id_type=MESH,
            ).start(),
        )

    def arrive(self, target, receive):
        pltpu.make_async_remote_copy(
            src_ref=target,
            dst_ref=target,
            send_sem=receive,
            recv_sem=receive,
            device_id=self.sib_dev,
            device_id_type=MESH,
        ).wait_recv()

    def left(self, extent, semaphore):
        pltpu.make_async_remote_copy(
            src_ref=extent,
            dst_ref=extent,
            send_sem=semaphore,
            recv_sem=semaphore,
            device_id=self.sib_dev,
            device_id_type=MESH,
        ).wait_send()

    def left_along(self, extent, semaphore):
        pl.when(self.at_end)(lambda: self.left(extent(1), semaphore))
        pl.when(jnp.logical_not(self.at_end))(lambda: self.left(extent(self.depth + 1), semaphore))


def near(k, distance):
    if distance == 0:
        return ((None, k.z, False),)
    return ((k.z >= distance, k.z - distance, True), (k.z + distance < k.depth, k.z + distance, False))


def gather_z_first(k, name, buf, index, low, rows, half, ss, rs, sib_index=None):
    depth = k.depth

    def block(yx, zs, lo=0, n=rows):
        return buf.at[index(yx, zs), pl.ds(low + lo, n)]

    def send(condition, yx, zs, lo, n, device, r, way=0):
        ref = lambda: block(yx, zs, lo, n)
        k.start(condition, ref, ref, ss.at[way], rs.at[r], device)

    def to_sib(condition, yx, zs):
        if sib_index is not None:
            send(condition, yx, zs, 0, rows, k.sib_dev, 4 * depth)

    def outward(condition, zs):
        send(condition, k.me, zs, 0, rows, k.x_dev, depth + zs)
        send(condition, k.me, zs, 0, rows, k.y_dev, 2 * depth + zs)
        to_sib(condition, k.me, zs)

    def along(condition, zs, up, down):
        if up:
            send(both(condition, k.has_up), k.me, zs, 0, rows, k.up_dev, zs, 1)
        if down:
            send(both(condition, k.has_down), k.me, zs, 0, rows, k.down_dev, zs, 1)

    def take(condition, yx, zs, r):
        when(condition, lambda: k.arrive(block(yx, zs), rs.at[r]))

    def own():
        along(None, k.z, True, True)
        outward(None, k.z)
        yield

    def z_steps():
        for d in range(1, depth):
            for condition, zs, below in near(k, d):
                take(condition, k.me, zs, zs)
                along(condition, zs, below, not below)
                outward(condition, zs)
            yield

    def x_steps():
        for d in range(depth):
            for condition, zs, _ in near(k, d):
                take(condition, k.xs, zs, depth + zs)
                send(condition, k.xs, zs, 0, half, k.y_dev, 3 * depth + zs)
                to_sib(condition, k.xs, zs)
            yield

    def y_steps():
        for d in range(depth):
            for condition, zs, _ in near(k, d):
                take(condition, k.ys, zs, 2 * depth + zs)
                send(condition, k.ys, zs, half, rows - half, k.x_dev, 3 * depth + zs)
                to_sib(condition, k.ys, zs)
            yield

    def d_steps():
        for d in range(depth):
            for condition, zs, _ in near(k, d):
                take(condition, k.ds, zs, 3 * depth + zs)
                to_sib(condition, k.ds, zs)
            yield

    def extent(blocks):
        return buf.at[pl.ds(0, blocks), pl.ds(low, rows)]

    def sib_steps():
        k.arrive(extent(4 * depth), rs.at[4 * depth])
        yield

    def left():
        k.left(extent((7 if sib_index is not None else 3) * depth), ss.at[0])
        k.left_along(extent, ss.at[1])
        yield

    steps = {"0": own(), "z": z_steps(), "x": x_steps(), "y": y_steps(), "d": d_steps(), "s": sib_steps(), ".": left()}
    return {name + key: step for key, step in steps.items()}


def gather_z_last(k, name, buf, index, low, rows, half, ss, rs):
    depth = k.depth
    yx_of = (k.me, k.xs, k.ys, k.ds)

    def block(yx, zs, lo=0, n=rows):
        return buf.at[index(yx, zs), pl.ds(low + lo, n)]

    def send(condition, yx, zs, lo, n, device, r, way=0):
        ref = lambda: block(yx, zs, lo, n)
        k.start(condition, ref, ref, ss.at[way], rs.at[r], device)

    def along(condition, which, zs, up, down):
        yx, place = yx_of[which], 3 + which * depth + zs
        if up:
            send(both(condition, k.has_up), yx, zs, 0, rows, k.up_dev, place, 1 + which)
        if down:
            send(both(condition, k.has_down), yx, zs, 0, rows, k.down_dev, place, 1 + which)

    def own():
        send(None, k.me, k.z, 0, rows, k.x_dev, 0)
        send(None, k.me, k.z, 0, rows, k.y_dev, 1)
        along(None, 0, k.z, True, True)
        yield

    def x_step():
        k.arrive(block(k.xs, k.z), rs.at[0])
        send(None, k.xs, k.z, 0, half, k.y_dev, 2)
        along(None, 1, k.z, True, True)
        yield

    def y_step():
        k.arrive(block(k.ys, k.z), rs.at[1])
        send(None, k.ys, k.z, half, rows - half, k.x_dev, 2)
        along(None, 2, k.z, True, True)
        yield

    def d_step():
        k.arrive(block(k.ds, k.z), rs.at[2])
        along(None, 3, k.z, True, True)
        yield

    def z_steps(which):
        for d in range(1, depth):
            for condition, zs, below in near(k, d):
                when(condition, lambda zs=zs: k.arrive(block(yx_of[which], zs), rs.at[3 + which * depth + zs]))
                along(condition, which, zs, below, not below)
            yield

    def extent(blocks):
        return buf.at[pl.ds(0, blocks), pl.ds(low, rows)]

    def left():
        k.left(extent(3), ss.at[0])
        for which in range(4):
            k.left_along(extent, ss.at[1 + which])
        yield

    steps = {"0": own(), "x": x_step(), "y": y_step(), "d": d_step(), ".": left()}
    for which in range(4):
        steps[str(4 + which)] = z_steps(which)
    return {name + key: step for key, step in steps.items()}


def add_into(ref, *others):
    total = ref[...].astype(f32)
    for other in others:
        total = total + other[...].astype(f32)
    ref[...] = total.astype(ref.dtype)


def scatter_order(depth):
    return ([0, depth - 1] + list(range(1, depth - 1)))[:depth]


def along_z(k, zd, wave, block, from_up, from_down, rs_up, rs_down, send):
    top, low = k.depth - 1 - wave, wave

    def take(slot, semaphore):
        k.arrive(slot, semaphore)
        add_into(block, slot)

    if zd < top:
        if wave:
            pl.when(k.z == top)(lambda: take(from_up, rs_up))
        send(k.z == top, False)
    if zd > low:
        if wave:
            pl.when(k.z == low)(lambda: take(from_down, rs_down))
        send(k.z == low, True)


def scatter_z_last(k, name, buf, index, low, rows, half, slots, ss, rs, finish):
    depth = k.depth
    from_x_diag, from_y_diag, from_xy, from_up, from_down = slots
    order = scatter_order(depth)
    rest = rows - half

    def block(yx, zd, lo=0, n=rows):
        return buf.at[index(yx, zd), pl.ds(low + lo, n)]

    def send(condition, source, target, device, r):
        k.start(condition, source, target, ss.at[0], rs.at[r], device)

    def x_part(zd, lo, n):
        return from_xy.at[zd, 0, pl.ds(lo, n)]

    def y_part(zd, lo, n):
        return from_xy.at[zd, 1, pl.ds(lo, n)]

    def pure_x():
        for zd in order:
            send(None, lambda zd=zd: block(k.xs, zd, half, rest), lambda zd=zd: x_part(zd, half, rest), k.x_dev, 2 * depth + zd)
        yield

    def pure_y():
        for zd in order:
            send(None, lambda zd=zd: block(k.ys, zd, 0, half), lambda zd=zd: y_part(zd, 0, half), k.y_dev, 2 * depth + zd)
        yield

    def diagonal():
        for zd in order:
            send(None, lambda zd=zd: block(k.ds, zd, 0, half), lambda zd=zd: from_y_diag.at[zd], k.y_dev, zd)
            send(None, lambda zd=zd: block(k.ds, zd, half, rest), lambda zd=zd: from_x_diag.at[zd], k.x_dev, depth + zd)
        yield

    def y_added():
        for zd in order:
            k.arrive(from_y_diag.at[zd], rs.at[zd])
            add_into(block(k.xs, zd, 0, half), from_y_diag.at[zd])
            send(None, lambda zd=zd: block(k.xs, zd, 0, half), lambda zd=zd: x_part(zd, 0, half), k.x_dev, 2 * depth + zd)
            yield

    def x_added():
        for zd in order:
            k.arrive(from_x_diag.at[zd], rs.at[depth + zd])
            add_into(block(k.ys, zd, half, rest), from_x_diag.at[zd])
            send(None, lambda zd=zd: block(k.ys, zd, half, rest), lambda zd=zd: y_part(zd, half, rest), k.y_dev, 2 * depth + zd)
            yield

    def wave(zd, number):
        def send_z(condition, up):
            place = (4 if up else 3) * depth + zd
            slot = from_down if up else from_up
            send(condition, lambda: block(k.me, zd), lambda: slot.at[zd], k.up_dev if up else k.down_dev, place)

        along_z(
            k, zd, number, block(k.me, zd), from_up.at[zd], from_down.at[zd],
            rs.at[3 * depth + zd], rs.at[4 * depth + zd], send_z,
        )

    def collect():
        for zd in order:
            k.arrive(from_xy.at[zd], rs.at[2 * depth + zd])
            add_into(block(k.me, zd), from_xy.at[zd, 0], from_xy.at[zd, 1])
            wave(zd, 0)
            yield

    def waves(number):
        for zd in order:
            if zd < depth - 1 - number or zd > number:
                wave(zd, number)
                yield

    def end():
        finish(block(k.me, k.z), False)

        def last_up():
            k.arrive(from_up.at[k.z], rs.at[3 * depth + k.z])
            finish(from_up.at[k.z], True)

        def last_down():
            k.arrive(from_down.at[k.z], rs.at[4 * depth + k.z])
            finish(from_down.at[k.z], True)

        pl.when(k.has_up)(last_up)
        pl.when(k.has_down)(last_down)
        yield

    def left():
        k.left(buf.at[pl.ds(0, 4 * depth - 1), pl.ds(low, rows)], ss.at[0])
        yield

    steps = {"X": pure_x(), "Y": pure_y(), "D": diagonal(), "a": y_added(), "b": x_added(), "c": collect(), "e": end()}
    steps |= {"v": waves(1), "w": waves(2), ".": left()}
    return {name + key: step for key, step in steps.items()}


def scatter_z_first(k, name, buf, index, low, rows, half, slots, ss, rs, finish):
    depth = k.depth
    from_x_diag, from_y_diag, from_xy, from_up, from_down = slots
    yx_of = (k.me, k.xs, k.ys, k.ds)
    rest = rows - half
    base = 8 * depth

    def block(yx, zd, lo=0, n=rows):
        return buf.at[index(yx, zd), pl.ds(low + lo, n)]

    def send(condition, source, target, device, r):
        k.start(condition, source, target, ss.at[0], rs.at[r], device)

    def x_part(lo, n):
        return from_xy.at[0, 0, pl.ds(lo, n)]

    def y_part(lo, n):
        return from_xy.at[0, 1, pl.ds(lo, n)]

    def waves(which):
        yx = yx_of[which]
        for number in range(depth - 1):
            for zd in scatter_order(depth):
                place = which * depth + zd

                def send_z(condition, up, zd=zd, place=place):
                    slot, number = (from_down, 4 * depth + place) if up else (from_up, place)
                    send(condition, lambda: block(yx, zd), lambda: slot.at[place], k.up_dev if up else k.down_dev, number)

                along_z(
                    k, zd, number, block(yx, zd), from_up.at[place], from_down.at[place],
                    rs.at[place], rs.at[4 * depth + place], send_z,
                )
            yield

    def own(which):
        yx = yx_of[which]
        place = which * depth + k.z

        def take(slot, semaphore):
            k.arrive(slot, semaphore)
            add_into(block(yx, k.z), slot)

        pl.when(k.has_up)(lambda: take(from_up.at[place], rs.at[place]))
        pl.when(k.has_down)(lambda: take(from_down.at[place], rs.at[4 * depth + place]))

    def own_me():
        own(0)
        yield

    def own_x():
        own(1)
        send(None, lambda: block(k.xs, k.z, half, rest), lambda: x_part(half, rest), k.x_dev, base + 2)
        yield

    def own_y():
        own(2)
        send(None, lambda: block(k.ys, k.z, 0, half), lambda: y_part(0, half), k.y_dev, base + 2)
        yield

    def own_d():
        own(3)
        send(None, lambda: block(k.ds, k.z, 0, half), lambda: from_y_diag.at[0], k.y_dev, base)
        send(None, lambda: block(k.ds, k.z, half, rest), lambda: from_x_diag.at[0], k.x_dev, base + 1)
        yield

    def y_added():
        k.arrive(from_y_diag.at[0], rs.at[base])
        add_into(block(k.xs, k.z, 0, half), from_y_diag.at[0])
        send(None, lambda: block(k.xs, k.z, 0, half), lambda: x_part(0, half), k.x_dev, base + 2)
        yield

    def x_added():
        k.arrive(from_x_diag.at[0], rs.at[base + 1])
        add_into(block(k.ys, k.z, half, rest), from_x_diag.at[0])
        send(None, lambda: block(k.ys, k.z, half, rest), lambda: y_part(half, rest), k.y_dev, base + 2)
        yield

    def end():
        k.arrive(from_xy.at[0], rs.at[base + 2])
        finish(block(k.me, k.z), False)
        finish(from_xy.at[0, 0], True)
        finish(from_xy.at[0, 1], True)
        yield

    def left():
        k.left(buf.at[pl.ds(0, 4 * depth - 1), pl.ds(low, rows)], ss.at[0])
        yield

    steps = {"O": own_me(), "X": own_x(), "Y": own_y(), "D": own_d(), "a": y_added(), "b": x_added(), "e": end()}
    steps["."] = left()
    steps |= {str(which): waves(which) for which in range(4)}
    return {name + key: step for key, step in steps.items()}


SEQ, WIDTH, UNITS = 256, 768, 96
HEADS = WIDTH // HEAD_SIZE


def row_loop(total, step, body):
    def once(i, carry):
        body(pl.multiple_of(i * step, step), step)
        return carry

    lax.fori_loop(0, total // step, once, 0)


def lane_shift(values, offset, left):
    extent = values.shape[1]
    lane = lax.broadcasted_iota(jnp.int32, values.shape, 1)
    if left:
        return jnp.where(lane < extent - offset, pltpu.roll(values, extent - offset, 1), 0.0)
    return jnp.where(lane >= offset, pltpu.roll(values, offset, 1), 0.0)


def three_heads(first, body):
    for h in range(first, first + 3):
        body(h)


def head_rows(h):
    return pl.ds(pl.multiple_of(h * HEAD_SIZE, HEAD_SIZE), HEAD_SIZE)


def scratch_of(depth):
    devices, blocks = 8 * depth, 4 * depth
    table = {
        "qk": ((devices, UNITS, WIDTH), bf16),
        "ff": ((blocks, 2 * UNITS, WIDTH), bf16),
        "sm": ((devices, 16, 128), f32),
        "gff": ((blocks, 2 * UNITS, WIDTH), bf16),
        "gs": ((devices, 16, 128), f32),
        "sr": ((blocks, UNITS, WIDTH), bf16),
        "srs": ((blocks, 16, 128), f32),
        "wq": ((WIDTH, WIDTH), bf16),
        "wk": ((WIDTH, WIDTH), bf16),
        "wv": ((WIDTH, WIDTH), bf16),
        "wo": ((WIDTH, WIDTH), bf16),
        "s1": ((SEQ, WIDTH), f32),
        "i1": ((SEQ, 128), f32),
        "nm": ((SEQ, WIDTH), bf16),
        "hid": ((SEQ, WIDTH), f32),
        "s2": ((SEQ, WIDTH), f32),
        "i2": ((SEQ, 128), f32),
        "n2": ((2 * SEQ, WIDTH), bf16),
        "ct": ((2 * SEQ, WIDTH), bf16),
        "outp": ((2 * SEQ, WIDTH), f32),
        "dn2": ((2 * SEQ, WIDTH), f32),
        "outr": ((SEQ, WIDTH), f32),
        "dn2r": ((SEQ, WIDTH), f32),
        "act": ((2 * SEQ, UNITS * depth), bf16),
        "dp": ((2 * SEQ, UNITS * depth), bf16),
        "da": ((SEQ, WIDTH), bf16),
        "dn": ((SEQ, WIDTH), f32),
        "nmt": ((WIDTH, SEQ), bf16),
        "qt": ((WIDTH, SEQ), bf16),
        "kt": ((WIDTH, SEQ), bf16),
        "vt": ((WIDTH, SEQ), bf16),
        "krt": ((WIDTH, SEQ), f32),
        "mt": ((WIDTH, SEQ), bf16),
        "dmt": ((WIDTH, SEQ), bf16),
        "dqt": ((WIDTH, SEQ), bf16),
        "dkt": ((WIDTH, SEQ), bf16),
        "dvt": ((WIDTH, SEQ), bf16),
        "kft": ((WIDTH, SEQ), bf16),
        "vft": ((WIDTH, SEQ), bf16),
        "ex": ((WIDTH, SEQ), f32),
        "tt": ((HEADS, SEQ, SEQ), f32),
        "vec": ((16, WIDTH), f32),
        "vecc": ((WIDTH, 128), f32),
        "colsum": ((WIDTH, 128), f32),
        "gvec": ((16, WIDTH), f32),
        "bias": ((4, 8, UNITS * depth), f32),
        "gbias": ((blocks, 8, 128), f32),
    }
    for name, rows, half, lanes, kind in (
        ("q", UNITS, UNITS // 2, WIDTH, bf16),
        ("b", 128, 64, WIDTH, bf16),
        ("t", 16, 8, 128, f32),
    ):
        table["r" + name + "dx"] = ((depth, rows - half, lanes), kind)
        table["r" + name + "dy"] = ((depth, half, lanes), kind)
        table["r" + name + "xy"] = ((depth, 2, rows, lanes), kind)
        table["r" + name + "u"] = table["r" + name + "d"] = ((depth, rows, lanes), kind)
    table["rcdx"] = table["rcdy"] = ((1, 32, WIDTH), bf16)
    table["rcxy"] = ((1, 2, 64, WIDTH), bf16)
    table["rcu"] = table["rcd"] = ((blocks, 64, WIDTH), bf16)
    table["out"] = table["dinp"] = ((SEQ, WIDTH), bf16)
    for name in ("gwq", "gwk", "gwv", "gwo"):
        table[name] = ((24, WIDTH), f32)
    table["gfc1"] = table["gfc2"] = ((UNITS, WIDTH), f32)
    table["gsmall"] = ((16, 128), f32)
    table["store"] = len(RESULTS)
    for name, sent, came in (
        ("gq", 2, 4 * depth + 1), ("gb", 2, 4 * depth), ("gt", 2, 4 * depth + 1), ("gc", 5, 4 * depth + 3),
        ("sq", 1, 5 * depth), ("sb", 1, 5 * depth), ("st", 1, 5 * depth), ("sc", 1, 8 * depth + 3), ("e", 6, 6),
    ):
        table[name + "_s"], table[name + "_r"] = sent, came
    return table


PLAN = (
    "own_blocks", "barrier", "S0", "M0", "Sz", "Sx", "L0", "Sz", "Sx", "Sy", "Mz", "My", "Mx", "Sz", "Ly",
    "Sd", "Sy", "norm1", "Mz", "My", "Mx", "Mz", "Sy", "L4", "L4", "Lx", "L4", "Sx", "own_cotangent", "Mx",
    "My", "My", "Sx", "Md", "Sd", "Sy", "F0", "Sd", "Md", "Sd", "Mx", "Ss", "Fz", "Md", "vectors", "L5",
    "Md", "mixer_kernels", "Fz", "Fx", "Ms", "unpack", "Fy", "L6", "L5", "gain1", "project", "mix0", "mix1",
    "mix2", "mix3", "Fz", "hidden", "Ld", "norm2", "flip", "sibling_rows", "Fy", "feed0", "Fx",
    "feed_grads0", "L6", "Fx", "L5", "Fy", "Fx", "l0", "feed1", "Fy", "L7", "feed_grads1", "fX", "l1", "Fd",
    "L6", "feed2", "feed_grads2", "Fd", "L7", "fY", "l2", "L7", "Fd", "Fd", "feed3", "feed_grads3", "l1",
    "fD", "feed_swap", "back2", "grad_mixed", "back4", "back5", "l1", "l2", "back6", "M.", "fb", "fa", "fa",
    "back7", "l3", "pack", "fb", "fb", "l3", "fa", "kernel1", "core_sums", "fc", "mD", "kernel2", "fc", "fa",
    "fb", "grad_normed", "mb", "l0", "mb", "finish_out", "fc", "fv", "l3", "mY", "l2", "fv", "mb", "back1",
    "kernel0", "ma", "kernel3", "vector_tiles", "small_sums", "fc", "ma", "fv", "fw", "mX", "fw", "fv", "ma",
    "sD", "sY", "mc", "ma", "l0", "mv", "mc", "mb", "mv", "mc", "lO", "sX", "sa", "mw", "sa", "sb", "sb",
    "sb", "sb", "lD", "fe", "sc", "lY", "sc", "mw", "sa", "sv", "sw", "sv", "mv", "mc", "lX", "sa", "sc",
    "la", "sw", "lb", "sc", "sv", "mv", "sv", "le", "me", "se", "store",
)
INPUTS = ("tok", "length", "cot", "iq", "ik", "iv", "io", "ifc1", "ifc2", "ibias", "ivec")
RESULTS = ("out", "dinp", "gwq", "gwk", "gwv", "gwo", "gfc1", "gfc2", "gsmall")
OUTPUTS = tuple("to_" + name for name in RESULTS)


def layer_kernel(depth, *refs):
    names = INPUTS + OUTPUTS + tuple(scratch_of(depth))
    m = SimpleNamespace(**dict(zip(names, refs, strict=True)))
    k = Links(depth)
    core = k.core

    def in_all(yx, zs):
        return (yx * 2 + core) * depth + zs

    def in_all_sib(yx, zs):
        return (yx * 2 + (1 - core)) * depth + zs

    def in_core(yx, zs):
        return yx * depth + zs

    def chip_rows(start, step):
        return pl.ds(pl.multiple_of(core * SEQ + start, step), step)

    def stored(name):
        place = RESULTS.index(name)
        return pltpu.make_async_copy(getattr(m, name), getattr(m, "to_" + name), m.store.at[place])

    core_rows = pl.ds(pl.multiple_of(core * SEQ, SEQ), SEQ)
    sib_rows = pl.ds(pl.multiple_of((1 - core) * SEQ, SEQ), SEQ)

    def swap(place, source, target):
        k.start(None, lambda: source, lambda: target, m.e_s.at[place], m.e_r.at[place], k.sib_dev)

    day = lax.broadcasted_iota(jnp.int32, (1, SEQ), 1).astype(f32)
    s_at = lax.broadcasted_iota(jnp.int32, (SEQ, SEQ), 0)
    t_at = lax.broadcasted_iota(jnp.int32, (SEQ, SEQ), 1)
    valid = (lax.broadcasted_iota(jnp.int32, (1, SEQ), 1) < m.length[0]).astype(f32)

    def own_blocks():
        here = in_all(k.me, k.z)
        for place, (first, second) in enumerate(((m.iq, m.ik), (m.iv, m.io))):
            pair = jnp.concatenate([first[...].astype(f32), second[...].astype(f32)], axis=0)
            m.qk[here, 48 * place : 48 * place + 48] = pair.astype(bf16)
        m.sm[here] = jnp.zeros((16, 128), f32)
        m.sm[here, 0:15, 0:24] = m.ivec[...].astype(f32)
        m.sm[here, 15:16, 0:UNITS] = m.ibias[...].astype(f32)
        m.ff[in_core(k.me, k.z), 0:UNITS] = m.ifc1[...]
        m.ff[in_core(k.me, k.z), UNITS : 2 * UNITS] = m.ifc2[...]

    def own_cotangent():
        m.ct[core_rows] = m.cot[...]
        swap(0, m.ct.at[core_rows], m.ct.at[core_rows])

    def norm1():
        def rows_of(start, step):
            rows = pl.ds(start, step)
            tokens = m.tok[rows].astype(f32)
            centred = tokens - jnp.mean(tokens, axis=1, keepdims=True)
            inverse = lax.rsqrt(jnp.mean(centred * centred, axis=1, keepdims=True) + EPSILON)
            m.s1[rows] = centred * inverse
            m.i1[rows] = jnp.broadcast_to(inverse, (step, 128))

        row_loop(SEQ, 32, rows_of)

    def vectors():
        total = jnp.zeros((16, WIDTH), f32)
        for wide in range(8):
            part = jnp.zeros((16, 128), f32)
            for zs in range(depth):
                tile = m.sm[wide * depth + zs]
                part = part + (pltpu.roll(tile, 24 * zs, 1) if zs else tile)
            padded = jnp.concatenate([part, jnp.zeros((16, WIDTH - 128), f32)], axis=1)
            total = total + (pltpu.roll(padded, 96 * wide, 1) if wide else padded)
        m.vec[...] = total
        m.vecc[...] = jnp.transpose(jnp.concatenate([total, jnp.zeros((112, WIDTH), f32)], axis=0))
        for yx in range(4):
            line = jnp.zeros((16, UNITS * depth), f32)
            for zs in range(depth):
                tile = jnp.concatenate([m.sm[in_all(yx, zs)], jnp.zeros((16, UNITS * depth - 128), f32)], axis=1)
                line = line + (pltpu.roll(tile, UNITS * zs, 1) if zs else tile)
            m.bias[yx] = line[8:16]

    def head_kernel(h, carry):
        rows = head_rows(h)
        decays = jnp.exp(-m.vecc[rows, 10:11] * day)
        m.ex[rows] = decays
        line = jnp.sum(m.vecc[rows, 9:10] * decays, axis=0, keepdims=True) * (1.0 / STATE)
        matrix = pltpu.roll(jnp.broadcast_to(line, (SEQ, SEQ)), 0, 1, stride=1, stride_axis=0)
        m.tt[h] = jnp.where(t_at >= s_at, matrix, 0.0)
        return carry

    def mixer_kernels():
        lax.fori_loop(0, HEADS, head_kernel, 0)

    def gain1():
        def rows_of(start, step):
            rows = pl.ds(start, step)
            m.nm[rows] = (m.s1[rows] * m.vec[0:1] + m.vec[1:2]).astype(bf16)

        row_loop(SEQ, 32, rows_of)
        m.nmt[...] = jnp.transpose(m.nm[...])

    def unpack_rows(w, carry):
        rows = pl.ds(pl.multiple_of(w * 96, 96), 96)
        for place, (first, second) in enumerate(((m.wq, m.wk), (m.wv, m.wo))):
            pair = m.qk[pl.ds(w * depth, depth), 48 * place : 48 * place + 48, :].astype(f32)
            first[rows] = pair[:, :24].reshape(96, WIDTH).astype(bf16)
            second[rows] = pair[:, 24:].reshape(96, WIDTH).astype(bf16)
        return carry

    def unpack():
        lax.fori_loop(0, 8, unpack_rows, 0)

    def project():
        m.qt[...] = jnp.transpose(dg(m.nm[...], m.wq[...], 1, 0) + m.vec[2:3]).astype(bf16)
        m.krt[...] = jnp.transpose(dg(m.nm[...], m.wk[...], 1, 0) + m.vec[3:4])
        m.vt[...] = (jnp.transpose(dg(m.nm[...], m.wv[...], 1, 0) + m.vec[4:5]) * valid).astype(bf16)

    def mix_head(h):
        rows = head_rows(h)
        raw = m.krt[rows]
        summed = raw * m.vecc[rows, 5:6]
        for j in range(1, 4):
            summed = summed + lane_shift(raw, j, False) * m.vecc[rows, 5 + j : 6 + j]
        keys = (summed * valid).astype(bf16)
        m.kt[rows] = keys
        scores = dg(keys, m.qt[rows], 0, 0) * (1.0 / HEAD_SIZE)
        weights = (scores * m.tt[h]).astype(bf16)
        m.mt[rows] = (dg(m.vt[rows], weights, 1, 0) * valid).astype(bf16)

    def hidden():
        m.hid[...] = dg(m.mt[...], m.wo[...], 0, 0)

    def norm2():
        def rows_of(start, step):
            rows = pl.ds(start, step)
            hidden = m.tok[rows].astype(f32) + m.hid[rows] + m.vec[11:12]
            m.hid[rows] = hidden
            centred = hidden - jnp.mean(hidden, axis=1, keepdims=True)
            inverse = lax.rsqrt(jnp.mean(centred * centred, axis=1, keepdims=True) + EPSILON)
            scaled = centred * inverse
            m.s2[rows] = scaled
            m.i2[rows] = jnp.broadcast_to(inverse, (step, 128))
            m.n2[chip_rows(start, step)] = (scaled * m.vec[12:13] + m.vec[13:14]).astype(bf16)

        row_loop(SEQ, 32, rows_of)
        swap(1, m.n2.at[core_rows], m.n2.at[core_rows])

    def sibling_rows():
        k.arrive(m.ct.at[sib_rows], m.e_r.at[0])
        k.arrive(m.n2.at[sib_rows], m.e_r.at[1])

    def finish_feed(ref, more):
        value = ref[...].astype(f32)
        for target, low, high in ((m.gfc1, 0, UNITS), (m.gfc2.at[0:32], UNITS, 128)):
            target[...] = target[...] + value[low:high] if more else value[low:high]

    def finish_last(ref, more):
        value = ref[...].astype(f32)
        m.gfc2[32:96] = m.gfc2[32:96] + value if more else value

    def finish_mats(ref, more):
        value = ref[...].astype(f32)
        for place, target in enumerate((m.gwq, m.gwk, m.gwv, m.gwo)):
            part = value[24 * place : 24 * place + 24]
            target[...] = target[...] + part if more else part

    def finish_small(ref, more):
        m.gsmall[...] = m.gsmall[...] + ref[...] if more else ref[...]

    steps = {}
    steps |= gather_z_first(k, "S", m.sm, in_all, 0, 16, 8, m.gt_s, m.gt_r, in_all_sib)
    steps |= gather_z_first(k, "M", m.qk, in_all, 0, UNITS, UNITS // 2, m.gq_s, m.gq_r, in_all_sib)
    steps |= gather_z_first(k, "F", m.ff, in_core, 0, 128, 64, m.gb_s, m.gb_r)
    steps |= gather_z_last(k, "L", m.ff, in_core, 128, 64, 32, m.gc_s, m.gc_r)
    slots = (m.rbdx, m.rbdy, m.rbxy, m.rbu, m.rbd)
    steps |= scatter_z_last(k, "f", m.gff, in_core, 0, 128, 64, slots, m.sb_s, m.sb_r, finish_feed)
    slots = (m.rcdx, m.rcdy, m.rcxy, m.rcu, m.rcd)
    steps |= scatter_z_first(k, "l", m.gff, in_core, 128, 64, 32, slots, m.sc_s, m.sc_r, finish_last)
    slots = (m.rqdx, m.rqdy, m.rqxy, m.rqu, m.rqd)
    steps |= scatter_z_last(k, "m", m.qk, in_all, 0, UNITS, UNITS // 2, slots, m.sq_s, m.sq_r, finish_mats)
    slots = (m.rtdx, m.rtdy, m.rtxy, m.rtu, m.rtd)
    steps |= scatter_z_last(k, "s", m.gs, in_all, 0, 16, 8, slots, m.st_s, m.st_r, finish_small)

    root = math.sqrt(2.0 / math.pi)
    chunk = UNITS * depth
    yx_of = (k.me, k.xs, k.ys, k.ds)

    def feed(which):
        yx = yx_of[which]
        blocks = pl.ds(yx * depth, depth)
        fc1 = m.ff[blocks, 0:UNITS, :].reshape(chunk, WIDTH)
        fc2 = m.ff[blocks, UNITS : 2 * UNITS, :].reshape(chunk, WIDTH)
        for r in range(2):
            rows = pl.ds(r * SEQ, SEQ)
            pre = dg(m.n2[rows], fc1, 1, 1) + m.bias[yx, 7:8]
            square = pre * pre
            tanh = jnp.tanh(root * pre * (1.0 + 0.044715 * square))
            half = 0.5 * (1.0 + tanh)
            slope = half + 0.5 * pre * (1.0 - tanh * tanh) * (root * (1.0 + 3 * 0.044715 * square))
            activated = (pre * half).astype(bf16)
            grad_pre = (dg(m.ct[rows], fc2, 1, 1) * slope).astype(bf16)
            m.act[rows] = activated
            m.dp[rows] = grad_pre
            if which == 0:
                m.outp[rows] = dg(activated, fc2, 1, 0)
                m.dn2[rows] = dg(grad_pre, fc1, 1, 0)
            else:
                m.outp[rows] += dg(activated, fc2, 1, 0)
                m.dn2[rows] += dg(grad_pre, fc1, 1, 0)

    def feed_swap():
        swap(2, m.dn2.at[sib_rows], m.dn2r)
        swap(3, m.outp.at[sib_rows], m.outr)

    def feed_grads(which):
        yx = yx_of[which]
        blocks = pl.ds(yx * depth, depth)
        m.gff[blocks, 0:UNITS] = dg(m.dp[...], m.n2[...], 0, 0).astype(bf16).reshape(depth, UNITS, WIDTH)
        m.gff[blocks, UNITS : 2 * UNITS] = (
            dg(m.act[...], m.ct[...], 0, 0).astype(bf16).reshape(depth, UNITS, WIDTH)
        )
        sums = jnp.sum(m.dp[...].astype(f32), axis=0, keepdims=True)
        lane = lax.broadcasted_iota(jnp.int32, (1, 128), 1)
        for zs in range(depth):
            line = (pltpu.roll(sums, chunk - UNITS * zs, 1) if zs else sums)[:, :128]
            m.gbias[yx * depth + zs] = jnp.broadcast_to(jnp.where(lane < UNITS, line, 0.0), (8, 128))

    def back2():
        m.gvec[...] = jnp.zeros((16, WIDTH), f32)
        k.arrive(m.dn2r, m.e_r.at[2])

        def rows_of(start, step):
            rows = pl.ds(start, step)
            grad_normed = m.dn2[chip_rows(start, step)] + m.dn2r[rows]
            scaled = m.s2[rows]
            grad_in = grad_normed * m.vec[12:13]
            first = jnp.mean(grad_in, axis=1, keepdims=True)
            second = jnp.mean(grad_in * scaled, axis=1, keepdims=True)
            top = m.cot[rows].astype(f32)
            grad_hidden = top + m.i2[rows, 0:1] * (grad_in - first - scaled * second)
            m.s2[rows] = grad_hidden
            rounded = grad_hidden.astype(bf16)
            m.da[rows] = rounded
            m.gvec[11:12] += jnp.sum(rounded.astype(f32), axis=0, keepdims=True)
            m.gvec[12:13] += jnp.sum(grad_normed * scaled, axis=0, keepdims=True)
            m.gvec[13:14] += jnp.sum(grad_normed, axis=0, keepdims=True)
            m.gvec[14:15] += jnp.sum(top, axis=0, keepdims=True)

        row_loop(SEQ, 32, rows_of)

    def grad_mixed():
        m.dmt[...] = (jnp.transpose(dg(m.da[...], m.wo[...], 1, 1)) * valid).astype(bf16)

    def back_head(h):
        rows = head_rows(h)
        queries, keys, grad_mixed, kernel = m.qt[rows], m.kt[rows], m.dmt[rows], m.tt[h]
        scores = dg(keys, queries, 0, 0) * (1.0 / HEAD_SIZE)
        weights = (scores * kernel).astype(bf16)
        grad_weights = dg(m.vt[rows], grad_mixed, 0, 0)
        grad_values = (dg(grad_mixed, weights, 1, 1) * valid).astype(bf16)
        m.dvt[rows] = grad_values
        grad_scores = (grad_weights * kernel).astype(bf16)
        grad_queries = (dg(keys, grad_scores, 1, 0) * (1.0 / HEAD_SIZE)).astype(bf16)
        m.dqt[rows] = grad_queries
        grad_keys = dg(queries, grad_scores, 1, 1) * (1.0 / HEAD_SIZE) * valid
        raw = m.krt[rows]
        at = lax.broadcasted_iota(jnp.int32, (HEAD_SIZE, 128), 1)
        grad_raw = grad_keys * m.vecc[rows, 5:6]
        sums = jnp.where(at == 5, jnp.sum(grad_keys * raw, axis=1, keepdims=True), 0.0)
        for j in range(1, 4):
            grad_raw = grad_raw + lane_shift(grad_keys, j, True) * m.vecc[rows, 5 + j : 6 + j]
            tap = jnp.sum(grad_keys * lane_shift(raw, j, False), axis=1, keepdims=True)
            sums = jnp.where(at == 5 + j, tap, sums)
        rounded = grad_raw.astype(bf16)
        m.dkt[rows] = rounded
        for place, value in ((2, grad_queries), (3, rounded), (4, grad_values)):
            sums = jnp.where(at == place, jnp.sum(value.astype(f32), axis=1, keepdims=True), sums)
        m.colsum[rows] = sums

    def pack_rows(part, carry):
        rows = pl.ds(pl.multiple_of(part * 384, 384), 384)
        normed = m.nmt[rows]
        grads = (
            dg(normed, m.dqt[...], 1, 1),
            dg(normed, m.dkt[...], 1, 1),
            dg(normed, m.dvt[...], 1, 1),
            dg(m.mt[rows], m.da[...], 1, 0),
        )
        for place in range(2):
            pair = [grad.reshape(4 * depth, 24, WIDTH) for grad in grads[2 * place : 2 * place + 2]]
            m.qk[pl.ds(part * 4 * depth, 4 * depth), 48 * place : 48 * place + 48, :] = jnp.concatenate(pair, axis=1).astype(bf16)
        return carry

    def pack():
        lax.fori_loop(0, 2, pack_rows, 0)
        for yx in range(4):
            swap(4, m.qk.at[pl.ds(in_all_sib(yx, 0), depth)], m.sr.at[pl.ds(yx * depth, depth)])

    def grad_normed():
        m.dn[...] = jnp.transpose(
            dg(m.wq[...], m.dqt[...], 1, 0) + dg(m.wk[...], m.dkt[...], 1, 0) + dg(m.wv[...], m.dvt[...], 1, 0)
        )

    def back1():
        def rows_of(start, step):
            rows = pl.ds(start, step)
            grad_out, scaled = m.dn[rows], m.s1[rows]
            grad_in = grad_out * m.vec[0:1]
            first = jnp.mean(grad_in, axis=1, keepdims=True)
            second = jnp.mean(grad_in * scaled, axis=1, keepdims=True)
            m.dinp[rows] = (m.s2[rows] + m.i1[rows, 0:1] * (grad_in - first - scaled * second)).astype(bf16)
            m.gvec[0:1] += jnp.sum(grad_out * scaled, axis=0, keepdims=True)
            m.gvec[1:2] += jnp.sum(grad_out, axis=0, keepdims=True)

        row_loop(SEQ, 32, rows_of)
        stored("dinp").start()

    def core_sums():
        k.arrive(m.sr, m.e_r.at[4])

        def block_sum(place, carry):
            yx, zs = lax.div(place, depth), lax.rem(place, depth)
            add_into(m.qk.at[in_all(yx, zs)], m.sr.at[place])
            return carry

        lax.fori_loop(0, 4 * depth, block_sum, 0)

    def flip():
        turn = (s_at + t_at == SEQ - 1).astype(bf16)
        m.kft[...] = dg(m.kt[...], turn, 1, 0).astype(bf16)
        m.vft[...] = dg(m.vt[...], turn, 1, 0).astype(bf16)

    def kernel_head(h):
        rows = head_rows(h)
        scores = dg(m.kft[rows], m.qt[rows], 0, 0) * (1.0 / HEAD_SIZE)
        grad_weights = dg(m.vft[rows], m.dmt[rows], 0, 0)
        product = jnp.where(s_at + t_at >= SEQ - 1, scores * grad_weights, 0.0)
        lined = pltpu.roll(product, 1, 1, stride=1, stride_axis=0)
        grad_kernel = jnp.sum(lined, axis=0, keepdims=True) * (1.0 / STATE)
        part = m.ex[rows] * grad_kernel
        at = lax.broadcasted_iota(jnp.int32, (HEAD_SIZE, 128), 1)
        grad_rate = -m.vecc[rows, 9:10] * jnp.sum(part * day, axis=1, keepdims=True)
        sums = jnp.where(at == 9, jnp.sum(part, axis=1, keepdims=True), m.colsum[rows])
        m.colsum[rows] = jnp.where(at == 10, grad_rate, sums)

    def vector_tiles():
        grads = m.gvec[...] + jnp.transpose(m.colsum[...])[0:16]
        row_at = lax.broadcasted_iota(jnp.int32, (16, 128), 0)
        lane_at = lax.broadcasted_iota(jnp.int32, (16, 128), 1)
        for wide in range(8):
            turned = (pltpu.roll(grads, WIDTH - 96 * wide, 1) if wide else grads)[:, :128]
            for zs in range(depth):
                tile = pltpu.roll(turned, 128 - 24 * zs, 1) if zs else turned
                tile = jnp.where((lane_at < 24) & (row_at < 15), tile, 0.0)
                own = jnp.concatenate([jnp.zeros((8, 128), f32), m.gbias[(wide // 2) * depth + zs]], axis=0)
                mine = (row_at == 15) & (core == wide % 2)
                m.gs[wide * depth + zs] = jnp.where(mine, own, tile)
        for yx in range(4):
            swap(5, m.gs.at[pl.ds(in_all_sib(yx, 0), depth)], m.srs.at[pl.ds(yx * depth, depth)])

    def small_sums():
        k.arrive(m.srs, m.e_r.at[5])
        for yx in range(4):
            for zs in range(depth):
                add_into(m.gs.at[in_all(yx, zs)], m.srs.at[yx * depth + zs])

    def finish_out():
        def rows_of(start, step):
            rows = pl.ds(start, step)
            m.out[rows] = (m.hid[rows] + (m.outp[chip_rows(start, step)] + m.outr[rows]) + m.vec[14:15]).astype(bf16)

        k.arrive(m.outr, m.e_r.at[3])
        row_loop(SEQ, 32, rows_of)
        stored("out").start()

    def store():
        for name in RESULTS[2:]:
            stored(name).start()
        for group in "SFLflms":
            next(steps[group + "."])
        for place, extent in enumerate((m.ct.at[core_rows], m.n2.at[core_rows], m.dn2r, m.outr, m.sr, m.srs)):
            k.left(extent, m.e_s.at[place])
        for name in RESULTS:
            stored(name).wait()

    compute = {
        "own_blocks": own_blocks, "barrier": k.barrier, "own_cotangent": own_cotangent, "norm1": norm1,
        "vectors": vectors, "mixer_kernels": mixer_kernels, "gain1": gain1, "unpack": unpack, "project": project,
        "hidden": hidden, "norm2": norm2, "sibling_rows": sibling_rows, "feed_swap": feed_swap, "store": store,
        "back2": back2, "grad_mixed": grad_mixed, "pack": pack, "grad_normed": grad_normed, "back1": back1,
        "core_sums": core_sums, "flip": flip, "vector_tiles": vector_tiles, "small_sums": small_sums, "finish_out": finish_out,
    }
    for which in range(4):
        compute["feed%d" % which] = partial(feed, which)
        compute["feed_grads%d" % which] = partial(feed_grads, which)
        compute["mix%d" % which] = partial(three_heads, 3 * which, mix_head)
        compute["back%d" % (4 + which)] = partial(three_heads, 3 * which, back_head)
        compute["kernel%d" % which] = partial(three_heads, 3 * which, kernel_head)
    for step in PLAN:
        if step in compute:
            compute[step]()
        else:
            next(steps[step])


def results_kernel(*refs):
    sources, tile, targets, bias, vectors = refs[:8], refs[8], refs[9:17], refs[17], refs[18]
    for source, target in zip(sources, targets, strict=True):
        target[...] = source[...]
    bias[...] = tile[15:16, :UNITS]
    vectors[...] = tile[0:15, 0:24]


def on_device_fast(
    tokens, lengths, cotangent, w_query, w_key, w_value, w_out, w_fc1, w_fc2, fc1_bias, vectors
):
    depth = lax.axis_size("narrow")
    scratch = []
    for entry in scratch_of(depth).values():
        scratch.append(pltpu.SemaphoreType.DMA((entry,)) if isinstance(entry, int) else pltpu.VMEM(*entry))
    in_vmem = pl.BlockSpec(memory_space=pltpu.VMEM)
    anywhere = pl.BlockSpec(memory_space=pl.ANY)
    in_smem = pl.BlockSpec(memory_space=pltpu.SMEM)
    shape = jax.ShapeDtypeStruct
    got = pl.pallas_call(
        partial(layer_kernel, depth),
        out_shape=[shape((SEQ, WIDTH), bf16)] * 2
        + [shape((24, WIDTH), f32)] * 4
        + [shape((UNITS, WIDTH), f32)] * 2
        + [shape((16, 128), f32)],
        in_specs=[in_vmem, in_smem] + [in_vmem] * 9,
        out_specs=[anywhere] * 9,
        scratch_shapes=scratch,
        compiler_params=pltpu.CompilerParams(
            collective_id=0, has_side_effects=True, vmem_limit_bytes=63 * 2**20
        ),
        name="h3_layer",
    )(
        tokens, lengths, cotangent, w_query, w_key, w_value, w_out, w_fc1.T, w_fc2, fc1_bias[None], vectors
    )
    results = pl.pallas_call(
        results_kernel,
        out_shape=[shape(x.shape, x.dtype) for x in got[:8]] + [shape((1, UNITS), f32), shape((15, 24), f32)],
        in_specs=[in_vmem] * 9,
        out_specs=[in_vmem] * 10,
        name="results",
    )(*got)
    out, grad_in, g_query, g_key, g_value, g_out, g_fc1, g_fc2, g_bias, g_vectors = results
    return out, grad_in, g_query, g_key, g_value, g_out, g_fc1.T, g_fc2, g_bias.reshape(-1), g_vectors


def fits(mesh):
    return mesh.shape["wide"] == 8 and mesh.shape["narrow"] == 4


def solution(mesh):
    placed = (
        P(("wide", "narrow"), None),
        P(("wide", "narrow")),
        P(("wide", "narrow"), None),
        P(("wide", "narrow"), None),
        P(("wide", "narrow"), None),
        P(("wide", "narrow"), None),
        P(("wide", "narrow"), None),
        P(None, ("wide", "narrow")),
        P(("wide", "narrow"), None),
        P(("wide", "narrow")),
        P(None, ("wide", "narrow")),
    )
    return jax.shard_map(
        on_device_fast if fits(mesh) else on_device,
        mesh=mesh,
        in_specs=placed,
        out_specs=(
            P(("wide", "narrow"), None),
            P(("wide", "narrow"), None),
            P(("wide", "narrow"), None),
            P(("wide", "narrow"), None),
            P(("wide", "narrow"), None),
            P(("wide", "narrow"), None),
            P(None, ("wide", "narrow")),
            P(("wide", "narrow"), None),
            P(("wide", "narrow")),
            P(None, ("wide", "narrow")),
        ),
        check_vma=False,
    )
```

```python
import math
from functools import partial
from types import SimpleNamespace

import jax
import jax.numpy as jnp
from jax import lax
from jax.experimental import pallas as pl
from jax.experimental.pallas import tpu as pltpu
from jax.sharding import PartitionSpec as P

HEAD_SIZE = 64
STATE = 64


EPSILON = 1e-05


def normalize(values):
    average = jnp.mean(values, axis=-1, keepdims=True)
    centred = values - average
    variance = jnp.mean(centred * centred, axis=-1, keepdims=True)
    inverse = lax.rsqrt(variance + EPSILON)
    return (centred * inverse, inverse)


def norm_back(grad_in, scaled, inverse):
    first = jnp.mean(grad_in, axis=-1, keepdims=True)
    second = jnp.mean(grad_in * scaled, axis=-1, keepdims=True)
    return inverse * (grad_in - first - scaled * second)


def shift_mix(key_raw, shift_taps):
    summed = key_raw * shift_taps[0]
    for offset in range(1, 4):
        delayed = jnp.concatenate(
            [jnp.zeros((offset, key_raw.shape[1]), key_raw.dtype), key_raw[:-offset]], axis=0
        )
        summed = summed + delayed * shift_taps[offset]
    return summed


def kernel_rows(coefficient, decay_rate, length_all):
    distance = jnp.arange(length_all).astype(jnp.float32)
    decays = jnp.exp(-decay_rate[:, :, None] * distance[None, None, :])
    return jnp.sum(coefficient[:, :, None] * decays, axis=1) / STATE


def toeplitz(kernel_row):
    length_all = kernel_row.shape[0]
    wrapped = jnp.concatenate(
        [kernel_row[:1], jnp.zeros((length_all,), kernel_row.dtype), kernel_row[:0:-1]]
    )
    tiled_row = jnp.tile(wrapped, length_all)[: length_all * (2 * length_all - 1)]
    return tiled_row.reshape(length_all, 2 * length_all - 1)[:, :length_all]


def split_heads(values, row_count):
    return values.reshape(row_count, -1, HEAD_SIZE).transpose(1, 0, 2)


def merge_heads(per_head):
    head_count = per_head.shape[0]
    row_count = per_head.shape[1]
    merged = per_head.transpose(1, 0, 2).reshape(row_count, head_count * HEAD_SIZE)
    return merged


def pack_rows(matrices, shard_count):
    return jnp.concatenate(
        [matrix.reshape(shard_count, -1) for matrix in matrices], axis=1
    ).reshape(-1)


def unpack_rows(flat, matrices, shard_count):
    pieces = []
    offset = 0
    for matrix in matrices:
        rows_own = matrix.shape[0] // shard_count
        extent = matrix.size // shard_count
        pieces.append(flat[offset : offset + extent].reshape((rows_own,) + matrix.shape[1:]))
        offset = offset + extent
    return pieces


def mixer_forward(queries, keys, values, kernel, row_count):

    def head_forward(parts):
        query_head, key_head, value_head, kernel_row = parts
        scores = jnp.dot(query_head, key_head.T, preferred_element_type=jnp.float32) / HEAD_SIZE
        weights_mix = (scores * toeplitz(kernel_row)).astype(jnp.bfloat16)
        return jnp.dot(weights_mix, value_head, preferred_element_type=jnp.float32)

    per_head = lax.map(
        head_forward,
        (
            split_heads(queries, row_count),
            split_heads(keys, row_count),
            split_heads(values, row_count),
            kernel,
        ),
    )
    return merge_heads(per_head)


def mixer_backward(queries, keys, values, grad_mixed, kernel, row_count):

    def head_backward(parts):
        query_head, key_head, value_head, grad_head, kernel_row = parts
        scores = jnp.dot(query_head, key_head.T, preferred_element_type=jnp.float32) / HEAD_SIZE
        toeplitz_mat, pullback = jax.vjp(toeplitz, kernel_row)
        weights_mix = (scores * toeplitz_mat).astype(jnp.bfloat16)
        grad_weights = jnp.dot(grad_head, value_head.T, preferred_element_type=jnp.float32)
        grad_values = jnp.dot(weights_mix.T, grad_head, preferred_element_type=jnp.float32)
        grad_scores = (grad_weights * toeplitz_mat).astype(jnp.bfloat16)
        grad_queries = (
            jnp.dot(grad_scores, key_head, preferred_element_type=jnp.float32) / HEAD_SIZE
        )
        grad_keys = (
            jnp.dot(grad_scores.T, query_head, preferred_element_type=jnp.float32) / HEAD_SIZE
        )
        grad_kernel = pullback(grad_weights * scores)[0]
        return (grad_queries, grad_keys, grad_values, grad_kernel)

    head_grads = lax.map(
        head_backward,
        (
            split_heads(queries, row_count),
            split_heads(keys, row_count),
            split_heads(values, row_count),
            split_heads(grad_mixed, row_count),
            kernel,
        ),
    )
    grad_kernel = head_grads[3]
    return (
        merge_heads(head_grads[0]),
        merge_heads(head_grads[1]),
        merge_heads(head_grads[2]),
        grad_kernel,
    )


def on_device(
    tokens, lengths, cotangent, w_query, w_key, w_value, w_out, w_fc1, w_fc2, fc1_bias, vectors
):
    shard_count = lax.axis_size(("wide", "narrow"))
    gathered = (
        lax.all_gather(w_query, ("wide", "narrow"), axis=0, tiled=True),
        lax.all_gather(w_key, ("wide", "narrow"), axis=0, tiled=True),
        lax.all_gather(w_value, ("wide", "narrow"), axis=0, tiled=True),
        lax.all_gather(w_out, ("wide", "narrow"), axis=0, tiled=True),
        lax.all_gather(w_fc1, ("wide", "narrow"), axis=1, tiled=True),
        lax.all_gather(w_fc2, ("wide", "narrow"), axis=0, tiled=True),
        lax.all_gather(fc1_bias, ("wide", "narrow"), axis=0, tiled=True),
        lax.all_gather(vectors, ("wide", "narrow"), axis=1, tiled=True),
    )
    query_full, key_full, value_full, out_full, fc1_full, fc2_full, bias_full, vector_full = (
        gathered
    )
    params = vector_full.astype(jnp.float32)
    fc1_shift = bias_full.astype(jnp.float32)
    seq_len = tokens.shape[0]
    head_count = params.shape[1] // HEAD_SIZE
    seq_length = lengths[0]
    valid_mask = (jnp.arange(seq_len) < seq_length).astype(jnp.float32)[:, None]
    residual = tokens.astype(jnp.float32)
    scaled1, inverse1 = normalize(residual)
    normed = (scaled1 * params[0] + params[1]).astype(jnp.bfloat16)
    queries = (jnp.dot(normed, query_full, preferred_element_type=jnp.float32) + params[2]).astype(
        jnp.bfloat16
    )
    key_raw = jnp.dot(normed, key_full, preferred_element_type=jnp.float32) + params[3]
    keys = (shift_mix(key_raw, params[5:9]) * valid_mask).astype(jnp.bfloat16)
    values = (
        (jnp.dot(normed, value_full, preferred_element_type=jnp.float32) + params[4]) * valid_mask
    ).astype(jnp.bfloat16)
    coefficient = params[9].reshape(head_count, STATE)
    decay_rate = params[10].reshape(head_count, STATE)
    kernel_fn = partial(kernel_rows, length_all=seq_len)
    kernel, kernel_pull = jax.vjp(kernel_fn, coefficient, decay_rate)
    mixed = mixer_forward(queries, keys, values, kernel, seq_len)
    mixed_out = (mixed * valid_mask).astype(jnp.bfloat16)
    hidden = (
        residual + jnp.dot(mixed_out, out_full, preferred_element_type=jnp.float32) + params[11]
    )
    scaled2, inverse2 = normalize(hidden)
    normed2 = (scaled2 * params[12] + params[13]).astype(jnp.bfloat16)
    pre_act = jnp.dot(normed2, fc1_full, preferred_element_type=jnp.float32) + fc1_shift
    activated = jax.nn.gelu(pre_act).astype(jnp.bfloat16)
    output = (
        hidden + jnp.dot(activated, fc2_full, preferred_element_type=jnp.float32) + params[14]
    ).astype(jnp.bfloat16)
    again = (
        lax.all_gather(w_query, ("wide", "narrow"), axis=0, tiled=True),
        lax.all_gather(w_key, ("wide", "narrow"), axis=0, tiled=True),
        lax.all_gather(w_value, ("wide", "narrow"), axis=0, tiled=True),
        lax.all_gather(w_out, ("wide", "narrow"), axis=0, tiled=True),
        lax.all_gather(w_fc1, ("wide", "narrow"), axis=1, tiled=True),
        lax.all_gather(w_fc2, ("wide", "narrow"), axis=0, tiled=True),
        lax.all_gather(fc1_bias, ("wide", "narrow"), axis=0, tiled=True),
        lax.all_gather(vectors, ("wide", "narrow"), axis=1, tiled=True),
    )
    query_back, key_back, value_back, out_back, fc1_back, fc2_back = (
        again[0],
        again[1],
        again[2],
        again[3],
        again[4],
        again[5],
    )
    grad_top = cotangent.astype(jnp.float32)
    grad_fc2 = jnp.dot(activated.T, cotangent, preferred_element_type=jnp.float32)
    grad_activated = jnp.dot(cotangent, fc2_back.T, preferred_element_type=jnp.float32)
    gelu_value, gelu_pull = jax.vjp(jax.nn.gelu, pre_act)
    grad_pre = gelu_pull(grad_activated)[0].astype(jnp.bfloat16)
    grad_fc1_turned = jnp.dot(grad_pre.T, normed2, preferred_element_type=jnp.float32)
    grad_fc1_bias = jnp.sum(grad_pre.astype(jnp.float32), axis=0)[:, None]
    mlp_terms = [grad_fc1_turned, grad_fc2, grad_fc1_bias]
    mlp_flat = lax.psum_scatter(
        pack_rows(mlp_terms, shard_count), ("wide", "narrow"), scatter_dimension=0, tiled=True
    )
    mlp_sums = unpack_rows(mlp_flat, mlp_terms, shard_count)
    grad_normed2 = jnp.dot(grad_pre, fc1_back.T, preferred_element_type=jnp.float32)
    grad_hidden = grad_top + norm_back(grad_normed2 * params[12], scaled2, inverse2)
    grad_attn = grad_hidden.astype(jnp.bfloat16)
    grad_out = jnp.dot(mixed_out.T, grad_attn, preferred_element_type=jnp.float32)
    grad_mixed = (
        jnp.dot(grad_attn, out_back.T, preferred_element_type=jnp.float32) * valid_mask
    ).astype(jnp.bfloat16)
    grad_q, grad_k, grad_v, grad_kernel = mixer_backward(
        queries, keys, values, grad_mixed, kernel, seq_len
    )
    grad_queries = grad_q.astype(jnp.bfloat16)
    grad_values = (grad_v * valid_mask).astype(jnp.bfloat16)
    shift_value, shift_pull = jax.vjp(shift_mix, key_raw, params[5:9])
    grad_key_full, grad_taps = shift_pull(grad_k * valid_mask)
    grad_key_raw = grad_key_full.astype(jnp.bfloat16)
    grad_query = jnp.dot(normed.T, grad_queries, preferred_element_type=jnp.float32)
    grad_key = jnp.dot(normed.T, grad_key_raw, preferred_element_type=jnp.float32)
    grad_value = jnp.dot(normed.T, grad_values, preferred_element_type=jnp.float32)
    grad_normed = jnp.dot(grad_queries, query_back.T, preferred_element_type=jnp.float32)
    grad_normed = grad_normed + jnp.dot(
        grad_key_raw, key_back.T, preferred_element_type=jnp.float32
    )
    grad_normed = grad_normed + jnp.dot(
        grad_values, value_back.T, preferred_element_type=jnp.float32
    )
    input_grad = (grad_hidden + norm_back(grad_normed * params[0], scaled1, inverse1)).astype(
        jnp.bfloat16
    )
    grad_coef, grad_rate = kernel_pull(grad_kernel)
    grad_vectors = jnp.concatenate(
        [
            jnp.sum(grad_normed * scaled1, axis=0)[None],
            jnp.sum(grad_normed, axis=0)[None],
            jnp.sum(grad_queries.astype(jnp.float32), axis=0)[None],
            jnp.sum(grad_key_raw.astype(jnp.float32), axis=0)[None],
            jnp.sum(grad_values.astype(jnp.float32), axis=0)[None],
            grad_taps,
            grad_coef.reshape(1, -1),
            grad_rate.reshape(1, -1),
            jnp.sum(grad_attn.astype(jnp.float32), axis=0)[None],
            jnp.sum(grad_normed2 * scaled2, axis=0)[None],
            jnp.sum(grad_normed2, axis=0)[None],
            jnp.sum(grad_top, axis=0)[None],
        ],
        axis=0,
    )
    mixer_terms = [grad_query, grad_key, grad_value, grad_out, grad_vectors.T]
    mixer_flat = lax.psum_scatter(
        pack_rows(mixer_terms, shard_count), ("wide", "narrow"), scatter_dimension=0, tiled=True
    )
    mixer_sums = unpack_rows(mixer_flat, mixer_terms, shard_count)
    return (
        output,
        input_grad,
        mixer_sums[0],
        mixer_sums[1],
        mixer_sums[2],
        mixer_sums[3],
        mlp_sums[0].T,
        mlp_sums[1],
        mlp_sums[2].reshape(-1),
        mixer_sums[4].T,
    )


f32, bf16 = jnp.float32, jnp.bfloat16
MESH = pl.DeviceIdType.MESH


def dg(left, right, left_dim, right_dim):
    return lax.dot_general(
        left, right, (((left_dim,), (right_dim,)), ((), ())), preferred_element_type=f32
    )


def when(condition, body):
    if condition is None:
        body()
    else:
        pl.when(condition)(body)


def both(first, second):
    if first is None:
        return second
    if second is None:
        return first
    return jnp.logical_and(first, second)


class Links:
    def __init__(self, depth):
        wide, z = lax.axis_index("wide"), lax.axis_index("narrow")
        self.depth = depth
        self.z, self.core = z, lax.rem(wide, 2)
        self.x, self.y = lax.rem(lax.div(wide, 2), 2), lax.div(wide, 4)
        self.me = self.y * 2 + self.x
        self.xs = self.y * 2 + (1 - self.x)
        self.ys = (1 - self.y) * 2 + self.x
        self.ds = (1 - self.y) * 2 + (1 - self.x)
        self.sib_dev = (self.me * 2 + (1 - self.core), z)
        self.x_dev = (self.xs * 2 + self.core, z)
        self.y_dev = (self.ys * 2 + self.core, z)
        self.up_dev = (wide, z + 1)
        self.down_dev = (wide, z - 1)
        self.has_up = z < depth - 1
        self.has_down = z > 0
        self.at_end = jnp.logical_or(z == 0, z == depth - 1)

    def barrier(self):
        semaphore = pltpu.get_barrier_semaphore()

        def greet(device):
            pl.semaphore_signal(semaphore, inc=1, device_id=device, device_id_type=MESH)

        for device in (self.sib_dev, self.x_dev, self.y_dev):
            greet(device)
        pl.when(self.has_up)(lambda: greet(self.up_dev))
        pl.when(self.has_down)(lambda: greet(self.down_dev))
        peers = 3 + self.has_up.astype(jnp.int32) + self.has_down.astype(jnp.int32)
        pl.semaphore_wait(semaphore, peers)

    def start(self, condition, source, target, send, receive, device):
        when(
            condition,
            lambda: pltpu.make_async_remote_copy(
                src_ref=source(),
                dst_ref=target(),
                send_sem=send,
                recv_sem=receive,
                device_id=device,
                device_id_type=MESH,
            ).start(),
        )

    def arrive(self, target, receive):
        pltpu.make_async_remote_copy(
            src_ref=target,
            dst_ref=target,
            send_sem=receive,
            recv_sem=receive,
            device_id=self.sib_dev,
            device_id_type=MESH,
        ).wait_recv()

    def left(self, extent, semaphore):
        pltpu.make_async_remote_copy(
            src_ref=extent,
            dst_ref=extent,
            send_sem=semaphore,
            recv_sem=semaphore,
            device_id=self.sib_dev,
            device_id_type=MESH,
        ).wait_send()

    def left_along(self, extent, semaphore):
        pl.when(self.at_end)(lambda: self.left(extent(1), semaphore))
        pl.when(jnp.logical_not(self.at_end))(lambda: self.left(extent(self.depth + 1), semaphore))


def near(k, distance):
    if distance == 0:
        return ((None, k.z, False),)
    return ((k.z >= distance, k.z - distance, True), (k.z + distance < k.depth, k.z + distance, False))


def gather_z_first(k, name, buf, index, low, rows, half, ss, rs, sib_index=None):
    depth = k.depth

    def block(yx, zs, lo=0, n=rows):
        return buf.at[index(yx, zs), pl.ds(low + lo, n)]

    def send(condition, yx, zs, lo, n, device, r, way=0):
        ref = lambda: block(yx, zs, lo, n)
        k.start(condition, ref, ref, ss.at[way], rs.at[r], device)

    def to_sib(condition, yx, zs):
        if sib_index is not None:
            send(condition, yx, zs, 0, rows, k.sib_dev, 4 * depth)

    def outward(condition, zs):
        send(condition, k.me, zs, 0, rows, k.x_dev, depth + zs)
        send(condition, k.me, zs, 0, rows, k.y_dev, 2 * depth + zs)
        to_sib(condition, k.me, zs)

    def along(condition, zs, up, down):
        if up:
            send(both(condition, k.has_up), k.me, zs, 0, rows, k.up_dev, zs, 1)
        if down:
            send(both(condition, k.has_down), k.me, zs, 0, rows, k.down_dev, zs, 1)

    def take(condition, yx, zs, r):
        when(condition, lambda: k.arrive(block(yx, zs), rs.at[r]))

    def own():
        along(None, k.z, True, True)
        outward(None, k.z)
        yield

    def z_steps():
        for d in range(1, depth):
            for condition, zs, below in near(k, d):
                take(condition, k.me, zs, zs)
                along(condition, zs, below, not below)
                outward(condition, zs)
            yield

    def x_steps():
        for d in range(depth):
            for condition, zs, _ in near(k, d):
                take(condition, k.xs, zs, depth + zs)
                send(condition, k.xs, zs, 0, half, k.y_dev, 3 * depth + zs)
                to_sib(condition, k.xs, zs)
            yield

    def y_steps():
        for d in range(depth):
            for condition, zs, _ in near(k, d):
                take(condition, k.ys, zs, 2 * depth + zs)
                send(condition, k.ys, zs, half, rows - half, k.x_dev, 3 * depth + zs)
                to_sib(condition, k.ys, zs)
            yield

    def d_steps():
        for d in range(depth):
            for condition, zs, _ in near(k, d):
                take(condition, k.ds, zs, 3 * depth + zs)
                to_sib(condition, k.ds, zs)
            yield

    def extent(blocks):
        return buf.at[pl.ds(0, blocks), pl.ds(low, rows)]

    def sib_steps():
        k.arrive(extent(4 * depth), rs.at[4 * depth])
        yield

    def left():
        k.left(extent((7 if sib_index is not None else 3) * depth), ss.at[0])
        k.left_along(extent, ss.at[1])
        yield

    steps = {"0": own(), "z": z_steps(), "x": x_steps(), "y": y_steps(), "d": d_steps(), "s": sib_steps(), ".": left()}
    return {name + key: step for key, step in steps.items()}


def gather_pair_z_first(k, name, buf, index, low, rows, ss, rs):
    depth = k.depth

    def block(yx, zs):
        return buf.at[index(yx, zs), pl.ds(low, rows)]

    def extent(blocks):
        return buf.at[pl.ds(0, blocks), pl.ds(low, rows)]

    def send(condition, zs, device, r, way):
        ref = lambda: block(k.me, zs)
        k.start(condition, ref, ref, ss.at[way], rs.at[r], device)

    def along(condition, zs, up, down):
        if up:
            send(both(condition, k.has_up), zs, k.up_dev, zs, 1)
        if down:
            send(both(condition, k.has_down), zs, k.down_dev, zs, 1)

    def own():
        along(None, k.z, True, True)
        send(None, k.z, k.y_dev, depth + k.z, 0)
        yield

    def z_steps():
        for d in range(1, depth):
            for condition, zs, below in near(k, d):
                when(condition, lambda zs=zs: k.arrive(block(k.me, zs), rs.at[zs]))
                along(condition, zs, below, not below)
                send(condition, zs, k.y_dev, depth + zs, 0)
            yield

    def y_steps():
        for d in range(depth):
            for condition, zs, _ in near(k, d):
                when(condition, lambda zs=zs: k.arrive(block(k.ys, zs), rs.at[depth + zs]))
            yield

    def left():
        k.left(extent(depth), ss.at[0])
        k.left_along(extent, ss.at[1])
        yield

    steps = {"0": own(), "z": z_steps(), "y": y_steps(), ".": left()}
    return {name + key: step for key, step in steps.items()}


def gather_pair_z_last(k, name, buf, index, low, rows, ss, rs):
    depth = k.depth
    yx_of = (k.me, k.ys)

    def block(yx, zs):
        return buf.at[index(yx, zs), pl.ds(low, rows)]

    def extent(blocks):
        return buf.at[pl.ds(0, blocks), pl.ds(low, rows)]

    def send(condition, yx, zs, device, r, way):
        ref = lambda: block(yx, zs)
        k.start(condition, ref, ref, ss.at[way], rs.at[r], device)

    def along(condition, which, zs, up, down):
        place = 1 + which * depth + zs
        if up:
            send(both(condition, k.has_up), yx_of[which], zs, k.up_dev, place, 1 + which)
        if down:
            send(both(condition, k.has_down), yx_of[which], zs, k.down_dev, place, 1 + which)

    def own():
        send(None, k.me, k.z, k.y_dev, 0, 0)
        along(None, 0, k.z, True, True)
        yield

    def y_step():
        k.arrive(block(k.ys, k.z), rs.at[0])
        along(None, 1, k.z, True, True)
        yield

    def z_steps(which):
        for d in range(1, depth):
            for condition, zs, below in near(k, d):
                when(condition, lambda zs=zs: k.arrive(block(yx_of[which], zs), rs.at[1 + which * depth + zs]))
                along(condition, which, zs, below, not below)
            yield

    def left():
        k.left(extent(1), ss.at[0])
        for which in range(2):
            k.left_along(extent, ss.at[1 + which])
        yield

    steps = {"0": own(), "y": y_step(), "4": z_steps(0), "5": z_steps(1), ".": left()}
    return {name + key: step for key, step in steps.items()}


def add_into(ref, *others):
    total = ref[...].astype(f32)
    for other in others:
        total = total + other[...].astype(f32)
    ref[...] = total.astype(ref.dtype)


def scatter_order(depth):
    return ([0, depth - 1] + list(range(1, depth - 1)))[:depth]


def along_z(k, zd, wave, block, from_up, from_down, rs_up, rs_down, send):
    top, low = k.depth - 1 - wave, wave

    def take(slot, semaphore):
        k.arrive(slot, semaphore)
        add_into(block, slot)

    if zd < top:
        if wave:
            pl.when(k.z == top)(lambda: take(from_up, rs_up))
        send(k.z == top, False)
    if zd > low:
        if wave:
            pl.when(k.z == low)(lambda: take(from_down, rs_down))
        send(k.z == low, True)


def scatter_z_last(k, name, buf, index, low, rows, half, slots, ss, rs, finish):
    depth = k.depth
    from_x_diag, from_y_diag, from_xy, from_up, from_down = slots
    order = scatter_order(depth)
    rest = rows - half

    def block(yx, zd, lo=0, n=rows):
        return buf.at[index(yx, zd), pl.ds(low + lo, n)]

    def send(condition, source, target, device, r):
        k.start(condition, source, target, ss.at[0], rs.at[r], device)

    def x_part(zd, lo, n):
        return from_xy.at[zd, 0, pl.ds(lo, n)]

    def y_part(zd, lo, n):
        return from_xy.at[zd, 1, pl.ds(lo, n)]

    def pure_x():
        for zd in order:
            send(None, lambda zd=zd: block(k.xs, zd, half, rest), lambda zd=zd: x_part(zd, half, rest), k.x_dev, 2 * depth + zd)
            yield

    def pure_y():
        for zd in order:
            send(None, lambda zd=zd: block(k.ys, zd, 0, half), lambda zd=zd: y_part(zd, 0, half), k.y_dev, 2 * depth + zd)
            yield

    def diagonal():
        for zd in order:
            send(None, lambda zd=zd: block(k.ds, zd, 0, half), lambda zd=zd: from_y_diag.at[zd], k.y_dev, zd)
            send(None, lambda zd=zd: block(k.ds, zd, half, rest), lambda zd=zd: from_x_diag.at[zd], k.x_dev, depth + zd)
            yield

    def y_added():
        for zd in order:
            k.arrive(from_y_diag.at[zd], rs.at[zd])
            add_into(block(k.xs, zd, 0, half), from_y_diag.at[zd])
            send(None, lambda zd=zd: block(k.xs, zd, 0, half), lambda zd=zd: x_part(zd, 0, half), k.x_dev, 2 * depth + zd)
            yield

    def x_added():
        for zd in order:
            k.arrive(from_x_diag.at[zd], rs.at[depth + zd])
            add_into(block(k.ys, zd, half, rest), from_x_diag.at[zd])
            send(None, lambda zd=zd: block(k.ys, zd, half, rest), lambda zd=zd: y_part(zd, half, rest), k.y_dev, 2 * depth + zd)
            yield

    def wave(zd, number):
        def send_z(condition, up):
            place = (4 if up else 3) * depth + zd
            slot = from_down if up else from_up
            send(condition, lambda: block(k.me, zd), lambda: slot.at[zd], k.up_dev if up else k.down_dev, place)

        along_z(
            k, zd, number, block(k.me, zd), from_up.at[zd], from_down.at[zd],
            rs.at[3 * depth + zd], rs.at[4 * depth + zd], send_z,
        )

    def collect():
        for zd in order:
            k.arrive(from_xy.at[zd], rs.at[2 * depth + zd])
            add_into(block(k.me, zd), from_xy.at[zd, 0], from_xy.at[zd, 1])
            wave(zd, 0)
            yield

    def waves(number):
        for zd in order:
            if zd < depth - 1 - number or zd > number:
                wave(zd, number)
                yield

    def end():
        finish(block(k.me, k.z), False)

        def last_up():
            k.arrive(from_up.at[k.z], rs.at[3 * depth + k.z])
            finish(from_up.at[k.z], True)

        def last_down():
            k.arrive(from_down.at[k.z], rs.at[4 * depth + k.z])
            finish(from_down.at[k.z], True)

        pl.when(k.has_up)(last_up)
        pl.when(k.has_down)(last_down)
        yield

    def left():
        k.left(buf.at[pl.ds(0, 4 * depth - 1), pl.ds(low, rows)], ss.at[0])
        yield

    steps = {"X": pure_x(), "Y": pure_y(), "D": diagonal(), "a": y_added(), "b": x_added(), "c": collect(), "e": end()}
    steps |= {"v": waves(1), "w": waves(2), ".": left()}
    return {name + key: step for key, step in steps.items()}


def scatter_pair_z_last(k, name, buf, index, low, rows, slots, ss, rs, finish):
    depth = k.depth
    from_y, from_up, from_down = slots
    order = scatter_order(depth)

    def block(yx, zd):
        return buf.at[index(yx, zd), pl.ds(low, rows)]

    def send(condition, source, target, device, r):
        k.start(condition, source, target, ss.at[0], rs.at[r], device)

    def pure_y():
        for zd in order:
            send(None, lambda zd=zd: block(k.ys, zd), lambda zd=zd: from_y.at[zd], k.y_dev, zd)
            yield

    def wave(zd, number):
        def send_z(condition, up):
            slot = from_down if up else from_up
            place = (2 if up else 1) * depth + zd
            send(condition, lambda: block(k.me, zd), lambda: slot.at[zd], k.up_dev if up else k.down_dev, place)

        along_z(
            k, zd, number, block(k.me, zd), from_up.at[zd], from_down.at[zd],
            rs.at[depth + zd], rs.at[2 * depth + zd], send_z,
        )

    def collect():
        for zd in order:
            k.arrive(from_y.at[zd], rs.at[zd])
            add_into(block(k.me, zd), from_y.at[zd])
            wave(zd, 0)
            yield

    def waves(number):
        for zd in order:
            if zd < depth - 1 - number or zd > number:
                wave(zd, number)
                yield

    def end():
        finish(block(k.me, k.z), False)

        def last_up():
            k.arrive(from_up.at[k.z], rs.at[depth + k.z])
            finish(from_up.at[k.z], True)

        def last_down():
            k.arrive(from_down.at[k.z], rs.at[2 * depth + k.z])
            finish(from_down.at[k.z], True)

        pl.when(k.has_up)(last_up)
        pl.when(k.has_down)(last_down)
        yield

    def left():
        k.left(buf.at[pl.ds(0, 2 * depth - 1), pl.ds(low, rows)], ss.at[0])
        yield

    steps = {"Y": pure_y(), "c": collect(), "v": waves(1), "w": waves(2), "e": end(), ".": left()}
    return {name + key: step for key, step in steps.items()}


def scatter_pair_z_first(k, name, buf, index, low, rows, slots, ss, rs, finish):
    depth = k.depth
    from_y, from_up, from_down = slots
    yx_of = (k.me, k.ys)

    def block(yx, zd):
        return buf.at[index(yx, zd), pl.ds(low, rows)]

    def send(condition, source, target, device, r):
        k.start(condition, source, target, ss.at[0], rs.at[r], device)

    def waves(which):
        yx = yx_of[which]
        for number in range(depth - 1):
            for zd in scatter_order(depth):
                place = which * depth + zd

                def send_z(condition, up, zd=zd, place=place):
                    slot, number = (from_down, 2 * depth + place) if up else (from_up, place)
                    send(condition, lambda: block(yx, zd), lambda: slot.at[place], k.up_dev if up else k.down_dev, number)

                along_z(
                    k, zd, number, block(yx, zd), from_up.at[place], from_down.at[place],
                    rs.at[place], rs.at[2 * depth + place], send_z,
                )
            yield

    def own(which):
        yx = yx_of[which]
        place = which * depth + k.z

        def take(slot, semaphore):
            k.arrive(slot, semaphore)
            add_into(block(yx, k.z), slot)

        pl.when(k.has_up)(lambda: take(from_up.at[place], rs.at[place]))
        pl.when(k.has_down)(lambda: take(from_down.at[place], rs.at[2 * depth + place]))

    def own_me():
        own(0)
        yield

    def own_y():
        own(1)
        send(None, lambda: block(k.ys, k.z), lambda: from_y.at[0], k.y_dev, 4 * depth)
        yield

    def end():
        k.arrive(from_y.at[0], rs.at[4 * depth])
        finish(block(k.me, k.z), False)
        finish(from_y.at[0], True)
        yield

    def left():
        k.left(buf.at[pl.ds(0, 2 * depth - 1), pl.ds(low, rows)], ss.at[0])
        yield

    steps = {"0": waves(0), "1": waves(1), "O": own_me(), "Y": own_y(), "e": end(), ".": left()}
    return {name + key: step for key, step in steps.items()}


SEQ, WIDTH, UNITS = 256, 768, 96
HEADS = WIDTH // HEAD_SIZE


def row_loop(total, step, body, first=0):
    def once(i, carry):
        body(pl.multiple_of(first + i * step, step), step)
        return carry

    lax.fori_loop(0, total // step, once, 0)


def lane_shift(values, offset, left):
    extent = values.shape[1]
    lane = lax.broadcasted_iota(jnp.int32, values.shape, 1)
    if left:
        return jnp.where(lane < extent - offset, pltpu.roll(values, extent - offset, 1), 0.0)
    return jnp.where(lane >= offset, pltpu.roll(values, offset, 1), 0.0)


def three_heads(first, body):
    for h in range(first, first + 3):
        body(h)


def head_rows(h):
    return pl.ds(pl.multiple_of(h * HEAD_SIZE, HEAD_SIZE), HEAD_SIZE)


def scratch_of(depth):
    devices, blocks, half = 8 * depth, 4 * depth, 2 * depth
    table = {
        "qk": ((devices, UNITS, WIDTH), bf16),
        "ff": ((half, 2 * UNITS, WIDTH), bf16),
        "sm": ((devices, 16, 128), f32),
        "gff": ((half, 2 * UNITS, WIDTH), bf16),
        "gs": ((devices, 16, 128), f32),
        "sr": ((blocks, UNITS, WIDTH), bf16),
        "srs": ((blocks, 16, 128), f32),
        "wq": ((WIDTH, WIDTH), bf16),
        "wk": ((WIDTH, WIDTH), bf16),
        "wv": ((WIDTH, WIDTH), bf16),
        "wo": ((WIDTH, WIDTH), bf16),
        "s1": ((SEQ, WIDTH), f32),
        "i1": ((SEQ, 128), f32),
        "nm": ((SEQ, WIDTH), bf16),
        "hid": ((SEQ, WIDTH), f32),
        "s2": ((SEQ, WIDTH), f32),
        "i2": ((SEQ, 128), f32),
        "n2": ((4 * SEQ, WIDTH), bf16),
        "ct": ((4 * SEQ, WIDTH), bf16),
        "outp": ((4 * SEQ, WIDTH), f32),
        "dn2": ((4 * SEQ, WIDTH), f32),
        "outs": ((SEQ, WIDTH), f32),
        "dn2s": ((SEQ, WIDTH), f32),
        "outb": ((SEQ, WIDTH), f32),
        "dn2b": ((SEQ, WIDTH), f32),
        "outx": ((2, SEQ, WIDTH), bf16),
        "dn2x": ((2, SEQ, WIDTH), bf16),
        "act": ((2, 4 * SEQ, UNITS * depth), bf16),
        "dp": ((2, 4 * SEQ, UNITS * depth), bf16),
        "da": ((SEQ, WIDTH), bf16),
        "dk": ((WIDTH, SEQ), f32),
        "dn": ((SEQ, WIDTH), f32),
        "nmt": ((WIDTH, SEQ), bf16),
        "qt": ((WIDTH, SEQ), bf16),
        "kt": ((WIDTH, SEQ), bf16),
        "vt": ((WIDTH, SEQ), bf16),
        "krt": ((WIDTH, SEQ), f32),
        "mt": ((WIDTH, SEQ), bf16),
        "dmt": ((WIDTH, SEQ), bf16),
        "dqt": ((WIDTH, SEQ), bf16),
        "dkt": ((WIDTH, SEQ), bf16),
        "dvt": ((WIDTH, SEQ), bf16),
        "kft": ((WIDTH, SEQ), bf16),
        "vft": ((WIDTH, SEQ), bf16),
        "ex": ((WIDTH, SEQ), f32),
        "tt": ((HEADS, SEQ, SEQ), f32),
        "vec": ((16, WIDTH), f32),
        "vecc": ((WIDTH, 128), f32),
        "colsum": ((WIDTH, 128), f32),
        "gvec": ((16, WIDTH), f32),
        "bias": ((2, 8, UNITS * depth), f32),
        "gbias": ((half, 8, 128), f32),
    }
    for name, rows, lanes, kind in (("q", UNITS, WIDTH, bf16), ("t", 16, 128, f32)):
        table["r" + name + "dx"] = table["r" + name + "dy"] = ((depth, rows // 2, lanes), kind)
        table["r" + name + "xy"] = ((depth, 2, rows, lanes), kind)
        table["r" + name + "u"] = table["r" + name + "d"] = ((depth, rows, lanes), kind)
    table["rby"] = table["rbu"] = table["rbd"] = ((depth, 128, WIDTH), bf16)
    table["rcy"] = ((1, 64, WIDTH), bf16)
    table["rcu"] = table["rcd"] = ((half, 64, WIDTH), bf16)
    table["out"] = table["dinp"] = ((SEQ, WIDTH), bf16)
    for name in ("gwq", "gwk", "gwv", "gwo"):
        table[name] = ((24, WIDTH), f32)
    table["gfc1"] = table["gfc2"] = ((UNITS, WIDTH), f32)
    table["gsmall"] = ((16, 128), f32)
    table["store"] = len(RESULTS)
    for name, sent, came in (
        ("gq", 2, 4 * depth + 1), ("gb", 2, 2 * depth), ("gt", 2, 4 * depth + 1), ("gc", 3, 2 * depth + 1),
        ("sq", 1, 5 * depth), ("sb", 1, 3 * depth), ("st", 1, 5 * depth), ("sc", 1, 4 * depth + 1), ("e", 21, 21),
    ):
        table[name + "_s"], table[name + "_r"] = sent, came
    return table


PLAN = (
    "own_blocks", "barrier", "S0", "M0", "Sx", "Sz", "L0", "Sy", "Sy", "Sz", "Sx", "Mz", "Sx", "Sd", "Sz",
    "My", "Sx", "Mx", "Sy", "Mz", "norm1", "Sy", "Sd", "Mz", "L4", "My", "Mx", "Mx", "Mx", "F0", "Ly", "My",
    "Sd", "Sd", "Ss", "vectors", "My", "own_cotangent", "mixer_kernels", "gain1", "Md", "Md", "Fz", "Md",
    "Md", "L4", "Ms", "unpack", "project", "mix0", "mix1", "mix2", "Fz", "mix3", "hidden", "norm2", "Fz",
    "Fy", "M.", "sibling_rows", "L5", "pass_ct", "L4", "feed0o", "pass_n2_0", "feed0x0", "Fy", "L5",
    "diagonal_rows0", "feed0s", "feed0d0", "pass_n2_1", "L5", "feed0x1", "Fy", "diagonal_rows1", "feed0d1",
    "Fy", "feed1d0", "to_diagonal0", "feed1x0", "feed1x1", "feed1s", "to_x0", "feed1o", "feed1d1",
    "feed_grads1", "fY", "flip", "to_diagonal1", "l1", "fY", "fY", "fY", "feed_grads0", "out_to_diagonal",
    "to_sibling", "l0", "to_x1", "out_to_x", "back2_0", "back2_1", "grad_mixed", "back4", "back5", "back6",
    "fc", "back7", "pack0", "pack1", "fc", "fc", "core_sum0", "l0", "mD", "grad_normed", "finish_out",
    "core_sum1", "mD", "mb", "mY", "back1", "core_sum2", "l1", "mX", "fv", "kernel0", "core_sum3", "l1",
    "ma", "l0", "fc", "kernel3", "fv", "fv", "ma", "mb", "mY", "mX", "kernel1", "mD", "kernel2", "fv", "mc",
    "vector_tiles", "small_sums", "fw", "sD", "sX", "mY", "sD", "mb", "mX", "mD", "mc", "sY", "mv", "mv",
    "sa", "sa", "ma", "fw", "sb", "sY", "mb", "sX", "sb", "mY", "sD", "mX", "mw", "mc", "sc", "sY", "lO",
    "sb", "ma", "mw", "sX", "sc", "sD", "fe", "lY", "sX", "sv", "sY", "sv", "mv", "mc", "sa", "sa", "sc",
    "sb", "sw", "sw", "le", "mv", "sv", "sc", "me", "sv", "se", "store",
)
INPUTS = ("tok", "length", "cot", "iq", "ik", "iv", "io", "ifc1", "ifc2", "ibias", "ivec")
RESULTS = ("out", "dinp", "gwq", "gwk", "gwv", "gwo", "gfc1", "gfc2", "gsmall")
OUTPUTS = tuple("to_" + name for name in RESULTS)


def layer_kernel(depth, *refs):
    names = INPUTS + OUTPUTS + tuple(scratch_of(depth))
    m = SimpleNamespace(**dict(zip(names, refs, strict=True)))
    k = Links(depth)
    core = k.core

    def in_all(yx, zs):
        return (yx * 2 + core) * depth + zs

    def in_all_sib(yx, zs):
        return (yx * 2 + (1 - core)) * depth + zs

    def in_pair(yx, zs):
        return lax.div(yx, 2) * depth + zs

    places = {"o": k.x * 2 + core, "s": k.x * 2 + 1 - core, "x": (1 - k.x) * 2 + core, "d": (1 - k.x) * 2 + 1 - core}

    def rows_at(who, start=0, step=SEQ):
        return pl.ds(pl.multiple_of(places[who] * SEQ + start, step), step)

    def stored(name):
        place = RESULTS.index(name)
        return pltpu.make_async_copy(getattr(m, name), getattr(m, "to_" + name), m.store.at[place])

    def swap(place, source, target, device=None):
        k.start(None, lambda: source, lambda: target, m.e_s.at[place], m.e_r.at[place], device or k.sib_dev)

    day = lax.broadcasted_iota(jnp.int32, (1, SEQ), 1).astype(f32)
    s_at = lax.broadcasted_iota(jnp.int32, (SEQ, SEQ), 0)
    t_at = lax.broadcasted_iota(jnp.int32, (SEQ, SEQ), 1)
    valid = (lax.broadcasted_iota(jnp.int32, (1, SEQ), 1) < m.length[0]).astype(f32)

    def own_blocks():
        here = in_all(k.me, k.z)
        for place, (first, second) in enumerate(((m.iq, m.ik), (m.iv, m.io))):
            pair = jnp.concatenate([first[...].astype(f32), second[...].astype(f32)], axis=0)
            m.qk[here, 48 * place : 48 * place + 48] = pair.astype(bf16)
        m.sm[here] = jnp.zeros((16, 128), f32)
        m.sm[here, 0:15, 0:24] = m.ivec[...].astype(f32)
        m.sm[here, 15:16, 0:UNITS] = m.ibias[...].astype(f32)
        m.ff[in_pair(k.me, k.z), 0:UNITS] = m.ifc1[...]
        m.ff[in_pair(k.me, k.z), UNITS : 2 * UNITS] = m.ifc2[...]

    def half_at(who, half):
        return rows_at(who, half * (SEQ // 2), SEQ // 2)

    def own_cotangent():
        m.ct[rows_at("o")] = m.cot[...]
        ref = m.ct.at[rows_at("o")]
        swap(0, ref, ref)
        swap(1, ref, ref, k.x_dev)

    def pass_ct():
        ref = m.ct.at[rows_at("x")]
        k.arrive(ref, m.e_r.at[1])
        swap(2, ref, ref)

    def norm1():
        def rows_of(start, step):
            rows = pl.ds(start, step)
            tokens = m.tok[rows].astype(f32)
            centred = tokens - jnp.mean(tokens, axis=1, keepdims=True)
            inverse = lax.rsqrt(jnp.mean(centred * centred, axis=1, keepdims=True) + EPSILON)
            m.s1[rows] = centred * inverse
            m.i1[rows] = jnp.broadcast_to(inverse, (step, 128))

        row_loop(SEQ, 32, rows_of)

    def vectors():
        total = jnp.zeros((16, WIDTH), f32)
        for wide in range(8):
            part = jnp.zeros((16, 128), f32)
            for zs in range(depth):
                tile = m.sm[wide * depth + zs]
                part = part + (pltpu.roll(tile, 24 * zs, 1) if zs else tile)
            padded = jnp.concatenate([part, jnp.zeros((16, WIDTH - 128), f32)], axis=1)
            total = total + (pltpu.roll(padded, 96 * wide, 1) if wide else padded)
        m.vec[...] = total
        m.vecc[...] = jnp.transpose(jnp.concatenate([total, jnp.zeros((112, WIDTH), f32)], axis=0))
        for y in range(2):
            line = jnp.zeros((16, UNITS * depth), f32)
            for zs in range(depth):
                tile = m.sm[in_all(y * 2 + k.x, zs)]
                tile = jnp.concatenate([tile, jnp.zeros((16, UNITS * depth - 128), f32)], axis=1)
                line = line + (pltpu.roll(tile, UNITS * zs, 1) if zs else tile)
            m.bias[y] = line[8:16]

    def head_kernel(h, carry):
        rows = head_rows(h)
        decays = jnp.exp(-m.vecc[rows, 10:11] * day)
        m.ex[rows] = decays
        line = jnp.sum(m.vecc[rows, 9:10] * decays, axis=0, keepdims=True) * (1.0 / STATE)
        matrix = pltpu.roll(jnp.broadcast_to(line, (SEQ, SEQ)), 0, 1, stride=1, stride_axis=0)
        m.tt[h] = jnp.where(t_at >= s_at, matrix, 0.0)
        return carry

    def mixer_kernels():
        lax.fori_loop(0, HEADS, head_kernel, 0)

    def gain1():
        def rows_of(start, step):
            rows = pl.ds(start, step)
            m.nm[rows] = (m.s1[rows] * m.vec[0:1] + m.vec[1:2]).astype(bf16)

        row_loop(SEQ, 32, rows_of)
        m.nmt[...] = jnp.transpose(m.nm[...])

    def unpack_rows(w, carry):
        rows = pl.ds(pl.multiple_of(w * 96, 96), 96)
        for place, (first, second) in enumerate(((m.wq, m.wk), (m.wv, m.wo))):
            pair = m.qk[pl.ds(w * depth, depth), 48 * place : 48 * place + 48, :].astype(f32)
            first[rows] = pair[:, :24].reshape(96, WIDTH).astype(bf16)
            second[rows] = pair[:, 24:].reshape(96, WIDTH).astype(bf16)
        return carry

    def unpack():
        lax.fori_loop(0, 8, unpack_rows, 0)

    def project():
        m.qt[...] = jnp.transpose(dg(m.nm[...], m.wq[...], 1, 0) + m.vec[2:3]).astype(bf16)
        m.krt[...] = jnp.transpose(dg(m.nm[...], m.wk[...], 1, 0) + m.vec[3:4])
        m.vt[...] = (jnp.transpose(dg(m.nm[...], m.wv[...], 1, 0) + m.vec[4:5]) * valid).astype(bf16)

    def mix_head(h):
        rows = head_rows(h)
        raw = m.krt[rows]
        summed = raw * m.vecc[rows, 5:6]
        for j in range(1, 4):
            summed = summed + lane_shift(raw, j, False) * m.vecc[rows, 5 + j : 6 + j]
        keys = (summed * valid).astype(bf16)
        m.kt[rows] = keys
        scores = dg(keys, m.qt[rows], 0, 0) * (1.0 / HEAD_SIZE)
        weights = (scores * m.tt[h]).astype(bf16)
        m.mt[rows] = (dg(m.vt[rows], weights, 1, 0) * valid).astype(bf16)

    def hidden():
        m.hid[...] = dg(m.mt[...], m.wo[...], 0, 0)

    def norm2():
        def rows_of(start, step):
            rows = pl.ds(start, step)
            hidden = m.tok[rows].astype(f32) + m.hid[rows] + m.vec[11:12]
            m.hid[rows] = hidden
            centred = hidden - jnp.mean(hidden, axis=1, keepdims=True)
            inverse = lax.rsqrt(jnp.mean(centred * centred, axis=1, keepdims=True) + EPSILON)
            scaled = centred * inverse
            m.s2[rows] = scaled
            m.i2[rows] = jnp.broadcast_to(inverse, (step, 128))
            m.n2[rows_at("o", start, step)] = (scaled * m.vec[12:13] + m.vec[13:14]).astype(bf16)

        row_loop(SEQ, 32, rows_of)
        ref = m.n2.at[rows_at("o")]
        swap(3, ref, ref)
        for half in range(2):
            ref = m.n2.at[half_at("o", half)]
            swap(4 + half, ref, ref, k.x_dev)

    def pass_n2(half):
        ref = m.n2.at[half_at("x", half)]
        k.arrive(ref, m.e_r.at[4 + half])
        swap(6 + half, ref, ref)

    def sibling_rows():
        k.arrive(m.ct.at[rows_at("s")], m.e_r.at[0])
        k.arrive(m.n2.at[rows_at("s")], m.e_r.at[3])

    def diagonal_rows(half):
        if half == 0:
            k.arrive(m.ct.at[rows_at("d")], m.e_r.at[2])
        k.arrive(m.n2.at[half_at("d", half)], m.e_r.at[6 + half])

    def finish_feed(ref, more):
        value = ref[...].astype(f32)
        for target, low, high in ((m.gfc1, 0, UNITS), (m.gfc2.at[0:32], UNITS, 128)):
            target[...] = target[...] + value[low:high] if more else value[low:high]

    def finish_last(ref, more):
        value = ref[...].astype(f32)
        m.gfc2[32:96] = m.gfc2[32:96] + value if more else value

    def finish_mats(ref, more):
        value = ref[...].astype(f32)
        for place, target in enumerate((m.gwq, m.gwk, m.gwv, m.gwo)):
            part = value[24 * place : 24 * place + 24]
            target[...] = target[...] + part if more else part

    def finish_small(ref, more):
        m.gsmall[...] = m.gsmall[...] + ref[...] if more else ref[...]

    steps = {}
    steps |= gather_z_first(k, "S", m.sm, in_all, 0, 16, 8, m.gt_s, m.gt_r, in_all_sib)
    steps |= gather_z_first(k, "M", m.qk, in_all, 0, UNITS, UNITS // 2, m.gq_s, m.gq_r, in_all_sib)
    steps |= gather_pair_z_first(k, "F", m.ff, in_pair, 0, 128, m.gb_s, m.gb_r)
    steps |= gather_pair_z_last(k, "L", m.ff, in_pair, 128, 64, m.gc_s, m.gc_r)
    slots = (m.rby, m.rbu, m.rbd)
    steps |= scatter_pair_z_last(k, "f", m.gff, in_pair, 0, 128, slots, m.sb_s, m.sb_r, finish_feed)
    slots = (m.rcy, m.rcu, m.rcd)
    steps |= scatter_pair_z_first(k, "l", m.gff, in_pair, 128, 64, slots, m.sc_s, m.sc_r, finish_last)
    slots = (m.rqdx, m.rqdy, m.rqxy, m.rqu, m.rqd)
    steps |= scatter_z_last(k, "m", m.qk, in_all, 0, UNITS, UNITS // 2, slots, m.sq_s, m.sq_r, finish_mats)
    slots = (m.rtdx, m.rtdy, m.rtxy, m.rtu, m.rtd)
    steps |= scatter_z_last(k, "s", m.gs, in_all, 0, 16, 8, slots, m.st_s, m.st_r, finish_small)

    root = math.sqrt(2.0 / math.pi)
    chunk = UNITS * depth
    ys = (k.y, 1 - k.y)

    def feed(which, who, half=None):
        blocks = pl.ds(ys[which] * depth, depth)
        rows = rows_at(who) if half is None else half_at(who, half)
        fc1 = m.ff[blocks, 0:UNITS, :].reshape(chunk, WIDTH)
        fc2 = m.ff[blocks, UNITS : 2 * UNITS, :].reshape(chunk, WIDTH)
        pre = dg(m.n2[rows], fc1, 1, 1) + m.bias[ys[which], 7:8]
        square = pre * pre
        tanh = jnp.tanh(root * pre * (1.0 + 0.044715 * square))
        half = 0.5 * (1.0 + tanh)
        slope = half + 0.5 * pre * (1.0 - tanh * tanh) * (root * (1.0 + 3 * 0.044715 * square))
        activated = (pre * half).astype(bf16)
        grad_pre = (dg(m.ct[rows], fc2, 1, 1) * slope).astype(bf16)
        m.act[which, rows] = activated
        m.dp[which, rows] = grad_pre
        if which == 0:
            m.outp[rows] = dg(activated, fc2, 1, 0)
            m.dn2[rows] = dg(grad_pre, fc1, 1, 0)
        else:
            m.outp[rows] += dg(activated, fc2, 1, 0)
            m.dn2[rows] += dg(grad_pre, fc1, 1, 0)

    def to_sibling():
        swap(8, m.dn2.at[rows_at("s")], m.dn2s)
        swap(9, m.outp.at[rows_at("s")], m.outs)

    def half_rows(half):
        return pl.ds(half * (SEQ // 2), SEQ // 2)

    def to_diagonal(half):
        swap(10 + half, m.dn2.at[half_at("d", half)], m.dn2b.at[half_rows(half)])

    def to_x(half):
        rows = half_rows(half)
        k.arrive(m.dn2b.at[rows], m.e_r.at[10 + half])
        m.dn2x[0, rows] = (m.dn2[half_at("x", half)] + m.dn2b[rows]).astype(bf16)
        swap(13 + half, m.dn2x.at[0, rows], m.dn2x.at[1, rows], k.x_dev)

    def out_to_diagonal():
        swap(12, m.outp.at[rows_at("d")], m.outb)

    def out_to_x():
        k.arrive(m.outb, m.e_r.at[12])
        m.outx[0] = (m.outp[rows_at("x")] + m.outb[...]).astype(bf16)
        swap(15, m.outx.at[0], m.outx.at[1], k.x_dev)

    def feed_grads(which):
        blocks = pl.ds(ys[which] * depth, depth)
        pre = m.dp[which]
        m.gff[blocks, 0:UNITS] = dg(pre, m.n2[...], 0, 0).astype(bf16).reshape(depth, UNITS, WIDTH)
        m.gff[blocks, UNITS : 2 * UNITS] = (
            dg(m.act[which], m.ct[...], 0, 0).astype(bf16).reshape(depth, UNITS, WIDTH)
        )
        sums = jnp.sum(pre.astype(f32), axis=0, keepdims=True)
        lane = lax.broadcasted_iota(jnp.int32, (1, 128), 1)
        for zs in range(depth):
            line = (pltpu.roll(sums, chunk - UNITS * zs, 1) if zs else sums)[:, :128]
            m.gbias[ys[which] * depth + zs] = jnp.broadcast_to(jnp.where(lane < UNITS, line, 0.0), (8, 128))

    def back2(half):
        if half == 0:
            m.gvec[...] = jnp.zeros((16, WIDTH), f32)
            k.arrive(m.dn2s, m.e_r.at[8])
        k.arrive(m.dn2x.at[1, half_rows(half)], m.e_r.at[13 + half])

        def rows_of(start, step):
            rows = pl.ds(start, step)
            grad_normed = m.dn2[rows_at("o", start, step)] + m.dn2s[rows] + m.dn2x[1, rows].astype(f32)
            scaled = m.s2[rows]
            grad_in = grad_normed * m.vec[12:13]
            first = jnp.mean(grad_in, axis=1, keepdims=True)
            second = jnp.mean(grad_in * scaled, axis=1, keepdims=True)
            top = m.cot[rows].astype(f32)
            grad_hidden = top + m.i2[rows, 0:1] * (grad_in - first - scaled * second)
            m.s2[rows] = grad_hidden
            rounded = grad_hidden.astype(bf16)
            m.da[rows] = rounded
            m.gvec[11:12] += jnp.sum(rounded.astype(f32), axis=0, keepdims=True)
            m.gvec[12:13] += jnp.sum(grad_normed * scaled, axis=0, keepdims=True)
            m.gvec[13:14] += jnp.sum(grad_normed, axis=0, keepdims=True)
            m.gvec[14:15] += jnp.sum(top, axis=0, keepdims=True)

        row_loop(SEQ // 2, 32, rows_of, half * (SEQ // 2))

    def grad_mixed():
        m.dmt[...] = (jnp.transpose(dg(m.da[...], m.wo[...], 1, 1)) * valid).astype(bf16)

    def back_head(h):
        rows = head_rows(h)
        queries, keys, grad_mixed, kernel = m.qt[rows], m.kt[rows], m.dmt[rows], m.tt[h]
        scores = dg(keys, queries, 0, 0) * (1.0 / HEAD_SIZE)
        weights = (scores * kernel).astype(bf16)
        grad_weights = dg(m.vt[rows], grad_mixed, 0, 0)
        grad_values = (dg(grad_mixed, weights, 1, 1) * valid).astype(bf16)
        m.dvt[rows] = grad_values
        grad_scores = (grad_weights * kernel).astype(bf16)
        grad_queries = (dg(keys, grad_scores, 1, 0) * (1.0 / HEAD_SIZE)).astype(bf16)
        m.dqt[rows] = grad_queries
        grad_keys = dg(queries, grad_scores, 1, 1) * (1.0 / HEAD_SIZE) * valid
        m.dk[rows] = grad_keys
        grad_raw = grad_keys * m.vecc[rows, 5:6]
        for j in range(1, 4):
            grad_raw = grad_raw + lane_shift(grad_keys, j, True) * m.vecc[rows, 5 + j : 6 + j]
        m.dkt[rows] = grad_raw.astype(bf16)

    def pack_rows(part):
        rows = pl.ds(pl.multiple_of(part * 384, 384), 384)
        normed = m.nmt[rows]
        grads = (
            dg(normed, m.dqt[...], 1, 1),
            dg(normed, m.dkt[...], 1, 1),
            dg(normed, m.dvt[...], 1, 1),
            dg(m.mt[rows], m.da[...], 1, 0),
        )
        for place in range(2):
            pair = [grad.reshape(4 * depth, 24, WIDTH) for grad in grads[2 * place : 2 * place + 2]]
            m.qk[pl.ds(part * 4 * depth, 4 * depth), 48 * place : 48 * place + 48, :] = jnp.concatenate(pair, axis=1).astype(bf16)

    def pack(which):
        pack_rows(ys[1 - which])
        for place in (2 * which, 2 * which + 1):
            yx = (k.ds, k.ys, k.xs, k.me)[place]
            swap(16 + place, m.qk.at[pl.ds(in_all_sib(yx, 0), depth)], m.sr.at[pl.ds(yx * depth, depth)])

    def grad_normed():
        m.dn[...] = jnp.transpose(
            dg(m.wq[...], m.dqt[...], 1, 0) + dg(m.wk[...], m.dkt[...], 1, 0) + dg(m.wv[...], m.dvt[...], 1, 0)
        )

    def back1():
        def rows_of(start, step):
            rows = pl.ds(start, step)
            grad_out, scaled = m.dn[rows], m.s1[rows]
            grad_in = grad_out * m.vec[0:1]
            first = jnp.mean(grad_in, axis=1, keepdims=True)
            second = jnp.mean(grad_in * scaled, axis=1, keepdims=True)
            m.dinp[rows] = (m.s2[rows] + m.i1[rows, 0:1] * (grad_in - first - scaled * second)).astype(bf16)
            m.gvec[0:1] += jnp.sum(grad_out * scaled, axis=0, keepdims=True)
            m.gvec[1:2] += jnp.sum(grad_out, axis=0, keepdims=True)

        row_loop(SEQ, 32, rows_of)
        stored("dinp").start()

    def core_sum(place):
        yx = (k.ds, k.ys, k.xs, k.me)[place]
        k.arrive(m.sr.at[pl.ds(yx * depth, depth)], m.e_r.at[16 + place])
        for zs in range(depth):
            add_into(m.qk.at[in_all(yx, zs)], m.sr.at[yx * depth + zs])

    def flip():
        turn = (s_at + t_at == SEQ - 1).astype(bf16)
        m.kft[...] = dg(m.kt[...], turn, 1, 0).astype(bf16)
        m.vft[...] = dg(m.vt[...], turn, 1, 0).astype(bf16)

    def kernel_head(h):
        rows = head_rows(h)
        scores = dg(m.kft[rows], m.qt[rows], 0, 0) * (1.0 / HEAD_SIZE)
        grad_weights = dg(m.vft[rows], m.dmt[rows], 0, 0)
        product = jnp.where(s_at + t_at >= SEQ - 1, scores * grad_weights, 0.0)
        lined = pltpu.roll(product, 1, 1, stride=1, stride_axis=0)
        grad_kernel = jnp.sum(lined, axis=0, keepdims=True) * (1.0 / STATE)
        part = m.ex[rows] * grad_kernel
        at = lax.broadcasted_iota(jnp.int32, (HEAD_SIZE, 128), 1)
        grad_rate = -m.vecc[rows, 9:10] * jnp.sum(part * day, axis=1, keepdims=True)
        sums = jnp.where(at == 9, jnp.sum(part, axis=1, keepdims=True), 0.0)
        sums = jnp.where(at == 10, grad_rate, sums)
        raw, grad_keys = m.krt[rows], m.dk[rows]
        for j in range(4):
            tap = jnp.sum(grad_keys * (lane_shift(raw, j, False) if j else raw), axis=1, keepdims=True)
            sums = jnp.where(at == 5 + j, tap, sums)
        for place, value in ((2, m.dqt), (3, m.dkt), (4, m.dvt)):
            sums = jnp.where(at == place, jnp.sum(value[rows].astype(f32), axis=1, keepdims=True), sums)
        m.colsum[rows] = sums

    def vector_tiles():
        grads = m.gvec[...] + jnp.transpose(m.colsum[...])[0:16]
        row_at = lax.broadcasted_iota(jnp.int32, (16, 128), 0)
        lane_at = lax.broadcasted_iota(jnp.int32, (16, 128), 1)
        for wide in range(8):
            turned = (pltpu.roll(grads, WIDTH - 96 * wide, 1) if wide else grads)[:, :128]
            for zs in range(depth):
                tile = pltpu.roll(turned, 128 - 24 * zs, 1) if zs else turned
                tile = jnp.where((lane_at < 24) & (row_at < 15), tile, 0.0)
                own = jnp.concatenate([jnp.zeros((8, 128), f32), m.gbias[(wide // 4) * depth + zs]], axis=0)
                mine = (row_at == 15) & (core == wide % 2) & (k.x == wide // 2 % 2)
                m.gs[wide * depth + zs] = jnp.where(mine, own, tile)
        for yx in range(4):
            swap(20, m.gs.at[pl.ds(in_all_sib(yx, 0), depth)], m.srs.at[pl.ds(yx * depth, depth)])

    def small_sums():
        k.arrive(m.srs, m.e_r.at[20])
        for yx in range(4):
            for zs in range(depth):
                add_into(m.gs.at[in_all(yx, zs)], m.srs.at[yx * depth + zs])

    def finish_out():
        def rows_of(start, step):
            rows = pl.ds(start, step)
            others = m.outs[rows] + m.outx[1, rows].astype(f32)
            m.out[rows] = (m.hid[rows] + (m.outp[rows_at("o", start, step)] + others) + m.vec[14:15]).astype(bf16)

        k.arrive(m.outs, m.e_r.at[9])
        k.arrive(m.outx.at[1], m.e_r.at[15])
        row_loop(SEQ, 32, rows_of)
        stored("out").start()

    def store():
        for name in RESULTS[2:]:
            stored(name).start()
        for group in "SFLflms":
            next(steps[group + "."])
        own, half = m.ct.at[rows_at("o")], m.ct.at[half_at("o", 0)]
        half_f32, own_f32, blocks = m.outb.at[half_rows(0)], m.outb, m.sr.at[pl.ds(0, depth)]
        extents = [own] * 4 + [half] * 4 + [own_f32] * 2 + [half_f32] * 2 + [own_f32] + [half] * 2 + [own] + [blocks] * 4
        extents.append(m.srs)
        for place, extent in enumerate(extents):
            k.left(extent, m.e_s.at[place])
        for name in RESULTS:
            stored(name).wait()

    compute = {
        "own_blocks": own_blocks, "barrier": k.barrier, "own_cotangent": own_cotangent, "norm1": norm1, "pass_ct": pass_ct,
        "vectors": vectors, "mixer_kernels": mixer_kernels, "gain1": gain1, "unpack": unpack, "project": project,
        "hidden": hidden, "norm2": norm2, "sibling_rows": sibling_rows, "to_sibling": to_sibling,
        "out_to_diagonal": out_to_diagonal, "out_to_x": out_to_x, "grad_mixed": grad_mixed, "grad_normed": grad_normed,
        "back1": back1, "flip": flip, "vector_tiles": vector_tiles, "small_sums": small_sums, "finish_out": finish_out,
        "store": store,
    }
    for which in range(2):
        for who in "os":
            compute["feed%d%s" % (which, who)] = partial(feed, which, who)
        for who in "xd":
            for half in range(2):
                compute["feed%d%s%d" % (which, who, half)] = partial(feed, which, who, half)
        compute["feed_grads%d" % which] = partial(feed_grads, which)
        compute["pass_n2_%d" % which] = partial(pass_n2, which)
        compute["diagonal_rows%d" % which] = partial(diagonal_rows, which)
        compute["to_diagonal%d" % which] = partial(to_diagonal, which)
        compute["to_x%d" % which] = partial(to_x, which)
        compute["back2_%d" % which] = partial(back2, which)
        compute["pack%d" % which] = partial(pack, which)
    for which in range(4):
        compute["mix%d" % which] = partial(three_heads, 3 * which, mix_head)
        compute["back%d" % (4 + which)] = partial(three_heads, 3 * which, back_head)
        compute["kernel%d" % which] = partial(three_heads, 3 * which, kernel_head)
        compute["core_sum%d" % which] = partial(core_sum, which)
    for step in PLAN:
        if step in compute:
            compute[step]()
        else:
            next(steps[step])


def results_kernel(*refs):
    sources, tile, targets, bias, vectors = refs[:8], refs[8], refs[9:17], refs[17], refs[18]
    for source, target in zip(sources, targets, strict=True):
        target[...] = source[...]
    bias[...] = tile[15:16, :UNITS]
    vectors[...] = tile[0:15, 0:24]


def on_device_fast(
    tokens, lengths, cotangent, w_query, w_key, w_value, w_out, w_fc1, w_fc2, fc1_bias, vectors
):
    depth = lax.axis_size("narrow")
    scratch = []
    for entry in scratch_of(depth).values():
        scratch.append(pltpu.SemaphoreType.DMA((entry,)) if isinstance(entry, int) else pltpu.VMEM(*entry))
    in_vmem = pl.BlockSpec(memory_space=pltpu.VMEM)
    anywhere = pl.BlockSpec(memory_space=pl.ANY)
    in_smem = pl.BlockSpec(memory_space=pltpu.SMEM)
    shape = jax.ShapeDtypeStruct
    got = pl.pallas_call(
        partial(layer_kernel, depth),
        out_shape=[shape((SEQ, WIDTH), bf16)] * 2
        + [shape((24, WIDTH), f32)] * 4
        + [shape((UNITS, WIDTH), f32)] * 2
        + [shape((16, 128), f32)],
        in_specs=[in_vmem, in_smem] + [in_vmem] * 9,
        out_specs=[anywhere] * 9,
        scratch_shapes=scratch,
        compiler_params=pltpu.CompilerParams(
            collective_id=0, has_side_effects=True, vmem_limit_bytes=63 * 2**20
        ),
        name="h3_layer",
    )(
        tokens, lengths, cotangent, w_query, w_key, w_value, w_out, w_fc1.T, w_fc2, fc1_bias[None], vectors
    )
    results = pl.pallas_call(
        results_kernel,
        out_shape=[shape(x.shape, x.dtype) for x in got[:8]] + [shape((1, UNITS), f32), shape((15, 24), f32)],
        in_specs=[in_vmem] * 9,
        out_specs=[in_vmem] * 10,
        name="results",
    )(*got)
    out, grad_in, g_query, g_key, g_value, g_out, g_fc1, g_fc2, g_bias, g_vectors = results
    return out, grad_in, g_query, g_key, g_value, g_out, g_fc1.T, g_fc2, g_bias.reshape(-1), g_vectors


def fits(mesh):
    return mesh.shape["wide"] == 8 and mesh.shape["narrow"] == 4


def solution(mesh):
    placed = (
        P(("wide", "narrow"), None),
        P(("wide", "narrow")),
        P(("wide", "narrow"), None),
        P(("wide", "narrow"), None),
        P(("wide", "narrow"), None),
        P(("wide", "narrow"), None),
        P(("wide", "narrow"), None),
        P(None, ("wide", "narrow")),
        P(("wide", "narrow"), None),
        P(("wide", "narrow")),
        P(None, ("wide", "narrow")),
    )
    return jax.shard_map(
        on_device_fast if fits(mesh) else on_device,
        mesh=mesh,
        in_specs=placed,
        out_specs=(
            P(("wide", "narrow"), None),
            P(("wide", "narrow"), None),
            P(("wide", "narrow"), None),
            P(("wide", "narrow"), None),
            P(("wide", "narrow"), None),
            P(("wide", "narrow"), None),
            P(None, ("wide", "narrow")),
            P(("wide", "narrow"), None),
            P(("wide", "narrow")),
            P(None, ("wide", "narrow")),
        ),
        check_vma=False,
    )
```

```python
import math
from functools import partial
from types import SimpleNamespace

import jax
import jax.numpy as jnp
from jax import lax
from jax.experimental import pallas as pl
from jax.experimental.pallas import tpu as pltpu
from jax.sharding import PartitionSpec as P

HEAD_SIZE = 64
STATE = 64


EPSILON = 1e-05


def normalize(values):
    average = jnp.mean(values, axis=-1, keepdims=True)
    centred = values - average
    variance = jnp.mean(centred * centred, axis=-1, keepdims=True)
    inverse = lax.rsqrt(variance + EPSILON)
    return (centred * inverse, inverse)


def norm_back(grad_in, scaled, inverse):
    first = jnp.mean(grad_in, axis=-1, keepdims=True)
    second = jnp.mean(grad_in * scaled, axis=-1, keepdims=True)
    return inverse * (grad_in - first - scaled * second)


def shift_mix(key_raw, shift_taps):
    summed = key_raw * shift_taps[0]
    for offset in range(1, 4):
        delayed = jnp.concatenate(
            [jnp.zeros((offset, key_raw.shape[1]), key_raw.dtype), key_raw[:-offset]], axis=0
        )
        summed = summed + delayed * shift_taps[offset]
    return summed


def kernel_rows(coefficient, decay_rate, length_all):
    distance = jnp.arange(length_all).astype(jnp.float32)
    decays = jnp.exp(-decay_rate[:, :, None] * distance[None, None, :])
    return jnp.sum(coefficient[:, :, None] * decays, axis=1) / STATE


def toeplitz(kernel_row):
    length_all = kernel_row.shape[0]
    wrapped = jnp.concatenate(
        [kernel_row[:1], jnp.zeros((length_all,), kernel_row.dtype), kernel_row[:0:-1]]
    )
    tiled_row = jnp.tile(wrapped, length_all)[: length_all * (2 * length_all - 1)]
    return tiled_row.reshape(length_all, 2 * length_all - 1)[:, :length_all]


def split_heads(values, row_count):
    return values.reshape(row_count, -1, HEAD_SIZE).transpose(1, 0, 2)


def merge_heads(per_head):
    head_count = per_head.shape[0]
    row_count = per_head.shape[1]
    merged = per_head.transpose(1, 0, 2).reshape(row_count, head_count * HEAD_SIZE)
    return merged


def pack_rows(matrices, shard_count):
    return jnp.concatenate(
        [matrix.reshape(shard_count, -1) for matrix in matrices], axis=1
    ).reshape(-1)


def unpack_rows(flat, matrices, shard_count):
    pieces = []
    offset = 0
    for matrix in matrices:
        rows_own = matrix.shape[0] // shard_count
        extent = matrix.size // shard_count
        pieces.append(flat[offset : offset + extent].reshape((rows_own,) + matrix.shape[1:]))
        offset = offset + extent
    return pieces


def mixer_forward(queries, keys, values, kernel, row_count):

    def head_forward(parts):
        query_head, key_head, value_head, kernel_row = parts
        scores = jnp.dot(query_head, key_head.T, preferred_element_type=jnp.float32) / HEAD_SIZE
        weights_mix = (scores * toeplitz(kernel_row)).astype(jnp.bfloat16)
        return jnp.dot(weights_mix, value_head, preferred_element_type=jnp.float32)

    per_head = lax.map(
        head_forward,
        (
            split_heads(queries, row_count),
            split_heads(keys, row_count),
            split_heads(values, row_count),
            kernel,
        ),
    )
    return merge_heads(per_head)


def mixer_backward(queries, keys, values, grad_mixed, kernel, row_count):

    def head_backward(parts):
        query_head, key_head, value_head, grad_head, kernel_row = parts
        scores = jnp.dot(query_head, key_head.T, preferred_element_type=jnp.float32) / HEAD_SIZE
        toeplitz_mat, pullback = jax.vjp(toeplitz, kernel_row)
        weights_mix = (scores * toeplitz_mat).astype(jnp.bfloat16)
        grad_weights = jnp.dot(grad_head, value_head.T, preferred_element_type=jnp.float32)
        grad_values = jnp.dot(weights_mix.T, grad_head, preferred_element_type=jnp.float32)
        grad_scores = (grad_weights * toeplitz_mat).astype(jnp.bfloat16)
        grad_queries = (
            jnp.dot(grad_scores, key_head, preferred_element_type=jnp.float32) / HEAD_SIZE
        )
        grad_keys = (
            jnp.dot(grad_scores.T, query_head, preferred_element_type=jnp.float32) / HEAD_SIZE
        )
        grad_kernel = pullback(grad_weights * scores)[0]
        return (grad_queries, grad_keys, grad_values, grad_kernel)

    head_grads = lax.map(
        head_backward,
        (
            split_heads(queries, row_count),
            split_heads(keys, row_count),
            split_heads(values, row_count),
            split_heads(grad_mixed, row_count),
            kernel,
        ),
    )
    grad_kernel = head_grads[3]
    return (
        merge_heads(head_grads[0]),
        merge_heads(head_grads[1]),
        merge_heads(head_grads[2]),
        grad_kernel,
    )


def on_device(
    tokens, lengths, cotangent, w_query, w_key, w_value, w_out, w_fc1, w_fc2, fc1_bias, vectors
):
    shard_count = lax.axis_size(("wide", "narrow"))
    gathered = (
        lax.all_gather(w_query, ("wide", "narrow"), axis=0, tiled=True),
        lax.all_gather(w_key, ("wide", "narrow"), axis=0, tiled=True),
        lax.all_gather(w_value, ("wide", "narrow"), axis=0, tiled=True),
        lax.all_gather(w_out, ("wide", "narrow"), axis=0, tiled=True),
        lax.all_gather(w_fc1, ("wide", "narrow"), axis=1, tiled=True),
        lax.all_gather(w_fc2, ("wide", "narrow"), axis=0, tiled=True),
        lax.all_gather(fc1_bias, ("wide", "narrow"), axis=0, tiled=True),
        lax.all_gather(vectors, ("wide", "narrow"), axis=1, tiled=True),
    )
    query_full, key_full, value_full, out_full, fc1_full, fc2_full, bias_full, vector_full = (
        gathered
    )
    params = vector_full.astype(jnp.float32)
    fc1_shift = bias_full.astype(jnp.float32)
    seq_len = tokens.shape[0]
    head_count = params.shape[1] // HEAD_SIZE
    seq_length = lengths[0]
    valid_mask = (jnp.arange(seq_len) < seq_length).astype(jnp.float32)[:, None]
    residual = tokens.astype(jnp.float32)
    scaled1, inverse1 = normalize(residual)
    normed = (scaled1 * params[0] + params[1]).astype(jnp.bfloat16)
    queries = (jnp.dot(normed, query_full, preferred_element_type=jnp.float32) + params[2]).astype(
        jnp.bfloat16
    )
    key_raw = jnp.dot(normed, key_full, preferred_element_type=jnp.float32) + params[3]
    keys = (shift_mix(key_raw, params[5:9]) * valid_mask).astype(jnp.bfloat16)
    values = (
        (jnp.dot(normed, value_full, preferred_element_type=jnp.float32) + params[4]) * valid_mask
    ).astype(jnp.bfloat16)
    coefficient = params[9].reshape(head_count, STATE)
    decay_rate = params[10].reshape(head_count, STATE)
    kernel_fn = partial(kernel_rows, length_all=seq_len)
    kernel, kernel_pull = jax.vjp(kernel_fn, coefficient, decay_rate)
    mixed = mixer_forward(queries, keys, values, kernel, seq_len)
    mixed_out = (mixed * valid_mask).astype(jnp.bfloat16)
    hidden = (
        residual + jnp.dot(mixed_out, out_full, preferred_element_type=jnp.float32) + params[11]
    )
    scaled2, inverse2 = normalize(hidden)
    normed2 = (scaled2 * params[12] + params[13]).astype(jnp.bfloat16)
    pre_act = jnp.dot(normed2, fc1_full, preferred_element_type=jnp.float32) + fc1_shift
    activated = jax.nn.gelu(pre_act).astype(jnp.bfloat16)
    output = (
        hidden + jnp.dot(activated, fc2_full, preferred_element_type=jnp.float32) + params[14]
    ).astype(jnp.bfloat16)
    again = (
        lax.all_gather(w_query, ("wide", "narrow"), axis=0, tiled=True),
        lax.all_gather(w_key, ("wide", "narrow"), axis=0, tiled=True),
        lax.all_gather(w_value, ("wide", "narrow"), axis=0, tiled=True),
        lax.all_gather(w_out, ("wide", "narrow"), axis=0, tiled=True),
        lax.all_gather(w_fc1, ("wide", "narrow"), axis=1, tiled=True),
        lax.all_gather(w_fc2, ("wide", "narrow"), axis=0, tiled=True),
        lax.all_gather(fc1_bias, ("wide", "narrow"), axis=0, tiled=True),
        lax.all_gather(vectors, ("wide", "narrow"), axis=1, tiled=True),
    )
    query_back, key_back, value_back, out_back, fc1_back, fc2_back = (
        again[0],
        again[1],
        again[2],
        again[3],
        again[4],
        again[5],
    )
    grad_top = cotangent.astype(jnp.float32)
    grad_fc2 = jnp.dot(activated.T, cotangent, preferred_element_type=jnp.float32)
    grad_activated = jnp.dot(cotangent, fc2_back.T, preferred_element_type=jnp.float32)
    gelu_value, gelu_pull = jax.vjp(jax.nn.gelu, pre_act)
    grad_pre = gelu_pull(grad_activated)[0].astype(jnp.bfloat16)
    grad_fc1_turned = jnp.dot(grad_pre.T, normed2, preferred_element_type=jnp.float32)
    grad_fc1_bias = jnp.sum(grad_pre.astype(jnp.float32), axis=0)[:, None]
    mlp_terms = [grad_fc1_turned, grad_fc2, grad_fc1_bias]
    mlp_flat = lax.psum_scatter(
        pack_rows(mlp_terms, shard_count), ("wide", "narrow"), scatter_dimension=0, tiled=True
    )
    mlp_sums = unpack_rows(mlp_flat, mlp_terms, shard_count)
    grad_normed2 = jnp.dot(grad_pre, fc1_back.T, preferred_element_type=jnp.float32)
    grad_hidden = grad_top + norm_back(grad_normed2 * params[12], scaled2, inverse2)
    grad_attn = grad_hidden.astype(jnp.bfloat16)
    grad_out = jnp.dot(mixed_out.T, grad_attn, preferred_element_type=jnp.float32)
    grad_mixed = (
        jnp.dot(grad_attn, out_back.T, preferred_element_type=jnp.float32) * valid_mask
    ).astype(jnp.bfloat16)
    grad_q, grad_k, grad_v, grad_kernel = mixer_backward(
        queries, keys, values, grad_mixed, kernel, seq_len
    )
    grad_queries = grad_q.astype(jnp.bfloat16)
    grad_values = (grad_v * valid_mask).astype(jnp.bfloat16)
    shift_value, shift_pull = jax.vjp(shift_mix, key_raw, params[5:9])
    grad_key_full, grad_taps = shift_pull(grad_k * valid_mask)
    grad_key_raw = grad_key_full.astype(jnp.bfloat16)
    grad_query = jnp.dot(normed.T, grad_queries, preferred_element_type=jnp.float32)
    grad_key = jnp.dot(normed.T, grad_key_raw, preferred_element_type=jnp.float32)
    grad_value = jnp.dot(normed.T, grad_values, preferred_element_type=jnp.float32)
    grad_normed = jnp.dot(grad_queries, query_back.T, preferred_element_type=jnp.float32)
    grad_normed = grad_normed + jnp.dot(
        grad_key_raw, key_back.T, preferred_element_type=jnp.float32
    )
    grad_normed = grad_normed + jnp.dot(
        grad_values, value_back.T, preferred_element_type=jnp.float32
    )
    input_grad = (grad_hidden + norm_back(grad_normed * params[0], scaled1, inverse1)).astype(
        jnp.bfloat16
    )
    grad_coef, grad_rate = kernel_pull(grad_kernel)
    grad_vectors = jnp.concatenate(
        [
            jnp.sum(grad_normed * scaled1, axis=0)[None],
            jnp.sum(grad_normed, axis=0)[None],
            jnp.sum(grad_queries.astype(jnp.float32), axis=0)[None],
            jnp.sum(grad_key_raw.astype(jnp.float32), axis=0)[None],
            jnp.sum(grad_values.astype(jnp.float32), axis=0)[None],
            grad_taps,
            grad_coef.reshape(1, -1),
            grad_rate.reshape(1, -1),
            jnp.sum(grad_attn.astype(jnp.float32), axis=0)[None],
            jnp.sum(grad_normed2 * scaled2, axis=0)[None],
            jnp.sum(grad_normed2, axis=0)[None],
            jnp.sum(grad_top, axis=0)[None],
        ],
        axis=0,
    )
    mixer_terms = [grad_query, grad_key, grad_value, grad_out, grad_vectors.T]
    mixer_flat = lax.psum_scatter(
        pack_rows(mixer_terms, shard_count), ("wide", "narrow"), scatter_dimension=0, tiled=True
    )
    mixer_sums = unpack_rows(mixer_flat, mixer_terms, shard_count)
    return (
        output,
        input_grad,
        mixer_sums[0],
        mixer_sums[1],
        mixer_sums[2],
        mixer_sums[3],
        mlp_sums[0].T,
        mlp_sums[1],
        mlp_sums[2].reshape(-1),
        mixer_sums[4].T,
    )


f32, bf16 = jnp.float32, jnp.bfloat16
MESH = pl.DeviceIdType.MESH


def dg(left, right, left_dim, right_dim):
    return lax.dot_general(
        left, right, (((left_dim,), (right_dim,)), ((), ())), preferred_element_type=f32
    )


def when(condition, body):
    if condition is None:
        body()
    else:
        pl.when(condition)(body)


def both(first, second):
    if first is None:
        return second
    if second is None:
        return first
    return jnp.logical_and(first, second)


class Links:
    def __init__(self, depth):
        wide, z = lax.axis_index("wide"), lax.axis_index("narrow")
        self.depth = depth
        self.z, self.core = z, lax.rem(wide, 2)
        self.x, self.y = lax.rem(lax.div(wide, 2), 2), lax.div(wide, 4)
        self.me = self.y * 2 + self.x
        self.xs = self.y * 2 + (1 - self.x)
        self.ys = (1 - self.y) * 2 + self.x
        self.ds = (1 - self.y) * 2 + (1 - self.x)
        self.sib_dev = (self.me * 2 + (1 - self.core), z)
        self.x_dev = (self.xs * 2 + self.core, z)
        self.y_dev = (self.ys * 2 + self.core, z)
        self.up_dev = (wide, z + 1)
        self.down_dev = (wide, z - 1)
        self.has_up = z < depth - 1
        self.has_down = z > 0
        self.at_end = jnp.logical_or(z == 0, z == depth - 1)

    def barrier(self):
        semaphore = pltpu.get_barrier_semaphore()

        def greet(device):
            pl.semaphore_signal(semaphore, inc=1, device_id=device, device_id_type=MESH)

        for device in (self.sib_dev, self.x_dev, self.y_dev):
            greet(device)
        pl.when(self.has_up)(lambda: greet(self.up_dev))
        pl.when(self.has_down)(lambda: greet(self.down_dev))
        peers = 3 + self.has_up.astype(jnp.int32) + self.has_down.astype(jnp.int32)
        pl.semaphore_wait(semaphore, peers)

    def start(self, condition, source, target, send, receive, device):
        when(
            condition,
            lambda: pltpu.make_async_remote_copy(
                src_ref=source(),
                dst_ref=target(),
                send_sem=send,
                recv_sem=receive,
                device_id=device,
                device_id_type=MESH,
            ).start(),
        )

    def arrive(self, target, receive):
        pltpu.make_async_remote_copy(
            src_ref=target,
            dst_ref=target,
            send_sem=receive,
            recv_sem=receive,
            device_id=self.sib_dev,
            device_id_type=MESH,
        ).wait_recv()

    def left(self, extent, semaphore):
        pltpu.make_async_remote_copy(
            src_ref=extent,
            dst_ref=extent,
            send_sem=semaphore,
            recv_sem=semaphore,
            device_id=self.sib_dev,
            device_id_type=MESH,
        ).wait_send()

    def left_along(self, extent, semaphore):
        pl.when(self.at_end)(lambda: self.left(extent(1), semaphore))
        pl.when(jnp.logical_not(self.at_end))(lambda: self.left(extent(self.depth + 1), semaphore))


def halved(ref, piece):
    rows, lanes = ref.shape[-2:]
    if lanes == 128:
        return ref.at[pl.ds(piece * (rows // 2), rows // 2)]
    return ref.at[:, pl.ds(piece * (lanes // 2), lanes // 2)]


def near(k, distance):
    if distance == 0:
        return ((None, k.z, False),)
    return ((k.z >= distance, k.z - distance, True), (k.z + distance < k.depth, k.z + distance, False))


def gather_z_first(k, name, buf, index, low, rows, ss, rs):
    depth = k.depth

    def block(yx, zs):
        return buf.at[index(yx, zs), pl.ds(low, rows)]

    def send(condition, yx, zs, device, r, way=0, piece=None):
        ref = lambda: block(yx, zs) if piece is None else halved(block(yx, zs), piece)
        k.start(condition, ref, ref, ss.at[way], rs.at[r], device)

    def to_sib(condition, yx, zs):
        send(condition, yx, zs, k.sib_dev, 4 * depth)

    def outward(condition, zs):
        send(condition, k.me, zs, k.x_dev, depth + zs)
        send(condition, k.me, zs, k.y_dev, 2 * depth + zs)
        to_sib(condition, k.me, zs)

    def along(condition, zs, up, down):
        if up:
            send(both(condition, k.has_up), k.me, zs, k.up_dev, zs, 1)
        if down:
            send(both(condition, k.has_down), k.me, zs, k.down_dev, zs, 1)

    def take(condition, yx, zs, r):
        when(condition, lambda: k.arrive(block(yx, zs), rs.at[r]))

    def own():
        along(None, k.z, True, True)
        outward(None, k.z)
        yield

    def z_steps():
        for d in range(1, depth):
            for condition, zs, below in near(k, d):
                take(condition, k.me, zs, zs)
                along(condition, zs, below, not below)
                outward(condition, zs)
            yield

    def x_steps():
        for d in range(depth):
            for condition, zs, _ in near(k, d):
                take(condition, k.xs, zs, depth + zs)
                send(condition, k.xs, zs, k.y_dev, 3 * depth + zs, piece=0)
                to_sib(condition, k.xs, zs)
            yield

    def y_steps():
        for d in range(depth):
            for condition, zs, _ in near(k, d):
                take(condition, k.ys, zs, 2 * depth + zs)
                send(condition, k.ys, zs, k.x_dev, 3 * depth + zs, piece=1)
                to_sib(condition, k.ys, zs)
            yield

    def d_steps():
        for d in range(depth):
            for condition, zs, _ in near(k, d):
                take(condition, k.ds, zs, 3 * depth + zs)
                to_sib(condition, k.ds, zs)
            yield

    def extent(blocks):
        return buf.at[pl.ds(0, blocks), pl.ds(low, rows)]

    def sib_steps():
        k.arrive(extent(4 * depth), rs.at[4 * depth])
        yield

    def left():
        k.left(extent(7 * depth), ss.at[0])
        k.left_along(extent, ss.at[1])
        yield

    steps = {"0": own(), "z": z_steps(), "x": x_steps(), "y": y_steps(), "d": d_steps(), "s": sib_steps(), ".": left()}
    return {name + key: step for key, step in steps.items()}


def gather_pair_z_first(k, name, buf, index, low, rows, ss, rs):
    depth = k.depth

    def block(yx, zs):
        return buf.at[index(yx, zs), pl.ds(low, rows)]

    def extent(blocks):
        return buf.at[pl.ds(0, blocks), pl.ds(low, rows)]

    def send(condition, zs, device, r, way):
        ref = lambda: block(k.me, zs)
        k.start(condition, ref, ref, ss.at[way], rs.at[r], device)

    def along(condition, zs, up, down):
        if up:
            send(both(condition, k.has_up), zs, k.up_dev, zs, 1)
        if down:
            send(both(condition, k.has_down), zs, k.down_dev, zs, 1)

    def own():
        along(None, k.z, True, True)
        send(None, k.z, k.y_dev, depth + k.z, 0)
        yield

    def z_steps():
        for d in range(1, depth):
            for condition, zs, below in near(k, d):
                when(condition, lambda zs=zs: k.arrive(block(k.me, zs), rs.at[zs]))
                along(condition, zs, below, not below)
                send(condition, zs, k.y_dev, depth + zs, 0)
            yield

    def y_steps():
        for d in range(depth):
            for condition, zs, _ in near(k, d):
                when(condition, lambda zs=zs: k.arrive(block(k.ys, zs), rs.at[depth + zs]))
            yield

    def left():
        k.left(extent(depth), ss.at[0])
        k.left_along(extent, ss.at[1])
        yield

    steps = {"0": own(), "z": z_steps(), "y": y_steps(), ".": left()}
    return {name + key: step for key, step in steps.items()}


def gather_pair_z_last(k, name, buf, index, low, rows, ss, rs):
    depth = k.depth
    yx_of = (k.me, k.ys)

    def block(yx, zs):
        return buf.at[index(yx, zs), pl.ds(low, rows)]

    def extent(blocks):
        return buf.at[pl.ds(0, blocks), pl.ds(low, rows)]

    def send(condition, yx, zs, device, r, way):
        ref = lambda: block(yx, zs)
        k.start(condition, ref, ref, ss.at[way], rs.at[r], device)

    def along(condition, which, zs, up, down):
        place = 1 + which * depth + zs
        if up:
            send(both(condition, k.has_up), yx_of[which], zs, k.up_dev, place, 1 + which)
        if down:
            send(both(condition, k.has_down), yx_of[which], zs, k.down_dev, place, 1 + which)

    def own():
        send(None, k.me, k.z, k.y_dev, 0, 0)
        along(None, 0, k.z, True, True)
        yield

    def y_step():
        k.arrive(block(k.ys, k.z), rs.at[0])
        along(None, 1, k.z, True, True)
        yield

    def z_steps(which):
        for d in range(1, depth):
            for condition, zs, below in near(k, d):
                when(condition, lambda zs=zs: k.arrive(block(yx_of[which], zs), rs.at[1 + which * depth + zs]))
                along(condition, which, zs, below, not below)
            yield

    def left():
        k.left(extent(1), ss.at[0])
        for which in range(2):
            k.left_along(extent, ss.at[1 + which])
        yield

    steps = {"0": own(), "y": y_step(), "4": z_steps(0), "5": z_steps(1), ".": left()}
    return {name + key: step for key, step in steps.items()}


def add_into(ref, *others):
    total = ref[...].astype(f32)
    for other in others:
        total = total + other[...].astype(f32)
    ref[...] = total.astype(ref.dtype)


def scatter_order(depth):
    return ([0, depth - 1] + list(range(1, depth - 1)))[:depth]


def along_z(k, zd, wave, block, from_up, from_down, rs_up, rs_down, send):
    top, low = k.depth - 1 - wave, wave

    def take(slot, semaphore):
        k.arrive(slot, semaphore)
        add_into(block, slot)

    if zd < top:
        if wave:
            pl.when(k.z == top)(lambda: take(from_up, rs_up))
        send(k.z == top, False)
    if zd > low:
        if wave:
            pl.when(k.z == low)(lambda: take(from_down, rs_down))
        send(k.z == low, True)


def scatter_z_last(k, name, buf, index, low, rows, slots, ss, rs, finish):
    depth = k.depth
    from_x_diag, from_y_diag, from_xy, from_up, from_down = slots
    order = scatter_order(depth)

    def block(yx, zd):
        return buf.at[index(yx, zd), pl.ds(low, rows)]

    def half(yx, zd, piece):
        return halved(block(yx, zd), piece)

    def send(condition, source, target, device, r):
        k.start(condition, source, target, ss.at[0], rs.at[r], device)

    def x_part(zd, piece):
        return halved(from_xy.at[zd, 0], piece)

    def y_part(zd, piece):
        return halved(from_xy.at[zd, 1], piece)

    def pure_x():
        for zd in order:
            send(None, lambda zd=zd: half(k.xs, zd, 1), lambda zd=zd: x_part(zd, 1), k.x_dev, 2 * depth + zd)
            yield

    def pure_y():
        for zd in order:
            send(None, lambda zd=zd: half(k.ys, zd, 0), lambda zd=zd: y_part(zd, 0), k.y_dev, 2 * depth + zd)
            yield

    def diagonal():
        for zd in order:
            send(None, lambda zd=zd: half(k.ds, zd, 0), lambda zd=zd: from_y_diag.at[zd], k.y_dev, zd)
            send(None, lambda zd=zd: half(k.ds, zd, 1), lambda zd=zd: from_x_diag.at[zd], k.x_dev, depth + zd)
            yield

    def y_added():
        for zd in order:
            k.arrive(from_y_diag.at[zd], rs.at[zd])
            add_into(half(k.xs, zd, 0), from_y_diag.at[zd])
            send(None, lambda zd=zd: half(k.xs, zd, 0), lambda zd=zd: x_part(zd, 0), k.x_dev, 2 * depth + zd)
            yield

    def x_added():
        for zd in order:
            k.arrive(from_x_diag.at[zd], rs.at[depth + zd])
            add_into(half(k.ys, zd, 1), from_x_diag.at[zd])
            send(None, lambda zd=zd: half(k.ys, zd, 1), lambda zd=zd: y_part(zd, 1), k.y_dev, 2 * depth + zd)
            yield

    def wave(zd, number):
        def send_z(condition, up):
            place = (4 if up else 3) * depth + zd
            slot = from_down if up else from_up
            send(condition, lambda: block(k.me, zd), lambda: slot.at[zd], k.up_dev if up else k.down_dev, place)

        along_z(
            k, zd, number, block(k.me, zd), from_up.at[zd], from_down.at[zd],
            rs.at[3 * depth + zd], rs.at[4 * depth + zd], send_z,
        )

    def collect():
        for zd in order:
            k.arrive(from_xy.at[zd], rs.at[2 * depth + zd])
            add_into(block(k.me, zd), from_xy.at[zd, 0], from_xy.at[zd, 1])
            wave(zd, 0)
            yield

    def waves(number):
        for zd in order:
            if zd < depth - 1 - number or zd > number:
                wave(zd, number)
                yield

    def end():
        finish(block(k.me, k.z), False)

        def last_up():
            k.arrive(from_up.at[k.z], rs.at[3 * depth + k.z])
            finish(from_up.at[k.z], True)

        def last_down():
            k.arrive(from_down.at[k.z], rs.at[4 * depth + k.z])
            finish(from_down.at[k.z], True)

        pl.when(k.has_up)(last_up)
        pl.when(k.has_down)(last_down)
        yield

    def left():
        k.left(buf.at[pl.ds(0, 4 * depth - 1), pl.ds(low, rows)], ss.at[0])
        yield

    steps = {"X": pure_x(), "Y": pure_y(), "D": diagonal(), "a": y_added(), "b": x_added(), "c": collect(), "e": end()}
    steps |= {"v": waves(1), "w": waves(2), ".": left()}
    return {name + key: step for key, step in steps.items()}


def scatter_pair_z_last(k, name, buf, index, low, rows, slots, ss, rs, finish):
    depth = k.depth
    from_y, from_up, from_down = slots
    order = scatter_order(depth)

    def block(yx, zd):
        return buf.at[index(yx, zd), pl.ds(low, rows)]

    def send(condition, source, target, device, r):
        k.start(condition, source, target, ss.at[0], rs.at[r], device)

    def pure_y():
        for zd in order:
            send(None, lambda zd=zd: block(k.ys, zd), lambda zd=zd: from_y.at[zd], k.y_dev, zd)
            yield

    def wave(zd, number):
        def send_z(condition, up):
            slot = from_down if up else from_up
            place = (2 if up else 1) * depth + zd
            send(condition, lambda: block(k.me, zd), lambda: slot.at[zd], k.up_dev if up else k.down_dev, place)

        along_z(
            k, zd, number, block(k.me, zd), from_up.at[zd], from_down.at[zd],
            rs.at[depth + zd], rs.at[2 * depth + zd], send_z,
        )

    def collect():
        for zd in order:
            k.arrive(from_y.at[zd], rs.at[zd])
            add_into(block(k.me, zd), from_y.at[zd])
            wave(zd, 0)
            yield

    def waves(number):
        for zd in order:
            if zd < depth - 1 - number or zd > number:
                wave(zd, number)
                yield

    def end():
        finish(block(k.me, k.z), False)

        def last_up():
            k.arrive(from_up.at[k.z], rs.at[depth + k.z])
            finish(from_up.at[k.z], True)

        def last_down():
            k.arrive(from_down.at[k.z], rs.at[2 * depth + k.z])
            finish(from_down.at[k.z], True)

        pl.when(k.has_up)(last_up)
        pl.when(k.has_down)(last_down)
        yield

    def left():
        k.left(buf.at[pl.ds(0, 2 * depth - 1), pl.ds(low, rows)], ss.at[0])
        yield

    steps = {"Y": pure_y(), "c": collect(), "v": waves(1), "w": waves(2), "e": end(), ".": left()}
    return {name + key: step for key, step in steps.items()}


def scatter_pair_z_first(k, name, buf, index, low, rows, slots, ss, rs, finish):
    depth = k.depth
    from_y, from_up, from_down = slots
    yx_of = (k.me, k.ys)

    def block(yx, zd):
        return buf.at[index(yx, zd), pl.ds(low, rows)]

    def send(condition, source, target, device, r):
        k.start(condition, source, target, ss.at[0], rs.at[r], device)

    def waves(which):
        yx = yx_of[which]
        for number in range(depth - 1):
            for zd in scatter_order(depth):
                place = which * depth + zd

                def send_z(condition, up, zd=zd, place=place):
                    slot, number = (from_down, 2 * depth + place) if up else (from_up, place)
                    send(condition, lambda: block(yx, zd), lambda: slot.at[place], k.up_dev if up else k.down_dev, number)

                along_z(
                    k, zd, number, block(yx, zd), from_up.at[place], from_down.at[place],
                    rs.at[place], rs.at[2 * depth + place], send_z,
                )
            yield

    def own(which):
        yx = yx_of[which]
        place = which * depth + k.z

        def take(slot, semaphore):
            k.arrive(slot, semaphore)
            add_into(block(yx, k.z), slot)

        pl.when(k.has_up)(lambda: take(from_up.at[place], rs.at[place]))
        pl.when(k.has_down)(lambda: take(from_down.at[place], rs.at[2 * depth + place]))

    def own_me():
        own(0)
        yield

    def own_y():
        own(1)
        send(None, lambda: block(k.ys, k.z), lambda: from_y.at[0], k.y_dev, 4 * depth)
        yield

    def end():
        k.arrive(from_y.at[0], rs.at[4 * depth])
        finish(block(k.me, k.z), False)
        finish(from_y.at[0], True)
        yield

    def left():
        k.left(buf.at[pl.ds(0, 2 * depth - 1), pl.ds(low, rows)], ss.at[0])
        yield

    steps = {"0": waves(0), "1": waves(1), "O": own_me(), "Y": own_y(), "e": end(), ".": left()}
    return {name + key: step for key, step in steps.items()}


SEQ, WIDTH, UNITS = 256, 768, 96
HEADS = WIDTH // HEAD_SIZE
FIRST = 112


def row_loop(total, step, body, first=0):
    def once(i, carry):
        body(pl.multiple_of(first + i * step, step), step)
        return carry

    lax.fori_loop(0, total // step, once, 0)


def lane_shift(values, offset, left):
    extent = values.shape[1]
    lane = lax.broadcasted_iota(jnp.int32, values.shape, 1)
    if left:
        return jnp.where(lane < extent - offset, pltpu.roll(values, extent - offset, 1), 0.0)
    return jnp.where(lane >= offset, pltpu.roll(values, offset, 1), 0.0)


def six_heads(first, body):
    for h in range(first, first + 6):
        body(h)


def three_heads(first, body):
    for h in range(first, first + 3):
        body(h)


def head_rows(h):
    return pl.ds(pl.multiple_of(h * HEAD_SIZE, HEAD_SIZE), HEAD_SIZE)


def scratch_of(depth):
    devices, blocks, half = 8 * depth, 4 * depth, 2 * depth
    table = {
        "qk": ((devices, UNITS, WIDTH), bf16),
        "ff": ((half, 2 * UNITS, WIDTH), bf16),
        "sm": ((devices, 16, 128), f32),
        "gff": ((half, 2 * UNITS, WIDTH), bf16),
        "gs": ((devices, 16, 128), f32),
        "sr": ((blocks, UNITS, WIDTH), bf16),
        "srs": ((blocks, 16, 128), f32),
        "wq": ((WIDTH, WIDTH), bf16),
        "wk": ((WIDTH, WIDTH), bf16),
        "wv": ((WIDTH, WIDTH), bf16),
        "wo": ((WIDTH, WIDTH), bf16),
        "s1": ((SEQ, WIDTH), f32),
        "i1": ((SEQ, 128), f32),
        "nm": ((SEQ, WIDTH), bf16),
        "hid": ((SEQ, WIDTH), f32),
        "s2": ((SEQ, WIDTH), f32),
        "i2": ((SEQ, 128), f32),
        "n2": ((4 * SEQ, WIDTH), bf16),
        "ct": ((4 * SEQ, WIDTH), bf16),
        "outp": ((4 * SEQ, WIDTH), f32),
        "dn2": ((4 * SEQ, WIDTH), f32),
        "outs": ((SEQ, WIDTH), f32),
        "dn2s": ((SEQ, WIDTH), f32),
        "outb": ((SEQ, WIDTH), f32),
        "dn2b": ((SEQ, WIDTH), f32),
        "outx": ((2, SEQ, WIDTH), bf16),
        "dn2x": ((2, SEQ, WIDTH), bf16),
        "act": ((2, 4 * SEQ, UNITS * depth), bf16),
        "dp": ((2, 4 * SEQ, UNITS * depth), bf16),
        "da": ((SEQ, WIDTH), bf16),
        "dk": ((WIDTH, SEQ), f32),
        "dn": ((SEQ, WIDTH), f32),
        "nmt": ((WIDTH, SEQ), bf16),
        "qt": ((WIDTH, SEQ), bf16),
        "kt": ((WIDTH, SEQ), bf16),
        "vt": ((WIDTH, SEQ), bf16),
        "wt": ((HEADS, SEQ, SEQ), bf16),
        "krt": ((WIDTH, SEQ), f32),
        "mt": ((WIDTH, SEQ), bf16),
        "dmt": ((WIDTH, SEQ), bf16),
        "dqt": ((WIDTH, SEQ), bf16),
        "dkt": ((WIDTH, SEQ), bf16),
        "dvt": ((WIDTH, SEQ), bf16),
        "kft": ((WIDTH, SEQ), bf16),
        "vft": ((WIDTH, SEQ), bf16),
        "ex": ((WIDTH, SEQ), f32),
        "tt": ((HEADS, SEQ, SEQ), f32),
        "vec": ((16, WIDTH), f32),
        "vecc": ((WIDTH, 128), f32),
        "colsum": ((WIDTH, 128), f32),
        "gvec": ((16, WIDTH), f32),
        "bias": ((2, 8, UNITS * depth), f32),
        "gbias": ((half, 8, 128), f32),
    }
    for name, rows, lanes, kind in (("q", 48, WIDTH, bf16), ("v", 48, WIDTH, bf16), ("t", 16, 128, f32)):
        part = (rows, lanes // 2) if lanes == WIDTH else (rows // 2, lanes)
        table["r" + name + "dx"] = table["r" + name + "dy"] = ((depth,) + part, kind)
        table["r" + name + "xy"] = ((depth, 2, rows, lanes), kind)
        table["r" + name + "u"] = table["r" + name + "d"] = ((depth, rows, lanes), kind)
    table["rby"] = table["rbu"] = table["rbd"] = ((depth, FIRST, WIDTH), bf16)
    table["rcy"] = ((1, 2 * UNITS - FIRST, WIDTH), bf16)
    table["rcu"] = table["rcd"] = ((half, 2 * UNITS - FIRST, WIDTH), bf16)
    for name, sent, came in (
        ("gq", 2, 4 * depth + 1), ("gv", 2, 4 * depth + 1), ("gb", 2, 2 * depth), ("gt", 2, 4 * depth + 1), ("gc", 3, 2 * depth + 1),
        ("sq", 1, 5 * depth), ("sv", 1, 5 * depth), ("sb", 1, 3 * depth), ("st", 1, 5 * depth), ("sc", 1, 4 * depth + 1), ("e", 3, 25),
    ):
        table[name + "_s"], table[name + "_r"] = sent, came
    return table


PLAN = (
    "own_blocks", "barrier", "S0", "Q0", "V0", "Sz", "Qy", "L0", "Sz", "Qx", "Sx", "Sy", "Qz", "Sy", "Vz",
    "Qz", "Sx", "Vy", "Sz", "Qx", "Qz", "Sx", "Ly", "Vz", "Qy", "Sy", "L4", "Qx", "Sx", "Vx", "Qy", "Qx",
    "Sy", "Sd", "Qd", "Qy", "Vz", "Vy", "Vx", "Vx", "F0", "Sd", "Qd", "Sd", "norm1", "Sd", "Ss", "vectors",
    "Qd", "gain1", "Vy", "Qd", "L4", "Vy", "Vd", "own_cotangent", "Qs", "Vx", "unpack0", "project_qk", "Fz",
    "mixer_kernels", "Vd", "score0", "Vd", "score1", "score2", "Vd", "Fy", "score3", "Fz", "Vs", "unpack1",
    "project_v", "L5", "mix0", "mix1", "hidden", "norm2", "L4", "Fz", "feed0o", "sibling_rows", "feed0s",
    "pass_ct", "L5", "flip", "Fy", "pass_n2_0", "Q.", "feed0x0", "diagonal_rows0", "Fy", "feed0d0", "L5",
    "Fy", "feed1d0", "to_diagonal0", "feed1o", "V.", "feed1x0", "pass_n2_1", "feed1s", "to_x0", "feed0x1",
    "diagonal_rows1", "feed0d1", "feed1d1", "to_diagonal1", "feed1x1", "feed_grads1", "fY", "l1",
    "out_to_diagonal", "to_x1", "to_sibling", "feed_grads0", "out_to_x", "fY", "back2_0", "fc", "fY", "l0",
    "back2_1", "grad_mixed", "back_v0", "back_v1", "pack_vo0", "back4", "sum_vo0", "pack_vo1", "sum_vo1",
    "vD", "fY", "back5", "sum_vo2", "back6", "l1", "back7", "va", "fc", "vX", "vD", "pack_qk0", "vD",
    "grad_normed", "sum_qk0", "qD", "fv", "back1", "l1", "qD", "l0", "sum_qk1", "fc", "vX", "pack_qk1", "vX",
    "qY", "vY", "kernel3", "sum_qk2", "sum_vo3", "qb", "vY", "qX", "qD", "qa", "vb", "qb", "qa", "va", "fc",
    "vb", "kernel0", "sum_qk3", "fv", "vX", "qY", "va", "kernel1", "vD", "fw", "l0", "vb", "qX", "vY", "fv",
    "kernel2", "qc", "vector_tiles", "vc", "fv", "vc", "qa", "small_sums", "sD", "fw", "sX", "sD", "qb",
    "qX", "sY", "qv", "sD", "sY", "qc", "sX", "qD", "sb", "sa", "vc", "vv", "sa", "sb", "qY", "vb", "vY",
    "vv", "va", "sc", "qb", "qa", "sc", "qY", "qv", "qc", "sv", "sD", "qX", "sY", "qw", "vv", "vw", "vw",
    "sv", "qv", "sX", "vc", "sY", "sw", "fe", "sb", "sb", "lY", "sa", "qw", "sX", "qc", "finish_out", "lO",
    "sa", "vv", "sw", "qv", "sc", "sv", "sc", "ve", "le", "sv", "qe", "se", "store",
)
INPUTS = ("tok", "length", "cot", "iq", "ik", "iv", "io", "ifc1", "ifc2", "ibias", "ivec")
RESULTS = ("out", "dinp", "gwq", "gwk", "gwv", "gwo", "gfc1", "gfc2", "gsmall")
OUTPUTS = RESULTS


def layer_kernel(depth, *refs):
    names = INPUTS + OUTPUTS + tuple(scratch_of(depth))
    m = SimpleNamespace(**dict(zip(names, refs, strict=True)))
    k = Links(depth)
    core = k.core

    def in_all(yx, zs):
        return (yx * 2 + core) * depth + zs

    def in_all_sib(yx, zs):
        return (yx * 2 + (1 - core)) * depth + zs

    def in_pair(yx, zs):
        return lax.div(yx, 2) * depth + zs

    places = {"o": k.x * 2 + core, "s": k.x * 2 + 1 - core, "x": (1 - k.x) * 2 + core, "d": (1 - k.x) * 2 + 1 - core}

    def rows_at(who, start=0, step=SEQ):
        return pl.ds(pl.multiple_of(places[who] * SEQ + start, step), step)

    def sent_by(place):
        return 2 if place == 24 else 1 if place in (9, 10, 11, 12) or place >= 16 else 0

    def swap(place, source, target, device=None):
        k.start(None, lambda: source, lambda: target, m.e_s.at[sent_by(place)], m.e_r.at[place], device or k.sib_dev)

    day = lax.broadcasted_iota(jnp.int32, (1, SEQ), 1).astype(f32)
    s_at = lax.broadcasted_iota(jnp.int32, (SEQ, SEQ), 0)
    t_at = lax.broadcasted_iota(jnp.int32, (SEQ, SEQ), 1)
    valid = (lax.broadcasted_iota(jnp.int32, (1, SEQ), 1) < m.length[0]).astype(f32)

    def own_blocks():
        here = in_all(k.me, k.z)
        for place, (first, second) in enumerate(((m.iq, m.ik), (m.iv, m.io))):
            pair = jnp.concatenate([first[...].astype(f32), second[...].astype(f32)], axis=0)
            m.qk[here, 48 * place : 48 * place + 48] = pair.astype(bf16)
        m.sm[here] = jnp.zeros((16, 128), f32)
        m.sm[here, 0:15, 0:24] = m.ivec[...].astype(f32)
        m.sm[here, 15:16, 0:UNITS] = m.ibias[...].astype(f32)
        m.ff[in_pair(k.me, k.z), 0:UNITS] = m.ifc1[...]
        m.ff[in_pair(k.me, k.z), UNITS : 2 * UNITS] = m.ifc2[...]

    def half_at(who, half):
        return rows_at(who, half * (SEQ // 2), SEQ // 2)

    def own_cotangent():
        m.ct[rows_at("o")] = m.cot[...]
        ref = m.ct.at[rows_at("o")]
        swap(0, ref, ref)
        swap(1, ref, ref, k.x_dev)

    def pass_ct():
        ref = m.ct.at[rows_at("x")]
        k.arrive(ref, m.e_r.at[1])
        swap(2, ref, ref)

    def norm1():
        def rows_of(start, step):
            rows = pl.ds(start, step)
            tokens = m.tok[rows].astype(f32)
            centred = tokens - jnp.mean(tokens, axis=1, keepdims=True)
            inverse = lax.rsqrt(jnp.mean(centred * centred, axis=1, keepdims=True) + EPSILON)
            m.s1[rows] = centred * inverse
            m.i1[rows] = jnp.broadcast_to(inverse, (step, 128))

        row_loop(SEQ, 32, rows_of)

    def vectors():
        total = jnp.zeros((16, WIDTH), f32)
        for wide in range(8):
            part = jnp.zeros((16, 128), f32)
            for zs in range(depth):
                tile = m.sm[wide * depth + zs]
                part = part + (pltpu.roll(tile, 24 * zs, 1) if zs else tile)
            padded = jnp.concatenate([part, jnp.zeros((16, WIDTH - 128), f32)], axis=1)
            total = total + (pltpu.roll(padded, 96 * wide, 1) if wide else padded)
        m.vec[...] = total
        m.vecc[...] = jnp.transpose(jnp.concatenate([total, jnp.zeros((112, WIDTH), f32)], axis=0))
        for y in range(2):
            line = jnp.zeros((16, UNITS * depth), f32)
            for zs in range(depth):
                tile = m.sm[in_all(y * 2 + k.x, zs)]
                tile = jnp.concatenate([tile, jnp.zeros((16, UNITS * depth - 128), f32)], axis=1)
                line = line + (pltpu.roll(tile, UNITS * zs, 1) if zs else tile)
            m.bias[y] = line[8:16]

    def head_kernel(h, carry):
        rows = head_rows(h)
        decays = jnp.exp(-m.vecc[rows, 10:11] * day)
        m.ex[rows] = decays
        line = jnp.sum(m.vecc[rows, 9:10] * decays, axis=0, keepdims=True) * (1.0 / STATE)
        matrix = pltpu.roll(jnp.broadcast_to(line, (SEQ, SEQ)), 0, 1, stride=1, stride_axis=0)
        m.tt[h] = jnp.where(t_at >= s_at, matrix, 0.0)
        return carry

    def mixer_kernels():
        lax.fori_loop(0, HEADS, head_kernel, 0)

    def gain1():
        def rows_of(start, step):
            rows = pl.ds(start, step)
            m.nm[rows] = (m.s1[rows] * m.vec[0:1] + m.vec[1:2]).astype(bf16)

        row_loop(SEQ, 32, rows_of)
        m.nmt[...] = jnp.transpose(m.nm[...])

    def unpack(place):
        first, second = ((m.wq, m.wk), (m.wv, m.wo))[place]

        def rows_of(w, carry):
            rows = pl.ds(pl.multiple_of(w * 96, 96), 96)
            pair = m.qk[pl.ds(w * depth, depth), 48 * place : 48 * place + 48, :].astype(f32)
            first[rows] = pair[:, :24].reshape(96, WIDTH).astype(bf16)
            second[rows] = pair[:, 24:].reshape(96, WIDTH).astype(bf16)
            return carry

        lax.fori_loop(0, 8, rows_of, 0)

    def project_qk():
        m.qt[...] = jnp.transpose(dg(m.nm[...], m.wq[...], 1, 0) + m.vec[2:3]).astype(bf16)
        m.krt[...] = jnp.transpose(dg(m.nm[...], m.wk[...], 1, 0) + m.vec[3:4])

    def project_v():
        m.vt[...] = (jnp.transpose(dg(m.nm[...], m.wv[...], 1, 0) + m.vec[4:5]) * valid).astype(bf16)

    def score_head(h):
        rows = head_rows(h)
        raw = m.krt[rows]
        summed = raw * m.vecc[rows, 5:6]
        for j in range(1, 4):
            summed = summed + lane_shift(raw, j, False) * m.vecc[rows, 5 + j : 6 + j]
        keys = (summed * valid).astype(bf16)
        m.kt[rows] = keys
        scores = dg(keys, m.qt[rows], 0, 0) * (1.0 / HEAD_SIZE)
        m.wt[h] = (scores * m.tt[h]).astype(bf16)

    def mix_head(h):
        rows = head_rows(h)
        m.mt[rows] = (dg(m.vt[rows], m.wt[h], 1, 0) * valid).astype(bf16)

    def hidden():
        m.hid[...] = dg(m.mt[...], m.wo[...], 0, 0)

    def norm2():
        def rows_of(start, step):
            rows = pl.ds(start, step)
            hidden = m.tok[rows].astype(f32) + m.hid[rows] + m.vec[11:12]
            m.hid[rows] = hidden
            centred = hidden - jnp.mean(hidden, axis=1, keepdims=True)
            inverse = lax.rsqrt(jnp.mean(centred * centred, axis=1, keepdims=True) + EPSILON)
            scaled = centred * inverse
            m.s2[rows] = scaled
            m.i2[rows] = jnp.broadcast_to(inverse, (step, 128))
            m.n2[rows_at("o", start, step)] = (scaled * m.vec[12:13] + m.vec[13:14]).astype(bf16)

        row_loop(SEQ, 32, rows_of)
        ref = m.n2.at[rows_at("o")]
        swap(3, ref, ref)
        for half in range(2):
            ref = m.n2.at[half_at("o", half)]
            swap(4 + half, ref, ref, k.x_dev)

    def pass_n2(half):
        ref = m.n2.at[half_at("x", half)]
        k.arrive(ref, m.e_r.at[4 + half])
        swap(6 + half, ref, ref)

    def sibling_rows():
        k.arrive(m.ct.at[rows_at("s")], m.e_r.at[0])
        k.arrive(m.n2.at[rows_at("s")], m.e_r.at[3])

    def diagonal_rows(half):
        if half == 0:
            k.arrive(m.ct.at[rows_at("d")], m.e_r.at[2])
        k.arrive(m.n2.at[half_at("d", half)], m.e_r.at[6 + half])

    def finish_rows(pieces):
        def finish(ref, more):
            value = ref[...].astype(f32)
            for target, (low, high), (first, last) in pieces:
                part = value[first:last]
                target[low:high] = target[low:high] + part if more else part

        return finish

    finish_feed = finish_rows(((m.gfc1, (0, UNITS), (0, UNITS)), (m.gfc2, (0, FIRST - UNITS), (UNITS, FIRST))))
    finish_last = finish_rows(((m.gfc2, (FIRST - UNITS, UNITS), (0, 2 * UNITS - FIRST)),))
    finish_qk = finish_rows(((m.gwq, (0, 24), (0, 24)), (m.gwk, (0, 24), (24, 48))))
    finish_vo = finish_rows(((m.gwv, (0, 24), (0, 24)), (m.gwo, (0, 24), (24, 48))))

    def finish_small(ref, more):
        m.gsmall[...] = m.gsmall[...] + ref[...] if more else ref[...]

    steps = {}
    steps |= gather_z_first(k, "S", m.sm, in_all, 0, 16, m.gt_s, m.gt_r)
    steps |= gather_z_first(k, "Q", m.qk, in_all, 0, 48, m.gq_s, m.gq_r)
    steps |= gather_z_first(k, "V", m.qk, in_all, 48, 48, m.gv_s, m.gv_r)
    steps |= gather_pair_z_first(k, "F", m.ff, in_pair, 0, FIRST, m.gb_s, m.gb_r)
    steps |= gather_pair_z_last(k, "L", m.ff, in_pair, FIRST, 2 * UNITS - FIRST, m.gc_s, m.gc_r)
    slots = (m.rby, m.rbu, m.rbd)
    steps |= scatter_pair_z_last(k, "f", m.gff, in_pair, 0, FIRST, slots, m.sb_s, m.sb_r, finish_feed)
    slots = (m.rcy, m.rcu, m.rcd)
    steps |= scatter_pair_z_first(k, "l", m.gff, in_pair, FIRST, 2 * UNITS - FIRST, slots, m.sc_s, m.sc_r, finish_last)
    slots = (m.rqdx, m.rqdy, m.rqxy, m.rqu, m.rqd)
    steps |= scatter_z_last(k, "q", m.qk, in_all, 0, 48, slots, m.sq_s, m.sq_r, finish_qk)
    slots = (m.rvdx, m.rvdy, m.rvxy, m.rvu, m.rvd)
    steps |= scatter_z_last(k, "v", m.qk, in_all, 48, 48, slots, m.sv_s, m.sv_r, finish_vo)
    slots = (m.rtdx, m.rtdy, m.rtxy, m.rtu, m.rtd)
    steps |= scatter_z_last(k, "s", m.gs, in_all, 0, 16, slots, m.st_s, m.st_r, finish_small)

    root = math.sqrt(2.0 / math.pi)
    chunk = UNITS * depth
    ys = (k.y, 1 - k.y)

    def feed(which, who, half=None):
        blocks = pl.ds(ys[which] * depth, depth)
        rows = rows_at(who) if half is None else half_at(who, half)
        fc1 = m.ff[blocks, 0:UNITS, :].reshape(chunk, WIDTH)
        fc2 = m.ff[blocks, UNITS : 2 * UNITS, :].reshape(chunk, WIDTH)
        pre = dg(m.n2[rows], fc1, 1, 1) + m.bias[ys[which], 7:8]
        square = pre * pre
        tanh = jnp.tanh(root * pre * (1.0 + 0.044715 * square))
        half = 0.5 * (1.0 + tanh)
        slope = half + 0.5 * pre * (1.0 - tanh * tanh) * (root * (1.0 + 3 * 0.044715 * square))
        activated = (pre * half).astype(bf16)
        grad_pre = (dg(m.ct[rows], fc2, 1, 1) * slope).astype(bf16)
        m.act[which, rows] = activated
        m.dp[which, rows] = grad_pre
        if which == 0:
            m.outp[rows] = dg(activated, fc2, 1, 0)
            m.dn2[rows] = dg(grad_pre, fc1, 1, 0)
        else:
            m.outp[rows] += dg(activated, fc2, 1, 0)
            m.dn2[rows] += dg(grad_pre, fc1, 1, 0)

    def to_sibling():
        swap(8, m.dn2.at[rows_at("s")], m.dn2s)
        swap(9, m.outp.at[rows_at("s")], m.outs)

    def half_rows(half):
        return pl.ds(half * (SEQ // 2), SEQ // 2)

    def to_diagonal(half):
        swap(10 + half, m.dn2.at[half_at("d", half)], m.dn2b.at[half_rows(half)])

    def to_x(half):
        rows = half_rows(half)
        k.arrive(m.dn2b.at[rows], m.e_r.at[10 + half])
        m.dn2x[0, rows] = (m.dn2[half_at("x", half)] + m.dn2b[rows]).astype(bf16)
        swap(13 + half, m.dn2x.at[0, rows], m.dn2x.at[1, rows], k.x_dev)

    def out_to_diagonal():
        swap(12, m.outp.at[rows_at("d")], m.outb)

    def out_to_x():
        k.arrive(m.outb, m.e_r.at[12])
        m.outx[0] = (m.outp[rows_at("x")] + m.outb[...]).astype(bf16)
        swap(15, m.outx.at[0], m.outx.at[1], k.x_dev)

    def feed_grads(which):
        blocks = pl.ds(ys[which] * depth, depth)
        pre = m.dp[which]
        m.gff[blocks, 0:UNITS] = dg(pre, m.n2[...], 0, 0).astype(bf16).reshape(depth, UNITS, WIDTH)
        m.gff[blocks, UNITS : 2 * UNITS] = (
            dg(m.act[which], m.ct[...], 0, 0).astype(bf16).reshape(depth, UNITS, WIDTH)
        )
        sums = jnp.sum(pre.astype(f32), axis=0, keepdims=True)
        lane = lax.broadcasted_iota(jnp.int32, (1, 128), 1)
        for zs in range(depth):
            line = (pltpu.roll(sums, chunk - UNITS * zs, 1) if zs else sums)[:, :128]
            m.gbias[ys[which] * depth + zs] = jnp.broadcast_to(jnp.where(lane < UNITS, line, 0.0), (8, 128))

    def back2(half):
        if half == 0:
            m.gvec[...] = jnp.zeros((16, WIDTH), f32)
            k.arrive(m.dn2s, m.e_r.at[8])
        k.arrive(m.dn2x.at[1, half_rows(half)], m.e_r.at[13 + half])

        def rows_of(start, step):
            rows = pl.ds(start, step)
            grad_normed = m.dn2[rows_at("o", start, step)] + m.dn2s[rows] + m.dn2x[1, rows].astype(f32)
            scaled = m.s2[rows]
            grad_in = grad_normed * m.vec[12:13]
            first = jnp.mean(grad_in, axis=1, keepdims=True)
            second = jnp.mean(grad_in * scaled, axis=1, keepdims=True)
            top = m.cot[rows].astype(f32)
            grad_hidden = top + m.i2[rows, 0:1] * (grad_in - first - scaled * second)
            m.s2[rows] = grad_hidden
            rounded = grad_hidden.astype(bf16)
            m.da[rows] = rounded
            m.gvec[11:12] += jnp.sum(rounded.astype(f32), axis=0, keepdims=True)
            m.gvec[12:13] += jnp.sum(grad_normed * scaled, axis=0, keepdims=True)
            m.gvec[13:14] += jnp.sum(grad_normed, axis=0, keepdims=True)
            m.gvec[14:15] += jnp.sum(top, axis=0, keepdims=True)

        row_loop(SEQ // 2, 32, rows_of, half * (SEQ // 2))

    def grad_mixed():
        m.dmt[...] = (jnp.transpose(dg(m.da[...], m.wo[...], 1, 1)) * valid).astype(bf16)

    def back_v_head(h):
        rows = head_rows(h)
        m.dvt[rows] = (dg(m.dmt[rows], m.wt[h], 1, 1) * valid).astype(bf16)

    def back_head(h):
        rows = head_rows(h)
        grad_scores = (dg(m.vt[rows], m.dmt[rows], 0, 0) * m.tt[h]).astype(bf16)
        m.dqt[rows] = (dg(m.kt[rows], grad_scores, 1, 0) * (1.0 / HEAD_SIZE)).astype(bf16)
        grad_keys = dg(m.qt[rows], grad_scores, 1, 1) * (1.0 / HEAD_SIZE) * valid
        m.dk[rows] = grad_keys
        grad_raw = grad_keys * m.vecc[rows, 5:6]
        for j in range(1, 4):
            grad_raw = grad_raw + lane_shift(grad_keys, j, True) * m.vecc[rows, 5 + j : 6 + j]
        m.dkt[rows] = grad_raw.astype(bf16)

    def pack(pair, which):
        y = ys[1 - which]
        rows = pl.ds(pl.multiple_of(y * 384, 384), 384)
        if pair == 0:
            grads = (dg(m.nmt[rows], m.dqt[...], 1, 1), dg(m.nmt[rows], m.dkt[...], 1, 1))
        else:
            grads = (dg(m.nmt[rows], m.dvt[...], 1, 1), dg(m.mt[rows], m.da[...], 1, 0))
        both_grads = jnp.concatenate([grad.reshape(4 * depth, 24, WIDTH) for grad in grads], axis=1)
        low = pl.ds(48 * pair, 48)
        m.qk[pl.ds(y * 4 * depth, 4 * depth), low, :] = both_grads.astype(bf16)
        for place in (2 * which, 2 * which + 1):
            yx = (k.ds, k.ys, k.xs, k.me)[place]
            source, target = pl.ds(in_all_sib(yx, 0), depth), pl.ds(yx * depth, depth)
            swap(16 + 4 * pair + place, m.qk.at[source, low], m.sr.at[target, low])

    def grad_normed():
        m.dn[...] = jnp.transpose(
            dg(m.wq[...], m.dqt[...], 1, 0) + dg(m.wk[...], m.dkt[...], 1, 0) + dg(m.wv[...], m.dvt[...], 1, 0)
        )

    def back1():
        def rows_of(start, step):
            rows = pl.ds(start, step)
            grad_out, scaled = m.dn[rows], m.s1[rows]
            grad_in = grad_out * m.vec[0:1]
            first = jnp.mean(grad_in, axis=1, keepdims=True)
            second = jnp.mean(grad_in * scaled, axis=1, keepdims=True)
            m.dinp[rows] = (m.s2[rows] + m.i1[rows, 0:1] * (grad_in - first - scaled * second)).astype(bf16)
            m.gvec[0:1] += jnp.sum(grad_out * scaled, axis=0, keepdims=True)
            m.gvec[1:2] += jnp.sum(grad_out, axis=0, keepdims=True)

        row_loop(SEQ, 32, rows_of)

    def core_sum(pair, place):
        yx, low = (k.ds, k.ys, k.xs, k.me)[place], pl.ds(48 * pair, 48)
        k.arrive(m.sr.at[pl.ds(yx * depth, depth), low], m.e_r.at[16 + 4 * pair + place])
        for zs in range(depth):
            add_into(m.qk.at[in_all(yx, zs), low], m.sr.at[yx * depth + zs, low])

    def flip():
        turn = (s_at + t_at == SEQ - 1).astype(bf16)
        m.kft[...] = dg(m.kt[...], turn, 1, 0).astype(bf16)
        m.vft[...] = dg(m.vt[...], turn, 1, 0).astype(bf16)

    def kernel_head(h):
        rows = head_rows(h)
        scores = dg(m.kft[rows], m.qt[rows], 0, 0) * (1.0 / HEAD_SIZE)
        grad_weights = dg(m.vft[rows], m.dmt[rows], 0, 0)
        product = jnp.where(s_at + t_at >= SEQ - 1, scores * grad_weights, 0.0)
        lined = pltpu.roll(product, 1, 1, stride=1, stride_axis=0)
        grad_kernel = jnp.sum(lined, axis=0, keepdims=True) * (1.0 / STATE)
        part = m.ex[rows] * grad_kernel
        at = lax.broadcasted_iota(jnp.int32, (HEAD_SIZE, 128), 1)
        grad_rate = -m.vecc[rows, 9:10] * jnp.sum(part * day, axis=1, keepdims=True)
        sums = jnp.where(at == 9, jnp.sum(part, axis=1, keepdims=True), 0.0)
        sums = jnp.where(at == 10, grad_rate, sums)
        raw, grad_keys = m.krt[rows], m.dk[rows]
        for j in range(4):
            tap = jnp.sum(grad_keys * (lane_shift(raw, j, False) if j else raw), axis=1, keepdims=True)
            sums = jnp.where(at == 5 + j, tap, sums)
        for place, value in ((2, m.dqt), (3, m.dkt), (4, m.dvt)):
            sums = jnp.where(at == place, jnp.sum(value[rows].astype(f32), axis=1, keepdims=True), sums)
        m.colsum[rows] = sums

    def vector_tiles():
        grads = m.gvec[...] + jnp.transpose(m.colsum[...])[0:16]
        row_at = lax.broadcasted_iota(jnp.int32, (16, 128), 0)
        lane_at = lax.broadcasted_iota(jnp.int32, (16, 128), 1)
        for wide in range(8):
            turned = (pltpu.roll(grads, WIDTH - 96 * wide, 1) if wide else grads)[:, :128]
            for zs in range(depth):
                tile = pltpu.roll(turned, 128 - 24 * zs, 1) if zs else turned
                tile = jnp.where((lane_at < 24) & (row_at < 15), tile, 0.0)
                own = jnp.concatenate([jnp.zeros((8, 128), f32), m.gbias[(wide // 4) * depth + zs]], axis=0)
                mine = (row_at == 15) & (core == wide % 2) & (k.x == wide // 2 % 2)
                m.gs[wide * depth + zs] = jnp.where(mine, own, tile)
        for yx in range(4):
            swap(24, m.gs.at[pl.ds(in_all_sib(yx, 0), depth)], m.srs.at[pl.ds(yx * depth, depth)])

    def small_sums():
        k.arrive(m.srs, m.e_r.at[24])
        for yx in range(4):
            for zs in range(depth):
                add_into(m.gs.at[in_all(yx, zs)], m.srs.at[yx * depth + zs])

    def finish_out():
        def rows_of(start, step):
            rows = pl.ds(start, step)
            others = m.outs[rows] + m.outx[1, rows].astype(f32)
            m.out[rows] = (m.hid[rows] + (m.outp[rows_at("o", start, step)] + others) + m.vec[14:15]).astype(bf16)

        k.arrive(m.outs, m.e_r.at[9])
        k.arrive(m.outx.at[1], m.e_r.at[15])
        row_loop(SEQ, 32, rows_of)

    def all_sent():
        for group in "SFLflqvs":
            next(steps[group + "."])
        extents = (m.qk.at[:, pl.ds(0, 80)], m.qk, m.srs)
        for place, extent in enumerate(extents):
            k.left(extent, m.e_s.at[place])

    compute = {
        "own_blocks": own_blocks, "barrier": k.barrier, "own_cotangent": own_cotangent, "norm1": norm1, "pass_ct": pass_ct,
        "vectors": vectors, "mixer_kernels": mixer_kernels, "gain1": gain1, "project_qk": project_qk, "project_v": project_v,
        "hidden": hidden, "norm2": norm2, "sibling_rows": sibling_rows, "to_sibling": to_sibling,
        "out_to_diagonal": out_to_diagonal, "out_to_x": out_to_x, "grad_mixed": grad_mixed, "grad_normed": grad_normed,
        "back1": back1, "flip": flip, "vector_tiles": vector_tiles, "small_sums": small_sums, "finish_out": finish_out,
        "store": all_sent,
    }
    for which in range(2):
        compute["unpack%d" % which] = partial(unpack, which)
        compute["mix%d" % which] = partial(six_heads, 6 * which, mix_head)
        compute["back_v%d" % which] = partial(six_heads, 6 * which, back_v_head)
        for who in "os":
            compute["feed%d%s" % (which, who)] = partial(feed, which, who)
        for who in "xd":
            for half in range(2):
                compute["feed%d%s%d" % (which, who, half)] = partial(feed, which, who, half)
        compute["feed_grads%d" % which] = partial(feed_grads, which)
        compute["pass_n2_%d" % which] = partial(pass_n2, which)
        compute["diagonal_rows%d" % which] = partial(diagonal_rows, which)
        compute["to_diagonal%d" % which] = partial(to_diagonal, which)
        compute["to_x%d" % which] = partial(to_x, which)
        compute["back2_%d" % which] = partial(back2, which)
        compute["pack_qk%d" % which] = partial(pack, 0, which)
        compute["pack_vo%d" % which] = partial(pack, 1, which)
    for which in range(4):
        compute["score%d" % which] = partial(three_heads, 3 * which, score_head)
        compute["back%d" % (4 + which)] = partial(three_heads, 3 * which, back_head)
        compute["kernel%d" % which] = partial(three_heads, 3 * which, kernel_head)
        compute["sum_qk%d" % which] = partial(core_sum, 0, which)
        compute["sum_vo%d" % which] = partial(core_sum, 1, which)
    for step in PLAN:
        if step in compute:
            compute[step]()
        else:
            next(steps[step])


def results_kernel(*refs):
    sources, tile, targets, bias, vectors = refs[:8], refs[8], refs[9:17], refs[17], refs[18]
    for source, target in zip(sources, targets, strict=True):
        target[...] = source[...]
    bias[...] = tile[15:16, :UNITS]
    vectors[...] = tile[0:15, 0:24]


def on_device_fast(
    tokens, lengths, cotangent, w_query, w_key, w_value, w_out, w_fc1, w_fc2, fc1_bias, vectors
):
    depth = lax.axis_size("narrow")
    scratch = []
    for entry in scratch_of(depth).values():
        scratch.append(pltpu.SemaphoreType.DMA((entry,)) if isinstance(entry, int) else pltpu.VMEM(*entry))
    in_vmem = pl.BlockSpec(memory_space=pltpu.VMEM)
    in_smem = pl.BlockSpec(memory_space=pltpu.SMEM)
    shape = jax.ShapeDtypeStruct
    got = pl.pallas_call(
        partial(layer_kernel, depth),
        out_shape=[pltpu.VMEM((SEQ, WIDTH), bf16)] * 2
        + [pltpu.VMEM((24, WIDTH), f32)] * 4
        + [pltpu.VMEM((UNITS, WIDTH), f32)] * 2
        + [pltpu.VMEM((16, 128), f32)],
        in_specs=[in_vmem, in_smem] + [in_vmem] * 9,
        out_specs=[in_vmem] * 9,
        scratch_shapes=scratch,
        compiler_params=pltpu.CompilerParams(
            collective_id=0, has_side_effects=True, vmem_limit_bytes=61 * 2**20
        ),
        name="h3_layer",
    )(
        tokens, lengths, cotangent, w_query, w_key, w_value, w_out, w_fc1.T, w_fc2, fc1_bias[None], vectors
    )
    results = pl.pallas_call(
        results_kernel,
        out_shape=[shape(x.shape, x.dtype) for x in got[:8]] + [shape((1, UNITS), f32), shape((15, 24), f32)],
        in_specs=[in_vmem] * 9,
        out_specs=[in_vmem] * 10,
        name="results",
    )(*[pltpu.with_memory_space_constraint(x, pltpu.VMEM) for x in got])
    out, grad_in, g_query, g_key, g_value, g_out, g_fc1, g_fc2, g_bias, g_vectors = results
    return out, grad_in, g_query, g_key, g_value, g_out, g_fc1.T, g_fc2, g_bias.reshape(-1), g_vectors


def fits(mesh):
    return mesh.shape["wide"] == 8 and mesh.shape["narrow"] == 4


def solution(mesh):
    placed = (
        P(("wide", "narrow"), None),
        P(("wide", "narrow")),
        P(("wide", "narrow"), None),
        P(("wide", "narrow"), None),
        P(("wide", "narrow"), None),
        P(("wide", "narrow"), None),
        P(("wide", "narrow"), None),
        P(None, ("wide", "narrow")),
        P(("wide", "narrow"), None),
        P(("wide", "narrow")),
        P(None, ("wide", "narrow")),
    )
    return jax.shard_map(
        on_device_fast if fits(mesh) else on_device,
        mesh=mesh,
        in_specs=placed,
        out_specs=(
            P(("wide", "narrow"), None),
            P(("wide", "narrow"), None),
            P(("wide", "narrow"), None),
            P(("wide", "narrow"), None),
            P(("wide", "narrow"), None),
            P(("wide", "narrow"), None),
            P(None, ("wide", "narrow")),
            P(("wide", "narrow"), None),
            P(("wide", "narrow")),
            P(None, ("wide", "narrow")),
        ),
        check_vma=False,
    )
```

```python
import math
from functools import partial
from types import SimpleNamespace

import jax
import jax.numpy as jnp
from jax import lax
from jax.experimental import pallas as pl
from jax.experimental.pallas import tpu as pltpu
from jax.sharding import PartitionSpec as P

HEAD_SIZE = 64
STATE = 64


EPSILON = 1e-05


def normalize(values):
    average = jnp.mean(values, axis=-1, keepdims=True)
    centred = values - average
    variance = jnp.mean(centred * centred, axis=-1, keepdims=True)
    inverse = lax.rsqrt(variance + EPSILON)
    return (centred * inverse, inverse)


def norm_back(grad_in, scaled, inverse):
    first = jnp.mean(grad_in, axis=-1, keepdims=True)
    second = jnp.mean(grad_in * scaled, axis=-1, keepdims=True)
    return inverse * (grad_in - first - scaled * second)


def shift_mix(key_raw, shift_taps):
    summed = key_raw * shift_taps[0]
    for offset in range(1, 4):
        delayed = jnp.concatenate(
            [jnp.zeros((offset, key_raw.shape[1]), key_raw.dtype), key_raw[:-offset]], axis=0
        )
        summed = summed + delayed * shift_taps[offset]
    return summed


def kernel_rows(coefficient, decay_rate, length_all):
    distance = jnp.arange(length_all).astype(jnp.float32)
    decays = jnp.exp(-decay_rate[:, :, None] * distance[None, None, :])
    return jnp.sum(coefficient[:, :, None] * decays, axis=1) / STATE


def toeplitz(kernel_row):
    length_all = kernel_row.shape[0]
    wrapped = jnp.concatenate(
        [kernel_row[:1], jnp.zeros((length_all,), kernel_row.dtype), kernel_row[:0:-1]]
    )
    tiled_row = jnp.tile(wrapped, length_all)[: length_all * (2 * length_all - 1)]
    return tiled_row.reshape(length_all, 2 * length_all - 1)[:, :length_all]


def split_heads(values, row_count):
    return values.reshape(row_count, -1, HEAD_SIZE).transpose(1, 0, 2)


def merge_heads(per_head):
    head_count = per_head.shape[0]
    row_count = per_head.shape[1]
    merged = per_head.transpose(1, 0, 2).reshape(row_count, head_count * HEAD_SIZE)
    return merged


def pack_rows(matrices, shard_count):
    return jnp.concatenate(
        [matrix.reshape(shard_count, -1) for matrix in matrices], axis=1
    ).reshape(-1)


def unpack_rows(flat, matrices, shard_count):
    pieces = []
    offset = 0
    for matrix in matrices:
        rows_own = matrix.shape[0] // shard_count
        extent = matrix.size // shard_count
        pieces.append(flat[offset : offset + extent].reshape((rows_own,) + matrix.shape[1:]))
        offset = offset + extent
    return pieces


def mixer_forward(queries, keys, values, kernel, row_count):

    def head_forward(parts):
        query_head, key_head, value_head, kernel_row = parts
        scores = jnp.dot(query_head, key_head.T, preferred_element_type=jnp.float32) / HEAD_SIZE
        weights_mix = (scores * toeplitz(kernel_row)).astype(jnp.bfloat16)
        return jnp.dot(weights_mix, value_head, preferred_element_type=jnp.float32)

    per_head = lax.map(
        head_forward,
        (
            split_heads(queries, row_count),
            split_heads(keys, row_count),
            split_heads(values, row_count),
            kernel,
        ),
    )
    return merge_heads(per_head)


def mixer_backward(queries, keys, values, grad_mixed, kernel, row_count):

    def head_backward(parts):
        query_head, key_head, value_head, grad_head, kernel_row = parts
        scores = jnp.dot(query_head, key_head.T, preferred_element_type=jnp.float32) / HEAD_SIZE
        toeplitz_mat, pullback = jax.vjp(toeplitz, kernel_row)
        weights_mix = (scores * toeplitz_mat).astype(jnp.bfloat16)
        grad_weights = jnp.dot(grad_head, value_head.T, preferred_element_type=jnp.float32)
        grad_values = jnp.dot(weights_mix.T, grad_head, preferred_element_type=jnp.float32)
        grad_scores = (grad_weights * toeplitz_mat).astype(jnp.bfloat16)
        grad_queries = (
            jnp.dot(grad_scores, key_head, preferred_element_type=jnp.float32) / HEAD_SIZE
        )
        grad_keys = (
            jnp.dot(grad_scores.T, query_head, preferred_element_type=jnp.float32) / HEAD_SIZE
        )
        grad_kernel = pullback(grad_weights * scores)[0]
        return (grad_queries, grad_keys, grad_values, grad_kernel)

    head_grads = lax.map(
        head_backward,
        (
            split_heads(queries, row_count),
            split_heads(keys, row_count),
            split_heads(values, row_count),
            split_heads(grad_mixed, row_count),
            kernel,
        ),
    )
    grad_kernel = head_grads[3]
    return (
        merge_heads(head_grads[0]),
        merge_heads(head_grads[1]),
        merge_heads(head_grads[2]),
        grad_kernel,
    )


def on_device(
    tokens, lengths, cotangent, w_query, w_key, w_value, w_out, w_fc1, w_fc2, fc1_bias, vectors
):
    shard_count = lax.axis_size(("wide", "narrow"))
    gathered = (
        lax.all_gather(w_query, ("wide", "narrow"), axis=0, tiled=True),
        lax.all_gather(w_key, ("wide", "narrow"), axis=0, tiled=True),
        lax.all_gather(w_value, ("wide", "narrow"), axis=0, tiled=True),
        lax.all_gather(w_out, ("wide", "narrow"), axis=0, tiled=True),
        lax.all_gather(w_fc1, ("wide", "narrow"), axis=1, tiled=True),
        lax.all_gather(w_fc2, ("wide", "narrow"), axis=0, tiled=True),
        lax.all_gather(fc1_bias, ("wide", "narrow"), axis=0, tiled=True),
        lax.all_gather(vectors, ("wide", "narrow"), axis=1, tiled=True),
    )
    query_full, key_full, value_full, out_full, fc1_full, fc2_full, bias_full, vector_full = (
        gathered
    )
    params = vector_full.astype(jnp.float32)
    fc1_shift = bias_full.astype(jnp.float32)
    seq_len = tokens.shape[0]
    head_count = params.shape[1] // HEAD_SIZE
    seq_length = lengths[0]
    valid_mask = (jnp.arange(seq_len) < seq_length).astype(jnp.float32)[:, None]
    residual = tokens.astype(jnp.float32)
    scaled1, inverse1 = normalize(residual)
    normed = (scaled1 * params[0] + params[1]).astype(jnp.bfloat16)
    queries = (jnp.dot(normed, query_full, preferred_element_type=jnp.float32) + params[2]).astype(
        jnp.bfloat16
    )
    key_raw = jnp.dot(normed, key_full, preferred_element_type=jnp.float32) + params[3]
    keys = (shift_mix(key_raw, params[5:9]) * valid_mask).astype(jnp.bfloat16)
    values = (
        (jnp.dot(normed, value_full, preferred_element_type=jnp.float32) + params[4]) * valid_mask
    ).astype(jnp.bfloat16)
    coefficient = params[9].reshape(head_count, STATE)
    decay_rate = params[10].reshape(head_count, STATE)
    kernel_fn = partial(kernel_rows, length_all=seq_len)
    kernel, kernel_pull = jax.vjp(kernel_fn, coefficient, decay_rate)
    mixed = mixer_forward(queries, keys, values, kernel, seq_len)
    mixed_out = (mixed * valid_mask).astype(jnp.bfloat16)
    hidden = (
        residual + jnp.dot(mixed_out, out_full, preferred_element_type=jnp.float32) + params[11]
    )
    scaled2, inverse2 = normalize(hidden)
    normed2 = (scaled2 * params[12] + params[13]).astype(jnp.bfloat16)
    pre_act = jnp.dot(normed2, fc1_full, preferred_element_type=jnp.float32) + fc1_shift
    activated = jax.nn.gelu(pre_act).astype(jnp.bfloat16)
    output = (
        hidden + jnp.dot(activated, fc2_full, preferred_element_type=jnp.float32) + params[14]
    ).astype(jnp.bfloat16)
    again = (
        lax.all_gather(w_query, ("wide", "narrow"), axis=0, tiled=True),
        lax.all_gather(w_key, ("wide", "narrow"), axis=0, tiled=True),
        lax.all_gather(w_value, ("wide", "narrow"), axis=0, tiled=True),
        lax.all_gather(w_out, ("wide", "narrow"), axis=0, tiled=True),
        lax.all_gather(w_fc1, ("wide", "narrow"), axis=1, tiled=True),
        lax.all_gather(w_fc2, ("wide", "narrow"), axis=0, tiled=True),
        lax.all_gather(fc1_bias, ("wide", "narrow"), axis=0, tiled=True),
        lax.all_gather(vectors, ("wide", "narrow"), axis=1, tiled=True),
    )
    query_back, key_back, value_back, out_back, fc1_back, fc2_back = (
        again[0],
        again[1],
        again[2],
        again[3],
        again[4],
        again[5],
    )
    grad_top = cotangent.astype(jnp.float32)
    grad_fc2 = jnp.dot(activated.T, cotangent, preferred_element_type=jnp.float32)
    grad_activated = jnp.dot(cotangent, fc2_back.T, preferred_element_type=jnp.float32)
    gelu_value, gelu_pull = jax.vjp(jax.nn.gelu, pre_act)
    grad_pre = gelu_pull(grad_activated)[0].astype(jnp.bfloat16)
    grad_fc1_turned = jnp.dot(grad_pre.T, normed2, preferred_element_type=jnp.float32)
    grad_fc1_bias = jnp.sum(grad_pre.astype(jnp.float32), axis=0)[:, None]
    mlp_terms = [grad_fc1_turned, grad_fc2, grad_fc1_bias]
    mlp_flat = lax.psum_scatter(
        pack_rows(mlp_terms, shard_count), ("wide", "narrow"), scatter_dimension=0, tiled=True
    )
    mlp_sums = unpack_rows(mlp_flat, mlp_terms, shard_count)
    grad_normed2 = jnp.dot(grad_pre, fc1_back.T, preferred_element_type=jnp.float32)
    grad_hidden = grad_top + norm_back(grad_normed2 * params[12], scaled2, inverse2)
    grad_attn = grad_hidden.astype(jnp.bfloat16)
    grad_out = jnp.dot(mixed_out.T, grad_attn, preferred_element_type=jnp.float32)
    grad_mixed = (
        jnp.dot(grad_attn, out_back.T, preferred_element_type=jnp.float32) * valid_mask
    ).astype(jnp.bfloat16)
    grad_q, grad_k, grad_v, grad_kernel = mixer_backward(
        queries, keys, values, grad_mixed, kernel, seq_len
    )
    grad_queries = grad_q.astype(jnp.bfloat16)
    grad_values = (grad_v * valid_mask).astype(jnp.bfloat16)
    shift_value, shift_pull = jax.vjp(shift_mix, key_raw, params[5:9])
    grad_key_full, grad_taps = shift_pull(grad_k * valid_mask)
    grad_key_raw = grad_key_full.astype(jnp.bfloat16)
    grad_query = jnp.dot(normed.T, grad_queries, preferred_element_type=jnp.float32)
    grad_key = jnp.dot(normed.T, grad_key_raw, preferred_element_type=jnp.float32)
    grad_value = jnp.dot(normed.T, grad_values, preferred_element_type=jnp.float32)
    grad_normed = jnp.dot(grad_queries, query_back.T, preferred_element_type=jnp.float32)
    grad_normed = grad_normed + jnp.dot(
        grad_key_raw, key_back.T, preferred_element_type=jnp.float32
    )
    grad_normed = grad_normed + jnp.dot(
        grad_values, value_back.T, preferred_element_type=jnp.float32
    )
    input_grad = (grad_hidden + norm_back(grad_normed * params[0], scaled1, inverse1)).astype(
        jnp.bfloat16
    )
    grad_coef, grad_rate = kernel_pull(grad_kernel)
    grad_vectors = jnp.concatenate(
        [
            jnp.sum(grad_normed * scaled1, axis=0)[None],
            jnp.sum(grad_normed, axis=0)[None],
            jnp.sum(grad_queries.astype(jnp.float32), axis=0)[None],
            jnp.sum(grad_key_raw.astype(jnp.float32), axis=0)[None],
            jnp.sum(grad_values.astype(jnp.float32), axis=0)[None],
            grad_taps,
            grad_coef.reshape(1, -1),
            grad_rate.reshape(1, -1),
            jnp.sum(grad_attn.astype(jnp.float32), axis=0)[None],
            jnp.sum(grad_normed2 * scaled2, axis=0)[None],
            jnp.sum(grad_normed2, axis=0)[None],
            jnp.sum(grad_top, axis=0)[None],
        ],
        axis=0,
    )
    mixer_terms = [grad_query, grad_key, grad_value, grad_out, grad_vectors.T]
    mixer_flat = lax.psum_scatter(
        pack_rows(mixer_terms, shard_count), ("wide", "narrow"), scatter_dimension=0, tiled=True
    )
    mixer_sums = unpack_rows(mixer_flat, mixer_terms, shard_count)
    return (
        output,
        input_grad,
        mixer_sums[0],
        mixer_sums[1],
        mixer_sums[2],
        mixer_sums[3],
        mlp_sums[0].T,
        mlp_sums[1],
        mlp_sums[2].reshape(-1),
        mixer_sums[4].T,
    )


f32, bf16 = jnp.float32, jnp.bfloat16
MESH = pl.DeviceIdType.MESH


def dg(left, right, left_dim, right_dim):
    return lax.dot_general(
        left, right, (((left_dim,), (right_dim,)), ((), ())), preferred_element_type=f32
    )


def when(condition, body):
    if condition is None:
        body()
    else:
        pl.when(condition)(body)


def both(first, second):
    if first is None:
        return second
    if second is None:
        return first
    return jnp.logical_and(first, second)


class Links:
    def __init__(self, depth):
        wide, z = lax.axis_index("wide"), lax.axis_index("narrow")
        self.depth = depth
        self.z, self.core = z, lax.rem(wide, 2)
        self.x, self.y = lax.rem(lax.div(wide, 2), 2), lax.div(wide, 4)
        self.me = self.y * 2 + self.x
        self.xs = self.y * 2 + (1 - self.x)
        self.ys = (1 - self.y) * 2 + self.x
        self.ds = (1 - self.y) * 2 + (1 - self.x)
        self.sib_dev = (self.me * 2 + (1 - self.core), z)
        self.x_dev = (self.xs * 2 + self.core, z)
        self.y_dev = (self.ys * 2 + self.core, z)
        self.up_dev = (wide, z + 1)
        self.down_dev = (wide, z - 1)
        self.has_up = z < depth - 1
        self.has_down = z > 0
        self.at_end = jnp.logical_or(z == 0, z == depth - 1)

    def barrier(self):
        semaphore = pltpu.get_barrier_semaphore()

        def greet(device):
            pl.semaphore_signal(semaphore, inc=1, device_id=device, device_id_type=MESH)

        for device in (self.sib_dev, self.x_dev, self.y_dev):
            greet(device)
        pl.when(self.has_up)(lambda: greet(self.up_dev))
        pl.when(self.has_down)(lambda: greet(self.down_dev))
        peers = 3 + self.has_up.astype(jnp.int32) + self.has_down.astype(jnp.int32)
        pl.semaphore_wait(semaphore, peers)

    def start(self, condition, source, target, send, receive, device):
        when(
            condition,
            lambda: pltpu.make_async_remote_copy(
                src_ref=source(),
                dst_ref=target(),
                send_sem=send,
                recv_sem=receive,
                device_id=device,
                device_id_type=MESH,
            ).start(),
        )

    def arrive(self, target, receive):
        pltpu.make_async_remote_copy(
            src_ref=target,
            dst_ref=target,
            send_sem=receive,
            recv_sem=receive,
            device_id=self.sib_dev,
            device_id_type=MESH,
        ).wait_recv()

    def left(self, extent, semaphore):
        pltpu.make_async_remote_copy(
            src_ref=extent,
            dst_ref=extent,
            send_sem=semaphore,
            recv_sem=semaphore,
            device_id=self.sib_dev,
            device_id_type=MESH,
        ).wait_send()

    def left_along(self, extent, semaphore):
        pl.when(self.at_end)(lambda: self.left(extent(1), semaphore))
        pl.when(jnp.logical_not(self.at_end))(lambda: self.left(extent(self.depth + 1), semaphore))


def halved(ref, piece):
    rows, lanes = ref.shape[-2:]
    if lanes == 128:
        return ref.at[pl.ds(piece * (rows // 2), rows // 2)]
    return ref.at[:, pl.ds(piece * (lanes // 2), lanes // 2)]


def near(k, distance):
    if distance == 0:
        return ((None, k.z, False),)
    return ((k.z >= distance, k.z - distance, True), (k.z + distance < k.depth, k.z + distance, False))


def gather_z_first(k, name, buf, index, low, rows, ss, rs):
    depth = k.depth

    def block(yx, zs):
        return buf.at[index(yx, zs), pl.ds(low, rows)]

    def send(condition, yx, zs, device, r, way=0, piece=None):
        ref = lambda: block(yx, zs) if piece is None else halved(block(yx, zs), piece)
        k.start(condition, ref, ref, ss.at[way], rs.at[r], device)

    def to_sib(condition, yx, zs):
        send(condition, yx, zs, k.sib_dev, 4 * depth)

    def outward(condition, zs):
        send(condition, k.me, zs, k.x_dev, depth + zs)
        send(condition, k.me, zs, k.y_dev, 2 * depth + zs)
        to_sib(condition, k.me, zs)

    def along(condition, zs, up, down):
        if up:
            send(both(condition, k.has_up), k.me, zs, k.up_dev, zs, 1)
        if down:
            send(both(condition, k.has_down), k.me, zs, k.down_dev, zs, 1)

    def take(condition, yx, zs, r):
        when(condition, lambda: k.arrive(block(yx, zs), rs.at[r]))

    def own():
        along(None, k.z, True, True)
        outward(None, k.z)
        yield

    def z_steps():
        for d in range(1, depth):
            for condition, zs, below in near(k, d):
                take(condition, k.me, zs, zs)
                along(condition, zs, below, not below)
                outward(condition, zs)
            yield

    def x_steps():
        for d in range(depth):
            for condition, zs, _ in near(k, d):
                take(condition, k.xs, zs, depth + zs)
                send(condition, k.xs, zs, k.y_dev, 3 * depth + zs, piece=0)
                to_sib(condition, k.xs, zs)
            yield

    def y_steps():
        for d in range(depth):
            for condition, zs, _ in near(k, d):
                take(condition, k.ys, zs, 2 * depth + zs)
                send(condition, k.ys, zs, k.x_dev, 3 * depth + zs, piece=1)
                to_sib(condition, k.ys, zs)
            yield

    def d_steps():
        for d in range(depth):
            for condition, zs, _ in near(k, d):
                take(condition, k.ds, zs, 3 * depth + zs)
                to_sib(condition, k.ds, zs)
            yield

    def extent(blocks):
        return buf.at[pl.ds(0, blocks), pl.ds(low, rows)]

    def sib_steps():
        k.arrive(extent(4 * depth), rs.at[4 * depth])
        yield

    def left():
        k.left(extent(7 * depth), ss.at[0])
        k.left_along(extent, ss.at[1])
        yield

    steps = {"0": own(), "z": z_steps(), "x": x_steps(), "y": y_steps(), "d": d_steps(), "s": sib_steps(), ".": left()}
    return {name + key: step for key, step in steps.items()}


def gather_pair_z_first(k, name, buf, index, low, rows, ss, rs):
    depth = k.depth

    def block(yx, zs):
        return buf.at[index(yx, zs), pl.ds(low, rows)]

    def extent(blocks):
        return buf.at[pl.ds(0, blocks), pl.ds(low, rows)]

    def send(condition, zs, device, r, way):
        ref = lambda: block(k.me, zs)
        k.start(condition, ref, ref, ss.at[way], rs.at[r], device)

    def along(condition, zs, up, down):
        if up:
            send(both(condition, k.has_up), zs, k.up_dev, zs, 1)
        if down:
            send(both(condition, k.has_down), zs, k.down_dev, zs, 1)

    def own():
        along(None, k.z, True, True)
        send(None, k.z, k.y_dev, depth + k.z, 0)
        yield

    def z_steps():
        for d in range(1, depth):
            for condition, zs, below in near(k, d):
                when(condition, lambda zs=zs: k.arrive(block(k.me, zs), rs.at[zs]))
                along(condition, zs, below, not below)
                send(condition, zs, k.y_dev, depth + zs, 0)
            yield

    def y_steps():
        for d in range(depth):
            for condition, zs, _ in near(k, d):
                when(condition, lambda zs=zs: k.arrive(block(k.ys, zs), rs.at[depth + zs]))
            yield

    def left():
        k.left(extent(depth), ss.at[0])
        k.left_along(extent, ss.at[1])
        yield

    steps = {"0": own(), "z": z_steps(), "y": y_steps(), ".": left()}
    return {name + key: step for key, step in steps.items()}


def gather_pair_z_last(k, name, buf, index, low, rows, ss, rs):
    depth = k.depth
    yx_of = (k.me, k.ys)

    def block(yx, zs):
        return buf.at[index(yx, zs), pl.ds(low, rows)]

    def extent(blocks):
        return buf.at[pl.ds(0, blocks), pl.ds(low, rows)]

    def send(condition, yx, zs, device, r, way):
        ref = lambda: block(yx, zs)
        k.start(condition, ref, ref, ss.at[way], rs.at[r], device)

    def along(condition, which, zs, up, down):
        place = 1 + which * depth + zs
        if up:
            send(both(condition, k.has_up), yx_of[which], zs, k.up_dev, place, 1 + which)
        if down:
            send(both(condition, k.has_down), yx_of[which], zs, k.down_dev, place, 1 + which)

    def own():
        send(None, k.me, k.z, k.y_dev, 0, 0)
        along(None, 0, k.z, True, True)
        yield

    def y_step():
        k.arrive(block(k.ys, k.z), rs.at[0])
        along(None, 1, k.z, True, True)
        yield

    def z_steps(which):
        for d in range(1, depth):
            for condition, zs, below in near(k, d):
                when(condition, lambda zs=zs: k.arrive(block(yx_of[which], zs), rs.at[1 + which * depth + zs]))
                along(condition, which, zs, below, not below)
            yield

    def left():
        k.left(extent(1), ss.at[0])
        for which in range(2):
            k.left_along(extent, ss.at[1 + which])
        yield

    steps = {"0": own(), "y": y_step(), "4": z_steps(0), "5": z_steps(1), ".": left()}
    return {name + key: step for key, step in steps.items()}


def add_into(ref, *others):
    total = ref[...].astype(f32)
    for other in others:
        total = total + other[...].astype(f32)
    ref[...] = total.astype(ref.dtype)


def scatter_order(depth):
    return ([0, depth - 1] + list(range(1, depth - 1)))[:depth]


def along_z(k, zd, wave, block, from_up, from_down, rs_up, rs_down, send):
    top, low = k.depth - 1 - wave, wave

    def take(slot, semaphore):
        k.arrive(slot, semaphore)
        add_into(block, slot)

    if zd < top:
        if wave:
            pl.when(k.z == top)(lambda: take(from_up, rs_up))
        send(k.z == top, False)
    if zd > low:
        if wave:
            pl.when(k.z == low)(lambda: take(from_down, rs_down))
        send(k.z == low, True)


def scatter_z_last(k, name, buf, index, low, rows, slots, ss, rs, finish):
    depth = k.depth
    from_x_diag, from_y_diag, from_xy, from_up, from_down = slots
    order = scatter_order(depth)

    def block(yx, zd):
        return buf.at[index(yx, zd), pl.ds(low, rows)]

    def half(yx, zd, piece):
        return halved(block(yx, zd), piece)

    def send(condition, source, target, device, r):
        k.start(condition, source, target, ss.at[0], rs.at[r], device)

    def x_part(zd, piece):
        return halved(from_xy.at[zd, 0], piece)

    def y_part(zd, piece):
        return halved(from_xy.at[zd, 1], piece)

    def pure_x():
        for zd in order:
            send(None, lambda zd=zd: half(k.xs, zd, 1), lambda zd=zd: x_part(zd, 1), k.x_dev, 2 * depth + zd)
            yield

    def pure_y():
        for zd in order:
            send(None, lambda zd=zd: half(k.ys, zd, 0), lambda zd=zd: y_part(zd, 0), k.y_dev, 2 * depth + zd)
            yield

    def diagonal():
        for zd in order:
            send(None, lambda zd=zd: half(k.ds, zd, 0), lambda zd=zd: from_y_diag.at[zd], k.y_dev, zd)
            send(None, lambda zd=zd: half(k.ds, zd, 1), lambda zd=zd: from_x_diag.at[zd], k.x_dev, depth + zd)
            yield

    def y_added():
        for zd in order:
            k.arrive(from_y_diag.at[zd], rs.at[zd])
            add_into(half(k.xs, zd, 0), from_y_diag.at[zd])
            send(None, lambda zd=zd: half(k.xs, zd, 0), lambda zd=zd: x_part(zd, 0), k.x_dev, 2 * depth + zd)
            yield

    def x_added():
        for zd in order:
            k.arrive(from_x_diag.at[zd], rs.at[depth + zd])
            add_into(half(k.ys, zd, 1), from_x_diag.at[zd])
            send(None, lambda zd=zd: half(k.ys, zd, 1), lambda zd=zd: y_part(zd, 1), k.y_dev, 2 * depth + zd)
            yield

    def wave(zd, number):
        def send_z(condition, up):
            place = (4 if up else 3) * depth + zd
            slot = from_down if up else from_up
            send(condition, lambda: block(k.me, zd), lambda: slot.at[zd], k.up_dev if up else k.down_dev, place)

        along_z(
            k, zd, number, block(k.me, zd), from_up.at[zd], from_down.at[zd],
            rs.at[3 * depth + zd], rs.at[4 * depth + zd], send_z,
        )

    def collect():
        for zd in order:
            k.arrive(from_xy.at[zd], rs.at[2 * depth + zd])
            add_into(block(k.me, zd), from_xy.at[zd, 0], from_xy.at[zd, 1])
            wave(zd, 0)
            yield

    def waves(number):
        for zd in order:
            if zd < depth - 1 - number or zd > number:
                wave(zd, number)
                yield

    def end():
        finish(block(k.me, k.z), False)

        def last_up():
            k.arrive(from_up.at[k.z], rs.at[3 * depth + k.z])
            finish(from_up.at[k.z], True)

        def last_down():
            k.arrive(from_down.at[k.z], rs.at[4 * depth + k.z])
            finish(from_down.at[k.z], True)

        pl.when(k.has_up)(last_up)
        pl.when(k.has_down)(last_down)
        yield

    def left():
        k.left(buf.at[pl.ds(0, 4 * depth - 1), pl.ds(low, rows)], ss.at[0])
        yield

    steps = {"X": pure_x(), "Y": pure_y(), "D": diagonal(), "a": y_added(), "b": x_added(), "c": collect(), "e": end()}
    steps |= {"v": waves(1), "w": waves(2), ".": left()}
    return {name + key: step for key, step in steps.items()}


def scatter_pair_z_last(k, name, buf, index, low, rows, slots, ss, rs, finish):
    depth = k.depth
    from_y, from_up, from_down = slots
    order = scatter_order(depth)

    def block(yx, zd):
        return buf.at[index(yx, zd), pl.ds(low, rows)]

    def send(condition, source, target, device, r):
        k.start(condition, source, target, ss.at[0], rs.at[r], device)

    def pure_y():
        for zd in order:
            send(None, lambda zd=zd: block(k.ys, zd), lambda zd=zd: from_y.at[zd], k.y_dev, zd)
            yield

    def wave(zd, number):
        def send_z(condition, up):
            slot = from_down if up else from_up
            place = (2 if up else 1) * depth + zd
            send(condition, lambda: block(k.me, zd), lambda: slot.at[zd], k.up_dev if up else k.down_dev, place)

        along_z(
            k, zd, number, block(k.me, zd), from_up.at[zd], from_down.at[zd],
            rs.at[depth + zd], rs.at[2 * depth + zd], send_z,
        )

    def collect():
        for zd in order:
            k.arrive(from_y.at[zd], rs.at[zd])
            add_into(block(k.me, zd), from_y.at[zd])
            wave(zd, 0)
            yield

    def waves(number):
        for zd in order:
            if zd < depth - 1 - number or zd > number:
                wave(zd, number)
                yield

    def end():
        finish(block(k.me, k.z), False)

        def last_up():
            k.arrive(from_up.at[k.z], rs.at[depth + k.z])
            finish(from_up.at[k.z], True)

        def last_down():
            k.arrive(from_down.at[k.z], rs.at[2 * depth + k.z])
            finish(from_down.at[k.z], True)

        pl.when(k.has_up)(last_up)
        pl.when(k.has_down)(last_down)
        yield

    def left():
        k.left(buf.at[pl.ds(0, 2 * depth - 1), pl.ds(low, rows)], ss.at[0])
        yield

    steps = {"Y": pure_y(), "c": collect(), "v": waves(1), "w": waves(2), "e": end(), ".": left()}
    return {name + key: step for key, step in steps.items()}


def scatter_pair_z_first(k, name, buf, index, low, rows, slots, ss, rs, finish):
    depth = k.depth
    from_y, from_up, from_down = slots
    yx_of = (k.me, k.ys)

    def block(yx, zd):
        return buf.at[index(yx, zd), pl.ds(low, rows)]

    def send(condition, source, target, device, r):
        k.start(condition, source, target, ss.at[0], rs.at[r], device)

    def waves(which):
        yx = yx_of[which]
        for number in range(depth - 1):
            for zd in scatter_order(depth):
                place = which * depth + zd

                def send_z(condition, up, zd=zd, place=place):
                    slot, number = (from_down, 2 * depth + place) if up else (from_up, place)
                    send(condition, lambda: block(yx, zd), lambda: slot.at[place], k.up_dev if up else k.down_dev, number)

                along_z(
                    k, zd, number, block(yx, zd), from_up.at[place], from_down.at[place],
                    rs.at[place], rs.at[2 * depth + place], send_z,
                )
            yield

    def own(which):
        yx = yx_of[which]
        place = which * depth + k.z

        def take(slot, semaphore):
            k.arrive(slot, semaphore)
            add_into(block(yx, k.z), slot)

        pl.when(k.has_up)(lambda: take(from_up.at[place], rs.at[place]))
        pl.when(k.has_down)(lambda: take(from_down.at[place], rs.at[2 * depth + place]))

    def own_me():
        own(0)
        yield

    def own_y():
        own(1)
        send(None, lambda: block(k.ys, k.z), lambda: from_y.at[0], k.y_dev, 4 * depth)
        yield

    def end():
        k.arrive(from_y.at[0], rs.at[4 * depth])
        finish(block(k.me, k.z), False)
        finish(from_y.at[0], True)
        yield

    def left():
        k.left(buf.at[pl.ds(0, 2 * depth - 1), pl.ds(low, rows)], ss.at[0])
        yield

    steps = {"0": waves(0), "1": waves(1), "O": own_me(), "Y": own_y(), "e": end(), ".": left()}
    return {name + key: step for key, step in steps.items()}


SEQ, WIDTH, UNITS = 256, 768, 96
HEADS = WIDTH // HEAD_SIZE
FIRST = 112


def row_loop(total, step, body, first=0):
    def once(i, carry):
        for part in range(4):
            body(pl.multiple_of(first + (i * 4 + part) * step, step), step)
        return carry

    lax.fori_loop(0, total // (step * 4), once, 0)


def lane_shift(values, offset, left):
    extent = values.shape[1]
    lane = lax.broadcasted_iota(jnp.int32, values.shape, 1)
    if left:
        return jnp.where(lane < extent - offset, pltpu.roll(values, extent - offset, 1), 0.0)
    return jnp.where(lane >= offset, pltpu.roll(values, offset, 1), 0.0)


def heads(which, body):
    for h in which:
        body(h)


def head_rows(h):
    return pl.ds(pl.multiple_of(h * HEAD_SIZE, HEAD_SIZE), HEAD_SIZE)


def scratch_of(depth):
    devices, blocks, half = 8 * depth, 4 * depth, 2 * depth
    table = {
        "qk": ((devices, UNITS, WIDTH), bf16),
        "ff": ((half, 2 * UNITS, WIDTH), bf16),
        "sm": ((devices, 16, 128), f32),
        "gff": ((half, 2 * UNITS, WIDTH), bf16),
        "gs": ((devices, 16, 128), f32),
        "sr": ((blocks, UNITS, WIDTH), bf16),
        "srs": ((blocks, 16, 128), f32),
        "wq": ((WIDTH, WIDTH), bf16),
        "wk": ((WIDTH, WIDTH), bf16),
        "wv": ((WIDTH, WIDTH), bf16),
        "wo": ((WIDTH, WIDTH), bf16),
        "s1": ((SEQ, WIDTH), f32),
        "i1": ((SEQ, 128), f32),
        "nm": ((SEQ, WIDTH), bf16),
        "hid": ((SEQ, WIDTH), f32),
        "s2": ((SEQ, WIDTH), f32),
        "i2": ((SEQ, 128), f32),
        "n2": ((4 * SEQ, WIDTH), bf16),
        "ct": ((4 * SEQ, WIDTH), bf16),
        "outp": ((4 * SEQ, WIDTH), f32),
        "dn2": ((4 * SEQ, WIDTH), f32),
        "outs": ((SEQ, WIDTH), f32),
        "dn2s": ((SEQ, WIDTH), f32),
        "outb": ((SEQ, WIDTH), f32),
        "dn2b": ((SEQ, WIDTH), f32),
        "outx": ((2, SEQ, WIDTH), bf16),
        "dn2x": ((2, SEQ, WIDTH), bf16),
        "act": ((2, 4 * SEQ, UNITS * depth), bf16),
        "dp": ((2, 4 * SEQ, UNITS * depth), bf16),
        "da": ((SEQ, WIDTH), bf16),
        "dk": ((WIDTH, SEQ), f32),
        "dn": ((SEQ, WIDTH), f32),
        "nmt": ((WIDTH, SEQ), bf16),
        "qt": ((WIDTH, SEQ), bf16),
        "kt": ((WIDTH, SEQ), bf16),
        "vt": ((WIDTH, SEQ), bf16),
        "wt": ((HEADS, SEQ, SEQ), bf16),
        "krt": ((WIDTH, SEQ), f32),
        "mt": ((WIDTH, SEQ), bf16),
        "dmt": ((WIDTH, SEQ), bf16),
        "dqt": ((WIDTH, SEQ), bf16),
        "dkt": ((WIDTH, SEQ), bf16),
        "dvt": ((WIDTH, SEQ), bf16),
        "kft": ((WIDTH, SEQ), bf16),
        "vft": ((WIDTH, SEQ), bf16),
        "ex": ((WIDTH, SEQ), f32),
        "tt": ((HEADS, SEQ, SEQ), f32),
        "vec": ((16, WIDTH), f32),
        "vecc": ((WIDTH, 128), f32),
        "colsum": ((WIDTH, 128), f32),
        "gvec": ((16, WIDTH), f32),
        "bias": ((2, 8, UNITS * depth), f32),
        "gbias": ((half, 8, 128), f32),
    }
    for name, rows, lanes, kind in (("q", 48, WIDTH, bf16), ("v", 48, WIDTH, bf16), ("t", 16, 128, f32)):
        part = (rows, lanes // 2) if lanes == WIDTH else (rows // 2, lanes)
        table["r" + name + "dx"] = table["r" + name + "dy"] = ((depth,) + part, kind)
        table["r" + name + "xy"] = ((depth, 2, rows, lanes), kind)
        table["r" + name + "u"] = table["r" + name + "d"] = ((depth, rows, lanes), kind)
    table["rby"] = table["rbu"] = table["rbd"] = ((depth, FIRST, WIDTH), bf16)
    table["rcy"] = ((1, 2 * UNITS - FIRST, WIDTH), bf16)
    table["rcu"] = table["rcd"] = ((half, 2 * UNITS - FIRST, WIDTH), bf16)
    table["tok"] = table["cot"] = ((SEQ, WIDTH), bf16)
    for name in ("iq", "ik", "iv", "io"):
        table[name] = ((24, WIDTH), bf16)
    table["ifc1"] = table["ifc2"] = ((UNITS, WIDTH), bf16)
    table["ibias"], table["ivec"] = ((1, UNITS), bf16), ((15, 24), bf16)
    table["load"] = len(OPERANDS)
    for name, sent, came in (
        ("gq", 2, 4 * depth + 1), ("gv", 2, 4 * depth + 1), ("gb", 2, 2 * depth), ("gt", 2, 4 * depth + 1), ("gc", 3, 2 * depth + 1),
        ("sq", 1, 5 * depth), ("sv", 1, 5 * depth), ("sb", 1, 3 * depth), ("st", 1, 5 * depth), ("sc", 1, 4 * depth + 1), ("e", 3, 25),
    ):
        table[name + "_s"], table[name + "_r"] = sent, came
    return table


PLAN = (
    "load", "barrier", "own_blocks", "S0", "Q0", "V0", "Sy", "Sz", "Sx", "L0", "Sy", "Vx", "Sz", "Vz", "Qz",
    "Vz", "Sd", "Sx", "Sz", "Sx", "Qz", "Vz", "Sy", "Ly", "L4", "Qz", "Sx", "Vx", "Vx", "Vx", "Vy", "Qx",
    "norm1", "Qy", "Qx", "Sy", "Sd", "Qx", "Vy", "Qx", "Vy", "Vy", "Sd", "F0", "Vd", "Qy", "Qy", "Sd", "Ss",
    "Vd", "Vd", "L4", "Vd", "Qy", "own_cotangent", "vectors", "gain1", "Vs", "unpack1", "project_v", "Fz",
    "Qd", "Qd", "Qd", "Qd", "mixer_kernels", "Qs", "unpack0", "project_qk", "L4", "score0", "mix0", "Fz",
    "score1", "L5", "mix1", "hidden", "norm2", "Fz", "pass_ct", "sibling_rows", "Fy", "feed0s", "feed0o",
    "Q.", "L5", "pass_n2_0", "feed0x0", "Fy", "diagonal_rows0", "feed0d0", "L5", "Fy", "Fy", "feed1d0",
    "feed1x0", "to_diagonal0", "feed1s", "pass_n2_1", "feed1o", "to_x0", "feed0x1", "diagonal_rows1",
    "feed0d1", "feed1d1", "to_diagonal1", "feed1x1", "V.", "feed_grads1", "fY", "out_to_diagonal", "l1",
    "to_x1", "feed_grads0", "fY", "to_sibling", "back2_0", "out_to_x", "fY", "flip", "fc", "l0", "back2_1",
    "grad_mixed", "back_v0", "back_v1", "pack_vo0", "fY", "pack_vo1", "back_qk0", "back_qk1", "sum_vo2",
    "sum_vo0", "vD", "l1", "pack_qk0", "pack_qk1", "vX", "grad_normed", "fc", "sum_qk0", "sum_vo1", "qD",
    "sum_qk2", "sum_qk1", "vY", "qX", "vD", "vX", "sum_vo3", "fc", "vb", "qY", "qY", "back1", "vY", "qX",
    "fv", "kernel1", "qD", "qb", "va", "l0", "vX", "kernel2", "vD", "qa", "vD", "l1", "va", "kernel3", "qD",
    "fc", "fw", "vb", "fv", "vX", "kernel0", "vector_tiles", "vb", "small_sums", "sD", "vc", "vY", "sD",
    "sY", "va", "qa", "fv", "qb", "vc", "va", "sY", "sum_qk3", "sD", "sD", "sb", "sX", "vY", "sX", "sa",
    "qc", "vb", "sY", "fv", "qD", "sb", "fw", "sX", "qX", "vc", "qX", "vv", "sa", "sa", "sX", "l0", "qb",
    "qc", "sc", "sb", "qY", "sY", "qa", "sa", "vv", "qv", "vc", "qb", "vw", "sc", "vv", "sb", "qv", "sv",
    "qa", "qY", "qw", "sc", "qc", "sv", "lY", "vv", "vw", "sw", "sv", "qw", "qv", "sw", "ve", "lO",
    "finish_out", "fe", "sc", "sv", "qc", "se", "qv", "le", "qe", "store",
)
OPERANDS = ("tok", "cot", "iq", "ik", "iv", "io", "ifc1", "ifc2", "ibias", "ivec")
INPUTS = ("length",) + tuple("from_" + name for name in OPERANDS)
RESULTS = ("out", "dinp", "gwq", "gwk", "gwv", "gwo", "gfc1", "gfc2", "gsmall")
OUTPUTS = RESULTS


def layer_kernel(depth, *refs):
    names = INPUTS + OUTPUTS + tuple(scratch_of(depth))
    m = SimpleNamespace(**dict(zip(names, refs, strict=True)))
    k = Links(depth)
    core = k.core

    def in_all(yx, zs):
        return (yx * 2 + core) * depth + zs

    def in_all_sib(yx, zs):
        return (yx * 2 + (1 - core)) * depth + zs

    def in_pair(yx, zs):
        return lax.div(yx, 2) * depth + zs

    places = {"o": k.x * 2 + core, "s": k.x * 2 + 1 - core, "x": (1 - k.x) * 2 + core, "d": (1 - k.x) * 2 + 1 - core}

    def rows_at(who, start=0, step=SEQ):
        return pl.ds(pl.multiple_of(places[who] * SEQ + start, step), step)

    def sent_by(place):
        return 2 if place == 24 else 1 if place in (9, 10, 11, 12) or place >= 16 else 0

    def swap(place, source, target, device=None):
        k.start(None, lambda: source, lambda: target, m.e_s.at[sent_by(place)], m.e_r.at[place], device or k.sib_dev)

    day = lax.broadcasted_iota(jnp.int32, (1, SEQ), 1).astype(f32)
    s_at = lax.broadcasted_iota(jnp.int32, (SEQ, SEQ), 0)
    t_at = lax.broadcasted_iota(jnp.int32, (SEQ, SEQ), 1)
    valid = (lax.broadcasted_iota(jnp.int32, (1, SEQ), 1) < m.length[0]).astype(f32)

    def loaded(name):
        place = OPERANDS.index(name)
        return pltpu.make_async_copy(getattr(m, "from_" + name), getattr(m, name), m.load.at[place])

    def load():
        for name in OPERANDS[2:] + OPERANDS[:2]:
            loaded(name).start()

    def own_blocks():
        for name in OPERANDS[2:]:
            loaded(name).wait()
        here = in_all(k.me, k.z)
        for place, (first, second) in enumerate(((m.iq, m.ik), (m.iv, m.io))):
            pair = jnp.concatenate([first[...].astype(f32), second[...].astype(f32)], axis=0)
            m.qk[here, 48 * place : 48 * place + 48] = pair.astype(bf16)
        m.sm[here] = jnp.zeros((16, 128), f32)
        m.sm[here, 0:15, 0:24] = m.ivec[...].astype(f32)
        m.sm[here, 15:16, 0:UNITS] = m.ibias[...].astype(f32)
        m.ff[in_pair(k.me, k.z), 0:UNITS] = m.ifc1[...]
        m.ff[in_pair(k.me, k.z), UNITS : 2 * UNITS] = m.ifc2[...]

    def half_at(who, half):
        return rows_at(who, half * (SEQ // 2), SEQ // 2)

    def own_cotangent():
        loaded("cot").wait()
        m.ct[rows_at("o")] = m.cot[...]
        ref = m.ct.at[rows_at("o")]
        swap(0, ref, ref)
        swap(1, ref, ref, k.x_dev)

    def pass_ct():
        ref = m.ct.at[rows_at("x")]
        k.arrive(ref, m.e_r.at[1])
        swap(2, ref, ref)

    def norm1():
        loaded("tok").wait()

        def rows_of(start, step):
            rows = pl.ds(start, step)
            tokens = m.tok[rows].astype(f32)
            centred = tokens - jnp.mean(tokens, axis=1, keepdims=True)
            inverse = lax.rsqrt(jnp.mean(centred * centred, axis=1, keepdims=True) + EPSILON)
            m.s1[rows] = centred * inverse
            m.i1[rows] = jnp.broadcast_to(inverse, (step, 128))

        row_loop(SEQ, 32, rows_of)

    def vectors():
        total = jnp.zeros((16, WIDTH), f32)
        for wide in range(8):
            part = jnp.zeros((16, 128), f32)
            for zs in range(depth):
                tile = m.sm[wide * depth + zs]
                part = part + (pltpu.roll(tile, 24 * zs, 1) if zs else tile)
            padded = jnp.concatenate([part, jnp.zeros((16, WIDTH - 128), f32)], axis=1)
            total = total + (pltpu.roll(padded, 96 * wide, 1) if wide else padded)
        m.vec[...] = total
        m.vecc[...] = jnp.transpose(jnp.concatenate([total, jnp.zeros((112, WIDTH), f32)], axis=0))
        for y in range(2):
            line = jnp.zeros((16, UNITS * depth), f32)
            for zs in range(depth):
                tile = m.sm[in_all(y * 2 + k.x, zs)]
                tile = jnp.concatenate([tile, jnp.zeros((16, UNITS * depth - 128), f32)], axis=1)
                line = line + (pltpu.roll(tile, UNITS * zs, 1) if zs else tile)
            m.bias[y] = line[8:16]

    def head_kernel(h):
        rows = head_rows(h)
        decays = jnp.exp(-m.vecc[rows, 10:11] * day)
        m.ex[rows] = decays
        line = jnp.sum(m.vecc[rows, 9:10] * decays, axis=0, keepdims=True) * (1.0 / STATE)
        matrix = pltpu.roll(jnp.broadcast_to(line, (SEQ, SEQ)), 0, 1, stride=1, stride_axis=0)
        m.tt[h] = jnp.where(t_at >= s_at, matrix, 0.0)

    def mixer_kernels():
        def four_heads(i, carry):
            for part in range(4):
                head_kernel(4 * i + part)
            return carry

        lax.fori_loop(0, HEADS // 4, four_heads, 0)

    def gain1():
        def rows_of(start, step):
            rows = pl.ds(start, step)
            m.nm[rows] = (m.s1[rows] * m.vec[0:1] + m.vec[1:2]).astype(bf16)

        row_loop(SEQ, 32, rows_of)
        m.nmt[...] = jnp.transpose(m.nm[...])

    def unpack(place):
        first, second = ((m.wq, m.wk), (m.wv, m.wo))[place]

        def rows_of(w, carry):
            rows = pl.ds(pl.multiple_of(w * 96, 96), 96)
            pair = m.qk[pl.ds(w * depth, depth), 48 * place : 48 * place + 48, :].astype(f32)
            first[rows] = pair[:, :24].reshape(96, WIDTH).astype(bf16)
            second[rows] = pair[:, 24:].reshape(96, WIDTH).astype(bf16)
            return carry

        lax.fori_loop(0, 8, rows_of, 0, unroll=4)

    def project_qk():
        m.qt[...] = jnp.transpose(dg(m.nm[...], m.wq[...], 1, 0) + m.vec[2:3]).astype(bf16)
        m.krt[...] = jnp.transpose(dg(m.nm[...], m.wk[...], 1, 0) + m.vec[3:4])

    def project_v():
        m.vt[...] = (jnp.transpose(dg(m.nm[...], m.wv[...], 1, 0) + m.vec[4:5]) * valid).astype(bf16)

    def score_head(h):
        rows = head_rows(h)
        raw = m.krt[rows]
        summed = raw * m.vecc[rows, 5:6]
        for j in range(1, 4):
            summed = summed + lane_shift(raw, j, False) * m.vecc[rows, 5 + j : 6 + j]
        keys = (summed * valid).astype(bf16)
        m.kt[rows] = keys
        scores = dg(keys, m.qt[rows], 0, 0) * (1.0 / HEAD_SIZE)
        m.wt[h] = (scores * m.tt[h]).astype(bf16)

    def mix_head(h):
        rows = head_rows(h)
        m.mt[rows] = (dg(m.vt[rows], m.wt[h], 1, 0) * valid).astype(bf16)

    def hidden():
        m.hid[...] = dg(m.mt[...], m.wo[...], 0, 0)

    def norm2():
        def rows_of(start, step):
            rows = pl.ds(start, step)
            hidden = m.tok[rows].astype(f32) + m.hid[rows] + m.vec[11:12]
            m.hid[rows] = hidden
            centred = hidden - jnp.mean(hidden, axis=1, keepdims=True)
            inverse = lax.rsqrt(jnp.mean(centred * centred, axis=1, keepdims=True) + EPSILON)
            scaled = centred * inverse
            m.s2[rows] = scaled
            m.i2[rows] = jnp.broadcast_to(inverse, (step, 128))
            m.n2[rows_at("o", start, step)] = (scaled * m.vec[12:13] + m.vec[13:14]).astype(bf16)

        row_loop(SEQ, 32, rows_of)
        ref = m.n2.at[rows_at("o")]
        swap(3, ref, ref)
        for half in range(2):
            ref = m.n2.at[half_at("o", half)]
            swap(4 + half, ref, ref, k.x_dev)

    def pass_n2(half):
        ref = m.n2.at[half_at("x", half)]
        k.arrive(ref, m.e_r.at[4 + half])
        swap(6 + half, ref, ref)

    def sibling_rows():
        k.arrive(m.ct.at[rows_at("s")], m.e_r.at[0])
        k.arrive(m.n2.at[rows_at("s")], m.e_r.at[3])

    def diagonal_rows(half):
        if half == 0:
            k.arrive(m.ct.at[rows_at("d")], m.e_r.at[2])
        k.arrive(m.n2.at[half_at("d", half)], m.e_r.at[6 + half])

    def finish_rows(pieces):
        def finish(ref, more):
            value = ref[...].astype(f32)
            for target, (low, high), (first, last) in pieces:
                part = value[first:last]
                target[low:high] = target[low:high] + part if more else part

        return finish

    finish_feed = finish_rows(((m.gfc1, (0, UNITS), (0, UNITS)), (m.gfc2, (0, FIRST - UNITS), (UNITS, FIRST))))
    finish_last = finish_rows(((m.gfc2, (FIRST - UNITS, UNITS), (0, 2 * UNITS - FIRST)),))
    finish_qk = finish_rows(((m.gwq, (0, 24), (0, 24)), (m.gwk, (0, 24), (24, 48))))
    finish_vo = finish_rows(((m.gwv, (0, 24), (0, 24)), (m.gwo, (0, 24), (24, 48))))

    def finish_small(ref, more):
        m.gsmall[...] = m.gsmall[...] + ref[...] if more else ref[...]

    steps = {}
    steps |= gather_z_first(k, "S", m.sm, in_all, 0, 16, m.gt_s, m.gt_r)
    steps |= gather_z_first(k, "Q", m.qk, in_all, 0, 48, m.gq_s, m.gq_r)
    steps |= gather_z_first(k, "V", m.qk, in_all, 48, 48, m.gv_s, m.gv_r)
    steps |= gather_pair_z_first(k, "F", m.ff, in_pair, 0, FIRST, m.gb_s, m.gb_r)
    steps |= gather_pair_z_last(k, "L", m.ff, in_pair, FIRST, 2 * UNITS - FIRST, m.gc_s, m.gc_r)
    slots = (m.rby, m.rbu, m.rbd)
    steps |= scatter_pair_z_last(k, "f", m.gff, in_pair, 0, FIRST, slots, m.sb_s, m.sb_r, finish_feed)
    slots = (m.rcy, m.rcu, m.rcd)
    steps |= scatter_pair_z_first(k, "l", m.gff, in_pair, FIRST, 2 * UNITS - FIRST, slots, m.sc_s, m.sc_r, finish_last)
    slots = (m.rqdx, m.rqdy, m.rqxy, m.rqu, m.rqd)
    steps |= scatter_z_last(k, "q", m.qk, in_all, 0, 48, slots, m.sq_s, m.sq_r, finish_qk)
    slots = (m.rvdx, m.rvdy, m.rvxy, m.rvu, m.rvd)
    steps |= scatter_z_last(k, "v", m.qk, in_all, 48, 48, slots, m.sv_s, m.sv_r, finish_vo)
    slots = (m.rtdx, m.rtdy, m.rtxy, m.rtu, m.rtd)
    steps |= scatter_z_last(k, "s", m.gs, in_all, 0, 16, slots, m.st_s, m.st_r, finish_small)

    root = math.sqrt(2.0 / math.pi)
    chunk = UNITS * depth
    ys = (k.y, 1 - k.y)

    def feed(which, who, half=None):
        blocks = pl.ds(ys[which] * depth, depth)
        rows = rows_at(who) if half is None else half_at(who, half)
        fc1 = m.ff[blocks, 0:UNITS, :].reshape(chunk, WIDTH)
        fc2 = m.ff[blocks, UNITS : 2 * UNITS, :].reshape(chunk, WIDTH)
        pre = dg(m.n2[rows], fc1, 1, 1) + m.bias[ys[which], 7:8]
        square = pre * pre
        tanh = jnp.tanh(root * pre * (1.0 + 0.044715 * square))
        half = 0.5 * (1.0 + tanh)
        slope = half + 0.5 * pre * (1.0 - tanh * tanh) * (root * (1.0 + 3 * 0.044715 * square))
        activated = (pre * half).astype(bf16)
        grad_pre = (dg(m.ct[rows], fc2, 1, 1) * slope).astype(bf16)
        m.act[which, rows] = activated
        m.dp[which, rows] = grad_pre
        if which == 0:
            m.outp[rows] = dg(activated, fc2, 1, 0)
            m.dn2[rows] = dg(grad_pre, fc1, 1, 0)
        else:
            m.outp[rows] += dg(activated, fc2, 1, 0)
            m.dn2[rows] += dg(grad_pre, fc1, 1, 0)

    def to_sibling():
        swap(8, m.dn2.at[rows_at("s")], m.dn2s)
        swap(9, m.outp.at[rows_at("s")], m.outs)

    def half_rows(half):
        return pl.ds(half * (SEQ // 2), SEQ // 2)

    def to_diagonal(half):
        swap(10 + half, m.dn2.at[half_at("d", half)], m.dn2b.at[half_rows(half)])

    def to_x(half):
        rows = half_rows(half)
        k.arrive(m.dn2b.at[rows], m.e_r.at[10 + half])
        m.dn2x[0, rows] = (m.dn2[half_at("x", half)] + m.dn2b[rows]).astype(bf16)
        swap(13 + half, m.dn2x.at[0, rows], m.dn2x.at[1, rows], k.x_dev)

    def out_to_diagonal():
        swap(12, m.outp.at[rows_at("d")], m.outb)

    def out_to_x():
        k.arrive(m.outb, m.e_r.at[12])
        m.outx[0] = (m.outp[rows_at("x")] + m.outb[...]).astype(bf16)
        swap(15, m.outx.at[0], m.outx.at[1], k.x_dev)

    def feed_grads(which):
        blocks = pl.ds(ys[which] * depth, depth)
        pre = m.dp[which]
        m.gff[blocks, 0:UNITS] = dg(pre, m.n2[...], 0, 0).astype(bf16).reshape(depth, UNITS, WIDTH)
        m.gff[blocks, UNITS : 2 * UNITS] = (
            dg(m.act[which], m.ct[...], 0, 0).astype(bf16).reshape(depth, UNITS, WIDTH)
        )
        sums = jnp.sum(pre.astype(f32), axis=0, keepdims=True)
        lane = lax.broadcasted_iota(jnp.int32, (1, 128), 1)
        for zs in range(depth):
            line = (pltpu.roll(sums, chunk - UNITS * zs, 1) if zs else sums)[:, :128]
            m.gbias[ys[which] * depth + zs] = jnp.broadcast_to(jnp.where(lane < UNITS, line, 0.0), (8, 128))

    def back2(half):
        if half == 0:
            m.gvec[...] = jnp.zeros((16, WIDTH), f32)
            k.arrive(m.dn2s, m.e_r.at[8])
        k.arrive(m.dn2x.at[1, half_rows(half)], m.e_r.at[13 + half])

        def rows_of(start, step):
            rows = pl.ds(start, step)
            grad_normed = m.dn2[rows_at("o", start, step)] + m.dn2s[rows] + m.dn2x[1, rows].astype(f32)
            scaled = m.s2[rows]
            grad_in = grad_normed * m.vec[12:13]
            first = jnp.mean(grad_in, axis=1, keepdims=True)
            second = jnp.mean(grad_in * scaled, axis=1, keepdims=True)
            top = m.cot[rows].astype(f32)
            grad_hidden = top + m.i2[rows, 0:1] * (grad_in - first - scaled * second)
            m.s2[rows] = grad_hidden
            rounded = grad_hidden.astype(bf16)
            m.da[rows] = rounded
            m.gvec[11:12] += jnp.sum(rounded.astype(f32), axis=0, keepdims=True)
            m.gvec[12:13] += jnp.sum(grad_normed * scaled, axis=0, keepdims=True)
            m.gvec[13:14] += jnp.sum(grad_normed, axis=0, keepdims=True)
            m.gvec[14:15] += jnp.sum(top, axis=0, keepdims=True)

        row_loop(SEQ // 2, 32, rows_of, half * (SEQ // 2))

    def grad_mixed():
        m.dmt[...] = (jnp.transpose(dg(m.da[...], m.wo[...], 1, 1)) * valid).astype(bf16)

    def back_v_head(h):
        rows = head_rows(h)
        m.dvt[rows] = (dg(m.dmt[rows], m.wt[h], 1, 1) * valid).astype(bf16)

    def back_head(h):
        rows = head_rows(h)
        grad_scores = (dg(m.vt[rows], m.dmt[rows], 0, 0) * m.tt[h]).astype(bf16)
        m.dqt[rows] = (dg(m.kt[rows], grad_scores, 1, 0) * (1.0 / HEAD_SIZE)).astype(bf16)
        grad_keys = dg(m.qt[rows], grad_scores, 1, 1) * (1.0 / HEAD_SIZE) * valid
        m.dk[rows] = grad_keys
        grad_raw = grad_keys * m.vecc[rows, 5:6]
        for j in range(1, 4):
            grad_raw = grad_raw + lane_shift(grad_keys, j, True) * m.vecc[rows, 5 + j : 6 + j]
        m.dkt[rows] = grad_raw.astype(bf16)

    def pack(pair, which):
        y = ys[1 - which]
        rows = pl.ds(pl.multiple_of(y * 384, 384), 384)
        if pair == 0:
            grads = (dg(m.nmt[rows], m.dqt[...], 1, 1), dg(m.nmt[rows], m.dkt[...], 1, 1))
        else:
            grads = (dg(m.nmt[rows], m.dvt[...], 1, 1), dg(m.mt[rows], m.da[...], 1, 0))
        both_grads = jnp.concatenate([grad.reshape(4 * depth, 24, WIDTH) for grad in grads], axis=1)
        low = pl.ds(48 * pair, 48)
        m.qk[pl.ds(y * 4 * depth, 4 * depth), low, :] = both_grads.astype(bf16)
        for place in (2 * which, 2 * which + 1):
            yx = (k.ds, k.ys, k.xs, k.me)[place]
            source, target = pl.ds(in_all_sib(yx, 0), depth), pl.ds(yx * depth, depth)
            swap(16 + 4 * pair + place, m.qk.at[source, low], m.sr.at[target, low])

    def grad_normed():
        m.dn[...] = jnp.transpose(
            dg(m.wq[...], m.dqt[...], 1, 0) + dg(m.wk[...], m.dkt[...], 1, 0) + dg(m.wv[...], m.dvt[...], 1, 0)
        )

    def back1():
        def rows_of(start, step):
            rows = pl.ds(start, step)
            grad_out, scaled = m.dn[rows], m.s1[rows]
            grad_in = grad_out * m.vec[0:1]
            first = jnp.mean(grad_in, axis=1, keepdims=True)
            second = jnp.mean(grad_in * scaled, axis=1, keepdims=True)
            m.dinp[rows] = (m.s2[rows] + m.i1[rows, 0:1] * (grad_in - first - scaled * second)).astype(bf16)
            m.gvec[0:1] += jnp.sum(grad_out * scaled, axis=0, keepdims=True)
            m.gvec[1:2] += jnp.sum(grad_out, axis=0, keepdims=True)

        row_loop(SEQ, 32, rows_of)

    def core_sum(pair, place):
        yx, low = (k.ds, k.ys, k.xs, k.me)[place], pl.ds(48 * pair, 48)
        k.arrive(m.sr.at[pl.ds(yx * depth, depth), low], m.e_r.at[16 + 4 * pair + place])
        for zs in range(depth):
            add_into(m.qk.at[in_all(yx, zs), low], m.sr.at[yx * depth + zs, low])

    def flip():
        turn = (s_at + t_at == SEQ - 1).astype(bf16)
        m.kft[...] = dg(m.kt[...], turn, 1, 0).astype(bf16)
        m.vft[...] = dg(m.vt[...], turn, 1, 0).astype(bf16)

    def kernel_head(h):
        rows = head_rows(h)
        scores = dg(m.kft[rows], m.qt[rows], 0, 0) * (1.0 / HEAD_SIZE)
        grad_weights = dg(m.vft[rows], m.dmt[rows], 0, 0)
        product = jnp.where(s_at + t_at >= SEQ - 1, scores * grad_weights, 0.0)
        lined = pltpu.roll(product, 1, 1, stride=1, stride_axis=0)
        grad_kernel = jnp.sum(lined, axis=0, keepdims=True) * (1.0 / STATE)
        part = m.ex[rows] * grad_kernel
        at = lax.broadcasted_iota(jnp.int32, (HEAD_SIZE, 128), 1)
        grad_rate = -m.vecc[rows, 9:10] * jnp.sum(part * day, axis=1, keepdims=True)
        sums = jnp.where(at == 9, jnp.sum(part, axis=1, keepdims=True), 0.0)
        sums = jnp.where(at == 10, grad_rate, sums)
        raw, grad_keys = m.krt[rows], m.dk[rows]
        for j in range(4):
            tap = jnp.sum(grad_keys * (lane_shift(raw, j, False) if j else raw), axis=1, keepdims=True)
            sums = jnp.where(at == 5 + j, tap, sums)
        for place, value in ((2, m.dqt), (3, m.dkt), (4, m.dvt)):
            sums = jnp.where(at == place, jnp.sum(value[rows].astype(f32), axis=1, keepdims=True), sums)
        m.colsum[rows] = sums

    def vector_tiles():
        grads = m.gvec[...] + jnp.transpose(m.colsum[...])[0:16]
        row_at = lax.broadcasted_iota(jnp.int32, (16, 128), 0)
        lane_at = lax.broadcasted_iota(jnp.int32, (16, 128), 1)
        for wide in range(8):
            turned = (pltpu.roll(grads, WIDTH - 96 * wide, 1) if wide else grads)[:, :128]
            for zs in range(depth):
                tile = pltpu.roll(turned, 128 - 24 * zs, 1) if zs else turned
                tile = jnp.where((lane_at < 24) & (row_at < 15), tile, 0.0)
                own = jnp.concatenate([jnp.zeros((8, 128), f32), m.gbias[(wide // 4) * depth + zs]], axis=0)
                mine = (row_at == 15) & (core == wide % 2) & (k.x == wide // 2 % 2)
                m.gs[wide * depth + zs] = jnp.where(mine, own, tile)
        for yx in range(4):
            swap(24, m.gs.at[pl.ds(in_all_sib(yx, 0), depth)], m.srs.at[pl.ds(yx * depth, depth)])

    def small_sums():
        k.arrive(m.srs, m.e_r.at[24])
        for yx in range(4):
            for zs in range(depth):
                add_into(m.gs.at[in_all(yx, zs)], m.srs.at[yx * depth + zs])

    def finish_out():
        def rows_of(start, step):
            rows = pl.ds(start, step)
            others = m.outs[rows] + m.outx[1, rows].astype(f32)
            m.out[rows] = (m.hid[rows] + (m.outp[rows_at("o", start, step)] + others) + m.vec[14:15]).astype(bf16)

        k.arrive(m.outs, m.e_r.at[9])
        k.arrive(m.outx.at[1], m.e_r.at[15])
        row_loop(SEQ, 32, rows_of)

    def all_sent():
        for group in "SFLflqvs":
            next(steps[group + "."])
        extents = (m.qk.at[:, pl.ds(0, 80)], m.qk, m.srs)
        for place, extent in enumerate(extents):
            k.left(extent, m.e_s.at[place])

    compute = {
        "load": load, "own_blocks": own_blocks, "barrier": k.barrier, "own_cotangent": own_cotangent, "norm1": norm1, "pass_ct": pass_ct,
        "vectors": vectors, "mixer_kernels": mixer_kernels, "gain1": gain1, "project_qk": project_qk, "project_v": project_v,
        "hidden": hidden, "norm2": norm2, "sibling_rows": sibling_rows, "to_sibling": to_sibling,
        "out_to_diagonal": out_to_diagonal, "out_to_x": out_to_x, "grad_mixed": grad_mixed, "grad_normed": grad_normed,
        "back1": back1, "flip": flip, "vector_tiles": vector_tiles, "small_sums": small_sums, "finish_out": finish_out,
        "store": all_sent,
    }
    for which in range(2):
        compute["unpack%d" % which] = partial(unpack, which)
        compute["score%d" % which] = partial(heads, range(6 * which, 6 * which + 6), score_head)
        compute["mix%d" % which] = partial(heads, range(6 * which, 6 * which + 6), mix_head)
        compute["back_qk%d" % which] = partial(heads, range(6 * which, 6 * which + 6), back_head)
        compute["back_v%d" % which] = partial(heads, range(6 * which, 6 * which + 6), back_v_head)
        for who in "os":
            compute["feed%d%s" % (which, who)] = partial(feed, which, who)
        for who in "xd":
            for half in range(2):
                compute["feed%d%s%d" % (which, who, half)] = partial(feed, which, who, half)
        compute["feed_grads%d" % which] = partial(feed_grads, which)
        compute["pass_n2_%d" % which] = partial(pass_n2, which)
        compute["diagonal_rows%d" % which] = partial(diagonal_rows, which)
        compute["to_diagonal%d" % which] = partial(to_diagonal, which)
        compute["to_x%d" % which] = partial(to_x, which)
        compute["back2_%d" % which] = partial(back2, which)
        compute["pack_qk%d" % which] = partial(pack, 0, which)
        compute["pack_vo%d" % which] = partial(pack, 1, which)
    for which in range(4):
        compute["kernel%d" % which] = partial(heads, range(3 * which, 3 * which + 3), kernel_head)
        compute["sum_qk%d" % which] = partial(core_sum, 0, which)
        compute["sum_vo%d" % which] = partial(core_sum, 1, which)
    for step in PLAN:
        if step in compute:
            compute[step]()
        else:
            next(steps[step])


def results_kernel(*refs):
    sources, tile, targets, bias, vectors = refs[:8], refs[8], refs[9:17], refs[17], refs[18]
    for source, target in zip(sources, targets, strict=True):
        target[...] = source[...]
    bias[...] = tile[15:16, :UNITS]
    vectors[...] = tile[0:15, 0:24]


def on_device_fast(
    tokens, lengths, cotangent, w_query, w_key, w_value, w_out, w_fc1, w_fc2, fc1_bias, vectors
):
    depth = lax.axis_size("narrow")
    scratch = []
    for entry in scratch_of(depth).values():
        scratch.append(pltpu.SemaphoreType.DMA((entry,)) if isinstance(entry, int) else pltpu.VMEM(*entry))
    in_vmem = pl.BlockSpec(memory_space=pltpu.VMEM)
    in_smem = pl.BlockSpec(memory_space=pltpu.SMEM)
    shape = jax.ShapeDtypeStruct
    got = pl.pallas_call(
        partial(layer_kernel, depth),
        out_shape=[pltpu.VMEM((SEQ, WIDTH), bf16)] * 2
        + [pltpu.VMEM((24, WIDTH), f32)] * 4
        + [pltpu.VMEM((UNITS, WIDTH), f32)] * 2
        + [pltpu.VMEM((16, 128), f32)],
        in_specs=[in_smem] + [pl.BlockSpec(memory_space=pl.ANY)] * 10,
        out_specs=[in_vmem] * 9,
        scratch_shapes=scratch,
        compiler_params=pltpu.CompilerParams(
            collective_id=0, has_side_effects=True, vmem_limit_bytes=61 * 2**20
        ),
        name="h3_layer",
    )(
        lengths, tokens, cotangent, w_query, w_key, w_value, w_out, w_fc1.T, w_fc2, fc1_bias[None], vectors
    )
    results = pl.pallas_call(
        results_kernel,
        out_shape=[shape(x.shape, x.dtype) for x in got[:8]] + [shape((1, UNITS), f32), shape((15, 24), f32)],
        in_specs=[in_vmem] * 9,
        out_specs=[in_vmem] * 10,
        name="results",
    )(*[pltpu.with_memory_space_constraint(x, pltpu.VMEM) for x in got])
    out, grad_in, g_query, g_key, g_value, g_out, g_fc1, g_fc2, g_bias, g_vectors = results
    return out, grad_in, g_query, g_key, g_value, g_out, g_fc1.T, g_fc2, g_bias.reshape(-1), g_vectors


def fits(mesh):
    return mesh.shape["wide"] == 8 and mesh.shape["narrow"] == 4


def solution(mesh):
    placed = (
        P(("wide", "narrow"), None),
        P(("wide", "narrow")),
        P(("wide", "narrow"), None),
        P(("wide", "narrow"), None),
        P(("wide", "narrow"), None),
        P(("wide", "narrow"), None),
        P(("wide", "narrow"), None),
        P(None, ("wide", "narrow")),
        P(("wide", "narrow"), None),
        P(("wide", "narrow")),
        P(None, ("wide", "narrow")),
    )
    return jax.shard_map(
        on_device_fast if fits(mesh) else on_device,
        mesh=mesh,
        in_specs=placed,
        out_specs=(
            P(("wide", "narrow"), None),
            P(("wide", "narrow"), None),
            P(("wide", "narrow"), None),
            P(("wide", "narrow"), None),
            P(("wide", "narrow"), None),
            P(("wide", "narrow"), None),
            P(None, ("wide", "narrow")),
            P(("wide", "narrow"), None),
            P(("wide", "narrow")),
            P(None, ("wide", "narrow")),
        ),
        check_vma=False,
    )
```

```python
import math
from functools import partial
from types import SimpleNamespace

import jax
import jax.numpy as jnp
from jax import lax
from jax.experimental import pallas as pl
from jax.experimental.pallas import tpu as pltpu
from jax.sharding import PartitionSpec as P

HEAD_SIZE = 64
STATE = 64


EPSILON = 1e-05


def normalize(values):
    average = jnp.mean(values, axis=-1, keepdims=True)
    centred = values - average
    variance = jnp.mean(centred * centred, axis=-1, keepdims=True)
    inverse = lax.rsqrt(variance + EPSILON)
    return (centred * inverse, inverse)


def norm_back(grad_in, scaled, inverse):
    first = jnp.mean(grad_in, axis=-1, keepdims=True)
    second = jnp.mean(grad_in * scaled, axis=-1, keepdims=True)
    return inverse * (grad_in - first - scaled * second)


def shift_mix(key_raw, shift_taps):
    summed = key_raw * shift_taps[0]
    for offset in range(1, 4):
        delayed = jnp.concatenate(
            [jnp.zeros((offset, key_raw.shape[1]), key_raw.dtype), key_raw[:-offset]], axis=0
        )
        summed = summed + delayed * shift_taps[offset]
    return summed


def kernel_rows(coefficient, decay_rate, length_all):
    distance = jnp.arange(length_all).astype(jnp.float32)
    decays = jnp.exp(-decay_rate[:, :, None] * distance[None, None, :])
    return jnp.sum(coefficient[:, :, None] * decays, axis=1) / STATE


def toeplitz(kernel_row):
    length_all = kernel_row.shape[0]
    wrapped = jnp.concatenate(
        [kernel_row[:1], jnp.zeros((length_all,), kernel_row.dtype), kernel_row[:0:-1]]
    )
    tiled_row = jnp.tile(wrapped, length_all)[: length_all * (2 * length_all - 1)]
    return tiled_row.reshape(length_all, 2 * length_all - 1)[:, :length_all]


def split_heads(values, row_count):
    return values.reshape(row_count, -1, HEAD_SIZE).transpose(1, 0, 2)


def merge_heads(per_head):
    head_count = per_head.shape[0]
    row_count = per_head.shape[1]
    merged = per_head.transpose(1, 0, 2).reshape(row_count, head_count * HEAD_SIZE)
    return merged


def pack_rows(matrices, shard_count):
    return jnp.concatenate(
        [matrix.reshape(shard_count, -1) for matrix in matrices], axis=1
    ).reshape(-1)


def unpack_rows(flat, matrices, shard_count):
    pieces = []
    offset = 0
    for matrix in matrices:
        rows_own = matrix.shape[0] // shard_count
        extent = matrix.size // shard_count
        pieces.append(flat[offset : offset + extent].reshape((rows_own,) + matrix.shape[1:]))
        offset = offset + extent
    return pieces


def mixer_forward(queries, keys, values, kernel, row_count):

    def head_forward(parts):
        query_head, key_head, value_head, kernel_row = parts
        scores = jnp.dot(query_head, key_head.T, preferred_element_type=jnp.float32) / HEAD_SIZE
        weights_mix = (scores * toeplitz(kernel_row)).astype(jnp.bfloat16)
        return jnp.dot(weights_mix, value_head, preferred_element_type=jnp.float32)

    per_head = lax.map(
        head_forward,
        (
            split_heads(queries, row_count),
            split_heads(keys, row_count),
            split_heads(values, row_count),
            kernel,
        ),
    )
    return merge_heads(per_head)


def mixer_backward(queries, keys, values, grad_mixed, kernel, row_count):

    def head_backward(parts):
        query_head, key_head, value_head, grad_head, kernel_row = parts
        scores = jnp.dot(query_head, key_head.T, preferred_element_type=jnp.float32) / HEAD_SIZE
        toeplitz_mat, pullback = jax.vjp(toeplitz, kernel_row)
        weights_mix = (scores * toeplitz_mat).astype(jnp.bfloat16)
        grad_weights = jnp.dot(grad_head, value_head.T, preferred_element_type=jnp.float32)
        grad_values = jnp.dot(weights_mix.T, grad_head, preferred_element_type=jnp.float32)
        grad_scores = (grad_weights * toeplitz_mat).astype(jnp.bfloat16)
        grad_queries = (
            jnp.dot(grad_scores, key_head, preferred_element_type=jnp.float32) / HEAD_SIZE
        )
        grad_keys = (
            jnp.dot(grad_scores.T, query_head, preferred_element_type=jnp.float32) / HEAD_SIZE
        )
        grad_kernel = pullback(grad_weights * scores)[0]
        return (grad_queries, grad_keys, grad_values, grad_kernel)

    head_grads = lax.map(
        head_backward,
        (
            split_heads(queries, row_count),
            split_heads(keys, row_count),
            split_heads(values, row_count),
            split_heads(grad_mixed, row_count),
            kernel,
        ),
    )
    grad_kernel = head_grads[3]
    return (
        merge_heads(head_grads[0]),
        merge_heads(head_grads[1]),
        merge_heads(head_grads[2]),
        grad_kernel,
    )


def on_device(
    tokens, lengths, cotangent, w_query, w_key, w_value, w_out, w_fc1, w_fc2, fc1_bias, vectors
):
    shard_count = lax.axis_size(("wide", "narrow"))
    gathered = (
        lax.all_gather(w_query, ("wide", "narrow"), axis=0, tiled=True),
        lax.all_gather(w_key, ("wide", "narrow"), axis=0, tiled=True),
        lax.all_gather(w_value, ("wide", "narrow"), axis=0, tiled=True),
        lax.all_gather(w_out, ("wide", "narrow"), axis=0, tiled=True),
        lax.all_gather(w_fc1, ("wide", "narrow"), axis=1, tiled=True),
        lax.all_gather(w_fc2, ("wide", "narrow"), axis=0, tiled=True),
        lax.all_gather(fc1_bias, ("wide", "narrow"), axis=0, tiled=True),
        lax.all_gather(vectors, ("wide", "narrow"), axis=1, tiled=True),
    )
    query_full, key_full, value_full, out_full, fc1_full, fc2_full, bias_full, vector_full = (
        gathered
    )
    params = vector_full.astype(jnp.float32)
    fc1_shift = bias_full.astype(jnp.float32)
    seq_len = tokens.shape[0]
    head_count = params.shape[1] // HEAD_SIZE
    seq_length = lengths[0]
    valid_mask = (jnp.arange(seq_len) < seq_length).astype(jnp.float32)[:, None]
    residual = tokens.astype(jnp.float32)
    scaled1, inverse1 = normalize(residual)
    normed = (scaled1 * params[0] + params[1]).astype(jnp.bfloat16)
    queries = (jnp.dot(normed, query_full, preferred_element_type=jnp.float32) + params[2]).astype(
        jnp.bfloat16
    )
    key_raw = jnp.dot(normed, key_full, preferred_element_type=jnp.float32) + params[3]
    keys = (shift_mix(key_raw, params[5:9]) * valid_mask).astype(jnp.bfloat16)
    values = (
        (jnp.dot(normed, value_full, preferred_element_type=jnp.float32) + params[4]) * valid_mask
    ).astype(jnp.bfloat16)
    coefficient = params[9].reshape(head_count, STATE)
    decay_rate = params[10].reshape(head_count, STATE)
    kernel_fn = partial(kernel_rows, length_all=seq_len)
    kernel, kernel_pull = jax.vjp(kernel_fn, coefficient, decay_rate)
    mixed = mixer_forward(queries, keys, values, kernel, seq_len)
    mixed_out = (mixed * valid_mask).astype(jnp.bfloat16)
    hidden = (
        residual + jnp.dot(mixed_out, out_full, preferred_element_type=jnp.float32) + params[11]
    )
    scaled2, inverse2 = normalize(hidden)
    normed2 = (scaled2 * params[12] + params[13]).astype(jnp.bfloat16)
    pre_act = jnp.dot(normed2, fc1_full, preferred_element_type=jnp.float32) + fc1_shift
    activated = jax.nn.gelu(pre_act).astype(jnp.bfloat16)
    output = (
        hidden + jnp.dot(activated, fc2_full, preferred_element_type=jnp.float32) + params[14]
    ).astype(jnp.bfloat16)
    again = (
        lax.all_gather(w_query, ("wide", "narrow"), axis=0, tiled=True),
        lax.all_gather(w_key, ("wide", "narrow"), axis=0, tiled=True),
        lax.all_gather(w_value, ("wide", "narrow"), axis=0, tiled=True),
        lax.all_gather(w_out, ("wide", "narrow"), axis=0, tiled=True),
        lax.all_gather(w_fc1, ("wide", "narrow"), axis=1, tiled=True),
        lax.all_gather(w_fc2, ("wide", "narrow"), axis=0, tiled=True),
        lax.all_gather(fc1_bias, ("wide", "narrow"), axis=0, tiled=True),
        lax.all_gather(vectors, ("wide", "narrow"), axis=1, tiled=True),
    )
    query_back, key_back, value_back, out_back, fc1_back, fc2_back = (
        again[0],
        again[1],
        again[2],
        again[3],
        again[4],
        again[5],
    )
    grad_top = cotangent.astype(jnp.float32)
    grad_fc2 = jnp.dot(activated.T, cotangent, preferred_element_type=jnp.float32)
    grad_activated = jnp.dot(cotangent, fc2_back.T, preferred_element_type=jnp.float32)
    gelu_value, gelu_pull = jax.vjp(jax.nn.gelu, pre_act)
    grad_pre = gelu_pull(grad_activated)[0].astype(jnp.bfloat16)
    grad_fc1_turned = jnp.dot(grad_pre.T, normed2, preferred_element_type=jnp.float32)
    grad_fc1_bias = jnp.sum(grad_pre.astype(jnp.float32), axis=0)[:, None]
    mlp_terms = [grad_fc1_turned, grad_fc2, grad_fc1_bias]
    mlp_flat = lax.psum_scatter(
        pack_rows(mlp_terms, shard_count), ("wide", "narrow"), scatter_dimension=0, tiled=True
    )
    mlp_sums = unpack_rows(mlp_flat, mlp_terms, shard_count)
    grad_normed2 = jnp.dot(grad_pre, fc1_back.T, preferred_element_type=jnp.float32)
    grad_hidden = grad_top + norm_back(grad_normed2 * params[12], scaled2, inverse2)
    grad_attn = grad_hidden.astype(jnp.bfloat16)
    grad_out = jnp.dot(mixed_out.T, grad_attn, preferred_element_type=jnp.float32)
    grad_mixed = (
        jnp.dot(grad_attn, out_back.T, preferred_element_type=jnp.float32) * valid_mask
    ).astype(jnp.bfloat16)
    grad_q, grad_k, grad_v, grad_kernel = mixer_backward(
        queries, keys, values, grad_mixed, kernel, seq_len
    )
    grad_queries = grad_q.astype(jnp.bfloat16)
    grad_values = (grad_v * valid_mask).astype(jnp.bfloat16)
    shift_value, shift_pull = jax.vjp(shift_mix, key_raw, params[5:9])
    grad_key_full, grad_taps = shift_pull(grad_k * valid_mask)
    grad_key_raw = grad_key_full.astype(jnp.bfloat16)
    grad_query = jnp.dot(normed.T, grad_queries, preferred_element_type=jnp.float32)
    grad_key = jnp.dot(normed.T, grad_key_raw, preferred_element_type=jnp.float32)
    grad_value = jnp.dot(normed.T, grad_values, preferred_element_type=jnp.float32)
    grad_normed = jnp.dot(grad_queries, query_back.T, preferred_element_type=jnp.float32)
    grad_normed = grad_normed + jnp.dot(
        grad_key_raw, key_back.T, preferred_element_type=jnp.float32
    )
    grad_normed = grad_normed + jnp.dot(
        grad_values, value_back.T, preferred_element_type=jnp.float32
    )
    input_grad = (grad_hidden + norm_back(grad_normed * params[0], scaled1, inverse1)).astype(
        jnp.bfloat16
    )
    grad_coef, grad_rate = kernel_pull(grad_kernel)
    grad_vectors = jnp.concatenate(
        [
            jnp.sum(grad_normed * scaled1, axis=0)[None],
            jnp.sum(grad_normed, axis=0)[None],
            jnp.sum(grad_queries.astype(jnp.float32), axis=0)[None],
            jnp.sum(grad_key_raw.astype(jnp.float32), axis=0)[None],
            jnp.sum(grad_values.astype(jnp.float32), axis=0)[None],
            grad_taps,
            grad_coef.reshape(1, -1),
            grad_rate.reshape(1, -1),
            jnp.sum(grad_attn.astype(jnp.float32), axis=0)[None],
            jnp.sum(grad_normed2 * scaled2, axis=0)[None],
            jnp.sum(grad_normed2, axis=0)[None],
            jnp.sum(grad_top, axis=0)[None],
        ],
        axis=0,
    )
    mixer_terms = [grad_query, grad_key, grad_value, grad_out, grad_vectors.T]
    mixer_flat = lax.psum_scatter(
        pack_rows(mixer_terms, shard_count), ("wide", "narrow"), scatter_dimension=0, tiled=True
    )
    mixer_sums = unpack_rows(mixer_flat, mixer_terms, shard_count)
    return (
        output,
        input_grad,
        mixer_sums[0],
        mixer_sums[1],
        mixer_sums[2],
        mixer_sums[3],
        mlp_sums[0].T,
        mlp_sums[1],
        mlp_sums[2].reshape(-1),
        mixer_sums[4].T,
    )


f32, bf16 = jnp.float32, jnp.bfloat16
MESH = pl.DeviceIdType.MESH


def dg(left, right, left_dim, right_dim):
    return lax.dot_general(
        left, right, (((left_dim,), (right_dim,)), ((), ())), preferred_element_type=f32
    )


def when(condition, body):
    if condition is None:
        body()
    else:
        pl.when(condition)(body)


def both(first, second):
    if first is None:
        return second
    if second is None:
        return first
    return jnp.logical_and(first, second)


class Links:
    def __init__(self, depth):
        wide, z = lax.axis_index("wide"), lax.axis_index("narrow")
        self.depth = depth
        self.z, self.core = z, lax.rem(wide, 2)
        self.x, self.y = lax.rem(lax.div(wide, 2), 2), lax.div(wide, 4)
        self.me = self.y * 2 + self.x
        self.xs = self.y * 2 + (1 - self.x)
        self.ys = (1 - self.y) * 2 + self.x
        self.ds = (1 - self.y) * 2 + (1 - self.x)
        self.sib_dev = (self.me * 2 + (1 - self.core), z)
        self.x_dev = (self.xs * 2 + self.core, z)
        self.y_dev = (self.ys * 2 + self.core, z)
        self.up_dev = (wide, z + 1)
        self.down_dev = (wide, z - 1)
        self.has_up = z < depth - 1
        self.has_down = z > 0
        self.at_end = jnp.logical_or(z == 0, z == depth - 1)

    def barrier(self):
        semaphore = pltpu.get_barrier_semaphore()

        def greet(device):
            pl.semaphore_signal(semaphore, inc=1, device_id=device, device_id_type=MESH)

        for device in (self.sib_dev, self.x_dev, self.y_dev):
            greet(device)
        pl.when(self.has_up)(lambda: greet(self.up_dev))
        pl.when(self.has_down)(lambda: greet(self.down_dev))
        peers = 3 + self.has_up.astype(jnp.int32) + self.has_down.astype(jnp.int32)
        pl.semaphore_wait(semaphore, peers)

    def start(self, condition, source, target, send, receive, device):
        when(
            condition,
            lambda: pltpu.make_async_remote_copy(
                src_ref=source(),
                dst_ref=target(),
                send_sem=send,
                recv_sem=receive,
                device_id=device,
                device_id_type=MESH,
            ).start(),
        )

    def arrive(self, target, receive):
        pltpu.make_async_remote_copy(
            src_ref=target,
            dst_ref=target,
            send_sem=receive,
            recv_sem=receive,
            device_id=self.sib_dev,
            device_id_type=MESH,
        ).wait_recv()

    def left(self, extent, semaphore):
        pltpu.make_async_remote_copy(
            src_ref=extent,
            dst_ref=extent,
            send_sem=semaphore,
            recv_sem=semaphore,
            device_id=self.sib_dev,
            device_id_type=MESH,
        ).wait_send()

    def left_along(self, extent, semaphore):
        pl.when(self.at_end)(lambda: self.left(extent(1), semaphore))
        pl.when(jnp.logical_not(self.at_end))(lambda: self.left(extent(self.depth + 1), semaphore))


def halved(ref, piece):
    rows, lanes = ref.shape[-2:]
    if lanes == 128:
        return ref.at[pl.ds(piece * (rows // 2), rows // 2)]
    return ref.at[:, pl.ds(piece * (lanes // 2), lanes // 2)]


def near(k, distance):
    if distance == 0:
        return ((None, k.z, False),)
    return ((k.z >= distance, k.z - distance, True), (k.z + distance < k.depth, k.z + distance, False))


def gather_z_first(k, name, buf, index, low, rows, ss, rs):
    depth = k.depth

    def block(yx, zs):
        return buf.at[index(yx, zs), pl.ds(low, rows)]

    def send(condition, yx, zs, device, r, way=0, piece=None):
        ref = lambda: block(yx, zs) if piece is None else halved(block(yx, zs), piece)
        k.start(condition, ref, ref, ss.at[way], rs.at[r], device)

    def to_sib(condition, yx, zs):
        send(condition, yx, zs, k.sib_dev, 4 * depth)

    def outward(condition, zs):
        send(condition, k.me, zs, k.x_dev, depth + zs)
        send(condition, k.me, zs, k.y_dev, 2 * depth + zs)
        to_sib(condition, k.me, zs)

    def along(condition, zs, up, down):
        if up:
            send(both(condition, k.has_up), k.me, zs, k.up_dev, zs, 1)
        if down:
            send(both(condition, k.has_down), k.me, zs, k.down_dev, zs, 1)

    def take(condition, yx, zs, r):
        when(condition, lambda: k.arrive(block(yx, zs), rs.at[r]))

    def own():
        along(None, k.z, True, True)
        outward(None, k.z)
        yield

    def z_steps():
        for d in range(1, depth):
            for condition, zs, below in near(k, d):
                take(condition, k.me, zs, zs)
                along(condition, zs, below, not below)
                outward(condition, zs)
            yield

    def x_steps():
        for d in range(depth):
            for condition, zs, _ in near(k, d):
                take(condition, k.xs, zs, depth + zs)
                send(condition, k.xs, zs, k.y_dev, 3 * depth + zs, piece=0)
                to_sib(condition, k.xs, zs)
            yield

    def y_steps():
        for d in range(depth):
            for condition, zs, _ in near(k, d):
                take(condition, k.ys, zs, 2 * depth + zs)
                send(condition, k.ys, zs, k.x_dev, 3 * depth + zs, piece=1)
                to_sib(condition, k.ys, zs)
            yield

    def d_steps():
        for d in range(depth):
            for condition, zs, _ in near(k, d):
                take(condition, k.ds, zs, 3 * depth + zs)
                to_sib(condition, k.ds, zs)
            yield

    def extent(blocks):
        return buf.at[pl.ds(0, blocks), pl.ds(low, rows)]

    def sib_steps():
        k.arrive(extent(4 * depth), rs.at[4 * depth])
        yield

    def left():
        k.left(extent(7 * depth), ss.at[0])
        k.left_along(extent, ss.at[1])
        yield

    steps = {"0": own(), "z": z_steps(), "x": x_steps(), "y": y_steps(), "d": d_steps(), "s": sib_steps(), ".": left()}
    return {name + key: step for key, step in steps.items()}


def gather_pair_z_first(k, name, buf, index, low, rows, ss, rs):
    depth = k.depth

    def block(yx, zs):
        return buf.at[index(yx, zs), pl.ds(low, rows)]

    def extent(blocks):
        return buf.at[pl.ds(0, blocks), pl.ds(low, rows)]

    def send(condition, zs, device, r, way):
        ref = lambda: block(k.me, zs)
        k.start(condition, ref, ref, ss.at[way], rs.at[r], device)

    def along(condition, zs, up, down):
        if up:
            send(both(condition, k.has_up), zs, k.up_dev, zs, 1)
        if down:
            send(both(condition, k.has_down), zs, k.down_dev, zs, 1)

    def own():
        along(None, k.z, True, True)
        send(None, k.z, k.y_dev, depth + k.z, 0)
        yield

    def z_steps():
        for d in range(1, depth):
            for condition, zs, below in near(k, d):
                when(condition, lambda zs=zs: k.arrive(block(k.me, zs), rs.at[zs]))
                along(condition, zs, below, not below)
                send(condition, zs, k.y_dev, depth + zs, 0)
            yield

    def y_steps():
        for d in range(depth):
            for condition, zs, _ in near(k, d):
                when(condition, lambda zs=zs: k.arrive(block(k.ys, zs), rs.at[depth + zs]))
            yield

    def left():
        k.left(extent(depth), ss.at[0])
        k.left_along(extent, ss.at[1])
        yield

    steps = {"0": own(), "z": z_steps(), "y": y_steps(), ".": left()}
    return {name + key: step for key, step in steps.items()}


def gather_pair_z_last(k, name, buf, index, low, rows, ss, rs):
    depth = k.depth
    yx_of = (k.me, k.ys)

    def block(yx, zs):
        return buf.at[index(yx, zs), pl.ds(low, rows)]

    def extent(blocks):
        return buf.at[pl.ds(0, blocks), pl.ds(low, rows)]

    def send(condition, yx, zs, device, r, way):
        ref = lambda: block(yx, zs)
        k.start(condition, ref, ref, ss.at[way], rs.at[r], device)

    def along(condition, which, zs, up, down):
        place = 1 + which * depth + zs
        if up:
            send(both(condition, k.has_up), yx_of[which], zs, k.up_dev, place, 1 + which)
        if down:
            send(both(condition, k.has_down), yx_of[which], zs, k.down_dev, place, 1 + which)

    def own():
        send(None, k.me, k.z, k.y_dev, 0, 0)
        along(None, 0, k.z, True, True)
        yield

    def y_step():
        k.arrive(block(k.ys, k.z), rs.at[0])
        along(None, 1, k.z, True, True)
        yield

    def z_steps(which):
        for d in range(1, depth):
            for condition, zs, below in near(k, d):
                when(condition, lambda zs=zs: k.arrive(block(yx_of[which], zs), rs.at[1 + which * depth + zs]))
                along(condition, which, zs, below, not below)
            yield

    def left():
        k.left(extent(1), ss.at[0])
        for which in range(2):
            k.left_along(extent, ss.at[1 + which])
        yield

    steps = {"0": own(), "y": y_step(), "4": z_steps(0), "5": z_steps(1), ".": left()}
    return {name + key: step for key, step in steps.items()}


def add_into(ref, *others):
    total = ref[...].astype(f32)
    for other in others:
        total = total + other[...].astype(f32)
    ref[...] = total.astype(ref.dtype)


def scatter_order(depth):
    return ([0, depth - 1] + list(range(1, depth - 1)))[:depth]


def along_z(k, zd, wave, block, from_up, from_down, rs_up, rs_down, send):
    top, low = k.depth - 1 - wave, wave

    def take(slot, semaphore):
        k.arrive(slot, semaphore)
        add_into(block, slot)

    if zd < top:
        if wave:
            pl.when(k.z == top)(lambda: take(from_up, rs_up))
        send(k.z == top, False)
    if zd > low:
        if wave:
            pl.when(k.z == low)(lambda: take(from_down, rs_down))
        send(k.z == low, True)


def scatter_z_last(k, name, buf, index, low, rows, slots, ss, rs, finish):
    depth = k.depth
    from_x_diag, from_y_diag, from_xy, from_up, from_down = slots
    distances = range(depth - 1, -1, -1)

    def block(yx, zd):
        return buf.at[index(yx, zd), pl.ds(low, rows)]

    def half(yx, zd, piece):
        return halved(block(yx, zd), piece)

    def send(condition, source, target, device, r):
        k.start(condition, source, target, ss.at[0], rs.at[r], device)

    def x_part(zd, piece):
        return halved(from_xy.at[zd, 0], piece)

    def y_part(zd, piece):
        return halved(from_xy.at[zd, 1], piece)

    def pure_x():
        for d in distances:
            for condition, zd, _ in near(k, d):
                send(condition, lambda zd=zd: half(k.xs, zd, 1), lambda zd=zd: x_part(zd, 1), k.x_dev, 2 * depth + zd)
            yield

    def pure_y():
        for d in distances:
            for condition, zd, _ in near(k, d):
                send(condition, lambda zd=zd: half(k.ys, zd, 0), lambda zd=zd: y_part(zd, 0), k.y_dev, 2 * depth + zd)
            yield

    def diagonal():
        for d in distances:
            for condition, zd, _ in near(k, d):
                send(condition, lambda zd=zd: half(k.ds, zd, 0), lambda zd=zd: from_y_diag.at[zd], k.y_dev, zd)
                send(condition, lambda zd=zd: half(k.ds, zd, 1), lambda zd=zd: from_x_diag.at[zd], k.x_dev, depth + zd)
            yield

    def y_added():
        for d in distances:
            for condition, zd, _ in near(k, d):

                def take(zd=zd):
                    k.arrive(from_y_diag.at[zd], rs.at[zd])
                    add_into(half(k.xs, zd, 0), from_y_diag.at[zd])

                when(condition, take)
                send(condition, lambda zd=zd: half(k.xs, zd, 0), lambda zd=zd: x_part(zd, 0), k.x_dev, 2 * depth + zd)
            yield

    def x_added():
        for d in distances:
            for condition, zd, _ in near(k, d):

                def take(zd=zd):
                    k.arrive(from_x_diag.at[zd], rs.at[depth + zd])
                    add_into(half(k.ys, zd, 1), from_x_diag.at[zd])

                when(condition, take)
                send(condition, lambda zd=zd: half(k.ys, zd, 1), lambda zd=zd: y_part(zd, 1), k.y_dev, 2 * depth + zd)
            yield

    def send_z(condition, zd, down):
        place, slot = (3 * depth + zd, from_up) if down else (4 * depth + zd, from_down)
        send(condition, lambda: block(k.me, zd), lambda: slot.at[zd], k.down_dev if down else k.up_dev, place)

    def collect():
        for d in distances:
            for condition, zd, below in near(k, d):

                def take(zd=zd):
                    k.arrive(from_xy.at[zd], rs.at[2 * depth + zd])
                    add_into(block(k.me, zd), from_xy.at[zd, 0], from_xy.at[zd, 1])

                when(condition, take)
                if d:
                    send_z(both(condition, jnp.logical_not(k.has_up if below else k.has_down)), zd, below)
            yield

    def between():
        for d in range(depth - 2, 0, -1):
            for condition, zd, below in near(k, d):
                condition = both(condition, k.has_up if below else k.has_down)
                slot, semaphore = (from_up, rs.at[3 * depth + zd]) if below else (from_down, rs.at[4 * depth + zd])

                def take(zd=zd, slot=slot, semaphore=semaphore):
                    k.arrive(slot.at[zd], semaphore)
                    add_into(block(k.me, zd), slot.at[zd])

                pl.when(condition)(take)
                send_z(condition, zd, below)
            yield

    def end():
        finish(block(k.me, k.z), False)

        def last_up():
            k.arrive(from_up.at[k.z], rs.at[3 * depth + k.z])
            finish(from_up.at[k.z], True)

        def last_down():
            k.arrive(from_down.at[k.z], rs.at[4 * depth + k.z])
            finish(from_down.at[k.z], True)

        pl.when(k.has_up)(last_up)
        pl.when(k.has_down)(last_down)
        yield

    def left():
        k.left(buf.at[pl.ds(0, 4 * depth - 1), pl.ds(low, rows)], ss.at[0])
        yield

    steps = {"X": pure_x(), "Y": pure_y(), "D": diagonal(), "a": y_added(), "b": x_added(), "c": collect(), "e": end()}
    steps |= {"v": between(), ".": left()}
    return {name + key: step for key, step in steps.items()}


def scatter_pair_z_last(k, name, buf, index, low, rows, slots, ss, rs, finish):
    depth = k.depth
    from_y, from_up, from_down = slots
    distances = range(depth - 1, -1, -1)

    def block(yx, zd):
        return buf.at[index(yx, zd), pl.ds(low, rows)]

    def send(condition, source, target, device, r):
        k.start(condition, source, target, ss.at[0], rs.at[r], device)

    def pure_y():
        for d in distances:
            for condition, zd, _ in near(k, d):
                send(condition, lambda zd=zd: block(k.ys, zd), lambda zd=zd: from_y.at[zd], k.y_dev, zd)
            yield

    def send_z(condition, zd, down):
        place, slot = (depth + zd, from_up) if down else (2 * depth + zd, from_down)
        send(condition, lambda: block(k.me, zd), lambda: slot.at[zd], k.down_dev if down else k.up_dev, place)

    def collect():
        for d in distances:
            for condition, zd, below in near(k, d):

                def take(zd=zd):
                    k.arrive(from_y.at[zd], rs.at[zd])
                    add_into(block(k.me, zd), from_y.at[zd])

                when(condition, take)
                if d:
                    send_z(both(condition, jnp.logical_not(k.has_up if below else k.has_down)), zd, below)
            yield

    def between():
        for d in range(depth - 2, 0, -1):
            for condition, zd, below in near(k, d):
                condition = both(condition, k.has_up if below else k.has_down)
                slot, semaphore = (from_up, rs.at[depth + zd]) if below else (from_down, rs.at[2 * depth + zd])

                def take(zd=zd, slot=slot, semaphore=semaphore):
                    k.arrive(slot.at[zd], semaphore)
                    add_into(block(k.me, zd), slot.at[zd])

                pl.when(condition)(take)
                send_z(condition, zd, below)
            yield

    def end():
        finish(block(k.me, k.z), False)

        def last_up():
            k.arrive(from_up.at[k.z], rs.at[depth + k.z])
            finish(from_up.at[k.z], True)

        def last_down():
            k.arrive(from_down.at[k.z], rs.at[2 * depth + k.z])
            finish(from_down.at[k.z], True)

        pl.when(k.has_up)(last_up)
        pl.when(k.has_down)(last_down)
        yield

    def left():
        k.left(buf.at[pl.ds(0, 2 * depth - 1), pl.ds(low, rows)], ss.at[0])
        yield

    steps = {"Y": pure_y(), "c": collect(), "v": between(), "e": end(), ".": left()}
    return {name + key: step for key, step in steps.items()}


def scatter_pair_z_first(k, name, buf, index, low, rows, slots, ss, rs, finish):
    depth = k.depth
    from_y, from_up, from_down = slots
    yx_of = (k.me, k.ys)

    def block(yx, zd):
        return buf.at[index(yx, zd), pl.ds(low, rows)]

    def send(condition, source, target, device, r):
        k.start(condition, source, target, ss.at[0], rs.at[r], device)

    def waves(which):
        yx = yx_of[which]
        for number in range(depth - 1):
            for zd in scatter_order(depth):
                place = which * depth + zd

                def send_z(condition, up, zd=zd, place=place):
                    slot, number = (from_down, 2 * depth + place) if up else (from_up, place)
                    send(condition, lambda: block(yx, zd), lambda: slot.at[place], k.up_dev if up else k.down_dev, number)

                along_z(
                    k, zd, number, block(yx, zd), from_up.at[place], from_down.at[place],
                    rs.at[place], rs.at[2 * depth + place], send_z,
                )
            yield

    def own(which):
        yx = yx_of[which]
        place = which * depth + k.z

        def take(slot, semaphore):
            k.arrive(slot, semaphore)
            add_into(block(yx, k.z), slot)

        pl.when(k.has_up)(lambda: take(from_up.at[place], rs.at[place]))
        pl.when(k.has_down)(lambda: take(from_down.at[place], rs.at[2 * depth + place]))

    def own_me():
        own(0)
        yield

    def own_y():
        own(1)
        send(None, lambda: block(k.ys, k.z), lambda: from_y.at[0], k.y_dev, 4 * depth)
        yield

    def end():
        k.arrive(from_y.at[0], rs.at[4 * depth])
        finish(block(k.me, k.z), False)
        finish(from_y.at[0], True)
        yield

    def left():
        k.left(buf.at[pl.ds(0, 2 * depth - 1), pl.ds(low, rows)], ss.at[0])
        yield

    steps = {"0": waves(0), "1": waves(1), "O": own_me(), "Y": own_y(), "e": end(), ".": left()}
    return {name + key: step for key, step in steps.items()}


SEQ, WIDTH, UNITS = 256, 768, 96
HEADS = WIDTH // HEAD_SIZE
FIRST = 112


def row_loop(total, step, body, first=0):
    def once(i, carry):
        for part in range(4):
            body(pl.multiple_of(first + (i * 4 + part) * step, step), step)
        return carry

    lax.fori_loop(0, total // (step * 4), once, 0)


def lane_shift(values, offset, left):
    extent = values.shape[1]
    lane = lax.broadcasted_iota(jnp.int32, values.shape, 1)
    if left:
        return jnp.where(lane < extent - offset, pltpu.roll(values, extent - offset, 1), 0.0)
    return jnp.where(lane >= offset, pltpu.roll(values, offset, 1), 0.0)


def heads(which, body):
    for h in which:
        body(h)


def head_rows(h):
    return pl.ds(pl.multiple_of(h * HEAD_SIZE, HEAD_SIZE), HEAD_SIZE)


def scratch_of(depth):
    devices, blocks, half = 8 * depth, 4 * depth, 2 * depth
    table = {
        "qk": ((devices, UNITS, WIDTH), bf16),
        "ff": ((half, 2 * UNITS, WIDTH), bf16),
        "sm": ((devices, 16, 128), f32),
        "gff": ((half, 2 * UNITS, WIDTH), bf16),
        "gs": ((devices, 16, 128), f32),
        "sr": ((blocks, UNITS, WIDTH), bf16),
        "srs": ((blocks, 16, 128), f32),
        "wq": ((WIDTH, WIDTH), bf16),
        "wk": ((WIDTH, WIDTH), bf16),
        "wv": ((WIDTH, WIDTH), bf16),
        "wo": ((WIDTH, WIDTH), bf16),
        "s1": ((SEQ, WIDTH), f32),
        "i1": ((SEQ, 128), f32),
        "nm": ((SEQ, WIDTH), bf16),
        "hid": ((SEQ, WIDTH), f32),
        "s2": ((SEQ, WIDTH), f32),
        "i2": ((SEQ, 128), f32),
        "n2": ((4 * SEQ, WIDTH), bf16),
        "ct": ((4 * SEQ, WIDTH), bf16),
        "outp": ((4 * SEQ, WIDTH), f32),
        "dn2": ((4 * SEQ, WIDTH), f32),
        "outs": ((SEQ, WIDTH), f32),
        "dn2s": ((SEQ, WIDTH), f32),
        "outb": ((SEQ, WIDTH), f32),
        "dn2b": ((SEQ, WIDTH), f32),
        "outx": ((2, SEQ, WIDTH), bf16),
        "dn2x": ((2, SEQ, WIDTH), bf16),
        "act": ((2, 4 * SEQ, UNITS * depth), bf16),
        "dp": ((2, 4 * SEQ, UNITS * depth), bf16),
        "da": ((SEQ, WIDTH), bf16),
        "dk": ((WIDTH, SEQ), f32),
        "dn": ((SEQ, WIDTH), f32),
        "nmt": ((WIDTH, SEQ), bf16),
        "qt": ((WIDTH, SEQ), bf16),
        "kt": ((WIDTH, SEQ), bf16),
        "vt": ((WIDTH, SEQ), bf16),
        "wt": ((HEADS, SEQ, SEQ), bf16),
        "krt": ((WIDTH, SEQ), f32),
        "mt": ((WIDTH, SEQ), bf16),
        "dmt": ((WIDTH, SEQ), bf16),
        "dqt": ((WIDTH, SEQ), bf16),
        "dkt": ((WIDTH, SEQ), bf16),
        "dvt": ((WIDTH, SEQ), bf16),
        "kft": ((WIDTH, SEQ), bf16),
        "vft": ((WIDTH, SEQ), bf16),
        "ex": ((WIDTH, SEQ), f32),
        "tt": ((HEADS, SEQ, SEQ), f32),
        "vec": ((16, WIDTH), f32),
        "vecc": ((WIDTH, 128), f32),
        "colsum": ((WIDTH, 128), f32),
        "gvec": ((16, WIDTH), f32),
        "bias": ((2, 8, UNITS * depth), f32),
        "gbias": ((half, 8, 128), f32),
    }
    for name, rows, lanes, kind in (("q", 48, WIDTH, bf16), ("v", 48, WIDTH, bf16), ("t", 16, 128, f32)):
        part = (rows, lanes // 2) if lanes == WIDTH else (rows // 2, lanes)
        table["r" + name + "dx"] = table["r" + name + "dy"] = ((depth,) + part, kind)
        table["r" + name + "xy"] = ((depth, 2, rows, lanes), kind)
        table["r" + name + "u"] = table["r" + name + "d"] = ((depth, rows, lanes), kind)
    table["rby"] = table["rbu"] = table["rbd"] = ((depth, FIRST, WIDTH), bf16)
    table["rcy"] = ((1, 2 * UNITS - FIRST, WIDTH), bf16)
    table["rcu"] = table["rcd"] = ((half, 2 * UNITS - FIRST, WIDTH), bf16)
    table["tok"] = table["cot"] = ((SEQ, WIDTH), bf16)
    for name in ("iq", "ik", "iv", "io"):
        table[name] = ((24, WIDTH), bf16)
    table["ifc1"] = table["ifc2"] = ((UNITS, WIDTH), bf16)
    table["ibias"], table["ivec"] = ((1, UNITS), bf16), ((15, 24), bf16)
    table["load"] = len(OPERANDS)
    for name, sent, came in (
        ("gq", 2, 4 * depth + 1), ("gv", 2, 4 * depth + 1), ("gb", 2, 2 * depth), ("gt", 2, 4 * depth + 1), ("gc", 3, 2 * depth + 1),
        ("sq", 1, 5 * depth), ("sv", 1, 5 * depth), ("sb", 1, 3 * depth), ("st", 1, 5 * depth), ("sc", 1, 4 * depth + 1), ("e", 3, 25),
    ):
        table[name + "_s"], table[name + "_r"] = sent, came
    return table


PLAN = (
    0, 2, 1, 69, 83, 76, 70, 71, 86, 72, 94, 84, 70, 77, 85, 79, 84, 71, 86, 71, 77, 70, 96, 84, 72, 85, 77,
    73, 95, 71, 72, 79, 85, 78, 78, 78, 87, 78, 85, 90, 96, 73, 72, 87, 73, 86, 79, 79, 73, 74, 86, 6, 3, 80,
    7, 80, 87, 91, 80, 80, 4, 8, 87, 81, 25, 96, 9, 88, 41, 10, 26, 42, 91, 27, 43, 11, 12, 97, 13, 92, 91, 5,
    30, 97, 34, 35, 31, 92, 92, 89, 97, 92, 47, 36, 50, 46, 37, 51, 32, 48, 52, 49, 99, 82, 15, 99, 105, 14,
    53, 33, 99, 16, 99, 104, 20, 38, 54, 17, 29, 45, 40, 28, 44, 39, 56, 105, 59, 121, 60, 58, 100, 112, 121,
    112, 55, 62, 61, 121, 65, 123, 121, 120, 112, 119, 114, 100, 18, 120, 104, 114, 64, 112, 122, 111, 57,
    111, 66, 110, 110, 68, 113, 101, 119, 124, 122, 123, 113, 111, 113, 100, 119, 19, 123, 63, 21, 105, 104,
    67, 22, 130, 130, 128, 115, 120, 124, 122, 130, 126, 128, 129, 120, 131, 101, 23, 129, 119, 132, 122, 132,
    128, 131, 110, 129, 123, 114, 115, 131, 130, 113, 117, 107, 133, 124, 100, 133, 126, 132, 115, 111, 102,
    106, 124, 114, 135, 129, 117, 110, 133, 128, 135, 132, 131, 125, 108, 115, 116, 133, 134, 24,
)
OPERANDS = ("tok", "cot", "iq", "ik", "iv", "io", "ifc1", "ifc2", "ibias", "ivec")
INPUTS = ("length",) + tuple("from_" + name for name in OPERANDS)
RESULTS = ("out", "dinp", "gwq", "gwk", "gwv", "gwo", "gfc1", "gfc2", "gsmall")
OUTPUTS = RESULTS


def layer_kernel(depth, *refs):
    names = INPUTS + OUTPUTS + tuple(scratch_of(depth))
    m = SimpleNamespace(**dict(zip(names, refs, strict=True)))
    k = Links(depth)
    core = k.core

    def in_all(yx, zs):
        return (yx * 2 + core) * depth + zs

    def in_all_sib(yx, zs):
        return (yx * 2 + (1 - core)) * depth + zs

    def in_pair(yx, zs):
        return lax.div(yx, 2) * depth + zs

    places = {"o": (k.x, core), "s": (k.x, 1 - core), "x": (1 - k.x, core), "d": (1 - k.x, 1 - core)}
    part_rows = SEQ // 2

    def rows_at(who, start, step):
        x, c = places[who]
        half, inside = (lax.div(start, part_rows), lax.rem(start, part_rows)) if hasattr(start, "dtype") else divmod(start, part_rows)
        return pl.ds(pl.multiple_of(x * (2 * SEQ) + half * SEQ + c * part_rows + inside, step), step)

    def sent_by(place):
        return 2 if place == 24 else 1 if place in (9, 10, 11, 12) or place >= 16 else 0

    def swap(place, source, target, device=None):
        k.start(None, lambda: source, lambda: target, m.e_s.at[sent_by(place)], m.e_r.at[place], device or k.sib_dev)

    day = lax.broadcasted_iota(jnp.int32, (1, SEQ), 1).astype(f32)
    s_at = lax.broadcasted_iota(jnp.int32, (SEQ, SEQ), 0)
    t_at = lax.broadcasted_iota(jnp.int32, (SEQ, SEQ), 1)
    valid = (lax.broadcasted_iota(jnp.int32, (1, SEQ), 1) < m.length[0]).astype(f32)

    def loaded(name):
        place = OPERANDS.index(name)
        return pltpu.make_async_copy(getattr(m, "from_" + name), getattr(m, name), m.load.at[place])

    def load():
        for name in OPERANDS[2:] + OPERANDS[:2]:
            loaded(name).start()

    def own_blocks():
        for name in OPERANDS[2:]:
            loaded(name).wait()
        here = in_all(k.me, k.z)
        for place, (first, second) in enumerate(((m.iq, m.ik), (m.iv, m.io))):
            pair = jnp.concatenate([first[...].astype(f32), second[...].astype(f32)], axis=0)
            m.qk[here, 48 * place : 48 * place + 48] = pair.astype(bf16)
        m.sm[here] = jnp.zeros((16, 128), f32)
        m.sm[here, 0:15, 0:24] = m.ivec[...].astype(f32)
        m.sm[here, 15:16, 0:UNITS] = m.ibias[...].astype(f32)
        m.ff[in_pair(k.me, k.z), 0:UNITS] = m.ifc1[...]
        m.ff[in_pair(k.me, k.z), UNITS : 2 * UNITS] = m.ifc2[...]

    def half_at(who, half):
        return rows_at(who, half * part_rows, part_rows)

    def send_halves(place, buf, who, device=None):
        for half in range(2):
            ref = buf.at[half_at(who, half)]
            swap(place, ref, ref, device)

    def own_cotangent():
        loaded("cot").wait()
        for half in range(2):
            m.ct[half_at("o", half)] = m.cot[half * part_rows : (half + 1) * part_rows]
        send_halves(0, m.ct, "o")
        send_halves(1, m.ct, "o", k.x_dev)

    def pass_ct():
        k.arrive(m.nm, m.e_r.at[1])
        send_halves(2, m.ct, "x")

    def norm1():
        loaded("tok").wait()

        def rows_of(start, step):
            rows = pl.ds(start, step)
            tokens = m.tok[rows].astype(f32)
            centred = tokens - jnp.mean(tokens, axis=1, keepdims=True)
            inverse = lax.rsqrt(jnp.mean(centred * centred, axis=1, keepdims=True) + EPSILON)
            m.s1[rows] = centred * inverse
            m.i1[rows] = jnp.broadcast_to(inverse, (step, 128))

        row_loop(SEQ, 32, rows_of)

    def vectors():
        total = jnp.zeros((16, WIDTH), f32)
        for wide in range(8):
            part = jnp.zeros((16, 128), f32)
            for zs in range(depth):
                tile = m.sm[wide * depth + zs]
                part = part + (pltpu.roll(tile, 24 * zs, 1) if zs else tile)
            padded = jnp.concatenate([part, jnp.zeros((16, WIDTH - 128), f32)], axis=1)
            total = total + (pltpu.roll(padded, 96 * wide, 1) if wide else padded)
        m.vec[...] = total
        m.vecc[...] = jnp.transpose(jnp.concatenate([total, jnp.zeros((112, WIDTH), f32)], axis=0))
        for y in range(2):
            line = jnp.zeros((16, UNITS * depth), f32)
            for zs in range(depth):
                tile = m.sm[in_all(y * 2 + k.x, zs)]
                tile = jnp.concatenate([tile, jnp.zeros((16, UNITS * depth - 128), f32)], axis=1)
                line = line + (pltpu.roll(tile, UNITS * zs, 1) if zs else tile)
            m.bias[y] = line[8:16]

    def head_kernel(h):
        rows = head_rows(h)
        decays = jnp.exp(-m.vecc[rows, 10:11] * day)
        m.ex[rows] = decays
        line = jnp.sum(m.vecc[rows, 9:10] * decays, axis=0, keepdims=True) * (1.0 / STATE)
        matrix = pltpu.roll(jnp.broadcast_to(line, (SEQ, SEQ)), 0, 1, stride=1, stride_axis=0)
        m.tt[h] = jnp.where(t_at >= s_at, matrix, 0.0)

    def mixer_kernels():
        def four_heads(i, carry):
            for part in range(4):
                head_kernel(4 * i + part)
            return carry

        lax.fori_loop(0, HEADS // 4, four_heads, 0)

    def gain1():
        def rows_of(start, step):
            rows = pl.ds(start, step)
            m.nm[rows] = (m.s1[rows] * m.vec[0:1] + m.vec[1:2]).astype(bf16)

        row_loop(SEQ, 32, rows_of)
        m.nmt[...] = jnp.transpose(m.nm[...])

    def unpack(place):
        first, second = ((m.wq, m.wk), (m.wv, m.wo))[place]

        def rows_of(w, carry):
            rows = pl.ds(pl.multiple_of(w * 96, 96), 96)
            pair = m.qk[pl.ds(w * depth, depth), 48 * place : 48 * place + 48, :].astype(f32)
            first[rows] = pair[:, :24].reshape(96, WIDTH).astype(bf16)
            second[rows] = pair[:, 24:].reshape(96, WIDTH).astype(bf16)
            return carry

        lax.fori_loop(0, 8, rows_of, 0, unroll=4)

    def project_qk():
        m.qt[...] = jnp.transpose(dg(m.nm[...], m.wq[...], 1, 0) + m.vec[2:3]).astype(bf16)
        m.krt[...] = jnp.transpose(dg(m.nm[...], m.wk[...], 1, 0) + m.vec[3:4])

    def project_v():
        m.vt[...] = (jnp.transpose(dg(m.nm[...], m.wv[...], 1, 0) + m.vec[4:5]) * valid).astype(bf16)

    def score_head(h):
        rows = head_rows(h)
        raw = m.krt[rows]
        summed = raw * m.vecc[rows, 5:6]
        for j in range(1, 4):
            summed = summed + lane_shift(raw, j, False) * m.vecc[rows, 5 + j : 6 + j]
        keys = (summed * valid).astype(bf16)
        m.kt[rows] = keys
        scores = dg(keys, m.qt[rows], 0, 0) * (1.0 / HEAD_SIZE)
        m.wt[h] = (scores * m.tt[h]).astype(bf16)

    def mix_head(h):
        rows = head_rows(h)
        m.mt[rows] = (dg(m.vt[rows], m.wt[h], 1, 0) * valid).astype(bf16)

    def hidden():
        m.hid[...] = dg(m.mt[...], m.wo[...], 0, 0)

    def norm2():
        def rows_of(start, step):
            rows = pl.ds(start, step)
            hidden = m.tok[rows].astype(f32) + m.hid[rows] + m.vec[11:12]
            m.hid[rows] = hidden
            centred = hidden - jnp.mean(hidden, axis=1, keepdims=True)
            inverse = lax.rsqrt(jnp.mean(centred * centred, axis=1, keepdims=True) + EPSILON)
            scaled = centred * inverse
            m.s2[rows] = scaled
            m.i2[rows] = jnp.broadcast_to(inverse, (step, 128))
            m.n2[rows_at("o", start, step)] = (scaled * m.vec[12:13] + m.vec[13:14]).astype(bf16)

        row_loop(SEQ, 32, rows_of)
        send_halves(3, m.n2, "o")
        for half in range(2):
            ref = m.n2.at[half_at("o", half)]
            swap(4 + half, ref, ref, k.x_dev)

    def pass_n2(half):
        ref = m.n2.at[half_at("x", half)]
        k.arrive(ref, m.e_r.at[4 + half])
        swap(6 + half, ref, ref)

    def sibling_rows():
        k.arrive(m.nm, m.e_r.at[0])
        k.arrive(m.nm, m.e_r.at[3])

    def diagonal_rows(half):
        if half == 0:
            k.arrive(m.nm, m.e_r.at[2])
        k.arrive(m.n2.at[half_at("d", half)], m.e_r.at[6 + half])

    def finish_rows(pieces):
        def finish(ref, more):
            value = ref[...].astype(f32)
            for target, (low, high), (first, last) in pieces:
                part = value[first:last]
                target[low:high] = target[low:high] + part if more else part

        return finish

    finish_feed = finish_rows(((m.gfc1, (0, UNITS), (0, UNITS)), (m.gfc2, (0, FIRST - UNITS), (UNITS, FIRST))))
    finish_last = finish_rows(((m.gfc2, (FIRST - UNITS, UNITS), (0, 2 * UNITS - FIRST)),))
    finish_qk = finish_rows(((m.gwq, (0, 24), (0, 24)), (m.gwk, (0, 24), (24, 48))))
    finish_vo = finish_rows(((m.gwv, (0, 24), (0, 24)), (m.gwo, (0, 24), (24, 48))))

    def finish_small(ref, more):
        m.gsmall[...] = m.gsmall[...] + ref[...] if more else ref[...]

    steps = {}
    steps |= gather_z_first(k, "S", m.sm, in_all, 0, 16, m.gt_s, m.gt_r)
    steps |= gather_z_first(k, "Q", m.qk, in_all, 0, 48, m.gq_s, m.gq_r)
    steps |= gather_z_first(k, "V", m.qk, in_all, 48, 48, m.gv_s, m.gv_r)
    steps |= gather_pair_z_first(k, "F", m.ff, in_pair, 0, FIRST, m.gb_s, m.gb_r)
    steps |= gather_pair_z_last(k, "L", m.ff, in_pair, FIRST, 2 * UNITS - FIRST, m.gc_s, m.gc_r)
    slots = (m.rby, m.rbu, m.rbd)
    steps |= scatter_pair_z_last(k, "f", m.gff, in_pair, 0, FIRST, slots, m.sb_s, m.sb_r, finish_feed)
    slots = (m.rcy, m.rcu, m.rcd)
    steps |= scatter_pair_z_first(k, "l", m.gff, in_pair, FIRST, 2 * UNITS - FIRST, slots, m.sc_s, m.sc_r, finish_last)
    slots = (m.rqdx, m.rqdy, m.rqxy, m.rqu, m.rqd)
    steps |= scatter_z_last(k, "q", m.qk, in_all, 0, 48, slots, m.sq_s, m.sq_r, finish_qk)
    slots = (m.rvdx, m.rvdy, m.rvxy, m.rvu, m.rvd)
    steps |= scatter_z_last(k, "v", m.qk, in_all, 48, 48, slots, m.sv_s, m.sv_r, finish_vo)
    slots = (m.rtdx, m.rtdy, m.rtxy, m.rtu, m.rtd)
    steps |= scatter_z_last(k, "s", m.gs, in_all, 0, 16, slots, m.st_s, m.st_r, finish_small)

    root = math.sqrt(2.0 / math.pi)
    chunk = UNITS * depth
    ys = (k.y, 1 - k.y)

    def feed(which, half=None):
        blocks = pl.ds(ys[which] * depth, depth)
        start, extent = (k.x * (2 * SEQ), 2 * SEQ) if half is None else ((1 - k.x) * (2 * SEQ) + half * SEQ, SEQ)
        rows = pl.ds(pl.multiple_of(start, SEQ), extent)
        fc1 = m.ff[blocks, 0:UNITS, :].reshape(chunk, WIDTH)
        fc2 = m.ff[blocks, UNITS : 2 * UNITS, :].reshape(chunk, WIDTH)
        pre = dg(m.n2[rows], fc1, 1, 1) + m.bias[ys[which], 7:8]
        square = pre * pre
        tanh = jnp.tanh(root * pre * (1.0 + 0.044715 * square))
        half = 0.5 * (1.0 + tanh)
        slope = half + 0.5 * pre * (1.0 - tanh * tanh) * (root * (1.0 + 3 * 0.044715 * square))
        activated = (pre * half).astype(bf16)
        grad_pre = (dg(m.ct[rows], fc2, 1, 1) * slope).astype(bf16)
        m.act[which, rows] = activated
        m.dp[which, rows] = grad_pre
        if which == 0:
            m.outp[rows] = dg(activated, fc2, 1, 0)
            m.dn2[rows] = dg(grad_pre, fc1, 1, 0)
        else:
            m.outp[rows] += dg(activated, fc2, 1, 0)
            m.dn2[rows] += dg(grad_pre, fc1, 1, 0)

    def to_sibling():
        for half in range(2):
            swap(8, m.dn2.at[half_at("s", half)], m.dn2s.at[half_rows(half)])
        for half in range(2):
            swap(9, m.outp.at[half_at("s", half)], m.outs.at[half_rows(half)])

    def half_rows(half):
        return pl.ds(half * (SEQ // 2), SEQ // 2)

    def to_diagonal(half):
        swap(10 + half, m.dn2.at[half_at("d", half)], m.dn2b.at[half_rows(half)])

    def to_x(half):
        rows = half_rows(half)
        k.arrive(m.dn2b.at[rows], m.e_r.at[10 + half])
        m.dn2x[0, rows] = (m.dn2[half_at("x", half)] + m.dn2b[rows]).astype(bf16)
        swap(13 + half, m.dn2x.at[0, rows], m.dn2x.at[1, rows], k.x_dev)

    def out_to_diagonal():
        for half in range(2):
            swap(12, m.outp.at[half_at("d", half)], m.outb.at[half_rows(half)])

    def out_to_x():
        k.arrive(m.outb, m.e_r.at[12])
        for half in range(2):
            rows = half_rows(half)
            m.outx[0, rows] = (m.outp[half_at("x", half)] + m.outb[rows]).astype(bf16)
        swap(15, m.outx.at[0], m.outx.at[1], k.x_dev)

    def feed_grads(which):
        blocks = pl.ds(ys[which] * depth, depth)
        pre = m.dp[which]
        m.gff[blocks, 0:UNITS] = dg(pre, m.n2[...], 0, 0).astype(bf16).reshape(depth, UNITS, WIDTH)
        m.gff[blocks, UNITS : 2 * UNITS] = (
            dg(m.act[which], m.ct[...], 0, 0).astype(bf16).reshape(depth, UNITS, WIDTH)
        )
        sums = jnp.sum(pre.astype(f32), axis=0, keepdims=True)
        lane = lax.broadcasted_iota(jnp.int32, (1, 128), 1)
        for zs in range(depth):
            line = (pltpu.roll(sums, chunk - UNITS * zs, 1) if zs else sums)[:, :128]
            m.gbias[ys[which] * depth + zs] = jnp.broadcast_to(jnp.where(lane < UNITS, line, 0.0), (8, 128))

    def back2(half):
        if half == 0:
            m.gvec[...] = jnp.zeros((16, WIDTH), f32)
            k.arrive(m.dn2s, m.e_r.at[8])
        k.arrive(m.dn2x.at[1, half_rows(half)], m.e_r.at[13 + half])

        def rows_of(start, step):
            rows = pl.ds(start, step)
            grad_normed = m.dn2[rows_at("o", start, step)] + m.dn2s[rows] + m.dn2x[1, rows].astype(f32)
            scaled = m.s2[rows]
            grad_in = grad_normed * m.vec[12:13]
            first = jnp.mean(grad_in, axis=1, keepdims=True)
            second = jnp.mean(grad_in * scaled, axis=1, keepdims=True)
            top = m.cot[rows].astype(f32)
            grad_hidden = top + m.i2[rows, 0:1] * (grad_in - first - scaled * second)
            m.s2[rows] = grad_hidden
            rounded = grad_hidden.astype(bf16)
            m.da[rows] = rounded
            m.gvec[11:12] += jnp.sum(rounded.astype(f32), axis=0, keepdims=True)
            m.gvec[12:13] += jnp.sum(grad_normed * scaled, axis=0, keepdims=True)
            m.gvec[13:14] += jnp.sum(grad_normed, axis=0, keepdims=True)
            m.gvec[14:15] += jnp.sum(top, axis=0, keepdims=True)

        row_loop(SEQ // 2, 32, rows_of, half * (SEQ // 2))

    def grad_mixed():
        m.dmt[...] = (jnp.transpose(dg(m.da[...], m.wo[...], 1, 1)) * valid).astype(bf16)

    def back_v_head(h):
        rows = head_rows(h)
        m.dvt[rows] = (dg(m.dmt[rows], m.wt[h], 1, 1) * valid).astype(bf16)

    def back_head(h):
        rows = head_rows(h)
        grad_scores = (dg(m.vt[rows], m.dmt[rows], 0, 0) * m.tt[h]).astype(bf16)
        m.dqt[rows] = (dg(m.kt[rows], grad_scores, 1, 0) * (1.0 / HEAD_SIZE)).astype(bf16)
        grad_keys = dg(m.qt[rows], grad_scores, 1, 1) * (1.0 / HEAD_SIZE) * valid
        m.dk[rows] = grad_keys
        grad_raw = grad_keys * m.vecc[rows, 5:6]
        for j in range(1, 4):
            grad_raw = grad_raw + lane_shift(grad_keys, j, True) * m.vecc[rows, 5 + j : 6 + j]
        m.dkt[rows] = grad_raw.astype(bf16)

    def pack(pair, which):
        y = ys[1 - which]
        rows = pl.ds(pl.multiple_of(y * 384, 384), 384)
        if pair == 0:
            grads = (dg(m.nmt[rows], m.dqt[...], 1, 1), dg(m.nmt[rows], m.dkt[...], 1, 1))
        else:
            grads = (dg(m.nmt[rows], m.dvt[...], 1, 1), dg(m.mt[rows], m.da[...], 1, 0))
        both_grads = jnp.concatenate([grad.reshape(4 * depth, 24, WIDTH) for grad in grads], axis=1)
        low = pl.ds(48 * pair, 48)
        m.qk[pl.ds(y * 4 * depth, 4 * depth), low, :] = both_grads.astype(bf16)
        for place in (2 * which, 2 * which + 1):
            yx = (k.ds, k.ys, k.xs, k.me)[place]
            source, target = pl.ds(in_all_sib(yx, 0), depth), pl.ds(yx * depth, depth)
            swap(16 + 4 * pair + place, m.qk.at[source, low], m.sr.at[target, low])

    def grad_normed():
        m.dn[...] = jnp.transpose(
            dg(m.wq[...], m.dqt[...], 1, 0) + dg(m.wk[...], m.dkt[...], 1, 0) + dg(m.wv[...], m.dvt[...], 1, 0)
        )

    def back1():
        def rows_of(start, step):
            rows = pl.ds(start, step)
            grad_out, scaled = m.dn[rows], m.s1[rows]
            grad_in = grad_out * m.vec[0:1]
            first = jnp.mean(grad_in, axis=1, keepdims=True)
            second = jnp.mean(grad_in * scaled, axis=1, keepdims=True)
            m.dinp[rows] = (m.s2[rows] + m.i1[rows, 0:1] * (grad_in - first - scaled * second)).astype(bf16)
            m.gvec[0:1] += jnp.sum(grad_out * scaled, axis=0, keepdims=True)
            m.gvec[1:2] += jnp.sum(grad_out, axis=0, keepdims=True)

        row_loop(SEQ, 32, rows_of)

    def core_sum(pair, place):
        yx, low = (k.ds, k.ys, k.xs, k.me)[place], pl.ds(48 * pair, 48)
        k.arrive(m.sr.at[pl.ds(yx * depth, depth), low], m.e_r.at[16 + 4 * pair + place])
        for zs in range(depth):
            add_into(m.qk.at[in_all(yx, zs), low], m.sr.at[yx * depth + zs, low])

    def flip():
        turn = (s_at + t_at == SEQ - 1).astype(bf16)
        m.kft[...] = dg(m.kt[...], turn, 1, 0).astype(bf16)
        m.vft[...] = dg(m.vt[...], turn, 1, 0).astype(bf16)

    def kernel_head(h):
        rows = head_rows(h)
        scores = dg(m.kft[rows], m.qt[rows], 0, 0) * (1.0 / HEAD_SIZE)
        grad_weights = dg(m.vft[rows], m.dmt[rows], 0, 0)
        product = jnp.where(s_at + t_at >= SEQ - 1, scores * grad_weights, 0.0)
        lined = pltpu.roll(product, 1, 1, stride=1, stride_axis=0)
        grad_kernel = jnp.sum(lined, axis=0, keepdims=True) * (1.0 / STATE)
        part = m.ex[rows] * grad_kernel
        at = lax.broadcasted_iota(jnp.int32, (HEAD_SIZE, 128), 1)
        grad_rate = -m.vecc[rows, 9:10] * jnp.sum(part * day, axis=1, keepdims=True)
        sums = jnp.where(at == 9, jnp.sum(part, axis=1, keepdims=True), 0.0)
        sums = jnp.where(at == 10, grad_rate, sums)
        raw, grad_keys = m.krt[rows], m.dk[rows]
        for j in range(4):
            tap = jnp.sum(grad_keys * (lane_shift(raw, j, False) if j else raw), axis=1, keepdims=True)
            sums = jnp.where(at == 5 + j, tap, sums)
        for place, value in ((2, m.dqt), (3, m.dkt), (4, m.dvt)):
            sums = jnp.where(at == place, jnp.sum(value[rows].astype(f32), axis=1, keepdims=True), sums)
        m.colsum[rows] = sums

    def vector_tiles():
        grads = m.gvec[...] + jnp.transpose(m.colsum[...])[0:16]
        row_at = lax.broadcasted_iota(jnp.int32, (16, 128), 0)
        lane_at = lax.broadcasted_iota(jnp.int32, (16, 128), 1)
        for wide in range(8):
            turned = (pltpu.roll(grads, WIDTH - 96 * wide, 1) if wide else grads)[:, :128]
            for zs in range(depth):
                tile = pltpu.roll(turned, 128 - 24 * zs, 1) if zs else turned
                tile = jnp.where((lane_at < 24) & (row_at < 15), tile, 0.0)
                own = jnp.concatenate([jnp.zeros((8, 128), f32), m.gbias[(wide // 4) * depth + zs]], axis=0)
                mine = (row_at == 15) & (core == wide % 2) & (k.x == wide // 2 % 2)
                m.gs[wide * depth + zs] = jnp.where(mine, own, tile)
        for yx in range(4):
            swap(24, m.gs.at[pl.ds(in_all_sib(yx, 0), depth)], m.srs.at[pl.ds(yx * depth, depth)])

    def small_sums():
        k.arrive(m.srs, m.e_r.at[24])
        for yx in range(4):
            for zs in range(depth):
                add_into(m.gs.at[in_all(yx, zs)], m.srs.at[yx * depth + zs])

    def finish_out():
        def rows_of(start, step):
            rows = pl.ds(start, step)
            others = m.outs[rows] + m.outx[1, rows].astype(f32)
            m.out[rows] = (m.hid[rows] + (m.outp[rows_at("o", start, step)] + others) + m.vec[14:15]).astype(bf16)

        k.arrive(m.outs, m.e_r.at[9])
        k.arrive(m.outx.at[1], m.e_r.at[15])
        row_loop(SEQ, 32, rows_of)

    def all_sent():
        for group in "SFLflqvs":
            next(steps[group + "."])
        extents = (m.qk.at[:, pl.ds(0, 80)], m.qk, m.srs)
        for place, extent in enumerate(extents):
            k.left(extent, m.e_s.at[place])

    compute = [
        load, own_blocks, k.barrier, own_cotangent, norm1, pass_ct, vectors, mixer_kernels, gain1, project_qk,
        project_v, hidden, norm2, sibling_rows, to_sibling, out_to_diagonal, out_to_x, grad_mixed,
        grad_normed, back1, flip, vector_tiles, small_sums, finish_out, all_sent,
    ]
    for which in range(2):
        compute.append(partial(unpack, which))
        compute.append(partial(heads, range(6 * which, 6 * which + 6), score_head))
        compute.append(partial(heads, range(6 * which, 6 * which + 6), mix_head))
        compute.append(partial(heads, range(6 * which, 6 * which + 6), back_head))
        compute.append(partial(heads, range(6 * which, 6 * which + 6), back_v_head))
        compute.append(partial(feed, which))
        for half in range(2):
            compute.append(partial(feed, which, half))
        compute.append(partial(feed_grads, which))
        compute.append(partial(pass_n2, which))
        compute.append(partial(diagonal_rows, which))
        compute.append(partial(to_diagonal, which))
        compute.append(partial(to_x, which))
        compute.append(partial(back2, which))
        compute.append(partial(pack, 0, which))
        compute.append(partial(pack, 1, which))
    for which in range(4):
        compute.append(partial(heads, range(3 * which, 3 * which + 3), kernel_head))
        compute.append(partial(core_sum, 0, which))
        compute.append(partial(core_sum, 1, which))
    everything = [*compute, *(partial(next, step) for step in steps.values())]
    for step in PLAN:
        everything[step]()


def results_kernel(*refs):
    sources, tile, targets, bias, vectors = refs[:8], refs[8], refs[9:17], refs[17], refs[18]
    for source, target in zip(sources, targets, strict=True):
        target[...] = source[...]
    bias[...] = tile[15:16, :UNITS]
    vectors[...] = tile[0:15, 0:24]


def on_device_fast(
    tokens, lengths, cotangent, w_query, w_key, w_value, w_out, w_fc1, w_fc2, fc1_bias, vectors
):
    depth = lax.axis_size("narrow")
    scratch = []
    for entry in scratch_of(depth).values():
        scratch.append(pltpu.SemaphoreType.DMA((entry,)) if isinstance(entry, int) else pltpu.VMEM(*entry))
    in_vmem = pl.BlockSpec(memory_space=pltpu.VMEM)
    in_smem = pl.BlockSpec(memory_space=pltpu.SMEM)
    shape = jax.ShapeDtypeStruct
    got = pl.pallas_call(
        partial(layer_kernel, depth),
        out_shape=[pltpu.VMEM((SEQ, WIDTH), bf16)] * 2
        + [pltpu.VMEM((24, WIDTH), f32)] * 4
        + [pltpu.VMEM((UNITS, WIDTH), f32)] * 2
        + [pltpu.VMEM((16, 128), f32)],
        in_specs=[in_smem] + [pl.BlockSpec(memory_space=pl.ANY)] * 10,
        out_specs=[in_vmem] * 9,
        scratch_shapes=scratch,
        compiler_params=pltpu.CompilerParams(
            collective_id=0, has_side_effects=True, vmem_limit_bytes=61 * 2**20
        ),
        name="h3_layer",
    )(
        lengths, tokens, cotangent, w_query, w_key, w_value, w_out, w_fc1.T, w_fc2, fc1_bias[None], vectors
    )
    results = pl.pallas_call(
        results_kernel,
        out_shape=[shape(x.shape, x.dtype) for x in got[:8]] + [shape((1, UNITS), f32), shape((15, 24), f32)],
        in_specs=[in_vmem] * 9,
        out_specs=[in_vmem] * 10,
        name="results",
    )(*[pltpu.with_memory_space_constraint(x, pltpu.VMEM) for x in got])
    out, grad_in, g_query, g_key, g_value, g_out, g_fc1, g_fc2, g_bias, g_vectors = results
    return out, grad_in, g_query, g_key, g_value, g_out, g_fc1.T, g_fc2, g_bias.reshape(-1), g_vectors


def fits(mesh):
    return mesh.shape["wide"] == 8 and mesh.shape["narrow"] == 4


def solution(mesh):
    placed = (
        P(("wide", "narrow"), None),
        P(("wide", "narrow")),
        P(("wide", "narrow"), None),
        P(("wide", "narrow"), None),
        P(("wide", "narrow"), None),
        P(("wide", "narrow"), None),
        P(("wide", "narrow"), None),
        P(None, ("wide", "narrow")),
        P(("wide", "narrow"), None),
        P(("wide", "narrow")),
        P(None, ("wide", "narrow")),
    )
    return jax.shard_map(
        on_device_fast if fits(mesh) else on_device,
        mesh=mesh,
        in_specs=placed,
        out_specs=(
            P(("wide", "narrow"), None),
            P(("wide", "narrow"), None),
            P(("wide", "narrow"), None),
            P(("wide", "narrow"), None),
            P(("wide", "narrow"), None),
            P(("wide", "narrow"), None),
            P(None, ("wide", "narrow")),
            P(("wide", "narrow"), None),
            P(("wide", "narrow")),
            P(None, ("wide", "narrow")),
        ),
        check_vma=False,
    )
```
